32 devices in a mesh: rep: 4 (over x, core), shard: 8 (over z, y).
Axes of the slice: x: 2, y: 2, z: 4, core: 2. Of those that a mesh axis runs over, the one named last changes fastest.
Arguments:
- inputs: bfloat16 [6144, 2048], P(('rep', 'shard')), may hold values from -6 to 6
- attn_gain: bfloat16 [2048], P('shard'), may hold values from 0.25 to 1.75
- in_proj: bfloat16 [2048, 6144], P('shard'), may hold values from -0.125 to 0.125
- query_gain: bfloat16 [2048], P('shard'), may hold values from 0.25 to 1.75
- key_gain: bfloat16 [2048], P('shard'), may hold values from 0.25 to 1.75
- out_proj: bfloat16 [2048, 2048], P('shard'), may hold values from -0.5 to 0.5
- ffn_gain: bfloat16 [2048], P('shard'), may hold values from 0.25 to 1.75
- router_weight: bfloat16 [2048, 32], P('shard'), may hold values from -0.0625 to 0.0625
- gate_weight: bfloat16 [32, 2048, 1024], P('shard'), may hold values from -0.125 to 0.125
- up_weight: bfloat16 [32, 2048, 1024], P('shard'), may hold values from -0.125 to 0.125
- down_weight: bfloat16 [32, 1024, 2048], P('shard'), may hold values from -3 to 3
- routes: int32 [6144, 8], P(('rep', 'shard')), may hold values from 0 to 31, all different within a row; in each aligned block of 192 rows (0 to 191, 192 to 383, ...) at most 96 rows name the same one
- priority: int32 [32, 1536], P(('rep', 'shard')), may hold values from 0 to 1535, each once within a row
- segments: int32 [32, 192], P(('rep', 'shard')), may hold values from 0 to 2, never falling along the last dimension, each value on 1 to 120 neighbouring positions
- grad_out: bfloat16 [6144, 2048], P(('rep', 'shard')), may hold values from -6 to 6
Outputs:
- outputs: bfloat16 [6144, 2048], P(('rep', 'shard'))
- grad_inputs: bfloat16 [6144, 2048], P(('rep', 'shard'))
- grad_attn_gain: float32 [2048], P('shard')
- grad_in_proj: float32 [2048, 6144], P('shard')
- grad_query_gain: float32 [2048], P('shard')
- grad_key_gain: float32 [2048], P('shard')
- grad_out_proj: float32 [2048, 2048], P('shard')
- grad_ffn_gain: float32 [2048], P('shard')
- grad_router: float32 [2048, 32], P('shard')
- grad_gate: float32 [32, 2048, 1024], P('shard')
- grad_up: float32 [32, 2048, 1024], P('shard')
- grad_down: float32 [32, 1024, 2048], P('shard')
The draws below stay inside these ranges and needn't reach their ends.
Inputs may be any that keep to these rules, and one draw needn't show every extreme that they name: `routes`: each row names 8 different experts. Among the rows of one sequence no expert is named more than 96 times, and in some sequence some expert exactly 96 times. `priority`: each row is a permutation. `segments`: each row never falls and holds all 3 documents, each 1 to 120 positions long, one exactly 120.
All inputs are finite; a program needn't handle non-finite values.
Results may differ from the reference program's by a relative error of at most 0.02.
Values may be sent and summed in bfloat16 or wider, within the bound.
No kernel may reach another device: no remote copies, remote signals or barrier semaphores. Data moves between devices by JAX's collectives and lax.ppermute only.
A program may use at most 448 MiB of HBM per device.

```python
import math
import jax
import jax.numpy as jnp
import numpy as np
from jax import lax

D = 2048
HEADS = 16
HEAD_DIM = 128
FF = 1024
TOP = 8
EXPERTS = 32
TOK_DEV = 192
SEQS = 32
TOKENS = 6144
MOST = 96
CAP = 480
DOCS = 3
DOC_MAX = 120
N_REP = 4
N_SHARD = 8


def block_scale(own_key, dims, split, smallest, top_value):
    loudness, own = 1.0, jax.random.fold_in(own_key, 6)
    for position, parts in split:
        heights = jnp.exp(jax.random.uniform(jax.random.fold_in(own, position), (parts,), jnp.float32, smallest / len(split), top_value / len(split)))
        loudness = loudness * jnp.repeat(heights, dims[position] // parts).reshape([-1 if axis == position else 1 for axis in range(len(dims))])
    return loudness


def split_up(amount, total, most, skew):
    weights = [(1 << 20) // math.isqrt(grade ** skew) + 1 for grade in range(2, amount + 1)]
    surplus, given = total - most - (amount - 1), [1] * (amount - 1)
    while surplus > 0:
        candidates = [i for i in range(amount - 1) if given[i] < most]
        mass, budget = sum([weights[i] for i in candidates]), surplus
        for i in candidates:
            addition = min(most - given[i], max(1, budget * weights[i] // mass), surplus)
            given[i] = given[i] + addition
            surplus = surplus - addition
    return np.array([most] + given)


def uneven(rng, amount, total, reach, lean):
    if amount == 2:
        one = jax.random.randint(rng, (), max(1, total - reach), min(reach, total - 1) + 1)
        return jnp.stack([one, total - one])
    tallies = jnp.asarray(split_up(amount, total, reach, lean), jnp.int32)
    couples = (amount - 1) // 2
    donor, receiver = tallies[1:1 + 2 * couples:2], tallies[2:2 + 2 * couples:2]
    slack = jnp.minimum(donor - 1, reach - receiver)
    moved = jax.random.randint(jax.random.fold_in(rng, 1), (couples,), 0, 1 << 20) % (slack + 1)
    tallies = tallies.at[1:1 + 2 * couples:2].set(donor - moved).at[2:2 + 2 * couples:2].set(receiver + moved)
    return tallies[jax.random.permutation(jax.random.fold_in(rng, 2), amount)]


def shared_out(own_key, own, number, rows, amount, top, limit, slope):
    sequence = jax.random.permutation(own_key, amount)
    crowded, common = portions_of(amount, rows * top, limit, slope, True), portions_of(amount, rows * top, limit, slope, False)
    places = jnp.arange(amount)

    def named(tallies, turn):
        used = int((tallies > 0).sum())
        fixed = max(1, used // 4)
        shifted = fixed + (places - fixed + turn * (used - fixed)) % max(1, amount - fixed)
        return jnp.zeros((amount,), jnp.int32).at[sequence[jnp.where(places < fixed, places, shifted)]].set(jnp.asarray(tallies, jnp.int32))

    tallies = jnp.where(number % 4 == 0, named(crowded, number // 4), named(common, number - number // 4 - 1))
    mixed = jax.random.permutation(jax.random.fold_in(own, 3), amount)
    source_of, taker = mixed[0:amount // 2 * 2:2], mixed[1:amount // 2 * 2:2]
    room = jnp.minimum(tallies[source_of] - 1, limit - tallies[taker]) // 2
    room = jnp.where((source_of == sequence[0]) | (taker == sequence[0]) | (tallies[taker] == 0), 0, jnp.maximum(room, 0))
    shifted = jax.random.randint(jax.random.fold_in(own, 4), (amount // 2,), 0, 1 << 20) % (room + 1)
    tallies = tallies.at[source_of].add(-shifted).at[taker].add(shifted)
    items = jnp.searchsorted(jnp.cumsum(tallies), jnp.arange(rows * top), side="right").astype(jnp.int32)
    grid = items.reshape(top, rows).T
    grid = grid[jax.random.permutation(jax.random.fold_in(own, 1), rows)]
    turn = jax.random.randint(jax.random.fold_in(own, 2), (rows, 1), 0, top)
    return jnp.take_along_axis(grid, (jnp.arange(top)[None, :] + turn) % top, axis=1)


def portions_of(number_of, total, limit, lean, full):
    portions = [(1 << 20) // math.isqrt(rank ** lean) + 1 for rank in range(1, number_of + 1)]
    largest = limit if full else min(limit, max(-(-total // number_of), total * portions[0] // sum(portions)))
    least = 1 if total - largest >= number_of - 1 else 0
    given, spare = [largest] + [least] * (number_of - 1), total - largest - least * (number_of - 1)
    while spare > 0:
        movable = [i for i in range(1, number_of) if given[i] < largest] or [i for i in range(1, number_of) if given[i] < limit]
        mass, remaining = sum([portions[i] for i in movable]), spare
        for i in movable:
            addition = min(limit - given[i], max(1, remaining * portions[i] // mass), spare)
            given[i] = given[i] + addition
            spare = spare - addition
    return np.array(given)


def noise(own_key, shape, spread, limit, cuts=(), kind=jnp.bfloat16):
    values = jax.random.normal(own_key, shape, jnp.float32) * spread
    if len(cuts) > 0:
        values = block_scale(own_key, shape, cuts, -0.22, 0.18) * values
    return jnp.clip(values, min=-limit, max=limit).astype(kind)


def setup_inputs(seed: int = 0) -> dict:
    splits = jax.random.split(jax.random.key(seed), 16)
    inputs = noise(splits[0], (TOKENS, D), 1.0, 6.0, ((0, 32),))
    attn_gain = jnp.clip(1.0 + 0.15 * jax.random.normal(splits[1], (D,), jnp.float32), 0.25, 1.75).astype(jnp.bfloat16)
    in_proj = noise(splits[2], (D, 3 * D), D ** -0.5, 0.125, ((0, 8),))
    query_gain = jnp.clip(1.0 + 0.15 * jax.random.normal(splits[3], (D,), jnp.float32), 0.25, 1.75).astype(jnp.bfloat16)
    key_gain = jnp.clip(1.0 + 0.15 * jax.random.normal(splits[4], (D,), jnp.float32), 0.25, 1.75).astype(jnp.bfloat16)
    out_proj = noise(splits[5], (D, D), (D // 16) ** -0.5, 0.5, ((0, 8),))
    ffn_gain = jnp.clip(1.0 + 0.15 * jax.random.normal(splits[6], (D,), jnp.float32), 0.25, 1.75).astype(jnp.bfloat16)
    router_weight = noise(splits[7], (D, EXPERTS), (4 * D) ** -0.5, 0.0625, ((0, 8),))
    gate_weight = noise(splits[8], (EXPERTS, D, FF), D ** -0.5, 0.125, ((0, 8),))
    up_weight = noise(splits[9], (EXPERTS, D, FF), D ** -0.5, 0.125, ((0, 8),))
    down_weight = noise(splits[10], (EXPERTS, FF, D), (max(FF // 256, 1)) ** -0.5, 3.0, ((0, 8),))
    routes_keys = jax.random.split(jax.random.fold_in(splits[11], 1), TOKENS // TOK_DEV)
    routes_turns = jax.random.permutation(jax.random.fold_in(splits[11], 3), TOKENS // TOK_DEV)
    routes = jax.vmap(lambda own, number: shared_out(jax.random.fold_in(splits[11], 2), own, number, TOK_DEV, EXPERTS, TOP, MOST, 2))(routes_keys, routes_turns).reshape((TOKENS, TOP))
    priority = jax.vmap(lambda own: jax.random.permutation(own, TOK_DEV * TOP))(jax.random.split(splits[12], SEQS)).reshape((SEQS, TOK_DEV * TOP)).astype(jnp.int32)
    segments = jax.vmap(lambda own: jnp.searchsorted(jnp.cumsum(uneven(own, DOCS, TOK_DEV, DOC_MAX, 1)), jnp.arange(TOK_DEV), side="right"))(jax.random.split(splits[13], SEQS)).reshape((SEQS, TOK_DEV)).astype(jnp.int32)
    grad_out = noise(splits[14], (TOKENS, D), 1.0, 6.0, ((0, 32),))
    return dict(inputs=inputs, attn_gain=attn_gain, in_proj=in_proj, query_gain=query_gain, key_gain=key_gain, out_proj=out_proj, ffn_gain=ffn_gain, router_weight=router_weight, gate_weight=gate_weight, up_weight=up_weight, down_weight=down_weight, routes=routes, priority=priority, segments=segments, grad_out=grad_out)


norm_eps = 1e-05
rope_base = 10000.0
masked_score = -1e+30

@jax.custom_vjp
def low(v):
    return lax.optimization_barrier(v.astype(jnp.bfloat16)).astype(jnp.float32)

@jax.custom_vjp
def low_back(v):
    return v

def low_keep(v):
    return (low(v), None)

def low_pass(kept, grad):
    return (grad,)

def back_keep(v):
    return (v, None)

def back_low(kept, grad):
    return (low(grad),)
low.defvjp(low_keep, low_pass)
low_back.defvjp(back_keep, back_low)

def exact_dot(left, right):
    return jnp.dot(left, right, precision=lax.Precision.HIGHEST)

def rms_scale(values, gains):
    normed = values * lax.rsqrt(lax.optimization_barrier(jnp.mean(values * values, axis=-1, keepdims=True)) + norm_eps)
    return normed * gains

def rotary_tables(segment_row):
    length = segment_row.shape[0]
    places = jnp.arange(length, dtype=jnp.int32)
    starting = jnp.concatenate([jnp.ones((1,), jnp.int32), (segment_row[1:] != segment_row[:-1]).astype(jnp.int32)])
    first_place = lax.cummax(jnp.where(starting > 0, places, 0), axis=0)
    offsets = (places - first_place).astype(jnp.float32)
    halves = HEAD_DIM // 2
    inverse = rope_base ** (-2.0 * jnp.arange(halves, dtype=jnp.float32) / HEAD_DIM)
    angles = offsets[:, None] * inverse[None, :]
    angles = jnp.concatenate([angles, angles], axis=1)
    return (jnp.cos(angles), jnp.sin(angles))

def rotate(values, cos_table, sin_table):
    halves = values.shape[-1] // 2
    turned = jnp.concatenate([-values[..., halves:], values[..., :halves]], axis=-1)
    return values * cos_table[:, None, :] + turned * sin_table[:, None, :]

def query_key(raw_query, raw_key, query_scale, key_scale, cos_table, sin_table):
    row_count = raw_query.shape[0]
    normed_query = rms_scale(raw_query, query_scale).reshape(row_count, HEADS, HEAD_DIM)
    normed_key = rms_scale(raw_key, key_scale).reshape(row_count, HEADS, HEAD_DIM)
    return (rotate(normed_query, cos_table, sin_table), rotate(normed_key, cos_table, sin_table))

def softmax_rows(logits):
    highest = lax.optimization_barrier(jnp.max(logits, axis=-1, keepdims=True))
    raised = jnp.exp(logits - highest)
    return raised / lax.optimization_barrier(jnp.sum(raised, axis=-1, keepdims=True))

def attend(pieces):
    queries, key_vecs, value_vecs, segment_row = pieces
    length = segment_row.shape[0]
    places = jnp.arange(length, dtype=jnp.int32)
    allowed = (segment_row[:, None] == segment_row[None, :]) & (places[None, :] <= places[:, None])
    products = jnp.einsum('qhd,khd->hqk', queries, key_vecs, precision=lax.Precision.HIGHEST)
    scores = low_back(products * HEAD_DIM ** (-0.5))
    scores = jnp.where(allowed[None], scores, masked_score)
    weights = softmax_rows(scores)
    return jnp.einsum('hqk,khd->qhd', low(weights), value_vecs, precision=lax.Precision.HIGHEST)

def slot_tables(routes, priority):
    pair_count = TOK_DEV * TOP
    grouped_routes = routes.reshape(N_REP, N_SHARD, pair_count)
    grouped_order = priority.reshape(N_REP, N_SHARD, pair_count)
    ranked_expert = jnp.take_along_axis(grouped_routes, grouped_order, axis=2)
    labels = jnp.arange(EXPERTS, dtype=jnp.int32)
    matches = (ranked_expert[..., None] == labels).astype(jnp.int32)
    rank_in = lax.optimization_barrier(jnp.sum(jnp.cumsum(matches, axis=2, dtype=jnp.int32) * matches, axis=3, dtype=jnp.int32)) - 1
    counts = lax.optimization_barrier(jnp.sum(matches, axis=2, dtype=jnp.int32))
    base_slots = jnp.cumsum(counts, axis=1, dtype=jnp.int32) - counts
    slot_index = jnp.take_along_axis(base_slots, ranked_expert, axis=2) + rank_in
    group_ids = jnp.arange(N_REP, dtype=jnp.int32)[:, None, None]
    shard_ids = jnp.arange(N_SHARD, dtype=jnp.int32)[None, :, None]
    token_ids = (group_ids * N_SHARD + shard_ids) * TOK_DEV + grouped_order // TOP
    positions = jnp.where(slot_index < CAP, (ranked_expert * N_REP + group_ids) * CAP + slot_index, EXPERTS * N_REP * CAP)
    token_table = jnp.zeros((EXPERTS * N_REP * CAP,), jnp.int32).at[positions.reshape(-1)].set(token_ids.reshape(-1), mode='drop')
    live_marks = jnp.zeros((EXPERTS * N_REP * CAP,), jnp.int32).at[positions.reshape(-1)].set(1, mode='drop')
    return (token_table.reshape(EXPERTS, N_REP * CAP), live_marks.reshape(EXPERTS, N_REP * CAP) > 0)

def reference(inputs, attn_gain, in_proj, query_gain, key_gain, out_proj, ffn_gain, router_weight, gate_weight, up_weight, down_weight, routes, priority, segments, grad_out):
    token_table, live_table = slot_tables(routes, priority)
    cos_table, sin_table = jax.vmap(rotary_tables)(segments)
    cos_table = cos_table.reshape(TOKENS, HEAD_DIM)
    sin_table = sin_table.reshape(TOKENS, HEAD_DIM)
    float_args = tuple((operand.astype(jnp.float32) for operand in (inputs, attn_gain, in_proj, query_gain, key_gain, out_proj, ffn_gain, router_weight, gate_weight, up_weight, down_weight)))

    def forward(hidden_in, attn_scale, in_matrix, query_scale, key_scale, out_matrix, ffn_scale, router_matrix, gate_matrix, up_matrix, down_matrix):
        normed_in = low(rms_scale(hidden_in, attn_scale))
        projected = low_back(exact_dot(normed_in, in_matrix))
        raw_query = projected[:, :D]
        raw_key = projected[:, D:2 * D]
        raw_value = projected[:, 2 * D:]
        turned_query, turned_key = query_key(raw_query, raw_key, query_scale, key_scale, cos_table, sin_table)
        queries = low(turned_query).reshape(SEQS, TOK_DEV, HEADS, HEAD_DIM)
        key_vecs = low(turned_key).reshape(SEQS, TOK_DEV, HEADS, HEAD_DIM)
        value_vecs = low(raw_value).reshape(SEQS, TOK_DEV, HEADS, HEAD_DIM)
        mixed = lax.map(jax.checkpoint(attend), (queries, key_vecs, value_vecs, segments))
        attended = low_back(low(mixed.reshape(TOKENS, D)))
        residual = hidden_in + low_back(exact_dot(attended, out_matrix))
        normed_ffn = low(rms_scale(residual, ffn_scale))
        logits = low_back(exact_dot(normed_ffn, router_matrix))
        router_probs = softmax_rows(logits)

        def expert_step(running, pieces):
            gate_part, up_part, down_part, token_ids, live_ids, expert_id = pieces
            rows_in = low_back(jnp.where(live_ids[:, None], normed_ffn[token_ids], 0.0))
            gate_pre = low_back(exact_dot(rows_in, gate_part))
            up_pre = low_back(exact_dot(rows_in, up_part))
            act_low = low(jax.nn.silu(gate_pre) * up_pre)
            expert_out = low_back(low(exact_dot(act_low, down_part)))
            route_weight = jnp.where(live_ids, router_probs[token_ids, expert_id], 0.0)
            return (running.at[token_ids].add(route_weight[:, None] * expert_out), None)
        expert_ids = jnp.arange(EXPERTS, dtype=jnp.int32)
        routed, _ = lax.scan(jax.checkpoint(expert_step), jnp.zeros((TOKENS, D), jnp.float32), (gate_matrix, up_matrix, down_matrix, token_table, live_table, expert_ids))
        return residual + routed
    result, backward = jax.vjp(forward, *float_args)
    grads = backward(grad_out.astype(jnp.float32))
    return (result.astype(jnp.bfloat16), grads[0].astype(jnp.bfloat16), grads[1], grads[2], grads[3], grads[4], grads[5], grads[6], grads[7], grads[8], grads[9], grads[10])
```

```python
import jax
import jax.numpy as jnp
from jax import lax
from jax.sharding import PartitionSpec as P

HEADS = 16
HEAD_DIM = 128


norm_eps = 1e-05
rope_base = 10000.0
masked_score = -1e30


def rms_scale(values, gains):
    normed = values * lax.rsqrt(jnp.mean(values * values, axis=-1, keepdims=True) + norm_eps)
    return normed * gains


def rotary_tables(segment_row):
    length = segment_row.shape[0]
    places = jnp.arange(length, dtype=jnp.int32)
    starting = jnp.concatenate(
        [jnp.ones((1,), jnp.int32), (segment_row[1:] != segment_row[:-1]).astype(jnp.int32)]
    )
    first_place = lax.cummax(jnp.where(starting > 0, places, 0), axis=0)
    offsets = (places - first_place).astype(jnp.float32)
    halves = HEAD_DIM // 2
    inverse = rope_base ** (-2.0 * jnp.arange(halves, dtype=jnp.float32) / HEAD_DIM)
    angles = offsets[:, None] * inverse[None, :]
    angles = jnp.concatenate([angles, angles], axis=1)
    return (jnp.cos(angles), jnp.sin(angles))


def rotate(values, cos_table, sin_table):
    halves = values.shape[-1] // 2
    turned = jnp.concatenate([-values[..., halves:], values[..., :halves]], axis=-1)
    return values * cos_table[:, None, :] + turned * sin_table[:, None, :]


def query_key(raw_query, raw_key, query_scale, key_scale, cos_table, sin_table):
    row_count = raw_query.shape[0]
    normed_query = rms_scale(raw_query, query_scale).reshape(row_count, HEADS, HEAD_DIM)
    normed_key = rms_scale(raw_key, key_scale).reshape(row_count, HEADS, HEAD_DIM)
    return (rotate(normed_query, cos_table, sin_table), rotate(normed_key, cos_table, sin_table))


def softmax_rows(logits):
    highest = jnp.max(logits, axis=-1, keepdims=True)
    raised = jnp.exp(logits - highest)
    return raised / jnp.sum(raised, axis=-1, keepdims=True)


def swiglu(gate_pre, up_pre):
    return jax.nn.silu(gate_pre) * up_pre


def contract_rows(left_side, right_side):
    return lax.dot_general(
        left_side, right_side, (((0,), (0,)), ((), ())), preferred_element_type=jnp.float32
    )


def contract_cols(left_side, right_side):
    return lax.dot_general(
        left_side, right_side, (((1,), (1,)), ((), ())), preferred_element_type=jnp.float32
    )


def pick_rows(source_rows, row_picks):
    return jax.vmap(lambda expert_rows, picked: expert_rows[picked])(source_rows, row_picks)


def local(
    inputs,
    attn_gain,
    in_proj,
    query_gain,
    key_gain,
    out_proj,
    ffn_gain,
    router_weight,
    gate_weight,
    up_weight,
    down_weight,
    routes,
    priority,
    segments,
    grad_out,
):
    tokens = inputs.shape[0]
    model_width = inputs.shape[1]
    local_experts = gate_weight.shape[0]
    group_count = lax.axis_size("shard")
    my_index = lax.axis_index("shard")
    expert_count = local_experts * group_count
    route_count = routes.shape[1]
    pair_count = tokens * route_count
    capacity = 5 * pair_count * group_count // (4 * expert_count)
    send_most = 2 * pair_count // expert_count
    segment_row = segments[0]
    cos_table, sin_table = rotary_tables(segment_row)
    hidden_in = inputs.astype(jnp.float32)
    unit_rows = hidden_in * lax.rsqrt(
        jnp.mean(hidden_in * hidden_in, axis=-1, keepdims=True) + norm_eps
    )
    weight_piece = lax.all_gather(in_proj, "shard", axis=0, tiled=True)
    attn_piece = lax.all_gather(attn_gain, "shard", axis=0, tiled=True)
    query_piece = lax.all_gather(query_gain, "shard", axis=0, tiled=True)
    key_piece = lax.all_gather(key_gain, "shard", axis=0, tiled=True)
    scaled = (unit_rows * attn_piece.astype(jnp.float32)).astype(jnp.bfloat16)
    result = (
        jnp.dot(scaled, weight_piece, preferred_element_type=jnp.float32),
        attn_piece.astype(jnp.float32),
        query_piece.astype(jnp.float32),
        key_piece.astype(jnp.float32),
    )
    folded_in = result
    projected = folded_in[0]
    normed_attn, attn_norm_back = jax.vjp(rms_scale, hidden_in, folded_in[1])
    normed_low = normed_attn.astype(jnp.bfloat16)
    raw_query = projected[:, :model_width]
    raw_key = projected[:, model_width : 2 * model_width]
    raw_value = projected[:, 2 * model_width :]

    def rotated_pair(query_raw, key_raw, query_scale, key_scale):
        return query_key(query_raw, key_raw, query_scale, key_scale, cos_table, sin_table)

    (turned_query, turned_key), query_key_back = jax.vjp(
        rotated_pair, raw_query, raw_key, folded_in[2], folded_in[3]
    )
    query_low = turned_query.astype(jnp.bfloat16)
    key_low = turned_key.astype(jnp.bfloat16)
    value_low = raw_value.astype(jnp.bfloat16).reshape(tokens, HEADS, HEAD_DIM)
    places = jnp.arange(tokens, dtype=jnp.int32)
    allowed = (segment_row[:, None] == segment_row[None, :]) & (places[None, :] <= places[:, None])
    score_scale = HEAD_DIM ** (-0.5)

    def masked_scores(queries, key_vecs):
        products = jnp.einsum("qhd,khd->hqk", queries, key_vecs, preferred_element_type=jnp.float32)
        return jnp.where(allowed[None], products * score_scale, masked_score)

    scores = masked_scores(query_low, key_low)
    highest = jnp.max(scores, axis=-1, keepdims=True)
    raised = jnp.exp(scores - highest)
    totals = jnp.sum(raised, axis=-1, keepdims=True)
    attn_probs = raised / totals
    log_total = highest + jnp.log(totals)
    mixed = jnp.einsum(
        "hqk,khd->qhd",
        attn_probs.astype(jnp.bfloat16),
        value_low,
        preferred_element_type=jnp.float32,
    )
    attended = mixed.reshape(tokens, model_width).astype(jnp.bfloat16)
    weight_piece = lax.all_gather(out_proj, "shard", axis=0, tiled=True)
    ffn_piece = lax.all_gather(ffn_gain, "shard", axis=0, tiled=True)
    router_piece = lax.all_gather(router_weight, "shard", axis=0, tiled=True)
    result = (
        jnp.dot(attended, weight_piece, preferred_element_type=jnp.float32),
        ffn_piece.astype(jnp.float32),
        router_piece,
    )
    residual = hidden_in + result[0]
    router_full = result[2]
    normed_ffn, ffn_norm_back = jax.vjp(rms_scale, residual, result[1])
    ffn_low = normed_ffn.astype(jnp.bfloat16)
    logits = jnp.dot(ffn_low, router_full, preferred_element_type=jnp.float32)
    router_probs, router_back = jax.vjp(softmax_rows, logits)
    flat_routes = routes.reshape(pair_count)
    order_row = priority[0]
    ranked_expert = flat_routes[order_row]
    labels = jnp.arange(expert_count, dtype=jnp.int32)
    matches = (ranked_expert[:, None] == labels[None, :]).astype(jnp.int32)
    rank_in = (
        jnp.sum(jnp.cumsum(matches, axis=0, dtype=jnp.int32) * matches, axis=1, dtype=jnp.int32) - 1
    )
    counts = jnp.sum(matches, axis=0, dtype=jnp.int32)
    all_counts = lax.all_gather(counts[None, :], "shard", axis=0, tiled=True)
    base_slots = jnp.cumsum(all_counts, axis=0, dtype=jnp.int32) - all_counts
    my_bases = lax.dynamic_index_in_dim(base_slots, my_index, 0, keepdims=False)
    slot_index = jnp.sum(matches * my_bases[None, :], axis=1, dtype=jnp.int32) + rank_in
    cell_index = ranked_expert * send_most + rank_in
    inverse_order = (
        jnp.zeros((pair_count,), jnp.int32)
        .at[order_row]
        .set(jnp.arange(pair_count, dtype=jnp.int32))
    )
    pair_cell = cell_index[inverse_order].reshape(tokens, route_count)
    pair_keep = (
        (slot_index[inverse_order] < capacity).astype(jnp.float32).reshape(tokens, route_count)
    )
    cell_pair = jnp.zeros((expert_count * send_most,), jnp.int32).at[cell_index].set(order_row)
    cell_live = (jnp.arange(send_most, dtype=jnp.int32)[None, :] < counts[:, None]).reshape(
        expert_count * send_most
    )
    cell_token = cell_pair // route_count
    outgoing = jnp.where(cell_live[:, None], ffn_low[cell_token], 0).reshape(
        expert_count, send_most, model_width
    )
    arrived = lax.all_to_all(outgoing, "shard", split_axis=0, concat_axis=1, tiled=True)
    own_counts = lax.dynamic_slice_in_dim(all_counts, my_index * local_experts, local_experts, 1).T
    own_bases = lax.dynamic_slice_in_dim(base_slots, my_index * local_experts, local_experts, 1).T
    slot_ids = jnp.arange(capacity, dtype=jnp.int32)
    slot_ends = own_bases + own_counts
    source_ids = jnp.sum(
        (slot_ends[:, None, :] <= slot_ids[None, :, None]).astype(jnp.int32),
        axis=2,
        dtype=jnp.int32,
    )
    slot_filled = source_ids < group_count
    source_safe = jnp.minimum(source_ids, group_count - 1)
    slot_rows = (
        source_safe * send_most
        + slot_ids[None, :]
        - jnp.take_along_axis(own_bases, source_safe, axis=1)
    )
    slot_rows = jnp.where(slot_filled, slot_rows, 0)
    expert_in = jnp.where(slot_filled[..., None], pick_rows(arrived, slot_rows), 0)
    gate_pre = jnp.einsum(
        "ecd,edf->ecf", expert_in, gate_weight, preferred_element_type=jnp.float32
    )
    up_pre = jnp.einsum("ecd,edf->ecf", expert_in, up_weight, preferred_element_type=jnp.float32)
    activated, swiglu_back = jax.vjp(swiglu, gate_pre, up_pre)
    act_low = activated.astype(jnp.bfloat16)
    expert_out = jnp.einsum(
        "ecf,efd->ecd", act_low, down_weight, preferred_element_type=jnp.float32
    ).astype(jnp.bfloat16)
    cell_positions = jnp.arange(send_most, dtype=jnp.int32)
    cell_slot = own_bases[:, :, None] + cell_positions[None, None, :]
    cell_used = (cell_positions[None, None, :] < own_counts[:, :, None]) & (cell_slot < capacity)
    cell_slot = jnp.where(cell_used, cell_slot, 0).reshape(local_experts, group_count * send_most)
    cell_used = cell_used.reshape(local_experts, group_count * send_most)
    returning = jnp.where(cell_used[..., None], pick_rows(expert_out, cell_slot), 0)
    returned = lax.all_to_all(returning, "shard", split_axis=1, concat_axis=0, tiled=True).reshape(
        expert_count * send_most, model_width
    )
    pair_rows = returned[pair_cell].astype(jnp.float32)
    pair_weight = jnp.take_along_axis(router_probs, routes, axis=1) * pair_keep
    outputs = (residual + jnp.sum(pair_weight[..., None] * pair_rows, axis=1)).astype(jnp.bfloat16)
    cotangent = grad_out.astype(jnp.float32)
    grad_rows = (
        (pair_weight[..., None] * cotangent[:, None, :])
        .astype(jnp.bfloat16)
        .reshape(pair_count, model_width)
    )
    grad_pair_weight = jnp.sum(pair_rows * cotangent[:, None, :], axis=2) * pair_keep
    route_hits = (routes[..., None] == labels[None, None, :]).astype(jnp.float32)
    grad_router_probs = jnp.sum(grad_pair_weight[..., None] * route_hits, axis=1)
    (grad_logits,) = router_back(grad_router_probs)
    grad_logits_low = grad_logits.astype(jnp.bfloat16)
    outgoing_grad = jnp.where(cell_live[:, None], grad_rows[cell_pair], 0).reshape(
        expert_count, send_most, model_width
    )
    arrived_grad = lax.all_to_all(outgoing_grad, "shard", split_axis=0, concat_axis=1, tiled=True)
    grad_expert_out = jnp.where(slot_filled[..., None], pick_rows(arrived_grad, slot_rows), 0)
    grad_act = jnp.einsum(
        "ecd,efd->ecf", grad_expert_out, down_weight, preferred_element_type=jnp.float32
    )
    grad_down = jnp.einsum(
        "ecf,ecd->efd", act_low, grad_expert_out, preferred_element_type=jnp.float32
    )
    grad_gate_pre, grad_up_pre = swiglu_back(grad_act)
    gate_grad_low = grad_gate_pre.astype(jnp.bfloat16)
    up_grad_low = grad_up_pre.astype(jnp.bfloat16)
    grad_gate = jnp.einsum(
        "ecd,ecf->edf", expert_in, gate_grad_low, preferred_element_type=jnp.float32
    )
    grad_up = jnp.einsum("ecd,ecf->edf", expert_in, up_grad_low, preferred_element_type=jnp.float32)
    grad_expert_in = (
        jnp.einsum("ecf,edf->ecd", gate_grad_low, gate_weight, preferred_element_type=jnp.float32)
        + jnp.einsum("ecf,edf->ecd", up_grad_low, up_weight, preferred_element_type=jnp.float32)
    ).astype(jnp.bfloat16)
    returning_grad = jnp.where(cell_used[..., None], pick_rows(grad_expert_in, cell_slot), 0)
    returned_grad = lax.all_to_all(
        returning_grad, "shard", split_axis=1, concat_axis=0, tiled=True
    ).reshape(expert_count * send_most, model_width)
    grad_ffn_in = jnp.sum(returned_grad[pair_cell].astype(jnp.float32), axis=1) + contract_cols(
        grad_logits_low, router_full
    )
    grad_router_local = contract_rows(ffn_low, grad_logits_low)
    grad_residual_norm, grad_ffn_local = ffn_norm_back(grad_ffn_in)
    grad_residual = cotangent + grad_residual_norm
    residual_low = grad_residual.astype(jnp.bfloat16)
    grad_out_local = lax.psum_scatter(
        contract_rows(attended, residual_low).astype(jnp.bfloat16),
        "shard",
        scatter_dimension=0,
        tiled=True,
    )
    grad_attended = contract_cols(
        residual_low, lax.all_gather(out_proj, "shard", axis=0, tiled=True)
    )
    grad_mixed = grad_attended.astype(jnp.bfloat16).reshape(tokens, HEADS, HEAD_DIM)
    scores_again = masked_scores(query_low, key_low)
    probs_again = jnp.exp(scores_again - log_total)
    grad_probs = jnp.einsum(
        "qhd,khd->hqk", grad_mixed, value_low, preferred_element_type=jnp.float32
    )
    spread = jnp.sum(probs_again * grad_probs, axis=-1, keepdims=True)
    grad_scores = (probs_again * (grad_probs - spread)).astype(jnp.bfloat16)
    grad_query = (
        jnp.einsum("hqk,khd->qhd", grad_scores, key_low, preferred_element_type=jnp.float32)
        * score_scale
    )
    grad_key = (
        jnp.einsum("hqk,qhd->khd", grad_scores, query_low, preferred_element_type=jnp.float32)
        * score_scale
    )
    grad_value = jnp.einsum(
        "hqk,qhd->khd",
        probs_again.astype(jnp.bfloat16),
        grad_mixed,
        preferred_element_type=jnp.float32,
    )
    grad_raw_query, grad_raw_key, grad_query_local, grad_key_local = query_key_back(
        (grad_query, grad_key)
    )
    grad_qkv = jnp.concatenate(
        [grad_raw_query, grad_raw_key, grad_value.reshape(tokens, model_width)], axis=1
    ).astype(jnp.bfloat16)
    grad_in_local = lax.psum_scatter(
        contract_rows(normed_low, grad_qkv).astype(jnp.bfloat16),
        "shard",
        scatter_dimension=0,
        tiled=True,
    )
    grad_normed = contract_cols(grad_qkv, lax.all_gather(in_proj, "shard", axis=0, tiled=True))
    grad_hidden_norm, grad_attn_local = attn_norm_back(grad_normed)
    grad_inputs = (grad_residual + grad_hidden_norm).astype(jnp.bfloat16)
    small_parts = (
        lax.psum_scatter(
            grad_attn_local.astype(jnp.bfloat16), "shard", scatter_dimension=0, tiled=True
        ).astype(jnp.float32),
        lax.psum_scatter(
            grad_query_local.astype(jnp.bfloat16), "shard", scatter_dimension=0, tiled=True
        ).astype(jnp.float32),
        lax.psum_scatter(
            grad_key_local.astype(jnp.bfloat16), "shard", scatter_dimension=0, tiled=True
        ).astype(jnp.float32),
        lax.psum_scatter(
            grad_ffn_local.astype(jnp.bfloat16), "shard", scatter_dimension=0, tiled=True
        ).astype(jnp.float32),
        lax.psum_scatter(
            grad_router_local.astype(jnp.bfloat16), "shard", scatter_dimension=0, tiled=True
        ).astype(jnp.float32),
    )
    summed = (
        lax.psum(grad_in_local, "rep").astype(jnp.float32),
        lax.psum(grad_out_local, "rep").astype(jnp.float32),
        lax.psum(small_parts[0].astype(jnp.bfloat16), "rep").astype(jnp.float32),
        lax.psum(small_parts[1].astype(jnp.bfloat16), "rep").astype(jnp.float32),
        lax.psum(small_parts[2].astype(jnp.bfloat16), "rep").astype(jnp.float32),
        lax.psum(small_parts[3].astype(jnp.bfloat16), "rep").astype(jnp.float32),
        lax.psum(small_parts[4].astype(jnp.bfloat16), "rep").astype(jnp.float32),
        lax.psum(grad_gate.astype(jnp.bfloat16), "rep").astype(jnp.float32),
        lax.psum(grad_up.astype(jnp.bfloat16), "rep").astype(jnp.float32),
        lax.psum(grad_down.astype(jnp.bfloat16), "rep").astype(jnp.float32),
    )
    return (
        outputs,
        grad_inputs,
        summed[2],
        summed[0],
        summed[3],
        summed[4],
        summed[1],
        summed[5],
        summed[6],
        summed[7],
        summed[8],
        summed[9],
    )


AXES = ("rep", "shard")
LINE = 4
SHARDS = 8
STAGES = ((3, 2, 1, 0), (0, 3, 2, 1), (3, 0, 1, 2), (0, 1, 2, 3))


def pairs_of(target):
    moves = []
    for rep in range(4):
        for shard in range(SHARDS):
            there = target(rep, shard)
            if there is not None:
                moves.append((rep * SHARDS + shard, there[0] * SHARDS + there[1]))
    return moves


CORE_SWAP = pairs_of(lambda rep, shard: (rep ^ 1, shard))
X_SWAP = pairs_of(lambda rep, shard: (rep ^ 2, shard))
Y_SWAP = pairs_of(lambda rep, shard: (rep, shard ^ 1))


def move(values, moves):
    return lax.ppermute(values, AXES, moves)


def in_order(own, other, position):
    return jnp.where(position == 0, jnp.stack([own, other]), jnp.stack([other, own]))


def z_ring(step):
    return pairs_of(lambda rep, shard: (rep, (shard + 2 * step) % SHARDS))


def gather_small(values, z, y):
    both = in_order(values, move(values, Y_SWAP), y)
    whole = jnp.zeros((LINE,) + both.shape, both.dtype)
    for step in range(LINE):
        piece = both if step == 0 else move(both, z_ring(step))
        whole = lax.dynamic_update_index_in_dim(whole, piece, lax.rem(z - step + LINE, LINE), 0)
    return whole.reshape((SHARDS,) + values.shape)


def scatter_small(values, z, y):
    pieces = values.reshape((LINE, 2) + values.shape[1:])
    mine = lax.dynamic_index_in_dim(pieces, y, 1, keepdims=False)
    theirs = lax.dynamic_index_in_dim(pieces, 1 - y, 1, keepdims=False)
    mine = mine + move(theirs, Y_SWAP)
    total = lax.dynamic_index_in_dim(mine, z, 0, keepdims=False)
    for step in range(1, LINE):
        piece = lax.dynamic_index_in_dim(mine, lax.rem(z + step, LINE), 0, keepdims=False)
        total = total + move(piece, z_ring(step))
    return total


def gather_rows(values, z, y):
    z_up = pairs_of(lambda rep, shard: (rep, shard + 2) if shard + 2 < SHARDS else None)
    z_down = pairs_of(lambda rep, shard: (rep, shard - 2) if shard >= 2 else None)
    up, down = [values], [values]
    other = [move(values, Y_SWAP)]
    for step in range(1, LINE):
        up.append(move(up[-1], z_up))
        down.append(move(down[-1], z_down))
    up_other, down_other = [None], [None]
    for step in range(1, LINE):
        from_low = lambda rep, shard: (rep, shard ^ 1) if shard // 2 >= step else None
        from_high = lambda rep, shard: (rep, shard ^ 1) if shard // 2 + step < LINE else None
        up_other.append(move(up[step], pairs_of(from_low)))
        down_other.append(move(down[step], pairs_of(from_high)))
    whole = jnp.zeros((LINE, 2) + values.shape, values.dtype)
    for step in range(LINE):
        if step == 0:
            own, beside = values, other[0]
        else:
            own = jnp.where(z >= step, up[step], down[LINE - step])
            beside = jnp.where(z >= step, up_other[step], down_other[LINE - step])
        place = lax.rem(z - step + LINE, LINE)
        both = in_order(own, beside, y)
        whole = lax.dynamic_update_index_in_dim(whole, both, place, 0)
    return whole.reshape((SHARDS,) + values.shape)


def added(first, *others):
    total = first.astype(jnp.float32)
    for other in others:
        total = total + other.astype(jnp.float32)
    return total.astype(first.dtype)


def scatter_rows(values, z, y):
    tail = values.shape[1:]
    pieces = values.reshape((LINE, 2) + tail)

    def piece(place, column):
        return lax.dynamic_slice(pieces, (place, column) + (0,) * len(tail), (1, 1) + tail).reshape(
            tail
        )

    order = jnp.asarray(STAGES, jnp.int32)[z]
    reduced = []
    for stage in range(LINE):
        place = order[stage]
        reduced.append(added(piece(place, y), move(piece(place, 1 - y), Y_SWAP)))

    def reduced_at(offset):
        found = None
        for own in range(LINE):
            if 0 <= own + offset < LINE:
                part = reduced[STAGES[own].index(own + offset)]
                found = part if found is None else jnp.where(z == own, part, found)
        return found

    from_low = from_high = None
    for step in range(1, LINE):
        far = LINE - step
        upward, downward = reduced_at(far), reduced_at(-far)
        if from_low is not None:
            upward, downward = added(upward, from_low), added(downward, from_high)
        z_up = lambda rep, shard: (rep, shard + 2) if shard // 2 + far < LINE else None
        z_down = lambda rep, shard: (rep, shard - 2) if shard // 2 >= far else None
        from_low = move(upward, pairs_of(z_up))
        from_high = move(downward, pairs_of(z_down))
    return added(reduced_at(0), from_low, from_high)


def turn(values, cos_table, sin_table):
    halves = values.shape[-1] // 2
    turned = jnp.concatenate([-values[..., halves:], values[..., :halves]], axis=-1)
    return values * cos_table + turned * sin_table


def turn_back(grads, cos_table, sin_table):
    halves = grads.shape[-1] // 2
    swung = grads * sin_table
    return grads * cos_table + jnp.concatenate([swung[..., halves:], -swung[..., :halves]], axis=-1)


def fast_local(
    inputs,
    attn_gain,
    in_proj,
    query_gain,
    key_gain,
    out_proj,
    ffn_gain,
    router_weight,
    gate_weight,
    up_weight,
    down_weight,
    routes,
    priority,
    segments,
    grad_out,
):
    f32, bf16 = jnp.float32, jnp.bfloat16
    tokens, width = inputs.shape
    rows_each = in_proj.shape[0]
    local_experts, _, hidden_units = gate_weight.shape
    expert_count = local_experts * SHARDS
    route_count = routes.shape[1]
    pair_count = tokens * route_count
    capacity = 5 * pair_count * SHARDS // (4 * expert_count)
    core_experts = local_experts // 2
    half_heads = HEADS // 2
    half_width = half_heads * HEAD_DIM
    rep, shard = lax.axis_index("rep"), lax.axis_index("shard")
    a, c = rep // 2, lax.rem(rep, 2)
    z, y = shard // 2, lax.rem(shard, 2)

    gains = jnp.stack([attn_gain, query_gain, key_gain, ffn_gain])
    gains = gather_small(gains, z, y)
    gains = gains.transpose(1, 0, 2).reshape(4, width).astype(f32)
    router_full = gather_small(router_weight, z, y).reshape(width, expert_count)
    half_gains = lax.dynamic_index_in_dim(
        gains[1:3].reshape(2, half_heads, 2, HEAD_DIM), a, 2, keepdims=False
    )

    order_row = priority[0]
    pair_ids = jnp.arange(pair_count, dtype=jnp.int32)
    place_of = jnp.sum(
        jnp.where(order_row[None, :] == pair_ids[:, None], pair_ids[None, :], 0), axis=1
    ).reshape(tokens, route_count)
    labels = jnp.arange(expert_count, dtype=jnp.int32)
    hits = routes.T[None, :, :] == labels[:, None, None]
    place_at = jnp.sum(jnp.where(hits, place_of.T[None], 0), axis=1)
    named = jnp.any(hits, axis=1)
    place_at = jnp.where(named, place_at, pair_count)
    earlier = jnp.sum((place_at[:, None, :] < place_at[:, :, None]).astype(jnp.int32), axis=2)
    ranks = jnp.where(named, earlier, -1).astype(bf16)
    ranks = in_order(ranks, move(ranks, CORE_SWAP), c)
    ranks = in_order(ranks, move(ranks, X_SWAP), a)
    ranks = gather_small(ranks, z, y)
    ranks = ranks.transpose(1, 2, 0, 3, 4).astype(jnp.int32)
    counts = jnp.sum((ranks >= 0).astype(jnp.int32), axis=4)
    bases = jnp.cumsum(counts, axis=2) - counts
    slots = bases[..., None] + ranks
    slots = jnp.where((ranks >= 0) & (slots < capacity), slots, -1)
    first_expert = shard * local_experts + c * core_experts
    slots = lax.dynamic_slice_in_dim(slots, first_expert, core_experts, 3)
    slots = slots.transpose(0, 1, 3, 2, 4).reshape(2, 2, core_experts, SHARDS * tokens)

    hidden_pair = in_order(inputs, move(inputs, X_SWAP), a).astype(f32)
    segment_pair = in_order(segments[0], move(segments[0], X_SWAP), a)
    cos_table, sin_table = jax.vmap(rotary_tables)(segment_pair)
    cos_table, sin_table = cos_table[:, :, None, :], sin_table[:, :, None, :]
    in_half = lax.dynamic_slice_in_dim(in_proj, c * (rows_each // 2), rows_each // 2, 0)
    in_half = lax.dynamic_index_in_dim(
        in_half.reshape(rows_each // 2, 3 * half_heads, 2, HEAD_DIM), a, 2, keepdims=False
    ).reshape(rows_each // 2, 3 * half_width)
    in_half = gather_rows(in_half, z, y)
    in_half = in_order(in_half, move(in_half, CORE_SWAP), c)
    in_half = in_half.transpose(1, 0, 2, 3).reshape(width, 3 * half_width)
    out_rows = rows_each // 4
    out_half = lax.dynamic_slice_in_dim(out_proj, a * 2 * out_rows + c * out_rows, out_rows, 0)
    out_half = gather_rows(out_half, z, y)
    out_half = in_order(out_half, move(out_half, CORE_SWAP), c)
    out_half = out_half.transpose(1, 0, 2, 3).reshape(half_width, width)

    attn_rate = lax.rsqrt(jnp.mean(hidden_pair * hidden_pair, axis=-1, keepdims=True) + norm_eps)
    normed_low = (hidden_pair * attn_rate * gains[0]).astype(bf16).reshape(2 * tokens, width)
    projected = jnp.dot(normed_low, in_half, preferred_element_type=f32)
    projected = projected.reshape(2, tokens, 3, half_heads, HEAD_DIM)
    raw_pair = projected[:, :, :2]
    squares = jnp.sum(raw_pair * raw_pair, axis=(3, 4))
    squares = squares + move(squares, X_SWAP)
    pair_rate = lax.rsqrt(squares / width + norm_eps)[..., None, None]
    pair_unit = raw_pair * pair_rate
    turned = turn(pair_unit * half_gains, cos_table[:, :, None], sin_table[:, :, None]).astype(bf16)
    query_low, key_low = turned[:, :, 0], turned[:, :, 1]
    value_low = projected[:, :, 2].astype(bf16)
    places = jnp.arange(tokens, dtype=jnp.int32)
    allowed = (segment_pair[:, :, None] == segment_pair[:, None, :]) & (
        places[None, :] <= places[:, None]
    )
    score_scale = HEAD_DIM ** (-0.5)
    scores = (
        jnp.einsum("bqhd,bkhd->bhqk", query_low, key_low, preferred_element_type=f32) * score_scale
    )
    scores = jnp.where(allowed[:, None], scores, masked_score)
    raised = jnp.exp(scores - jnp.max(scores, axis=-1, keepdims=True))
    probs = raised / jnp.sum(raised, axis=-1, keepdims=True)
    probs_low = probs.astype(bf16)
    attended = jnp.einsum("bhqk,bkhd->bqhd", probs_low, value_low, preferred_element_type=f32)
    attended = attended.astype(bf16).reshape(2 * tokens, half_width)
    mixed = jnp.dot(attended, out_half, preferred_element_type=f32).reshape(2, tokens, width)
    mixed_own = lax.dynamic_index_in_dim(mixed, a, 0, keepdims=False)
    mixed_other = lax.dynamic_index_in_dim(mixed, 1 - a, 0, keepdims=False).astype(bf16)
    hidden = inputs.astype(f32)
    residual = hidden + mixed_own + move(mixed_other, X_SWAP).astype(f32)

    ffn_rate = lax.rsqrt(jnp.mean(residual * residual, axis=-1, keepdims=True) + norm_eps)
    ffn_unit = residual * ffn_rate
    ffn_low = (ffn_unit * gains[3]).astype(bf16)
    router_probs = softmax_rows(jnp.dot(ffn_low, router_full, preferred_element_type=f32))

    ffn_own = gather_rows(ffn_low, z, y)
    cot_own = gather_rows(grad_out, z, y)
    ffn_near = in_order(ffn_own, move(ffn_own, CORE_SWAP), c)
    cot_near = in_order(cot_own, move(cot_own, CORE_SWAP), c)
    ffn_far = move(ffn_own, X_SWAP)
    cot_far = move(cot_own, X_SWAP)
    ffn_far = in_order(ffn_far, move(ffn_far, CORE_SWAP), c)
    cot_far = in_order(cot_far, move(cot_far, CORE_SWAP), c)
    group_rows = SHARDS * tokens

    gate_own = lax.dynamic_slice_in_dim(gate_weight, c * core_experts, core_experts, 0)
    up_own = lax.dynamic_slice_in_dim(up_weight, c * core_experts, core_experts, 0)
    down_own = lax.dynamic_slice_in_dim(down_weight, c * core_experts, core_experts, 0)

    def expert_part(ffn_rows, cot_rows, own_slots):
        ffn_rows = ffn_rows.reshape(2, group_rows, width)
        cot_rows = cot_rows.reshape(2, group_rows, width)
        part_probs = softmax_rows(jnp.dot(ffn_rows, router_full, preferred_element_type=f32))
        part_probs = lax.dynamic_slice_in_dim(part_probs, first_expert, core_experts, 2)
        part_probs = part_probs.transpose(0, 2, 1).astype(bf16)
        match = own_slots[:, :, None, :] == jnp.arange(capacity, dtype=jnp.int32)[:, None]
        choice = match.astype(bf16).reshape(2, core_experts * capacity, group_rows)
        weighted = jnp.where(match, part_probs[:, :, None, :], 0).reshape(choice.shape)
        shape = (2, core_experts, capacity)
        expert_in = jnp.einsum("gct,gtd->gcd", choice, ffn_rows).reshape(shape + (width,))
        grad_expert_out = jnp.einsum("gct,gtd->gcd", weighted, cot_rows).reshape(shape + (width,))
        gate_pre = jnp.einsum("gecd,edf->gecf", expert_in, gate_own, preferred_element_type=f32)
        up_pre = jnp.einsum("gecd,edf->gecf", expert_in, up_own, preferred_element_type=f32)
        act, swiglu_back = jax.vjp(swiglu, gate_pre, up_pre)
        grad_act = jnp.einsum(
            "gecd,efd->gecf", grad_expert_out, down_own, preferred_element_type=f32
        )
        grad_gate_pre, grad_up_pre = swiglu_back(grad_act)
        act_low = act.astype(bf16)
        return (
            choice,
            weighted,
            expert_in,
            grad_expert_out,
            act_low,
            grad_gate_pre.astype(bf16),
            grad_up_pre.astype(bf16),
            jnp.sum(act * grad_act, axis=3),
        )

    near = expert_part(
        ffn_near, cot_near, lax.dynamic_index_in_dim(slots, a, 0, keepdims=False)
    )
    choice, weighted, _, _, act_low, gate_low, up_low, slot_score = near
    expert_out = jnp.einsum("gecf,efd->gecd", act_low, down_own, preferred_element_type=f32)
    expert_out = expert_out.astype(bf16).reshape(2, core_experts * capacity, width)
    routed = jnp.einsum("gct,gcd->gtd", weighted, expert_out)
    grad_expert_in = (
        jnp.einsum("gecf,edf->gecd", gate_low, gate_own, preferred_element_type=f32)
        + jnp.einsum("gecf,edf->gecd", up_low, up_own, preferred_element_type=f32)
    ).astype(bf16)
    grad_expert_in = grad_expert_in.reshape(2, core_experts * capacity, width)
    grad_rows = jnp.einsum("gct,gcd->gtd", choice, grad_expert_in)
    slot_score = slot_score.reshape(2, core_experts, capacity)
    token_score = jnp.einsum(
        "gec,gect->get",
        slot_score,
        choice.astype(f32).reshape(2, core_experts, capacity, group_rows),
        precision=lax.Precision.HIGHEST,
    )

    def core_sum(values):
        own = lax.dynamic_index_in_dim(values, c, 0, keepdims=False)
        other = lax.dynamic_index_in_dim(values, 1 - c, 0, keepdims=False)
        return added(own, move(other, CORE_SWAP))

    grad_rows = core_sum(grad_rows).reshape(SHARDS, tokens, width)
    grad_ffn_home = scatter_rows(grad_rows, z, y).astype(f32)
    routed = core_sum(routed).reshape(SHARDS, tokens, width)
    outputs = (residual + scatter_rows(routed, z, y).astype(f32)).astype(bf16)
    scores_all = jnp.zeros((2, expert_count, group_rows), f32)
    scores_all = lax.dynamic_update_slice_in_dim(scores_all, token_score, first_expert, 1)
    scores_all = core_sum(scores_all).reshape(expert_count, SHARDS, tokens).transpose(1, 0, 2)
    home_score = scatter_small(scores_all, z, y).T

    grad_logits = home_score - router_probs * jnp.sum(home_score, axis=1, keepdims=True)
    grad_logits_low = grad_logits.astype(bf16)
    grad_ffn_in = grad_ffn_home + contract_cols(grad_logits_low, router_full)
    grad_router_local = contract_rows(ffn_low, grad_logits_low)
    grad_ffn_local = jnp.sum(grad_ffn_in * ffn_unit, axis=0)
    scaled = gains[3] * grad_ffn_in
    cotangent = grad_out.astype(f32)
    grad_residual = cotangent + ffn_rate * (
        scaled - ffn_unit * jnp.mean(scaled * ffn_unit, axis=-1, keepdims=True)
    )
    residual_low = grad_residual.astype(bf16)
    residual_pair = in_order(residual_low, move(residual_low, X_SWAP), a)
    residual_pair = residual_pair.reshape(2 * tokens, width)

    grad_attended = contract_cols(residual_pair, out_half).astype(bf16)
    grad_attended = grad_attended.reshape(2, tokens, half_heads, HEAD_DIM)
    grad_out_half = contract_rows(attended, residual_pair).astype(bf16)
    grad_probs = jnp.einsum("bqhd,bkhd->bhqk", grad_attended, value_low, preferred_element_type=f32)
    spread = jnp.sum(probs * grad_probs, axis=-1, keepdims=True)
    grad_scores = (probs * (grad_probs - spread)).astype(bf16)
    grad_query = (
        jnp.einsum("bhqk,bkhd->bqhd", grad_scores, key_low, preferred_element_type=f32)
        * score_scale
    )
    grad_key = (
        jnp.einsum("bhqk,bqhd->bkhd", grad_scores, query_low, preferred_element_type=f32)
        * score_scale
    )
    grad_value = jnp.einsum(
        "bhqk,bqhd->bkhd", probs_low, grad_attended, preferred_element_type=f32
    )
    grad_turned = jnp.stack([grad_query, grad_key], axis=2)
    grad_pair = turn_back(grad_turned, cos_table[:, :, None], sin_table[:, :, None])
    grad_pair_gain = jnp.sum(grad_pair * pair_unit, axis=(0, 1))
    grad_pair = grad_pair * half_gains
    dots = jnp.sum(grad_pair * pair_unit, axis=(3, 4))
    dots = (dots + move(dots, X_SWAP)) / width
    grad_raw = pair_rate * (grad_pair - pair_unit * dots[..., None, None])
    grad_projected = jnp.concatenate([grad_raw, grad_value[:, :, None]], axis=2).astype(bf16)
    grad_projected = grad_projected.reshape(2 * tokens, 3 * half_width)
    grad_in_half = contract_rows(normed_low, grad_projected).astype(bf16)
    grad_normed = contract_cols(grad_projected, in_half).reshape(2, tokens, width)
    normed_own = lax.dynamic_index_in_dim(grad_normed, a, 0, keepdims=False)
    normed_other = lax.dynamic_index_in_dim(grad_normed, 1 - a, 0, keepdims=False).astype(bf16)
    grad_normed = normed_own + move(normed_other, X_SWAP).astype(f32)
    home_rate = lax.rsqrt(jnp.mean(hidden * hidden, axis=-1, keepdims=True) + norm_eps)
    home_unit = hidden * home_rate
    grad_attn_local = jnp.sum(grad_normed * home_unit, axis=0)
    scaled = gains[0] * grad_normed
    grad_inputs = (
        grad_residual
        + home_rate * (scaled - home_unit * jnp.mean(scaled * home_unit, axis=-1, keepdims=True))
    ).astype(bf16)

    in_parts = grad_in_half.reshape(SHARDS, 2, rows_each // 2, 3 * half_width)
    in_sum = scatter_rows(core_sum(in_parts.transpose(1, 0, 2, 3)), z, y)
    out_parts = grad_out_half.reshape(SHARDS, 2, out_rows, width)
    out_sum = scatter_rows(core_sum(out_parts.transpose(1, 0, 2, 3)), z, y)
    in_sum = in_order(in_sum, move(in_sum, CORE_SWAP), c).reshape(rows_each, 3 * half_width)
    in_sum = in_order(in_sum, move(in_sum, X_SWAP), a)
    grad_in = in_sum.reshape(2, rows_each, 3 * half_heads, HEAD_DIM).transpose(1, 2, 0, 3)
    grad_in = grad_in.reshape(rows_each, 3 * width).astype(f32)
    out_sum = in_order(out_sum, move(out_sum, CORE_SWAP), c).reshape(2 * out_rows, width)
    out_sum = in_order(out_sum, move(out_sum, X_SWAP), a)
    grad_out_proj = out_sum.reshape(rows_each, width).astype(f32)

    pair_gains = jnp.zeros((2, half_heads, 2, HEAD_DIM), f32)
    pair_gains = lax.dynamic_update_index_in_dim(pair_gains, grad_pair_gain, a, 2)
    pair_gains = pair_gains.reshape(2, SHARDS, rows_each)
    small = jnp.concatenate(
        [
            grad_attn_local.reshape(SHARDS, 1, rows_each),
            grad_ffn_local.reshape(SHARDS, 1, rows_each),
            pair_gains.transpose(1, 0, 2),
            grad_router_local.T.reshape(expert_count, SHARDS, rows_each).transpose(1, 0, 2),
        ],
        axis=1,
    )
    small = small + move(small, CORE_SWAP)
    small = small + move(small, X_SWAP)
    small = scatter_small(small, z, y)

    far = expert_part(ffn_far, cot_far, lax.dynamic_index_in_dim(slots, 1 - a, 0, keepdims=False))

    def expert_rows(index):
        return jnp.concatenate([near[index], far[index]], axis=0)

    all_in, all_out, all_act, all_gate, all_up = [expert_rows(index) for index in range(2, 7)]
    grads = (
        jnp.einsum("gecd,gecf->edf", all_in, all_gate, preferred_element_type=f32).astype(bf16),
        jnp.einsum("gecd,gecf->edf", all_in, all_up, preferred_element_type=f32).astype(bf16),
        jnp.einsum("gecf,gecd->efd", all_act, all_out, preferred_element_type=f32).astype(bf16),
    )
    grads = [
        in_order(grad, move(grad, CORE_SWAP), c)
        .reshape((local_experts,) + grad.shape[1:])
        .astype(f32)
        for grad in grads
    ]
    return (
        outputs,
        grad_inputs,
        small[0],
        grad_in,
        small[2],
        small[3],
        grad_out_proj,
        small[1],
        small[4:].T,
        grads[0],
        grads[1],
        grads[2],
    )


def solution(mesh):
    fits = dict(mesh.shape) == {"rep": 4, "shard": SHARDS}
    body = fast_local if fits else local
    in_specs = (
        P(("rep", "shard"), None),
        P("shard"),
        P("shard", None),
        P("shard"),
        P("shard"),
        P("shard", None),
        P("shard"),
        P("shard", None),
        P("shard", None, None),
        P("shard", None, None),
        P("shard", None, None),
        P(("rep", "shard"), None),
        P(("rep", "shard"), None),
        P(("rep", "shard"), None),
        P(("rep", "shard"), None),
    )
    out_specs = (
        P(("rep", "shard"), None),
        P(("rep", "shard"), None),
        P("shard"),
        P("shard", None),
        P("shard"),
        P("shard"),
        P("shard", None),
        P("shard"),
        P("shard", None),
        P("shard", None, None),
        P("shard", None, None),
        P("shard", None, None),
    )
    return jax.shard_map(body, mesh=mesh, in_specs=in_specs, out_specs=out_specs, check_vma=False)
```

```python
import jax
import jax.numpy as jnp
from jax import lax
from jax.experimental import pallas as pl
from jax.experimental.pallas import tpu as pltpu
from jax.sharding import PartitionSpec as P

HEADS = 16
HEAD_DIM = 128


norm_eps = 1e-05
rope_base = 10000.0
masked_score = -1e30


def rms_scale(values, gains):
    normed = values * lax.rsqrt(jnp.mean(values * values, axis=-1, keepdims=True) + norm_eps)
    return normed * gains


def rotary_tables(segment_row):
    length = segment_row.shape[0]
    places = jnp.arange(length, dtype=jnp.int32)
    starting = jnp.concatenate(
        [jnp.ones((1,), jnp.int32), (segment_row[1:] != segment_row[:-1]).astype(jnp.int32)]
    )
    first_place = lax.cummax(jnp.where(starting > 0, places, 0), axis=0)
    offsets = (places - first_place).astype(jnp.float32)
    halves = HEAD_DIM // 2
    inverse = rope_base ** (-2.0 * jnp.arange(halves, dtype=jnp.float32) / HEAD_DIM)
    angles = offsets[:, None] * inverse[None, :]
    angles = jnp.concatenate([angles, angles], axis=1)
    return (jnp.cos(angles), jnp.sin(angles))


def rotate(values, cos_table, sin_table):
    halves = values.shape[-1] // 2
    turned = jnp.concatenate([-values[..., halves:], values[..., :halves]], axis=-1)
    return values * cos_table[:, None, :] + turned * sin_table[:, None, :]


def query_key(raw_query, raw_key, query_scale, key_scale, cos_table, sin_table):
    row_count = raw_query.shape[0]
    normed_query = rms_scale(raw_query, query_scale).reshape(row_count, HEADS, HEAD_DIM)
    normed_key = rms_scale(raw_key, key_scale).reshape(row_count, HEADS, HEAD_DIM)
    return (rotate(normed_query, cos_table, sin_table), rotate(normed_key, cos_table, sin_table))


def softmax_rows(logits):
    highest = jnp.max(logits, axis=-1, keepdims=True)
    raised = jnp.exp(logits - highest)
    return raised / jnp.sum(raised, axis=-1, keepdims=True)


def swiglu(gate_pre, up_pre):
    return jax.nn.silu(gate_pre) * up_pre


def contract_rows(left_side, right_side):
    return lax.dot_general(
        left_side, right_side, (((0,), (0,)), ((), ())), preferred_element_type=jnp.float32
    )


def contract_cols(left_side, right_side):
    return lax.dot_general(
        left_side, right_side, (((1,), (1,)), ((), ())), preferred_element_type=jnp.float32
    )


def pick_rows(source_rows, row_picks):
    return jax.vmap(lambda expert_rows, picked: expert_rows[picked])(source_rows, row_picks)


def local(
    inputs,
    attn_gain,
    in_proj,
    query_gain,
    key_gain,
    out_proj,
    ffn_gain,
    router_weight,
    gate_weight,
    up_weight,
    down_weight,
    routes,
    priority,
    segments,
    grad_out,
):
    tokens = inputs.shape[0]
    model_width = inputs.shape[1]
    local_experts = gate_weight.shape[0]
    group_count = lax.axis_size("shard")
    my_index = lax.axis_index("shard")
    expert_count = local_experts * group_count
    route_count = routes.shape[1]
    pair_count = tokens * route_count
    capacity = 5 * pair_count * group_count // (4 * expert_count)
    send_most = 2 * pair_count // expert_count
    segment_row = segments[0]
    cos_table, sin_table = rotary_tables(segment_row)
    hidden_in = inputs.astype(jnp.float32)
    unit_rows = hidden_in * lax.rsqrt(
        jnp.mean(hidden_in * hidden_in, axis=-1, keepdims=True) + norm_eps
    )
    weight_piece = lax.all_gather(in_proj, "shard", axis=0, tiled=True)
    attn_piece = lax.all_gather(attn_gain, "shard", axis=0, tiled=True)
    query_piece = lax.all_gather(query_gain, "shard", axis=0, tiled=True)
    key_piece = lax.all_gather(key_gain, "shard", axis=0, tiled=True)
    scaled = (unit_rows * attn_piece.astype(jnp.float32)).astype(jnp.bfloat16)
    result = (
        jnp.dot(scaled, weight_piece, preferred_element_type=jnp.float32),
        attn_piece.astype(jnp.float32),
        query_piece.astype(jnp.float32),
        key_piece.astype(jnp.float32),
    )
    folded_in = result
    projected = folded_in[0]
    normed_attn, attn_norm_back = jax.vjp(rms_scale, hidden_in, folded_in[1])
    normed_low = normed_attn.astype(jnp.bfloat16)
    raw_query = projected[:, :model_width]
    raw_key = projected[:, model_width : 2 * model_width]
    raw_value = projected[:, 2 * model_width :]

    def rotated_pair(query_raw, key_raw, query_scale, key_scale):
        return query_key(query_raw, key_raw, query_scale, key_scale, cos_table, sin_table)

    (turned_query, turned_key), query_key_back = jax.vjp(
        rotated_pair, raw_query, raw_key, folded_in[2], folded_in[3]
    )
    query_low = turned_query.astype(jnp.bfloat16)
    key_low = turned_key.astype(jnp.bfloat16)
    value_low = raw_value.astype(jnp.bfloat16).reshape(tokens, HEADS, HEAD_DIM)
    places = jnp.arange(tokens, dtype=jnp.int32)
    allowed = (segment_row[:, None] == segment_row[None, :]) & (places[None, :] <= places[:, None])
    score_scale = HEAD_DIM ** (-0.5)

    def masked_scores(queries, key_vecs):
        products = jnp.einsum("qhd,khd->hqk", queries, key_vecs, preferred_element_type=jnp.float32)
        return jnp.where(allowed[None], products * score_scale, masked_score)

    scores = masked_scores(query_low, key_low)
    highest = jnp.max(scores, axis=-1, keepdims=True)
    raised = jnp.exp(scores - highest)
    totals = jnp.sum(raised, axis=-1, keepdims=True)
    attn_probs = raised / totals
    log_total = highest + jnp.log(totals)
    mixed = jnp.einsum(
        "hqk,khd->qhd",
        attn_probs.astype(jnp.bfloat16),
        value_low,
        preferred_element_type=jnp.float32,
    )
    attended = mixed.reshape(tokens, model_width).astype(jnp.bfloat16)
    weight_piece = lax.all_gather(out_proj, "shard", axis=0, tiled=True)
    ffn_piece = lax.all_gather(ffn_gain, "shard", axis=0, tiled=True)
    router_piece = lax.all_gather(router_weight, "shard", axis=0, tiled=True)
    result = (
        jnp.dot(attended, weight_piece, preferred_element_type=jnp.float32),
        ffn_piece.astype(jnp.float32),
        router_piece,
    )
    residual = hidden_in + result[0]
    router_full = result[2]
    normed_ffn, ffn_norm_back = jax.vjp(rms_scale, residual, result[1])
    ffn_low = normed_ffn.astype(jnp.bfloat16)
    logits = jnp.dot(ffn_low, router_full, preferred_element_type=jnp.float32)
    router_probs, router_back = jax.vjp(softmax_rows, logits)
    flat_routes = routes.reshape(pair_count)
    order_row = priority[0]
    ranked_expert = flat_routes[order_row]
    labels = jnp.arange(expert_count, dtype=jnp.int32)
    matches = (ranked_expert[:, None] == labels[None, :]).astype(jnp.int32)
    rank_in = (
        jnp.sum(jnp.cumsum(matches, axis=0, dtype=jnp.int32) * matches, axis=1, dtype=jnp.int32) - 1
    )
    counts = jnp.sum(matches, axis=0, dtype=jnp.int32)
    all_counts = lax.all_gather(counts[None, :], "shard", axis=0, tiled=True)
    base_slots = jnp.cumsum(all_counts, axis=0, dtype=jnp.int32) - all_counts
    my_bases = lax.dynamic_index_in_dim(base_slots, my_index, 0, keepdims=False)
    slot_index = jnp.sum(matches * my_bases[None, :], axis=1, dtype=jnp.int32) + rank_in
    cell_index = ranked_expert * send_most + rank_in
    inverse_order = (
        jnp.zeros((pair_count,), jnp.int32)
        .at[order_row]
        .set(jnp.arange(pair_count, dtype=jnp.int32))
    )
    pair_cell = cell_index[inverse_order].reshape(tokens, route_count)
    pair_keep = (
        (slot_index[inverse_order] < capacity).astype(jnp.float32).reshape(tokens, route_count)
    )
    cell_pair = jnp.zeros((expert_count * send_most,), jnp.int32).at[cell_index].set(order_row)
    cell_live = (jnp.arange(send_most, dtype=jnp.int32)[None, :] < counts[:, None]).reshape(
        expert_count * send_most
    )
    cell_token = cell_pair // route_count
    outgoing = jnp.where(cell_live[:, None], ffn_low[cell_token], 0).reshape(
        expert_count, send_most, model_width
    )
    arrived = lax.all_to_all(outgoing, "shard", split_axis=0, concat_axis=1, tiled=True)
    own_counts = lax.dynamic_slice_in_dim(all_counts, my_index * local_experts, local_experts, 1).T
    own_bases = lax.dynamic_slice_in_dim(base_slots, my_index * local_experts, local_experts, 1).T
    slot_ids = jnp.arange(capacity, dtype=jnp.int32)
    slot_ends = own_bases + own_counts
    source_ids = jnp.sum(
        (slot_ends[:, None, :] <= slot_ids[None, :, None]).astype(jnp.int32),
        axis=2,
        dtype=jnp.int32,
    )
    slot_filled = source_ids < group_count
    source_safe = jnp.minimum(source_ids, group_count - 1)
    slot_rows = (
        source_safe * send_most
        + slot_ids[None, :]
        - jnp.take_along_axis(own_bases, source_safe, axis=1)
    )
    slot_rows = jnp.where(slot_filled, slot_rows, 0)
    expert_in = jnp.where(slot_filled[..., None], pick_rows(arrived, slot_rows), 0)
    gate_pre = jnp.einsum(
        "ecd,edf->ecf", expert_in, gate_weight, preferred_element_type=jnp.float32
    )
    up_pre = jnp.einsum("ecd,edf->ecf", expert_in, up_weight, preferred_element_type=jnp.float32)
    activated, swiglu_back = jax.vjp(swiglu, gate_pre, up_pre)
    act_low = activated.astype(jnp.bfloat16)
    expert_out = jnp.einsum(
        "ecf,efd->ecd", act_low, down_weight, preferred_element_type=jnp.float32
    ).astype(jnp.bfloat16)
    cell_positions = jnp.arange(send_most, dtype=jnp.int32)
    cell_slot = own_bases[:, :, None] + cell_positions[None, None, :]
    cell_used = (cell_positions[None, None, :] < own_counts[:, :, None]) & (cell_slot < capacity)
    cell_slot = jnp.where(cell_used, cell_slot, 0).reshape(local_experts, group_count * send_most)
    cell_used = cell_used.reshape(local_experts, group_count * send_most)
    returning = jnp.where(cell_used[..., None], pick_rows(expert_out, cell_slot), 0)
    returned = lax.all_to_all(returning, "shard", split_axis=1, concat_axis=0, tiled=True).reshape(
        expert_count * send_most, model_width
    )
    pair_rows = returned[pair_cell].astype(jnp.float32)
    pair_weight = jnp.take_along_axis(router_probs, routes, axis=1) * pair_keep
    outputs = (residual + jnp.sum(pair_weight[..., None] * pair_rows, axis=1)).astype(jnp.bfloat16)
    cotangent = grad_out.astype(jnp.float32)
    grad_rows = (
        (pair_weight[..., None] * cotangent[:, None, :])
        .astype(jnp.bfloat16)
        .reshape(pair_count, model_width)
    )
    grad_pair_weight = jnp.sum(pair_rows * cotangent[:, None, :], axis=2) * pair_keep
    route_hits = (routes[..., None] == labels[None, None, :]).astype(jnp.float32)
    grad_router_probs = jnp.sum(grad_pair_weight[..., None] * route_hits, axis=1)
    (grad_logits,) = router_back(grad_router_probs)
    grad_logits_low = grad_logits.astype(jnp.bfloat16)
    outgoing_grad = jnp.where(cell_live[:, None], grad_rows[cell_pair], 0).reshape(
        expert_count, send_most, model_width
    )
    arrived_grad = lax.all_to_all(outgoing_grad, "shard", split_axis=0, concat_axis=1, tiled=True)
    grad_expert_out = jnp.where(slot_filled[..., None], pick_rows(arrived_grad, slot_rows), 0)
    grad_act = jnp.einsum(
        "ecd,efd->ecf", grad_expert_out, down_weight, preferred_element_type=jnp.float32
    )
    grad_down = jnp.einsum(
        "ecf,ecd->efd", act_low, grad_expert_out, preferred_element_type=jnp.float32
    )
    grad_gate_pre, grad_up_pre = swiglu_back(grad_act)
    gate_grad_low = grad_gate_pre.astype(jnp.bfloat16)
    up_grad_low = grad_up_pre.astype(jnp.bfloat16)
    grad_gate = jnp.einsum(
        "ecd,ecf->edf", expert_in, gate_grad_low, preferred_element_type=jnp.float32
    )
    grad_up = jnp.einsum("ecd,ecf->edf", expert_in, up_grad_low, preferred_element_type=jnp.float32)
    grad_expert_in = (
        jnp.einsum("ecf,edf->ecd", gate_grad_low, gate_weight, preferred_element_type=jnp.float32)
        + jnp.einsum("ecf,edf->ecd", up_grad_low, up_weight, preferred_element_type=jnp.float32)
    ).astype(jnp.bfloat16)
    returning_grad = jnp.where(cell_used[..., None], pick_rows(grad_expert_in, cell_slot), 0)
    returned_grad = lax.all_to_all(
        returning_grad, "shard", split_axis=1, concat_axis=0, tiled=True
    ).reshape(expert_count * send_most, model_width)
    grad_ffn_in = jnp.sum(returned_grad[pair_cell].astype(jnp.float32), axis=1) + contract_cols(
        grad_logits_low, router_full
    )
    grad_router_local = contract_rows(ffn_low, grad_logits_low)
    grad_residual_norm, grad_ffn_local = ffn_norm_back(grad_ffn_in)
    grad_residual = cotangent + grad_residual_norm
    residual_low = grad_residual.astype(jnp.bfloat16)
    grad_out_local = lax.psum_scatter(
        contract_rows(attended, residual_low).astype(jnp.bfloat16),
        "shard",
        scatter_dimension=0,
        tiled=True,
    )
    grad_attended = contract_cols(
        residual_low, lax.all_gather(out_proj, "shard", axis=0, tiled=True)
    )
    grad_mixed = grad_attended.astype(jnp.bfloat16).reshape(tokens, HEADS, HEAD_DIM)
    scores_again = masked_scores(query_low, key_low)
    probs_again = jnp.exp(scores_again - log_total)
    grad_probs = jnp.einsum(
        "qhd,khd->hqk", grad_mixed, value_low, preferred_element_type=jnp.float32
    )
    spread = jnp.sum(probs_again * grad_probs, axis=-1, keepdims=True)
    grad_scores = (probs_again * (grad_probs - spread)).astype(jnp.bfloat16)
    grad_query = (
        jnp.einsum("hqk,khd->qhd", grad_scores, key_low, preferred_element_type=jnp.float32)
        * score_scale
    )
    grad_key = (
        jnp.einsum("hqk,qhd->khd", grad_scores, query_low, preferred_element_type=jnp.float32)
        * score_scale
    )
    grad_value = jnp.einsum(
        "hqk,qhd->khd",
        probs_again.astype(jnp.bfloat16),
        grad_mixed,
        preferred_element_type=jnp.float32,
    )
    grad_raw_query, grad_raw_key, grad_query_local, grad_key_local = query_key_back(
        (grad_query, grad_key)
    )
    grad_qkv = jnp.concatenate(
        [grad_raw_query, grad_raw_key, grad_value.reshape(tokens, model_width)], axis=1
    ).astype(jnp.bfloat16)
    grad_in_local = lax.psum_scatter(
        contract_rows(normed_low, grad_qkv).astype(jnp.bfloat16),
        "shard",
        scatter_dimension=0,
        tiled=True,
    )
    grad_normed = contract_cols(grad_qkv, lax.all_gather(in_proj, "shard", axis=0, tiled=True))
    grad_hidden_norm, grad_attn_local = attn_norm_back(grad_normed)
    grad_inputs = (grad_residual + grad_hidden_norm).astype(jnp.bfloat16)
    small_parts = (
        lax.psum_scatter(
            grad_attn_local.astype(jnp.bfloat16), "shard", scatter_dimension=0, tiled=True
        ).astype(jnp.float32),
        lax.psum_scatter(
            grad_query_local.astype(jnp.bfloat16), "shard", scatter_dimension=0, tiled=True
        ).astype(jnp.float32),
        lax.psum_scatter(
            grad_key_local.astype(jnp.bfloat16), "shard", scatter_dimension=0, tiled=True
        ).astype(jnp.float32),
        lax.psum_scatter(
            grad_ffn_local.astype(jnp.bfloat16), "shard", scatter_dimension=0, tiled=True
        ).astype(jnp.float32),
        lax.psum_scatter(
            grad_router_local.astype(jnp.bfloat16), "shard", scatter_dimension=0, tiled=True
        ).astype(jnp.float32),
    )
    summed = (
        lax.psum(grad_in_local, "rep").astype(jnp.float32),
        lax.psum(grad_out_local, "rep").astype(jnp.float32),
        lax.psum(small_parts[0].astype(jnp.bfloat16), "rep").astype(jnp.float32),
        lax.psum(small_parts[1].astype(jnp.bfloat16), "rep").astype(jnp.float32),
        lax.psum(small_parts[2].astype(jnp.bfloat16), "rep").astype(jnp.float32),
        lax.psum(small_parts[3].astype(jnp.bfloat16), "rep").astype(jnp.float32),
        lax.psum(small_parts[4].astype(jnp.bfloat16), "rep").astype(jnp.float32),
        lax.psum(grad_gate.astype(jnp.bfloat16), "rep").astype(jnp.float32),
        lax.psum(grad_up.astype(jnp.bfloat16), "rep").astype(jnp.float32),
        lax.psum(grad_down.astype(jnp.bfloat16), "rep").astype(jnp.float32),
    )
    return (
        outputs,
        grad_inputs,
        summed[2],
        summed[0],
        summed[3],
        summed[4],
        summed[1],
        summed[5],
        summed[6],
        summed[7],
        summed[8],
        summed[9],
    )


AXES = ("rep", "shard")
LINE = 4
SHARDS = 8
REPS = 4


def pairs_of(target):
    moves = []
    for rep in range(REPS):
        for shard in range(SHARDS):
            there = target(rep, shard)
            moves.append((rep * SHARDS + shard, there[0] * SHARDS + there[1]))
    return moves


CORE_SWAP = pairs_of(lambda rep, shard: (rep ^ 1, shard))
X_SWAP = pairs_of(lambda rep, shard: (rep ^ 2, shard))
Y_SWAP = pairs_of(lambda rep, shard: (rep, shard ^ 1))
Z_FROM = [pairs_of(lambda rep, shard: (rep, (shard - 2 * k) % SHARDS)) for k in range(LINE)]
Z_TO = [pairs_of(lambda rep, shard: (rep, (shard + 2 * k) % SHARDS)) for k in range(LINE)]


def move(values, moves):
    return lax.ppermute(values, AXES, moves)


def after(values, *others):
    return lax.optimization_barrier((values,) + others)[0]


def gather_small(values):
    line = jnp.stack([values] + [move(values, Z_FROM[k]) for k in range(1, LINE)])
    both = jnp.stack([line, move(line, Y_SWAP)], axis=1)
    return both.reshape((SHARDS,) + values.shape)


def gather_rows(values, early=None, late=None, fill=None):
    moved = {k: move(values, Z_FROM[k]) for k in (1, 3)}
    moved[2] = move(after(values, moved[1]), Z_FROM[2])
    mine, beside = {0: values}, {0: move(values, Y_SWAP)}
    for k in (1, 3, 2):
        mine[k] = moved[k] if early is None else after(moved[k], early)
        if k == 2 and fill is not None:
            mine[k] = after(mine[k], *fill(mine[3]))
        beside[k] = move(mine[k], Y_SWAP)
    if late is not None:
        beside = {k: after(beside[k], late) for k in beside}
    return [(mine[k], beside[k]) for k in range(LINE)]


def flat(pieces):
    return jnp.concatenate([piece for pair in pieces for piece in pair], axis=0)


def added(first, *others):
    total = first.astype(jnp.float32)
    for other in others:
        total = total + other.astype(jnp.float32)
    return total.astype(first.dtype)


def scatter_rows(parts, fills):
    moved = {}
    for k in (2, 1, 3, 0):
        moved[k] = move(added(*[part(2 * k + 1) for part in parts]), Y_SWAP)
    arrived, reduced, last = [], None, moved[2]
    for k, fill in zip((2, 1, 3, 0), fills):
        here = moved[k]
        if fill is not None:
            here = after(here, *fill(() if reduced is None else (reduced,)))
        reduced = added(here, *[part(2 * k) for part in parts])
        if k > 0:
            arrived.append(move(reduced, Z_TO[k]))
    if fills[4] is not None:
        reduced = after(reduced, *fills[4]((reduced,)))
    return added(reduced, *arrived)


LIMIT = 56 * 2**20
HIDDEN_BLOCK = 256
WIDTH_BLOCK = 512
QUIET = pl.CostEstimate(flops=0, bytes_accessed=0, transcendentals=0)


def ordered(kernel, behind):
    def body(scalar_ref, *refs):
        return kernel(scalar_ref, *refs[behind:])

    return body


HELD = pl.BlockSpec(memory_space=pl.ANY)


def copy_block(order_ref, from_ref, into_ref):
    into_ref[...] = from_ref[...]


def pick_columns(values, order, block):
    rows = values.shape[0]
    picks = order.shape[0]
    return pl.pallas_call(
        copy_block,
        grid_spec=pltpu.PrefetchScalarGridSpec(
            num_scalar_prefetch=1,
            grid=(picks,),
            in_specs=[pl.BlockSpec((rows, block), lambda i, order: (0, order[i]))],
            out_specs=pl.BlockSpec((rows, block), lambda i, order: (0, i)),
        ),
        out_shape=jax.ShapeDtypeStruct((rows, picks * block), values.dtype),
        compiler_params=pltpu.CompilerParams(vmem_limit_bytes=32 * 2**20),
    )(order, values)


def thin_kernel(rep_ref, from_ref, into_ref):
    heads = into_ref.shape[1] // HEAD_DIM

    def take(parity):
        for head in range(heads):
            start = (2 * head + parity) * HEAD_DIM
            into_ref[:, head * HEAD_DIM : (head + 1) * HEAD_DIM] = from_ref[
                :, start : start + HEAD_DIM
            ]

    @pl.when(rep_ref[0] < 2)
    def _():
        take(0)

    @pl.when(rep_ref[0] >= 2)
    def _():
        take(1)


def thin_columns(weights, rep, width):
    rows = weights.shape[0]
    return pl.pallas_call(
        thin_kernel,
        grid_spec=pltpu.PrefetchScalarGridSpec(
            num_scalar_prefetch=1,
            grid=(3,),
            in_specs=[
                pl.BlockSpec((rows, width // 2), lambda i, rep: (0, 2 * i + lax.rem(rep[0], 2)))
            ],
            out_specs=pl.BlockSpec((rows, width // 4), lambda i, rep: (0, i)),
        ),
        out_shape=jax.ShapeDtypeStruct((rows, 3 * width // 4), weights.dtype),
        compiler_params=pltpu.CompilerParams(vmem_limit_bytes=32 * 2**20),
    )(rep, weights)


def weave_kernel(rep_ref, even_ref, odd_ref, into_ref):
    for head in range(even_ref.shape[2] // HEAD_DIM):
        part = slice(head * HEAD_DIM, (head + 1) * HEAD_DIM)
        start = 2 * head * HEAD_DIM
        into_ref[:, start : start + HEAD_DIM] = even_ref[0, :, part].astype(jnp.float32)
        into_ref[:, start + HEAD_DIM : start + 2 * HEAD_DIM] = odd_ref[0, :, part].astype(
            jnp.float32
        )


def weave_columns(pieces, rep, columns, behind):
    rows = pieces.shape[1]
    block = columns // 3
    return pl.pallas_call(
        ordered(weave_kernel, len(behind)),
        grid_spec=pltpu.PrefetchScalarGridSpec(
            num_scalar_prefetch=1,
            grid=(3, 2),
            in_specs=[HELD] * len(behind)
            + [
                pl.BlockSpec((1, rows, block), lambda i, j, rep: (j ^ rep[0], 0, i)),
                pl.BlockSpec((1, rows, block), lambda i, j, rep: ((j + 2) ^ rep[0], 0, i)),
            ],
            out_specs=pl.BlockSpec((rows, 2 * block), lambda i, j, rep: (0, 2 * i + j)),
        ),
        out_shape=jax.ShapeDtypeStruct((rows, 4 * columns), jnp.float32),
        compiler_params=pltpu.CompilerParams(vmem_limit_bytes=32 * 2**20),
    )(rep, *behind, pieces, pieces)


def widen_kernel(core_ref, own_ref, other_ref, into_ref):
    mine = pl.program_id(0) == core_ref[0]

    @pl.when(mine)
    def _():
        into_ref[...] = own_ref[...].astype(jnp.float32)

    @pl.when(jnp.logical_not(mine))
    def _():
        into_ref[...] = other_ref[...].astype(jnp.float32)


def widen(own, other, core, behind=()):
    experts, rows, columns = own.shape
    block = rows // 4
    steps = experts * 4

    def place(hold, core, i, j):
        return jnp.where(i == hold, j, jnp.where(hold == 0, steps - 1, 0))

    own_map = lambda i, j, core: (place(core[0], core, i, j), 0)
    other_map = lambda i, j, core: (place(1 - core[0], core, i, j), 0)
    result = pl.pallas_call(
        ordered(widen_kernel, len(behind)),
        grid_spec=pltpu.PrefetchScalarGridSpec(
            num_scalar_prefetch=1,
            grid=(2, steps),
            in_specs=[HELD] * len(behind)
            + [
                pl.BlockSpec((block, columns), own_map),
                pl.BlockSpec((block, columns), other_map),
            ],
            out_specs=pl.BlockSpec((block, columns), lambda i, j, core: (i * steps + j, 0)),
        ),
        out_shape=jax.ShapeDtypeStruct((2 * experts * rows, columns), jnp.float32),
        compiler_params=pltpu.CompilerParams(vmem_limit_bytes=32 * 2**20),
        cost_estimate=QUIET,
    )(
        core,
        *behind,
        own.reshape(experts * rows, columns),
        other.reshape(experts * rows, columns),
    )
    return result.reshape(2 * experts, rows, columns)


def slot_rows(slots, capacity):
    places = lax.broadcasted_iota(jnp.int32, (capacity, slots.shape[1]), 0)
    return jnp.where(places == slots, 1.0, 0.0).astype(jnp.bfloat16)


def slot_columns(slots, columns):
    places = lax.broadcasted_iota(jnp.int32, (slots.shape[0], columns), 1)
    found = places == slots[:, 0:1]
    for expert in range(1, slots.shape[1]):
        found = found | (places == slots[:, expert : expert + 1])
    return jnp.where(found, 1.0, 0.0).astype(jnp.bfloat16)


def dot_wide(left, right):
    return jnp.dot(left, right, preferred_element_type=jnp.float32)


def pick_rows_into(slots_ref, rows_ref, into_ref):
    choice = slot_rows(slots_ref[0], into_ref.shape[1])
    for start in range(0, rows_ref.shape[1], WIDTH_BLOCK):
        part = slice(start, start + WIDTH_BLOCK)
        into_ref[0, :, part] = dot_wide(choice, rows_ref[:, part]).astype(jnp.bfloat16)


def cotangent_kernel(core_ref, slots_ref, rows_ref, down_ref, picked_ref, slot_ref):
    @pl.when(pl.program_id(1) == 0)
    def _():
        pick_rows_into(slots_ref, rows_ref, picked_ref)

    slot_ref[0] = contract_cols(picked_ref[0], down_ref[0])


def cotangent_part(core, slots, rows, down_weight, capacity, behind=()):
    experts, tokens = slots.shape
    width, hidden = rows.shape[1], down_weight.shape[1]
    return pl.pallas_call(
        ordered(cotangent_kernel, len(behind)),
        grid_spec=pltpu.PrefetchScalarGridSpec(
            num_scalar_prefetch=1,
            grid=(experts, hidden // HIDDEN_BLOCK),
            in_specs=[HELD] * len(behind)
            + [
                pl.BlockSpec((1, 1, tokens), lambda e, n, core: (e, 0, 0)),
                pl.BlockSpec((tokens, width), lambda e, n, core: (0, 0)),
                pl.BlockSpec(
                    (1, HIDDEN_BLOCK, width), lambda e, n, core: (core[0] * experts + e, n, 0)
                ),
            ],
            out_specs=[
                pl.BlockSpec((1, capacity, width), lambda e, n, core: (e, 0, 0)),
                pl.BlockSpec((1, capacity, HIDDEN_BLOCK), lambda e, n, core: (e, 0, n)),
            ],
        ),
        out_shape=[
            jax.ShapeDtypeStruct((experts, capacity, width), jnp.bfloat16),
            jax.ShapeDtypeStruct((experts, capacity, hidden), jnp.float32),
        ],
        compiler_params=pltpu.CompilerParams(vmem_limit_bytes=LIMIT),
        cost_estimate=QUIET,
    )(core, *behind, slots[:, None, :], rows, down_weight)


def forward_kernel(
    first_ref,
    slots_ref,
    rows_ref,
    router_ref,
    gate_ref,
    up_ref,
    slot_ref,
    picked_ref,
    act_ref,
    grad_gate_ref,
    grad_up_ref,
    score_ref,
    weight_ref,
    total_ref,
):
    step = pl.program_id(1)
    mine = first_ref[1] + pl.program_id(0)

    @pl.when(step == 0)
    def _():
        pick_rows_into(slots_ref, rows_ref, picked_ref)
        logits = contract_cols(picked_ref[0], router_ref[...])
        raised = jnp.exp(logits - jnp.max(logits, axis=1, keepdims=True))
        label = lax.broadcasted_iota(jnp.int32, raised.shape, 1)
        own = jnp.sum(jnp.where(label == mine, raised, 0.0), axis=1, keepdims=True)
        weight_ref[...] = own / jnp.sum(raised, axis=1, keepdims=True)
        total_ref[...] = jnp.zeros_like(total_ref)

    gate_pre = dot_wide(picked_ref[0], gate_ref[0])
    up_pre = dot_wide(picked_ref[0], up_ref[0])
    sigmoid = 1.0 / (1.0 + jnp.exp(-gate_pre))
    smooth = gate_pre * sigmoid
    grad_act = weight_ref[...] * slot_ref[0]
    act = smooth * up_pre
    act_ref[0] = (weight_ref[...] * act).astype(jnp.bfloat16)
    grad_gate_ref[0] = (grad_act * up_pre * (sigmoid + smooth * (1.0 - sigmoid))).astype(
        jnp.bfloat16
    )
    grad_up_ref[0] = (grad_act * smooth).astype(jnp.bfloat16)
    total_ref[...] += jnp.sum(act * grad_act, axis=1, keepdims=True)

    @pl.when(step == pl.num_programs(1) - 1)
    def _():
        label = lax.broadcasted_iota(jnp.int32, score_ref.shape[1:], 1)
        score_ref[0] = jnp.where(label == mine, total_ref[...], 0.0).astype(jnp.bfloat16)


def forward_part(first, slots, rows, router_rows, gate_weight, up_weight, slot_cot, behind=()):
    experts, tokens = slots.shape
    capacity, hidden = slot_cot.shape[1:]
    width = rows.shape[1]
    labels = router_rows.shape[0]
    weight_spec = pl.BlockSpec(
        (1, width, HIDDEN_BLOCK), lambda e, n, first: (first[0] * experts + e, 0, n)
    )
    hidden_spec = pl.BlockSpec((1, capacity, HIDDEN_BLOCK), lambda e, n, first: (e, 0, n))
    hidden_shape = jax.ShapeDtypeStruct((experts, capacity, hidden), jnp.bfloat16)
    return pl.pallas_call(
        ordered(forward_kernel, len(behind)),
        grid_spec=pltpu.PrefetchScalarGridSpec(
            num_scalar_prefetch=1,
            grid=(experts, hidden // HIDDEN_BLOCK),
            in_specs=[HELD] * len(behind)
            + [
                pl.BlockSpec((1, 1, tokens), lambda e, n, first: (e, 0, 0)),
                pl.BlockSpec((tokens, width), lambda e, n, first: (0, 0)),
                pl.BlockSpec((labels, width), lambda e, n, first: (0, 0)),
                weight_spec,
                weight_spec,
                hidden_spec,
            ],
            out_specs=[
                pl.BlockSpec((1, capacity, width), lambda e, n, first: (e, 0, 0)),
                hidden_spec,
                hidden_spec,
                hidden_spec,
                pl.BlockSpec((1, capacity, HEAD_DIM), lambda e, n, first: (e, 0, 0)),
            ],
            scratch_shapes=[
                pltpu.VMEM((capacity, 1), jnp.float32),
                pltpu.VMEM((capacity, 1), jnp.float32),
            ],
        ),
        out_shape=[
            jax.ShapeDtypeStruct((experts, capacity, width), jnp.bfloat16),
            hidden_shape,
            hidden_shape,
            hidden_shape,
            jax.ShapeDtypeStruct((experts, capacity, HEAD_DIM), jnp.bfloat16),
        ],
        compiler_params=pltpu.CompilerParams(vmem_limit_bytes=LIMIT),
        cost_estimate=QUIET,
    )(first, *behind, slots[:, None, :], rows, router_rows, gate_weight, up_weight, slot_cot)


def backward_kernel(
    core_ref, slots_ref, grad_gate_ref, grad_up_ref, score_ref, *rest
):
    experts, capacity, _ = grad_gate_ref.shape
    gates, ups = rest[:experts], rest[experts : 2 * experts]
    into_ref, spread_ref, slot_ref = rest[2 * experts :]
    step = pl.program_id(0)
    width = pl.num_programs(0) * WIDTH_BLOCK

    @pl.when(step == 0)
    def _():
        spread_ref[...] = slot_columns(slots_ref[...], experts * capacity)
        scores = score_ref[...].reshape(experts * capacity, HEAD_DIM)
        into_ref[:, width:] = dot_wide(spread_ref[...], scores).astype(jnp.bfloat16)

    for expert in range(experts):
        rows = contract_cols(grad_gate_ref[expert], gates[expert][0]) + contract_cols(
            grad_up_ref[expert], ups[expert][0]
        )
        slot_ref[expert * capacity : (expert + 1) * capacity, :] = rows.astype(jnp.bfloat16)
    start = pl.multiple_of(step * WIDTH_BLOCK, WIDTH_BLOCK)
    into_ref[:, pl.ds(start, WIDTH_BLOCK)] = dot_wide(spread_ref[...], slot_ref[...]).astype(
        jnp.bfloat16
    )


def backward_part(core, columns, grad_gate, grad_up, scores, gate_weight, up_weight, behind=()):
    experts, capacity, hidden = grad_gate.shape
    tokens, width = columns.shape[0], gate_weight.shape[1]

    def weight_spec(expert):
        return pl.BlockSpec(
            (1, WIDTH_BLOCK, hidden), lambda n, core: (core[0] * experts + expert, n, 0)
        )

    whole = pl.BlockSpec((experts, capacity, hidden), lambda n, core: (0, 0, 0))
    return pl.pallas_call(
        ordered(backward_kernel, len(behind)),
        grid_spec=pltpu.PrefetchScalarGridSpec(
            num_scalar_prefetch=1,
            grid=(width // WIDTH_BLOCK,),
            in_specs=[HELD] * len(behind)
            + [
                pl.BlockSpec(columns.shape, lambda n, core: (0, 0)),
                whole,
                whole,
                pl.BlockSpec((experts, capacity, HEAD_DIM), lambda n, core: (0, 0, 0)),
            ]
            + [weight_spec(expert) for expert in range(experts)] * 2,
            out_specs=pl.BlockSpec((tokens, width + HEAD_DIM), lambda n, core: (0, 0)),
            scratch_shapes=[
                pltpu.VMEM((tokens, experts * capacity), jnp.bfloat16),
                pltpu.VMEM((experts * capacity, WIDTH_BLOCK), jnp.bfloat16),
            ],
        ),
        out_shape=jax.ShapeDtypeStruct((tokens, width + HEAD_DIM), jnp.bfloat16),
        compiler_params=pltpu.CompilerParams(vmem_limit_bytes=LIMIT),
        cost_estimate=QUIET,
    )(
        core,
        *behind,
        columns,
        grad_gate,
        grad_up,
        scores,
        *[gate_weight] * experts,
        *[up_weight] * experts,
    )


def routed_kernel(core_ref, slots_ref, act_ref, *rest):
    experts, capacity, _ = act_ref.shape
    downs = rest[:experts]
    into_ref, spread_ref, slot_ref = rest[experts:]

    @pl.when(pl.program_id(0) == 0)
    def _():
        spread_ref[...] = slot_columns(slots_ref[...], experts * capacity)

    for expert in range(experts):
        rows = dot_wide(act_ref[expert], downs[expert][0])
        slot_ref[expert * capacity : (expert + 1) * capacity, :] = rows.astype(jnp.bfloat16)
    into_ref[...] = dot_wide(spread_ref[...], slot_ref[...]).astype(jnp.bfloat16)


def routed_part(core, columns, act, down_weight, behind=()):
    experts, capacity, hidden = act.shape
    tokens, width = columns.shape[0], down_weight.shape[2]

    def weight_spec(expert):
        return pl.BlockSpec(
            (1, hidden, WIDTH_BLOCK), lambda n, core: (core[0] * experts + expert, 0, n)
        )

    return pl.pallas_call(
        ordered(routed_kernel, len(behind)),
        grid_spec=pltpu.PrefetchScalarGridSpec(
            num_scalar_prefetch=1,
            grid=(width // WIDTH_BLOCK,),
            in_specs=[HELD] * len(behind)
            + [
                pl.BlockSpec(columns.shape, lambda n, core: (0, 0)),
                pl.BlockSpec((experts, capacity, hidden), lambda n, core: (0, 0, 0)),
            ]
            + [weight_spec(expert) for expert in range(experts)],
            out_specs=pl.BlockSpec((tokens, WIDTH_BLOCK), lambda n, core: (0, n)),
            scratch_shapes=[
                pltpu.VMEM((tokens, experts * capacity), jnp.bfloat16),
                pltpu.VMEM((experts * capacity, WIDTH_BLOCK), jnp.bfloat16),
            ],
        ),
        out_shape=jax.ShapeDtypeStruct((tokens, width), jnp.bfloat16),
        compiler_params=pltpu.CompilerParams(vmem_limit_bytes=LIMIT),
        cost_estimate=QUIET,
    )(core, *behind, columns, act, *[down_weight] * experts)


def roll_half(values):
    return pltpu.roll(values, HEAD_DIM // 2, 1)


def head_parts(raw_ref, rate_ref, gain_ref, cos_ref, sin_ref, head):
    part_width = gain_ref.shape[1]
    units, turned = [], []
    for which in range(2):
        start = which * part_width + head * HEAD_DIM
        unit = raw_ref[:, start : start + HEAD_DIM] * rate_ref[:, which : which + 1]
        gain = gain_ref[which : which + 1, head * HEAD_DIM : (head + 1) * HEAD_DIM]
        scaled = unit * gain
        units.append((unit, gain))
        turned.append(
            (scaled * cos_ref[...] + roll_half(scaled) * sin_ref[...]).astype(jnp.bfloat16)
        )
    start = 2 * part_width + head * HEAD_DIM
    value = raw_ref[:, start : start + HEAD_DIM].astype(jnp.bfloat16)
    return units, turned, value


def head_probs(turned, column_ref, row_ref):
    scores = contract_cols(turned[0], turned[1]) * HEAD_DIM ** (-0.5)
    length = scores.shape[0]
    reader = lax.broadcasted_iota(jnp.int32, (length, length), 0)
    source = lax.broadcasted_iota(jnp.int32, (length, length), 1)
    allowed = (column_ref[...] == row_ref[0]) & (source <= reader)
    scores = jnp.where(allowed, scores, masked_score)
    raised = jnp.exp(scores - jnp.max(scores, axis=1, keepdims=True))
    return raised / jnp.sum(raised, axis=1, keepdims=True)


def attend_kernel(raw_ref, rate_ref, gain_ref, cos_ref, sin_ref, column_ref, row_ref, into_ref):
    for head in range(gain_ref.shape[1] // HEAD_DIM):
        _, turned, value = head_parts(raw_ref, rate_ref, gain_ref, cos_ref, sin_ref, head)
        probs = head_probs(turned, column_ref, row_ref).astype(jnp.bfloat16)
        into_ref[:, head * HEAD_DIM : (head + 1) * HEAD_DIM] = dot_wide(probs, value).astype(
            jnp.bfloat16
        )


def attend_back_kernel(
    raw_ref,
    rate_ref,
    gain_ref,
    cos_ref,
    sin_ref,
    column_ref,
    row_ref,
    grad_ref,
    pair_ref,
    value_ref,
    dots_ref,
    gains_ref,
):
    score_scale = HEAD_DIM ** (-0.5)
    part_width = gain_ref.shape[1]
    dots = [0.0, 0.0]
    for head in range(part_width // HEAD_DIM):
        units, turned, value = head_parts(raw_ref, rate_ref, gain_ref, cos_ref, sin_ref, head)
        probs = head_probs(turned, column_ref, row_ref)
        here = slice(head * HEAD_DIM, (head + 1) * HEAD_DIM)
        grad = grad_ref[:, here]
        grad_probs = contract_cols(grad, value)
        mean_grad = jnp.sum(probs * grad_probs, axis=1, keepdims=True)
        grad_scores = (probs * (grad_probs - mean_grad)).astype(jnp.bfloat16)
        value_ref[:, here] = contract_rows(probs.astype(jnp.bfloat16), grad).astype(jnp.bfloat16)
        grads = (
            dot_wide(grad_scores, turned[1]) * score_scale,
            contract_rows(grad_scores, turned[0]) * score_scale,
        )
        for which in range(2):
            unit, gain = units[which]
            back = grads[which] * cos_ref[...] + roll_half(grads[which] * sin_ref[...])
            gains_ref[0, which : which + 1, here] = jnp.sum(back * unit, axis=0, keepdims=True)
            back = back * gain
            start = which * part_width + head * HEAD_DIM
            pair_ref[:, start : start + HEAD_DIM] = back
            dots[which] += jnp.sum(back * unit, axis=1, keepdims=True)
    dots_ref[:, 0:1] = dots[0]
    dots_ref[:, 1:2] = dots[1]


def join_kernel(raw_ref, rate_ref, pair_ref, value_ref, dots_ref, into_ref):
    part_width = value_ref.shape[1]
    for which in range(2):
        here = slice(which * part_width, (which + 1) * part_width)
        rate = rate_ref[:, which : which + 1]
        shift = dots_ref[:, which : which + 1] * rate
        into_ref[:, here] = (rate * (pair_ref[:, here] - raw_ref[:, here] * shift)).astype(
            jnp.bfloat16
        )
    into_ref[:, 2 * part_width :] = value_ref[...]


def row_blocks(count, *arrays):
    return [pl.BlockSpec((array.shape[0] // count, array.shape[1]), lambda i: (i, 0)) for array in arrays]


def attention_specs(raw, rate, gains, cos_table, sin_table, columns, rows):
    count = rows.shape[0]
    return (
        row_blocks(count, raw, rate)
        + [pl.BlockSpec(gains.shape, lambda i: (0, 0))]
        + row_blocks(count, cos_table, sin_table, columns)
        + [pl.BlockSpec((1, 1, rows.shape[2]), lambda i: (i, 0, 0))]
    )


def attend(raw, rate, gains, cos_table, sin_table, columns, rows):
    count = rows.shape[0]
    operands = (raw, rate, gains, cos_table, sin_table, columns, rows)
    result = jax.ShapeDtypeStruct((raw.shape[0], gains.shape[1]), jnp.bfloat16)
    return pl.pallas_call(
        attend_kernel,
        grid=(count,),
        in_specs=attention_specs(*operands),
        out_specs=row_blocks(count, result)[0],
        out_shape=result,
        compiler_params=pltpu.CompilerParams(vmem_limit_bytes=LIMIT),
        cost_estimate=QUIET,
    )(*operands)


def attend_back(raw, rate, gains, cos_table, sin_table, columns, rows, grads, behind=()):
    count = rows.shape[0]
    operands = (raw, rate, gains, cos_table, sin_table, columns, rows)
    results = [
        jax.ShapeDtypeStruct((raw.shape[0], 2 * gains.shape[1]), jnp.float32),
        jax.ShapeDtypeStruct((raw.shape[0], gains.shape[1]), jnp.bfloat16),
        jax.ShapeDtypeStruct((raw.shape[0], 2), jnp.float32),
    ]
    gain_result = jax.ShapeDtypeStruct((count,) + gains.shape, jnp.float32)
    return pl.pallas_call(
        lambda *refs: attend_back_kernel(*refs[len(behind) :]),
        grid=(count,),
        in_specs=[HELD] * len(behind) + attention_specs(*operands) + row_blocks(count, grads),
        out_specs=row_blocks(count, *results)
        + [pl.BlockSpec((1,) + gains.shape, lambda i: (i, 0, 0))],
        out_shape=results + [gain_result],
        compiler_params=pltpu.CompilerParams(vmem_limit_bytes=LIMIT),
        cost_estimate=QUIET,
    )(*behind, *operands, grads)


def join_grads(raw, rate, pair, value, dots, count):
    operands = (raw, rate, pair, value, dots)
    result = jax.ShapeDtypeStruct(raw.shape, jnp.bfloat16)
    return pl.pallas_call(
        join_kernel,
        grid=(count,),
        in_specs=row_blocks(count, *operands),
        out_specs=row_blocks(count, result)[0],
        out_shape=result,
        compiler_params=pltpu.CompilerParams(vmem_limit_bytes=LIMIT),
        cost_estimate=QUIET,
    )(*operands)


def rep_sum(values):
    values = values + move(values, CORE_SWAP).reshape((2, 2) + values.shape[1:])[:, ::-1].reshape(
        values.shape
    )
    swapped = move(values, X_SWAP)
    return values + jnp.concatenate([swapped[2:], swapped[:2]], axis=0)


def fast_local(
    inputs,
    attn_gain,
    in_proj,
    query_gain,
    key_gain,
    out_proj,
    ffn_gain,
    router_weight,
    gate_weight,
    up_weight,
    down_weight,
    routes,
    priority,
    segments,
    grad_out,
):
    f32, bf16 = jnp.float32, jnp.bfloat16
    tokens, width = inputs.shape
    rows_each = in_proj.shape[0]
    local_experts, _, hidden_units = gate_weight.shape
    expert_count = local_experts * SHARDS
    route_count = routes.shape[1]
    pair_count = tokens * route_count
    capacity = 5 * pair_count * SHARDS // (4 * expert_count)
    core_experts = local_experts // 2
    heads = HEADS // REPS
    part_width = heads * HEAD_DIM
    group_rows = SHARDS * tokens
    rep, shard = lax.axis_index("rep"), lax.axis_index("shard")
    a, c = rep // 2, lax.rem(rep, 2)
    z, y = shard // 2, lax.rem(shard, 2)
    rep_ref = rep.astype(jnp.int32).reshape(1)
    core_ref = c.astype(jnp.int32).reshape(1)
    near_shards = lax.rem(z + jnp.arange(LINE, dtype=jnp.int32), LINE)[:, None] * 2 + (
        y ^ jnp.arange(2, dtype=jnp.int32)[None, :]
    )
    near_shards = near_shards.reshape(SHARDS)
    shard_ids = jnp.arange(SHARDS, dtype=jnp.int32)
    place_of_shard = jnp.sum(
        jnp.where(near_shards[None, :] == shard_ids[:, None], shard_ids[None, :], 0), axis=1
    )

    in_pieces = gather_rows(thin_columns(in_proj, rep_ref, width))
    in_part = flat(in_pieces)

    order_row = priority[0]
    pair_ids = jnp.arange(pair_count, dtype=jnp.int32)
    place_of = jnp.sum(
        jnp.where(order_row[None, :] == pair_ids[:, None], pair_ids[None, :], 0), axis=1
    ).reshape(tokens, route_count)
    labels = jnp.arange(expert_count, dtype=jnp.int32)
    hits = routes.T[None, :, :] == labels[:, None, None]
    place_at = jnp.sum(jnp.where(hits, place_of.T[None], 0), axis=1)
    named = jnp.any(hits, axis=1)
    place_at = jnp.where(named, place_at, pair_count)
    earlier = jnp.sum((place_at[:, None, :] < place_at[:, :, None]).astype(jnp.int32), axis=2)
    ranks = jnp.where(named, earlier, -1).astype(bf16)
    ranks = jnp.concatenate([ranks, segments.astype(bf16)], axis=0)
    ranks = jnp.stack([ranks, move(ranks, CORE_SWAP)])
    ranks = jnp.concatenate([ranks, move(ranks, X_SWAP)])
    segment_rows = ranks[:, expert_count, :].astype(jnp.int32)
    ranks = gather_small(ranks)[:, :, :expert_count].astype(jnp.int32)
    counts = jnp.sum((ranks >= 0).astype(jnp.int32), axis=3)
    before = (near_shards[None, :] < near_shards[:, None])[:, :, None, None]
    bases = jnp.sum(jnp.where(before, counts[None], 0), axis=1)
    slots = bases[..., None] + ranks
    slots = jnp.where((ranks >= 0) & (slots < capacity), slots, -1)
    first_expert = shard * local_experts + c * core_experts
    slots = lax.dynamic_slice_in_dim(slots, first_expert, core_experts, 2)
    slots = slots.transpose(1, 2, 0, 3)
    shard_slots = jnp.take(slots, place_of_shard, axis=2)
    slots = slots.reshape(REPS, core_experts, group_rows)
    shard_slots = shard_slots.reshape(REPS, core_experts, group_rows)
    shifts = jnp.arange(core_experts, dtype=jnp.int32)[:, None] * capacity

    def columns_of(table):
        return jnp.where(table >= 0, table + shifts, -1).transpose(0, 2, 1)

    columns, shard_columns = columns_of(slots[:2]), columns_of(shard_slots[:2])

    small_in = jnp.stack([attn_gain, query_gain, key_gain, ffn_gain])
    small_in = jnp.concatenate([small_in, router_weight.T], axis=0)
    small_in = jnp.take(gather_small(small_in), place_of_shard, axis=0)
    small_in = small_in.transpose(1, 0, 2).reshape(4 + expert_count, width)
    gains = small_in[:4].astype(f32)
    router_rows = small_in[4:]
    part_gains = lax.dynamic_slice(
        gains[1:3].reshape(2, HEADS // 2, 2, HEAD_DIM),
        (0, c * heads, a, 0),
        (2, heads, 1, HEAD_DIM),
    ).reshape(2, part_width)

    hidden = inputs.astype(f32)
    home_rate = lax.rsqrt(jnp.mean(hidden * hidden, axis=-1, keepdims=True) + norm_eps)
    inputs_all = jnp.stack([inputs, move(inputs, X_SWAP)])
    inputs_all = jnp.stack([inputs_all, move(inputs_all, CORE_SWAP)], axis=1)
    inputs_all = inputs_all.reshape(REPS * tokens, width)
    inputs_all = pick_columns(inputs_all, near_shards, rows_each).astype(f32)
    unit_all = inputs_all * lax.rsqrt(
        jnp.mean(inputs_all * inputs_all, axis=-1, keepdims=True) + norm_eps
    )
    near_gain = jnp.take(gains[0].reshape(SHARDS, rows_each), near_shards, axis=0).reshape(width)
    normed_low = (unit_all * near_gain).astype(bf16)
    cot_across = move(grad_out, X_SWAP)
    normed_low = after(normed_low, slots, shard_slots, columns, shard_columns, cot_across)
    cot_own = after(grad_out, in_part)
    cot_own = lax.all_gather(cot_own, "shard", tiled=True)
    cos_table, sin_table = jax.vmap(rotary_tables)(segment_rows)
    sin_table = jnp.where(jnp.arange(HEAD_DIM) < HEAD_DIM // 2, -sin_table, sin_table)
    cos_table = cos_table.reshape(REPS * tokens, HEAD_DIM)
    sin_table = sin_table.reshape(REPS * tokens, HEAD_DIM)

    out_rows = rows_each // 4
    out_own = lax.dynamic_slice_in_dim(out_proj, rep * out_rows, out_rows, 0)
    out_own = after(out_own, in_pieces[2][0])

    projected = jnp.dot(normed_low, in_part, preferred_element_type=f32)
    squares = jnp.stack(
        [
            jnp.sum(projected[:, k * part_width : (k + 1) * part_width] ** 2, axis=1)
            for k in range(2)
        ],
        axis=1,
    )
    squares = rep_sum(squares.reshape(REPS, tokens, 2)).reshape(REPS * tokens, 2)
    pair_rate = lax.rsqrt(squares / width + norm_eps)
    attention_operands = (
        projected,
        pair_rate,
        part_gains,
        cos_table,
        sin_table,
        segment_rows.reshape(REPS * tokens, 1),
        segment_rows[:, None, :],
    )
    attended = attend(*attention_operands).reshape(2, 2, tokens, part_width)
    out_pieces = gather_rows(out_own, early=projected, late=attended)
    out_own = flat(out_pieces).reshape(SHARDS, out_rows, width)
    out_other = move(out_own, CORE_SWAP)
    out_part = jnp.where(
        c == 0,
        jnp.concatenate([out_own, out_other], axis=1),
        jnp.concatenate([out_other, out_own], axis=1),
    ).reshape(SHARDS * 2 * out_rows, width)
    attended = jnp.concatenate([attended[:, 0], move(attended[:, 1], CORE_SWAP)], axis=2)
    attended = attended.reshape(2 * tokens, 2 * part_width)
    head_of_place = ((near_shards // heads) ^ c) * heads + lax.rem(near_shards, heads)
    place_of_head = jnp.sum(
        jnp.where(head_of_place[None, :] == shard_ids[:, None], shard_ids[None, :], 0), axis=1
    )
    attended = pick_columns(attended, head_of_place, HEAD_DIM)
    mixed = jnp.dot(attended, out_part, preferred_element_type=f32).reshape(2, tokens, width)
    residual = hidden + mixed[0] + move(mixed[1].astype(bf16), X_SWAP).astype(f32)

    ffn_rate = lax.rsqrt(jnp.mean(residual * residual, axis=-1, keepdims=True) + norm_eps)
    ffn_unit = residual * ffn_rate
    ffn_low = (ffn_unit * gains[3]).astype(bf16)
    router_probs = softmax_rows(contract_cols(ffn_low, router_rows))

    def cot_part(group, rows, behind=()):
        return cotangent_part(core_ref, shard_slots[group], rows, down_weight, capacity, behind)

    first_ref = jnp.stack([c, first_expert]).astype(jnp.int32)

    def ffn_part(group, rows, slot_cot, behind=()):
        return forward_part(
            first_ref, slots[group], rows, router_rows, gate_weight, up_weight, slot_cot, behind
        )

    made = {}

    def fill_cot(follow):
        beside = move(cot_own, CORE_SWAP)
        own_part = cot_part(0, cot_own, (follow,))
        made["cot"] = [own_part, cot_part(1, beside, (own_part[1],))]
        return [made["cot"][1][1]]

    ffn_pieces = gather_rows(ffn_low, fill=fill_cot)
    near_cot = made["cot"]
    ffn_own = flat(ffn_pieces)
    ffn_beside = move(ffn_own, CORE_SWAP)
    ffn_far = move(ffn_own, X_SWAP)
    cot_across = lax.all_gather(after(cot_across, ffn_own), "shard", tiled=True)

    near = [ffn_part(0, ffn_own, near_cot[0][1]), ffn_part(1, ffn_beside, near_cot[1][1])]

    def rows_back(group, behind=()):
        _, _, grad_gate, grad_up, scores = near[group]
        return backward_part(
            core_ref, columns[group], grad_gate, grad_up, scores, gate_weight, up_weight, behind
        ).reshape(SHARDS, tokens, -1)

    grad_other = rows_back(1)
    grad_own = rows_back(0, (grad_other,))
    grad_other = move(grad_other, CORE_SWAP)

    def routed_rows(group, behind):
        return routed_part(core_ref, shard_columns[group], near[group][1], down_weight, behind)

    def fill_routed_other(follow):
        made["routed_other"] = routed_rows(1, (grad_own,))
        return [made["routed_other"]]

    def fill_routed_own(follow):
        made["routed_own"] = routed_rows(0, follow + (made["routed_other"], ffn_far))
        return [made["routed_own"]]

    def fill_far_cot(follow):
        made["far_cot"] = cot_part(2, cot_across, follow + (made["routed_own"],))
        return [made["far_cot"][1]]

    def fill_other_cot(follow):
        rows = move(after(cot_across, made["routed_other"]), CORE_SWAP)
        made["other_cot"] = cot_part(3, rows, follow + (made["far_cot"][1],))
        return [made["other_cot"][1]]

    grad_home = scatter_rows(
        [lambda place: grad_own[place], lambda place: grad_other[place]],
        [fill_routed_other, fill_routed_own, fill_far_cot, fill_other_cot, None],
    )
    routed = added(made["routed_own"], move(made["routed_other"], CORE_SWAP))
    routed = lax.psum_scatter(
        after(routed, grad_home), "shard", scatter_dimension=0, tiled=True
    )
    ffn_far = [ffn_far, move(ffn_far, CORE_SWAP)]

    grad_ffn_home = grad_home[:, :width]
    home_score = grad_home[:, width : width + expert_count].astype(f32)
    grad_logits = home_score - router_probs * jnp.sum(home_score, axis=1, keepdims=True)
    grad_logits_low = grad_logits.astype(bf16)

    grad_ffn_in = grad_ffn_home.astype(f32) + jnp.dot(
        grad_logits_low, router_rows, preferred_element_type=f32
    )
    grad_router_local = contract_rows(grad_logits_low, ffn_low)
    grad_ffn_local = jnp.sum(grad_ffn_in * ffn_unit, axis=0)
    scaled = gains[3] * grad_ffn_in
    grad_residual = grad_out.astype(f32) + ffn_rate * (
        scaled - ffn_unit * jnp.mean(scaled * ffn_unit, axis=-1, keepdims=True)
    )
    residual_low = grad_residual.astype(bf16)
    residual_other = move(residual_low, X_SWAP)
    residual_pair = jnp.concatenate([residual_low, residual_other], axis=0)

    grad_attended = contract_cols(residual_pair, out_part).astype(bf16)
    grad_attended = pick_columns(grad_attended, place_of_head, HEAD_DIM)
    grad_attended = grad_attended.reshape(2, tokens, 2 * part_width)
    mine, theirs = grad_attended[:, :, :part_width], grad_attended[:, :, part_width:]
    grad_attended = jnp.stack([mine, move(theirs, CORE_SWAP)], axis=1)
    grad_attended = grad_attended.reshape(REPS * tokens, part_width)
    grad_pair, grad_value, dots, grad_pair_gain = attend_back(*attention_operands, grad_attended)
    grad_pair_gain = jnp.sum(grad_pair_gain, axis=0).reshape(2, heads, HEAD_DIM)
    dots = rep_sum(dots.reshape(REPS, tokens, 2)).reshape(REPS * tokens, 2) / width
    grad_projected = join_grads(projected, pair_rate, grad_pair, grad_value, dots, REPS)

    grad_in_part = contract_rows(normed_low, grad_projected).astype(bf16)
    grad_in_part = grad_in_part.reshape(SHARDS, rows_each, 3 * part_width)
    grad_normed = contract_cols(grad_projected, in_part)
    grad_attn_part = jnp.sum(grad_normed * unit_all, axis=0)

    pair_gains = jnp.zeros((2, HEADS // 2, 2, HEAD_DIM), f32)
    pair_gains = lax.dynamic_update_slice(
        pair_gains, grad_pair_gain[:, :, None], (0, c * heads, a, 0)
    )
    small = jnp.concatenate(
        [grad_ffn_local[None], pair_gains.reshape(2, width), grad_router_local], axis=0
    )
    small = jnp.take(small.reshape(-1, SHARDS, rows_each), near_shards, axis=1)
    small = jnp.concatenate([grad_attn_part.reshape(1, SHARDS, rows_each), small], axis=0)
    small = jnp.pad(small, ((0, HEAD_DIM - small.shape[0]), (0, 0), (0, 0)))
    small = small.astype(bf16).transpose(1, 2, 0)

    far_cot = [made["far_cot"], made["other_cot"]]

    def fill_far(follow):
        made["far"] = ffn_part(2, ffn_far[0], far_cot[0][1], (grad_projected,))
        return [made["far"][3]]

    normed_other = grad_normed.astype(bf16).reshape(2, 2, tokens, width)
    normed_mine = added(normed_other[:, 0], move(normed_other[:, 1], CORE_SWAP))
    normed_across = move(normed_mine[1], X_SWAP)

    def fill_other(follow):
        made["other"] = ffn_part(
            3, ffn_far[1], far_cot[1][1], follow + (made["far"][3], normed_mine)
        )
        return [made["other"][3]]

    def weight_grad(left, right, follow):
        left = jnp.concatenate([after(left[0], *follow)] + left[1:], axis=1)
        right = jnp.concatenate(right, axis=1)
        return jnp.einsum("ecd,ecf->edf", left, right, preferred_element_type=f32).astype(bf16)

    def groups(index):
        return [part[index] for part in (near[0], near[1], made["far"], made["other"])]

    def fill_down(follow):
        cots = [part[0] for part in near_cot + far_cot]
        made["down"] = weight_grad(groups(1), cots, follow + (normed_across,))
        return [made["down"]]

    def fill_gate(follow):
        made["gate"] = weight_grad(groups(0), groups(2), follow)
        return [made["gate"]]

    in_sum = scatter_rows(
        [lambda place: jnp.concatenate([grad_in_part[place], small[place]], axis=1)],
        [fill_far, fill_other, None, fill_down, fill_gate],
    )
    in_other = move(in_sum, X_SWAP)
    grad_up = weight_grad(groups(0), groups(3), (in_sum,))
    in_all = jnp.stack([in_sum, after(in_other, grad_up)])
    in_beside = move(in_all, CORE_SWAP)
    down_all = widen(made["down"], move(made["down"], CORE_SWAP), core_ref, (grad_up,))
    in_all = jnp.stack([in_all, in_beside], axis=1).reshape((REPS,) + in_sum.shape)
    grad_in = weave_columns(in_all, rep_ref, 3 * part_width, (down_all,))
    small = jnp.sum(in_all[:, :, 3 * part_width :].astype(f32), axis=0).T
    gate_all = widen(made["gate"], move(made["gate"], CORE_SWAP), core_ref, (down_all,))
    up_all = widen(grad_up, move(grad_up, CORE_SWAP), core_ref, (gate_all,))

    outputs = (residual + after(routed, in_sum).astype(f32)).astype(bf16)
    grad_normed = added(normed_mine[0], normed_across)
    grad_normed = pick_columns(grad_normed, place_of_shard, rows_each).astype(f32)
    home_unit = hidden * home_rate
    scaled = gains[0] * grad_normed
    grad_inputs = (
        grad_residual
        + home_rate * (scaled - home_unit * jnp.mean(scaled * home_unit, axis=-1, keepdims=True))
    ).astype(bf16)

    grad_out_part = contract_rows(after(attended, made["far"][3]), residual_pair).astype(bf16)
    out_parts = grad_out_part.reshape(SHARDS, 2, out_rows, width)
    out_own = lax.dynamic_index_in_dim(out_parts, c, 1, keepdims=False)
    out_other = lax.dynamic_index_in_dim(out_parts, 1 - c, 1, keepdims=False)
    out_sum = added(out_own, move(out_other, CORE_SWAP))
    out_sum = jnp.take(out_sum, place_of_shard, axis=0).reshape(SHARDS * out_rows, width)
    out_sum = after(out_sum, in_sum, routed)
    out_sum = lax.psum_scatter(out_sum, "shard", scatter_dimension=0, tiled=True)
    out_sum = jnp.stack([out_sum, move(out_sum, X_SWAP)])
    out_sum = jnp.stack([out_sum, move(out_sum, CORE_SWAP)], axis=1)
    out_sum = out_sum.reshape(REPS, out_rows, width)
    out_sum = jnp.take(out_sum, rep ^ jnp.arange(REPS, dtype=jnp.int32), axis=0)
    grad_out_proj = out_sum.reshape(rows_each, width).astype(f32)
    return (
        outputs,
        grad_inputs,
        small[0],
        grad_in,
        small[2],
        small[3],
        grad_out_proj,
        small[1],
        small[4 : 4 + expert_count].T,
        gate_all,
        up_all,
        down_all,
    )


def solution(mesh):
    fits = dict(mesh.shape) == {"rep": REPS, "shard": SHARDS}
    body = fast_local if fits else local
    in_specs = (
        P(("rep", "shard"), None),
        P("shard"),
        P("shard", None),
        P("shard"),
        P("shard"),
        P("shard", None),
        P("shard"),
        P("shard", None),
        P("shard", None, None),
        P("shard", None, None),
        P("shard", None, None),
        P(("rep", "shard"), None),
        P(("rep", "shard"), None),
        P(("rep", "shard"), None),
        P(("rep", "shard"), None),
    )
    out_specs = (
        P(("rep", "shard"), None),
        P(("rep", "shard"), None),
        P("shard"),
        P("shard", None),
        P("shard"),
        P("shard"),
        P("shard", None),
        P("shard"),
        P("shard", None),
        P("shard", None, None),
        P("shard", None, None),
        P("shard", None, None),
    )
    return jax.shard_map(body, mesh=mesh, in_specs=in_specs, out_specs=out_specs, check_vma=False)
```

```python
import functools

import jax
import jax.numpy as jnp
from jax import lax
from jax.experimental import pallas as pl
from jax.experimental.pallas import tpu as pltpu
from jax.sharding import PartitionSpec as P

HEADS = 16
HEAD_DIM = 128


norm_eps = 1e-05
rope_base = 10000.0
masked_score = -1e30


def rms_scale(values, gains):
    normed = values * lax.rsqrt(jnp.mean(values * values, axis=-1, keepdims=True) + norm_eps)
    return normed * gains


def rotary_tables(segment_row):
    length = segment_row.shape[0]
    places = jnp.arange(length, dtype=jnp.int32)
    starting = jnp.concatenate(
        [jnp.ones((1,), jnp.int32), (segment_row[1:] != segment_row[:-1]).astype(jnp.int32)]
    )
    first_place = lax.cummax(jnp.where(starting > 0, places, 0), axis=0)
    offsets = (places - first_place).astype(jnp.float32)
    halves = HEAD_DIM // 2
    inverse = rope_base ** (-2.0 * jnp.arange(halves, dtype=jnp.float32) / HEAD_DIM)
    angles = offsets[:, None] * inverse[None, :]
    angles = jnp.concatenate([angles, angles], axis=1)
    return (jnp.cos(angles), jnp.sin(angles))


def rotate(values, cos_table, sin_table):
    halves = values.shape[-1] // 2
    turned = jnp.concatenate([-values[..., halves:], values[..., :halves]], axis=-1)
    return values * cos_table[:, None, :] + turned * sin_table[:, None, :]


def query_key(raw_query, raw_key, query_scale, key_scale, cos_table, sin_table):
    row_count = raw_query.shape[0]
    normed_query = rms_scale(raw_query, query_scale).reshape(row_count, HEADS, HEAD_DIM)
    normed_key = rms_scale(raw_key, key_scale).reshape(row_count, HEADS, HEAD_DIM)
    return (rotate(normed_query, cos_table, sin_table), rotate(normed_key, cos_table, sin_table))


def softmax_rows(logits):
    highest = jnp.max(logits, axis=-1, keepdims=True)
    raised = jnp.exp(logits - highest)
    return raised / jnp.sum(raised, axis=-1, keepdims=True)


def swiglu(gate_pre, up_pre):
    return jax.nn.silu(gate_pre) * up_pre


def contract_rows(left_side, right_side):
    return lax.dot_general(
        left_side, right_side, (((0,), (0,)), ((), ())), preferred_element_type=jnp.float32
    )


def contract_cols(left_side, right_side):
    return lax.dot_general(
        left_side, right_side, (((1,), (1,)), ((), ())), preferred_element_type=jnp.float32
    )


def pick_rows(source_rows, row_picks):
    return jax.vmap(lambda expert_rows, picked: expert_rows[picked])(source_rows, row_picks)


def local(
    inputs,
    attn_gain,
    in_proj,
    query_gain,
    key_gain,
    out_proj,
    ffn_gain,
    router_weight,
    gate_weight,
    up_weight,
    down_weight,
    routes,
    priority,
    segments,
    grad_out,
):
    tokens = inputs.shape[0]
    model_width = inputs.shape[1]
    local_experts = gate_weight.shape[0]
    group_count = lax.axis_size("shard")
    my_index = lax.axis_index("shard")
    expert_count = local_experts * group_count
    route_count = routes.shape[1]
    pair_count = tokens * route_count
    capacity = 5 * pair_count * group_count // (4 * expert_count)
    send_most = 2 * pair_count // expert_count
    segment_row = segments[0]
    cos_table, sin_table = rotary_tables(segment_row)
    hidden_in = inputs.astype(jnp.float32)
    unit_rows = hidden_in * lax.rsqrt(
        jnp.mean(hidden_in * hidden_in, axis=-1, keepdims=True) + norm_eps
    )
    weight_piece = lax.all_gather(in_proj, "shard", axis=0, tiled=True)
    attn_piece = lax.all_gather(attn_gain, "shard", axis=0, tiled=True)
    query_piece = lax.all_gather(query_gain, "shard", axis=0, tiled=True)
    key_piece = lax.all_gather(key_gain, "shard", axis=0, tiled=True)
    scaled = (unit_rows * attn_piece.astype(jnp.float32)).astype(jnp.bfloat16)
    result = (
        jnp.dot(scaled, weight_piece, preferred_element_type=jnp.float32),
        attn_piece.astype(jnp.float32),
        query_piece.astype(jnp.float32),
        key_piece.astype(jnp.float32),
    )
    folded_in = result
    projected = folded_in[0]
    normed_attn, attn_norm_back = jax.vjp(rms_scale, hidden_in, folded_in[1])
    normed_low = normed_attn.astype(jnp.bfloat16)
    raw_query = projected[:, :model_width]
    raw_key = projected[:, model_width : 2 * model_width]
    raw_value = projected[:, 2 * model_width :]

    def rotated_pair(query_raw, key_raw, query_scale, key_scale):
        return query_key(query_raw, key_raw, query_scale, key_scale, cos_table, sin_table)

    (turned_query, turned_key), query_key_back = jax.vjp(
        rotated_pair, raw_query, raw_key, folded_in[2], folded_in[3]
    )
    query_low = turned_query.astype(jnp.bfloat16)
    key_low = turned_key.astype(jnp.bfloat16)
    value_low = raw_value.astype(jnp.bfloat16).reshape(tokens, HEADS, HEAD_DIM)
    places = jnp.arange(tokens, dtype=jnp.int32)
    allowed = (segment_row[:, None] == segment_row[None, :]) & (places[None, :] <= places[:, None])
    score_scale = HEAD_DIM ** (-0.5)

    def masked_scores(queries, key_vecs):
        products = jnp.einsum("qhd,khd->hqk", queries, key_vecs, preferred_element_type=jnp.float32)
        return jnp.where(allowed[None], products * score_scale, masked_score)

    scores = masked_scores(query_low, key_low)
    highest = jnp.max(scores, axis=-1, keepdims=True)
    raised = jnp.exp(scores - highest)
    totals = jnp.sum(raised, axis=-1, keepdims=True)
    attn_probs = raised / totals
    log_total = highest + jnp.log(totals)
    mixed = jnp.einsum(
        "hqk,khd->qhd",
        attn_probs.astype(jnp.bfloat16),
        value_low,
        preferred_element_type=jnp.float32,
    )
    attended = mixed.reshape(tokens, model_width).astype(jnp.bfloat16)
    weight_piece = lax.all_gather(out_proj, "shard", axis=0, tiled=True)
    ffn_piece = lax.all_gather(ffn_gain, "shard", axis=0, tiled=True)
    router_piece = lax.all_gather(router_weight, "shard", axis=0, tiled=True)
    result = (
        jnp.dot(attended, weight_piece, preferred_element_type=jnp.float32),
        ffn_piece.astype(jnp.float32),
        router_piece,
    )
    residual = hidden_in + result[0]
    router_full = result[2]
    normed_ffn, ffn_norm_back = jax.vjp(rms_scale, residual, result[1])
    ffn_low = normed_ffn.astype(jnp.bfloat16)
    logits = jnp.dot(ffn_low, router_full, preferred_element_type=jnp.float32)
    router_probs, router_back = jax.vjp(softmax_rows, logits)
    flat_routes = routes.reshape(pair_count)
    order_row = priority[0]
    ranked_expert = flat_routes[order_row]
    labels = jnp.arange(expert_count, dtype=jnp.int32)
    matches = (ranked_expert[:, None] == labels[None, :]).astype(jnp.int32)
    rank_in = (
        jnp.sum(jnp.cumsum(matches, axis=0, dtype=jnp.int32) * matches, axis=1, dtype=jnp.int32) - 1
    )
    counts = jnp.sum(matches, axis=0, dtype=jnp.int32)
    all_counts = lax.all_gather(counts[None, :], "shard", axis=0, tiled=True)
    base_slots = jnp.cumsum(all_counts, axis=0, dtype=jnp.int32) - all_counts
    my_bases = lax.dynamic_index_in_dim(base_slots, my_index, 0, keepdims=False)
    slot_index = jnp.sum(matches * my_bases[None, :], axis=1, dtype=jnp.int32) + rank_in
    cell_index = ranked_expert * send_most + rank_in
    inverse_order = (
        jnp.zeros((pair_count,), jnp.int32)
        .at[order_row]
        .set(jnp.arange(pair_count, dtype=jnp.int32))
    )
    pair_cell = cell_index[inverse_order].reshape(tokens, route_count)
    pair_keep = (
        (slot_index[inverse_order] < capacity).astype(jnp.float32).reshape(tokens, route_count)
    )
    cell_pair = jnp.zeros((expert_count * send_most,), jnp.int32).at[cell_index].set(order_row)
    cell_live = (jnp.arange(send_most, dtype=jnp.int32)[None, :] < counts[:, None]).reshape(
        expert_count * send_most
    )
    cell_token = cell_pair // route_count
    outgoing = jnp.where(cell_live[:, None], ffn_low[cell_token], 0).reshape(
        expert_count, send_most, model_width
    )
    arrived = lax.all_to_all(outgoing, "shard", split_axis=0, concat_axis=1, tiled=True)
    own_counts = lax.dynamic_slice_in_dim(all_counts, my_index * local_experts, local_experts, 1).T
    own_bases = lax.dynamic_slice_in_dim(base_slots, my_index * local_experts, local_experts, 1).T
    slot_ids = jnp.arange(capacity, dtype=jnp.int32)
    slot_ends = own_bases + own_counts
    source_ids = jnp.sum(
        (slot_ends[:, None, :] <= slot_ids[None, :, None]).astype(jnp.int32),
        axis=2,
        dtype=jnp.int32,
    )
    slot_filled = source_ids < group_count
    source_safe = jnp.minimum(source_ids, group_count - 1)
    slot_rows = (
        source_safe * send_most
        + slot_ids[None, :]
        - jnp.take_along_axis(own_bases, source_safe, axis=1)
    )
    slot_rows = jnp.where(slot_filled, slot_rows, 0)
    expert_in = jnp.where(slot_filled[..., None], pick_rows(arrived, slot_rows), 0)
    gate_pre = jnp.einsum(
        "ecd,edf->ecf", expert_in, gate_weight, preferred_element_type=jnp.float32
    )
    up_pre = jnp.einsum("ecd,edf->ecf", expert_in, up_weight, preferred_element_type=jnp.float32)
    activated, swiglu_back = jax.vjp(swiglu, gate_pre, up_pre)
    act_low = activated.astype(jnp.bfloat16)
    expert_out = jnp.einsum(
        "ecf,efd->ecd", act_low, down_weight, preferred_element_type=jnp.float32
    ).astype(jnp.bfloat16)
    cell_positions = jnp.arange(send_most, dtype=jnp.int32)
    cell_slot = own_bases[:, :, None] + cell_positions[None, None, :]
    cell_used = (cell_positions[None, None, :] < own_counts[:, :, None]) & (cell_slot < capacity)
    cell_slot = jnp.where(cell_used, cell_slot, 0).reshape(local_experts, group_count * send_most)
    cell_used = cell_used.reshape(local_experts, group_count * send_most)
    returning = jnp.where(cell_used[..., None], pick_rows(expert_out, cell_slot), 0)
    returned = lax.all_to_all(returning, "shard", split_axis=1, concat_axis=0, tiled=True).reshape(
        expert_count * send_most, model_width
    )
    pair_rows = returned[pair_cell].astype(jnp.float32)
    pair_weight = jnp.take_along_axis(router_probs, routes, axis=1) * pair_keep
    outputs = (residual + jnp.sum(pair_weight[..., None] * pair_rows, axis=1)).astype(jnp.bfloat16)
    cotangent = grad_out.astype(jnp.float32)
    grad_rows = (
        (pair_weight[..., None] * cotangent[:, None, :])
        .astype(jnp.bfloat16)
        .reshape(pair_count, model_width)
    )
    grad_pair_weight = jnp.sum(pair_rows * cotangent[:, None, :], axis=2) * pair_keep
    route_hits = (routes[..., None] == labels[None, None, :]).astype(jnp.float32)
    grad_router_probs = jnp.sum(grad_pair_weight[..., None] * route_hits, axis=1)
    (grad_logits,) = router_back(grad_router_probs)
    grad_logits_low = grad_logits.astype(jnp.bfloat16)
    outgoing_grad = jnp.where(cell_live[:, None], grad_rows[cell_pair], 0).reshape(
        expert_count, send_most, model_width
    )
    arrived_grad = lax.all_to_all(outgoing_grad, "shard", split_axis=0, concat_axis=1, tiled=True)
    grad_expert_out = jnp.where(slot_filled[..., None], pick_rows(arrived_grad, slot_rows), 0)
    grad_act = jnp.einsum(
        "ecd,efd->ecf", grad_expert_out, down_weight, preferred_element_type=jnp.float32
    )
    grad_down = jnp.einsum(
        "ecf,ecd->efd", act_low, grad_expert_out, preferred_element_type=jnp.float32
    )
    grad_gate_pre, grad_up_pre = swiglu_back(grad_act)
    gate_grad_low = grad_gate_pre.astype(jnp.bfloat16)
    up_grad_low = grad_up_pre.astype(jnp.bfloat16)
    grad_gate = jnp.einsum(
        "ecd,ecf->edf", expert_in, gate_grad_low, preferred_element_type=jnp.float32
    )
    grad_up = jnp.einsum("ecd,ecf->edf", expert_in, up_grad_low, preferred_element_type=jnp.float32)
    grad_expert_in = (
        jnp.einsum("ecf,edf->ecd", gate_grad_low, gate_weight, preferred_element_type=jnp.float32)
        + jnp.einsum("ecf,edf->ecd", up_grad_low, up_weight, preferred_element_type=jnp.float32)
    ).astype(jnp.bfloat16)
    returning_grad = jnp.where(cell_used[..., None], pick_rows(grad_expert_in, cell_slot), 0)
    returned_grad = lax.all_to_all(
        returning_grad, "shard", split_axis=1, concat_axis=0, tiled=True
    ).reshape(expert_count * send_most, model_width)
    grad_ffn_in = jnp.sum(returned_grad[pair_cell].astype(jnp.float32), axis=1) + contract_cols(
        grad_logits_low, router_full
    )
    grad_router_local = contract_rows(ffn_low, grad_logits_low)
    grad_residual_norm, grad_ffn_local = ffn_norm_back(grad_ffn_in)
    grad_residual = cotangent + grad_residual_norm
    residual_low = grad_residual.astype(jnp.bfloat16)
    grad_out_local = lax.psum_scatter(
        contract_rows(attended, residual_low).astype(jnp.bfloat16),
        "shard",
        scatter_dimension=0,
        tiled=True,
    )
    grad_attended = contract_cols(
        residual_low, lax.all_gather(out_proj, "shard", axis=0, tiled=True)
    )
    grad_mixed = grad_attended.astype(jnp.bfloat16).reshape(tokens, HEADS, HEAD_DIM)
    scores_again = masked_scores(query_low, key_low)
    probs_again = jnp.exp(scores_again - log_total)
    grad_probs = jnp.einsum(
        "qhd,khd->hqk", grad_mixed, value_low, preferred_element_type=jnp.float32
    )
    spread = jnp.sum(probs_again * grad_probs, axis=-1, keepdims=True)
    grad_scores = (probs_again * (grad_probs - spread)).astype(jnp.bfloat16)
    grad_query = (
        jnp.einsum("hqk,khd->qhd", grad_scores, key_low, preferred_element_type=jnp.float32)
        * score_scale
    )
    grad_key = (
        jnp.einsum("hqk,qhd->khd", grad_scores, query_low, preferred_element_type=jnp.float32)
        * score_scale
    )
    grad_value = jnp.einsum(
        "hqk,qhd->khd",
        probs_again.astype(jnp.bfloat16),
        grad_mixed,
        preferred_element_type=jnp.float32,
    )
    grad_raw_query, grad_raw_key, grad_query_local, grad_key_local = query_key_back(
        (grad_query, grad_key)
    )
    grad_qkv = jnp.concatenate(
        [grad_raw_query, grad_raw_key, grad_value.reshape(tokens, model_width)], axis=1
    ).astype(jnp.bfloat16)
    grad_in_local = lax.psum_scatter(
        contract_rows(normed_low, grad_qkv).astype(jnp.bfloat16),
        "shard",
        scatter_dimension=0,
        tiled=True,
    )
    grad_normed = contract_cols(grad_qkv, lax.all_gather(in_proj, "shard", axis=0, tiled=True))
    grad_hidden_norm, grad_attn_local = attn_norm_back(grad_normed)
    grad_inputs = (grad_residual + grad_hidden_norm).astype(jnp.bfloat16)
    small_parts = (
        lax.psum_scatter(
            grad_attn_local.astype(jnp.bfloat16), "shard", scatter_dimension=0, tiled=True
        ).astype(jnp.float32),
        lax.psum_scatter(
            grad_query_local.astype(jnp.bfloat16), "shard", scatter_dimension=0, tiled=True
        ).astype(jnp.float32),
        lax.psum_scatter(
            grad_key_local.astype(jnp.bfloat16), "shard", scatter_dimension=0, tiled=True
        ).astype(jnp.float32),
        lax.psum_scatter(
            grad_ffn_local.astype(jnp.bfloat16), "shard", scatter_dimension=0, tiled=True
        ).astype(jnp.float32),
        lax.psum_scatter(
            grad_router_local.astype(jnp.bfloat16), "shard", scatter_dimension=0, tiled=True
        ).astype(jnp.float32),
    )
    summed = (
        lax.psum(grad_in_local, "rep").astype(jnp.float32),
        lax.psum(grad_out_local, "rep").astype(jnp.float32),
        lax.psum(small_parts[0].astype(jnp.bfloat16), "rep").astype(jnp.float32),
        lax.psum(small_parts[1].astype(jnp.bfloat16), "rep").astype(jnp.float32),
        lax.psum(small_parts[2].astype(jnp.bfloat16), "rep").astype(jnp.float32),
        lax.psum(small_parts[3].astype(jnp.bfloat16), "rep").astype(jnp.float32),
        lax.psum(small_parts[4].astype(jnp.bfloat16), "rep").astype(jnp.float32),
        lax.psum(grad_gate.astype(jnp.bfloat16), "rep").astype(jnp.float32),
        lax.psum(grad_up.astype(jnp.bfloat16), "rep").astype(jnp.float32),
        lax.psum(grad_down.astype(jnp.bfloat16), "rep").astype(jnp.float32),
    )
    return (
        outputs,
        grad_inputs,
        summed[2],
        summed[0],
        summed[3],
        summed[4],
        summed[1],
        summed[5],
        summed[6],
        summed[7],
        summed[8],
        summed[9],
    )


AXES = ("rep", "shard")
LINE = 4
SHARDS = 8
REPS = 4


def pairs_of(target):
    moves = []
    for rep in range(REPS):
        for shard in range(SHARDS):
            there = target(rep, shard)
            moves.append((rep * SHARDS + shard, there[0] * SHARDS + there[1]))
    return moves


CORE_SWAP = pairs_of(lambda rep, shard: (rep ^ 1, shard))
X_SWAP = pairs_of(lambda rep, shard: (rep ^ 2, shard))
Y_SWAP = pairs_of(lambda rep, shard: (rep, shard ^ 1))
SHARD_SWAP = [
    pairs_of(lambda rep, shard: (rep, shard ^ 1)),
    pairs_of(lambda rep, shard: (rep, shard ^ 2)),
    pairs_of(lambda rep, shard: (rep, shard ^ 4)),
]
Z_FROM = [pairs_of(lambda rep, shard: (rep, (shard - 2 * k) % SHARDS)) for k in range(LINE)]
Z_TO = [pairs_of(lambda rep, shard: (rep, (shard + 2 * k) % SHARDS)) for k in range(LINE)]


def move(values, moves):
    return lax.ppermute(values, AXES, moves)


def after(values, *others):
    return lax.optimization_barrier((values,) + others)[0]


def gather_small(values, hold):
    low = jnp.stack([values, move(values, SHARD_SWAP[1])])
    high = jnp.stack([low, move(low, SHARD_SWAP[2])])
    both = jnp.stack([high, move(after(high, *hold), SHARD_SWAP[0])], axis=2)
    return both.reshape((SHARDS,) + values.shape)


def gather_rows(values, early=None, late=(), fill=None, first=()):
    moved = {k: move(values, Z_FROM[k]) for k in (1, 3)}
    moved[2] = move(after(values, moved[1], *first), Z_FROM[2])
    mine, beside = {0: values}, {0: move(values, Y_SWAP)}
    for k in (1, 3, 2):
        mine[k] = moved[k] if early is None else after(moved[k], early)
        if k == 2 and fill is not None:
            mine[k] = after(mine[k], *fill(mine[3]))
        beside[k] = move(mine[k], Y_SWAP)
    if late:
        beside = {k: after(beside[k], *late) for k in beside}
    return [(mine[k], beside[k]) for k in range(LINE)]


def flat(pieces):
    return jnp.concatenate([piece for pair in pieces for piece in pair], axis=0)


def added(first, *others):
    total = first.astype(jnp.float32)
    for other in others:
        total = total + other.astype(jnp.float32)
    return total.astype(first.dtype)


def scatter_rows(parts, fills):
    away = {k: added(*[part(2 * k + 1) for part in parts]) for k in (2, 1, 3, 0)}
    moved = {k: move(away[k], Y_SWAP) for k in (2, 1, 3, 0)}
    arrived, reduced = [], away[2]
    for k, fill in zip((2, 1, 3, 0), fills):
        here = moved[k]
        if fill is not None:
            here = after(here, *fill((reduced,)))
        reduced = added(here, *[part(2 * k) for part in parts])
        if k > 0:
            arrived.append(move(reduced, Z_TO[k]))
    if fills[4] is not None:
        reduced, *arrived = fills[4]((reduced, *arrived))
    return added(reduced, *arrived)


LIMIT = 56 * 2**20
HIDDEN_BLOCK = 256
WIDTH_BLOCK = 512
QUIET = pl.CostEstimate(flops=0, bytes_accessed=0, transcendentals=0)
LOUD = pl.CostEstimate(flops=10**11, bytes_accessed=0, transcendentals=0)


def ordered(kernel, behind):
    def body(scalar_ref, *refs):
        return kernel(scalar_ref, *refs[behind:])

    return body


HELD = pl.BlockSpec(memory_space=pl.ANY)


def copy_block(order_ref, from_ref, into_ref):
    into_ref[...] = from_ref[...]


def pick_columns(values, order, block):
    rows = values.shape[0]
    picks = order.shape[0]
    return pl.pallas_call(
        copy_block,
        grid_spec=pltpu.PrefetchScalarGridSpec(
            num_scalar_prefetch=1,
            grid=(picks,),
            in_specs=[pl.BlockSpec((rows, block), lambda i, order: (0, order[i]))],
            out_specs=pl.BlockSpec((rows, block), lambda i, order: (0, i)),
        ),
        out_shape=jax.ShapeDtypeStruct((rows, picks * block), values.dtype),
        compiler_params=pltpu.CompilerParams(vmem_limit_bytes=32 * 2**20),
    )(order, values)


def thin_kernel(rep_ref, from_ref, into_ref):
    heads = into_ref.shape[1] // HEAD_DIM

    def take(parity):
        for head in range(heads):
            start = (2 * head + parity) * HEAD_DIM
            into_ref[:, head * HEAD_DIM : (head + 1) * HEAD_DIM] = from_ref[
                :, start : start + HEAD_DIM
            ]

    @pl.when(rep_ref[0] < 2)
    def _():
        take(0)

    @pl.when(rep_ref[0] >= 2)
    def _():
        take(1)


def thin_columns(weights, rep, width):
    rows = weights.shape[0]
    return pl.pallas_call(
        thin_kernel,
        grid_spec=pltpu.PrefetchScalarGridSpec(
            num_scalar_prefetch=1,
            grid=(3,),
            in_specs=[
                pl.BlockSpec((rows, width // 2), lambda i, rep: (0, 2 * i + lax.rem(rep[0], 2)))
            ],
            out_specs=pl.BlockSpec((rows, width // 4), lambda i, rep: (0, i)),
        ),
        out_shape=jax.ShapeDtypeStruct((rows, 3 * width // 4), weights.dtype),
        compiler_params=pltpu.CompilerParams(vmem_limit_bytes=32 * 2**20),
    )(rep, weights)


def weave_kernel(rep_ref, even_ref, odd_ref, into_ref):
    for head in range(even_ref.shape[2] // HEAD_DIM):
        part = slice(head * HEAD_DIM, (head + 1) * HEAD_DIM)
        start = 2 * head * HEAD_DIM
        into_ref[:, start : start + HEAD_DIM] = even_ref[0, :, part].astype(jnp.float32)
        into_ref[:, start + HEAD_DIM : start + 2 * HEAD_DIM] = odd_ref[0, :, part].astype(
            jnp.float32
        )


def weave_columns(pieces, rep, columns, behind):
    rows = pieces.shape[1]
    block = columns // 3
    return pl.pallas_call(
        ordered(weave_kernel, len(behind)),
        grid_spec=pltpu.PrefetchScalarGridSpec(
            num_scalar_prefetch=1,
            grid=(3, 2),
            in_specs=[HELD] * len(behind)
            + [
                pl.BlockSpec((1, rows, block), lambda i, j, rep: (j ^ rep[0], 0, i)),
                pl.BlockSpec((1, rows, block), lambda i, j, rep: ((j + 2) ^ rep[0], 0, i)),
            ],
            out_specs=pl.BlockSpec((rows, 2 * block), lambda i, j, rep: (0, 2 * i + j)),
        ),
        out_shape=jax.ShapeDtypeStruct((rows, 4 * columns), jnp.float32),
        compiler_params=pltpu.CompilerParams(vmem_limit_bytes=32 * 2**20),
    )(rep, *behind, pieces, pieces)


def widen_kernel(core_ref, own_ref, other_ref, into_ref):
    mine = pl.program_id(0) == core_ref[0]

    @pl.when(mine)
    def _():
        into_ref[...] = own_ref[...].astype(jnp.float32)

    @pl.when(jnp.logical_not(mine))
    def _():
        into_ref[...] = other_ref[...].astype(jnp.float32)


def widen(own, other, core, behind=()):
    experts, rows, columns = own.shape
    block = rows // 4
    steps = experts * 4

    def place(hold, core, i, j):
        return jnp.where(i == hold, j, jnp.where(hold == 0, steps - 1, 0))

    own_map = lambda i, j, core: (place(core[0], core, i, j), 0)
    other_map = lambda i, j, core: (place(1 - core[0], core, i, j), 0)
    result = pl.pallas_call(
        ordered(widen_kernel, len(behind)),
        grid_spec=pltpu.PrefetchScalarGridSpec(
            num_scalar_prefetch=1,
            grid=(2, steps),
            in_specs=[HELD] * len(behind)
            + [
                pl.BlockSpec((block, columns), own_map),
                pl.BlockSpec((block, columns), other_map),
            ],
            out_specs=pl.BlockSpec((block, columns), lambda i, j, core: (i * steps + j, 0)),
        ),
        out_shape=jax.ShapeDtypeStruct((2 * experts * rows, columns), jnp.float32),
        compiler_params=pltpu.CompilerParams(vmem_limit_bytes=32 * 2**20),
        cost_estimate=QUIET,
    )(
        core,
        *behind,
        own.reshape(experts * rows, columns),
        other.reshape(experts * rows, columns),
    )
    return result.reshape(2 * experts, rows, columns)


def slot_rows(slots, capacity):
    places = lax.broadcasted_iota(jnp.int32, (capacity, slots.shape[1]), 0)
    return jnp.where(places == slots, 1.0, 0.0).astype(jnp.bfloat16)


def slot_columns(slots, columns):
    places = lax.broadcasted_iota(jnp.int32, (slots.shape[0], columns), 1)
    found = places == slots[:, 0:1]
    for expert in range(1, slots.shape[1]):
        found = found | (places == slots[:, expert : expert + 1])
    return jnp.where(found, 1.0, 0.0).astype(jnp.bfloat16)


def dot_wide(left, right):
    return jnp.dot(left, right, preferred_element_type=jnp.float32)


def pick_rows_into(slots_ref, rows_ref, into_ref):
    choice = slot_rows(slots_ref[0], into_ref.shape[1])
    for start in range(0, rows_ref.shape[1], WIDTH_BLOCK):
        part = slice(start, start + WIDTH_BLOCK)
        into_ref[0, :, part] = dot_wide(choice, rows_ref[:, part]).astype(jnp.bfloat16)


def cotangent_kernel(core_ref, slots_ref, rows_ref, down_ref, picked_ref, slot_ref):
    @pl.when(pl.program_id(1) == 0)
    def _():
        pick_rows_into(slots_ref, rows_ref, picked_ref)

    slot_ref[0] = contract_cols(picked_ref[0], down_ref[0])


def cotangent_part(core, slots, rows, down_weight, capacity, behind=()):
    experts, tokens = slots.shape
    width, hidden = rows.shape[1], down_weight.shape[1]
    return pl.pallas_call(
        ordered(cotangent_kernel, len(behind)),
        grid_spec=pltpu.PrefetchScalarGridSpec(
            num_scalar_prefetch=1,
            grid=(experts, hidden // HIDDEN_BLOCK),
            in_specs=[HELD] * len(behind)
            + [
                pl.BlockSpec((1, 1, tokens), lambda e, n, core: (e, 0, 0)),
                pl.BlockSpec((tokens, width), lambda e, n, core: (0, 0)),
                pl.BlockSpec(
                    (1, HIDDEN_BLOCK, width), lambda e, n, core: (core[0] * experts + e, n, 0)
                ),
            ],
            out_specs=[
                pl.BlockSpec((1, capacity, width), lambda e, n, core: (e, 0, 0)),
                pl.BlockSpec((1, capacity, HIDDEN_BLOCK), lambda e, n, core: (e, 0, n)),
            ],
        ),
        out_shape=[
            jax.ShapeDtypeStruct((experts, capacity, width), jnp.bfloat16),
            jax.ShapeDtypeStruct((experts, capacity, hidden), jnp.float32),
        ],
        compiler_params=pltpu.CompilerParams(vmem_limit_bytes=LIMIT),
        cost_estimate=LOUD,
    )(core, *behind, slots[:, None, :], rows, down_weight)


def forward_kernel(
    first_ref,
    slots_ref,
    rows_ref,
    router_ref,
    gate_ref,
    up_ref,
    slot_ref,
    picked_ref,
    act_ref,
    grad_gate_ref,
    grad_up_ref,
    score_ref,
    weight_ref,
    total_ref,
):
    step = pl.program_id(1)
    mine = first_ref[1] + pl.program_id(0)

    @pl.when(step == 0)
    def _():
        pick_rows_into(slots_ref, rows_ref, picked_ref)
        logits = contract_cols(picked_ref[0], router_ref[...])
        raised = jnp.exp(logits - jnp.max(logits, axis=1, keepdims=True))
        label = lax.broadcasted_iota(jnp.int32, raised.shape, 1)
        own = jnp.sum(jnp.where(label == mine, raised, 0.0), axis=1, keepdims=True)
        weight_ref[...] = own / jnp.sum(raised, axis=1, keepdims=True)
        total_ref[...] = jnp.zeros_like(total_ref)

    gate_pre = dot_wide(picked_ref[0], gate_ref[0])
    up_pre = dot_wide(picked_ref[0], up_ref[0])
    sigmoid = 1.0 / (1.0 + jnp.exp(-gate_pre))
    smooth = gate_pre * sigmoid
    grad_act = weight_ref[...] * slot_ref[0]
    act = smooth * up_pre
    act_ref[0] = (weight_ref[...] * act).astype(jnp.bfloat16)
    grad_gate_ref[0] = (grad_act * up_pre * (sigmoid + smooth * (1.0 - sigmoid))).astype(
        jnp.bfloat16
    )
    grad_up_ref[0] = (grad_act * smooth).astype(jnp.bfloat16)
    total_ref[...] += jnp.sum(act * grad_act, axis=1, keepdims=True)

    @pl.when(step == pl.num_programs(1) - 1)
    def _():
        label = lax.broadcasted_iota(jnp.int32, score_ref.shape[1:], 1)
        score_ref[0] = jnp.where(label == mine, total_ref[...], 0.0).astype(jnp.bfloat16)


def forward_part(first, slots, rows, router_rows, gate_weight, up_weight, slot_cot, behind=(), cost=QUIET):
    experts, tokens = slots.shape
    capacity, hidden = slot_cot.shape[1:]
    width = rows.shape[1]
    labels = router_rows.shape[0]
    weight_spec = pl.BlockSpec(
        (1, width, HIDDEN_BLOCK), lambda e, n, first: (first[0] * experts + e, 0, n)
    )
    hidden_spec = pl.BlockSpec((1, capacity, HIDDEN_BLOCK), lambda e, n, first: (e, 0, n))
    hidden_shape = jax.ShapeDtypeStruct((experts, capacity, hidden), jnp.bfloat16)
    return pl.pallas_call(
        ordered(forward_kernel, len(behind)),
        grid_spec=pltpu.PrefetchScalarGridSpec(
            num_scalar_prefetch=1,
            grid=(experts, hidden // HIDDEN_BLOCK),
            in_specs=[HELD] * len(behind)
            + [
                pl.BlockSpec((1, 1, tokens), lambda e, n, first: (e, 0, 0)),
                pl.BlockSpec((tokens, width), lambda e, n, first: (0, 0)),
                pl.BlockSpec((labels, width), lambda e, n, first: (0, 0)),
                weight_spec,
                weight_spec,
                hidden_spec,
            ],
            out_specs=[
                pl.BlockSpec((1, capacity, width), lambda e, n, first: (e, 0, 0)),
                hidden_spec,
                hidden_spec,
                hidden_spec,
                pl.BlockSpec((1, capacity, HEAD_DIM), lambda e, n, first: (e, 0, 0)),
            ],
            scratch_shapes=[
                pltpu.VMEM((capacity, 1), jnp.float32),
                pltpu.VMEM((capacity, 1), jnp.float32),
            ],
        ),
        out_shape=[
            jax.ShapeDtypeStruct((experts, capacity, width), jnp.bfloat16),
            hidden_shape,
            hidden_shape,
            hidden_shape,
            jax.ShapeDtypeStruct((experts, capacity, HEAD_DIM), jnp.bfloat16),
        ],
        compiler_params=pltpu.CompilerParams(vmem_limit_bytes=LIMIT),
        cost_estimate=cost,
    )(first, *behind, slots[:, None, :], rows, router_rows, gate_weight, up_weight, slot_cot)


def backward_kernel(
    core_ref, slots_ref, grad_gate_ref, grad_up_ref, score_ref, *rest
):
    experts, capacity, _ = grad_gate_ref.shape
    gates, ups = rest[:experts], rest[experts : 2 * experts]
    into_ref, spread_ref, slot_ref = rest[2 * experts :]
    step = pl.program_id(0)
    width = pl.num_programs(0) * WIDTH_BLOCK

    @pl.when(step == 0)
    def _():
        spread_ref[...] = slot_columns(slots_ref[...], experts * capacity)
        scores = score_ref[...].reshape(experts * capacity, HEAD_DIM)
        into_ref[:, width:] = dot_wide(spread_ref[...], scores).astype(jnp.bfloat16)

    for expert in range(experts):
        rows = contract_cols(grad_gate_ref[expert], gates[expert][0]) + contract_cols(
            grad_up_ref[expert], ups[expert][0]
        )
        slot_ref[expert * capacity : (expert + 1) * capacity, :] = rows.astype(jnp.bfloat16)
    start = pl.multiple_of(step * WIDTH_BLOCK, WIDTH_BLOCK)
    into_ref[:, pl.ds(start, WIDTH_BLOCK)] = dot_wide(spread_ref[...], slot_ref[...]).astype(
        jnp.bfloat16
    )


def backward_part(core, columns, grad_gate, grad_up, scores, gate_weight, up_weight, behind=()):
    experts, capacity, hidden = grad_gate.shape
    tokens, width = columns.shape[0], gate_weight.shape[1]

    def weight_spec(expert):
        return pl.BlockSpec(
            (1, WIDTH_BLOCK, hidden), lambda n, core: (core[0] * experts + expert, n, 0)
        )

    whole = pl.BlockSpec((experts, capacity, hidden), lambda n, core: (0, 0, 0))
    return pl.pallas_call(
        ordered(backward_kernel, len(behind)),
        grid_spec=pltpu.PrefetchScalarGridSpec(
            num_scalar_prefetch=1,
            grid=(width // WIDTH_BLOCK,),
            in_specs=[HELD] * len(behind)
            + [
                pl.BlockSpec(columns.shape, lambda n, core: (0, 0)),
                whole,
                whole,
                pl.BlockSpec((experts, capacity, HEAD_DIM), lambda n, core: (0, 0, 0)),
            ]
            + [weight_spec(expert) for expert in range(experts)] * 2,
            out_specs=pl.BlockSpec((tokens, width + HEAD_DIM), lambda n, core: (0, 0)),
            scratch_shapes=[
                pltpu.VMEM((tokens, experts * capacity), jnp.bfloat16),
                pltpu.VMEM((experts * capacity, WIDTH_BLOCK), jnp.bfloat16),
            ],
        ),
        out_shape=jax.ShapeDtypeStruct((tokens, width + HEAD_DIM), jnp.bfloat16),
        compiler_params=pltpu.CompilerParams(vmem_limit_bytes=LIMIT),
        cost_estimate=QUIET,
    )(
        core,
        *behind,
        columns,
        grad_gate,
        grad_up,
        scores,
        *[gate_weight] * experts,
        *[up_weight] * experts,
    )


def routed_kernel(more, core_ref, slots_ref, act_ref, *rest):
    experts, capacity, _ = act_ref.shape
    downs = rest[:experts]
    into_ref, spread_ref, slot_ref = rest[experts + more :]

    @pl.when(pl.program_id(0) == 0)
    def _():
        spread_ref[...] = slot_columns(slots_ref[...], experts * capacity)

    for expert in range(experts):
        rows = dot_wide(act_ref[expert], downs[expert][0])
        slot_ref[expert * capacity : (expert + 1) * capacity, :] = rows.astype(jnp.bfloat16)
    total = dot_wide(spread_ref[...], slot_ref[...])
    for extra in rest[experts : experts + more]:
        total += extra[...].astype(jnp.float32)
    into_ref[...] = total.astype(jnp.bfloat16)


def routed_part(core, columns, act, down_weight, extra=(), behind=()):
    experts, capacity, hidden = act.shape
    tokens, width = columns.shape[0], down_weight.shape[2]

    def weight_spec(expert):
        return pl.BlockSpec(
            (1, hidden, WIDTH_BLOCK), lambda n, core: (core[0] * experts + expert, 0, n)
        )

    rows_spec = pl.BlockSpec((tokens, WIDTH_BLOCK), lambda n, core: (0, n))
    return pl.pallas_call(
        ordered(functools.partial(routed_kernel, len(extra)), len(behind)),
        grid_spec=pltpu.PrefetchScalarGridSpec(
            num_scalar_prefetch=1,
            grid=(width // WIDTH_BLOCK,),
            in_specs=[HELD] * len(behind)
            + [
                pl.BlockSpec(columns.shape, lambda n, core: (0, 0)),
                pl.BlockSpec((experts, capacity, hidden), lambda n, core: (0, 0, 0)),
            ]
            + [weight_spec(expert) for expert in range(experts)]
            + [rows_spec] * len(extra),
            out_specs=rows_spec,
            scratch_shapes=[
                pltpu.VMEM((tokens, experts * capacity), jnp.bfloat16),
                pltpu.VMEM((experts * capacity, WIDTH_BLOCK), jnp.bfloat16),
            ],
        ),
        out_shape=jax.ShapeDtypeStruct((tokens, width), jnp.bfloat16),
        compiler_params=pltpu.CompilerParams(vmem_limit_bytes=LIMIT),
        cost_estimate=LOUD,
    )(core, *behind, columns, act, *[down_weight] * experts, *extra)


def roll_half(values):
    return pltpu.roll(values, HEAD_DIM // 2, 1)


def head_parts(raw_ref, rate_ref, gain_ref, cos_ref, sin_ref, head):
    part_width = gain_ref.shape[1]
    units, turned = [], []
    for which in range(2):
        start = which * part_width + head * HEAD_DIM
        unit = raw_ref[:, start : start + HEAD_DIM] * rate_ref[:, which : which + 1]
        gain = gain_ref[which : which + 1, head * HEAD_DIM : (head + 1) * HEAD_DIM]
        scaled = unit * gain
        units.append((unit, gain))
        turned.append(
            (scaled * cos_ref[...] + roll_half(scaled) * sin_ref[...]).astype(jnp.bfloat16)
        )
    start = 2 * part_width + head * HEAD_DIM
    value = raw_ref[:, start : start + HEAD_DIM].astype(jnp.bfloat16)
    return units, turned, value


def head_probs(turned, column_ref, row_ref):
    scores = contract_cols(turned[0], turned[1]) * HEAD_DIM ** (-0.5)
    length = scores.shape[0]
    reader = lax.broadcasted_iota(jnp.int32, (length, length), 0)
    source = lax.broadcasted_iota(jnp.int32, (length, length), 1)
    allowed = (column_ref[...] == row_ref[0]) & (source <= reader)
    scores = jnp.where(allowed, scores, masked_score)
    raised = jnp.exp(scores - jnp.max(scores, axis=1, keepdims=True))
    return raised / jnp.sum(raised, axis=1, keepdims=True)


def attend_kernel(raw_ref, rate_ref, gain_ref, cos_ref, sin_ref, column_ref, row_ref, into_ref):
    for head in range(gain_ref.shape[1] // HEAD_DIM):
        _, turned, value = head_parts(raw_ref, rate_ref, gain_ref, cos_ref, sin_ref, head)
        probs = head_probs(turned, column_ref, row_ref).astype(jnp.bfloat16)
        into_ref[:, head * HEAD_DIM : (head + 1) * HEAD_DIM] = dot_wide(probs, value).astype(
            jnp.bfloat16
        )


def attend_back_kernel(
    raw_ref,
    rate_ref,
    gain_ref,
    cos_ref,
    sin_ref,
    column_ref,
    row_ref,
    grad_ref,
    pair_ref,
    value_ref,
    dots_ref,
    gains_ref,
):
    score_scale = HEAD_DIM ** (-0.5)
    part_width = gain_ref.shape[1]
    dots = [0.0, 0.0]
    for head in range(part_width // HEAD_DIM):
        units, turned, value = head_parts(raw_ref, rate_ref, gain_ref, cos_ref, sin_ref, head)
        probs = head_probs(turned, column_ref, row_ref)
        here = slice(head * HEAD_DIM, (head + 1) * HEAD_DIM)
        grad = grad_ref[:, here]
        grad_probs = contract_cols(grad, value)
        mean_grad = jnp.sum(probs * grad_probs, axis=1, keepdims=True)
        grad_scores = (probs * (grad_probs - mean_grad)).astype(jnp.bfloat16)
        value_ref[:, here] = contract_rows(probs.astype(jnp.bfloat16), grad).astype(jnp.bfloat16)
        grads = (
            dot_wide(grad_scores, turned[1]) * score_scale,
            contract_rows(grad_scores, turned[0]) * score_scale,
        )
        for which in range(2):
            unit, gain = units[which]
            back = grads[which] * cos_ref[...] + roll_half(grads[which] * sin_ref[...])
            gains_ref[0, which : which + 1, here] = jnp.sum(back * unit, axis=0, keepdims=True)
            back = back * gain
            start = which * part_width + head * HEAD_DIM
            pair_ref[:, start : start + HEAD_DIM] = back
            dots[which] += jnp.sum(back * unit, axis=1, keepdims=True)
    dots_ref[:, 0:1] = dots[0]
    dots_ref[:, 1:2] = dots[1]


def join_kernel(raw_ref, rate_ref, pair_ref, value_ref, dots_ref, into_ref):
    part_width = value_ref.shape[1]
    for which in range(2):
        here = slice(which * part_width, (which + 1) * part_width)
        rate = rate_ref[:, which : which + 1]
        shift = dots_ref[:, which : which + 1] * rate
        into_ref[:, here] = (rate * (pair_ref[:, here] - raw_ref[:, here] * shift)).astype(
            jnp.bfloat16
        )
    into_ref[:, 2 * part_width :] = value_ref[...]


def row_blocks(count, *arrays):
    return [pl.BlockSpec((array.shape[0] // count, array.shape[1]), lambda i: (i, 0)) for array in arrays]


def attention_specs(raw, rate, gains, cos_table, sin_table, columns, rows):
    count = rows.shape[0]
    return (
        row_blocks(count, raw, rate)
        + [pl.BlockSpec(gains.shape, lambda i: (0, 0))]
        + row_blocks(count, cos_table, sin_table, columns)
        + [pl.BlockSpec((1, 1, rows.shape[2]), lambda i: (i, 0, 0))]
    )


def attend(raw, rate, gains, cos_table, sin_table, columns, rows):
    count = rows.shape[0]
    operands = (raw, rate, gains, cos_table, sin_table, columns, rows)
    result = jax.ShapeDtypeStruct((raw.shape[0], gains.shape[1]), jnp.bfloat16)
    return pl.pallas_call(
        attend_kernel,
        grid=(count,),
        in_specs=attention_specs(*operands),
        out_specs=row_blocks(count, result)[0],
        out_shape=result,
        compiler_params=pltpu.CompilerParams(vmem_limit_bytes=LIMIT),
        cost_estimate=QUIET,
    )(*operands)


def attend_back(raw, rate, gains, cos_table, sin_table, columns, rows, grads, behind=()):
    count = rows.shape[0]
    operands = (raw, rate, gains, cos_table, sin_table, columns, rows)
    results = [
        jax.ShapeDtypeStruct((raw.shape[0], 2 * gains.shape[1]), jnp.float32),
        jax.ShapeDtypeStruct((raw.shape[0], gains.shape[1]), jnp.bfloat16),
        jax.ShapeDtypeStruct((raw.shape[0], 2), jnp.float32),
    ]
    gain_result = jax.ShapeDtypeStruct((count,) + gains.shape, jnp.float32)
    return pl.pallas_call(
        lambda *refs: attend_back_kernel(*refs[len(behind) :]),
        grid=(count,),
        in_specs=[HELD] * len(behind) + attention_specs(*operands) + row_blocks(count, grads),
        out_specs=row_blocks(count, *results)
        + [pl.BlockSpec((1,) + gains.shape, lambda i: (i, 0, 0))],
        out_shape=results + [gain_result],
        compiler_params=pltpu.CompilerParams(vmem_limit_bytes=LIMIT),
        cost_estimate=QUIET,
    )(*behind, *operands, grads)


def join_grads(raw, rate, pair, value, dots, count):
    operands = (raw, rate, pair, value, dots)
    result = jax.ShapeDtypeStruct(raw.shape, jnp.bfloat16)
    return pl.pallas_call(
        join_kernel,
        grid=(count,),
        in_specs=row_blocks(count, *operands),
        out_specs=row_blocks(count, result)[0],
        out_shape=result,
        compiler_params=pltpu.CompilerParams(vmem_limit_bytes=LIMIT),
        cost_estimate=QUIET,
    )(*operands)


def rep_sum(values):
    values = values + move(values, CORE_SWAP).reshape((2, 2) + values.shape[1:])[:, ::-1].reshape(
        values.shape
    )
    swapped = move(values, X_SWAP)
    return values + jnp.concatenate([swapped[2:], swapped[:2]], axis=0)


def fast_local(
    inputs,
    attn_gain,
    in_proj,
    query_gain,
    key_gain,
    out_proj,
    ffn_gain,
    router_weight,
    gate_weight,
    up_weight,
    down_weight,
    routes,
    priority,
    segments,
    grad_out,
):
    f32, bf16 = jnp.float32, jnp.bfloat16
    tokens, width = inputs.shape
    rows_each = in_proj.shape[0]
    local_experts, _, hidden_units = gate_weight.shape
    expert_count = local_experts * SHARDS
    route_count = routes.shape[1]
    pair_count = tokens * route_count
    capacity = 5 * pair_count * SHARDS // (4 * expert_count)
    core_experts = local_experts // 2
    heads = HEADS // REPS
    part_width = heads * HEAD_DIM
    group_rows = SHARDS * tokens
    rep, shard = lax.axis_index("rep"), lax.axis_index("shard")
    a, c = rep // 2, lax.rem(rep, 2)
    z, y = shard // 2, lax.rem(shard, 2)
    rep_ref = rep.astype(jnp.int32).reshape(1)
    core_ref = c.astype(jnp.int32).reshape(1)
    near_shards = lax.rem(z + jnp.arange(LINE, dtype=jnp.int32), LINE)[:, None] * 2 + (
        y ^ jnp.arange(2, dtype=jnp.int32)[None, :]
    )
    near_shards = near_shards.reshape(SHARDS)
    shard_ids = jnp.arange(SHARDS, dtype=jnp.int32)
    place_of_shard = jnp.sum(
        jnp.where(near_shards[None, :] == shard_ids[:, None], shard_ids[None, :], 0), axis=1
    )

    order_row = priority[0]
    pair_ids = jnp.arange(pair_count, dtype=jnp.int32)
    place_of = jnp.sum(
        jnp.where(order_row[None, :] == pair_ids[:, None], pair_ids[None, :], 0), axis=1
    ).reshape(tokens, route_count)
    labels = jnp.arange(expert_count, dtype=jnp.int32)
    hits = routes.T[None, :, :] == labels[:, None, None]
    place_at = jnp.sum(jnp.where(hits, place_of.T[None], 0), axis=1)
    named = jnp.any(hits, axis=1)
    place_at = jnp.where(named, place_at, pair_count)
    earlier = jnp.sum((place_at[:, None, :] < place_at[:, :, None]).astype(jnp.int32), axis=2)
    ranks = jnp.where(named, earlier, -1).astype(bf16)
    ranks = jnp.concatenate([ranks, segments.astype(bf16)], axis=0)
    ranks = jnp.pad(ranks, ((0, 0), (0, rows_each - tokens)))
    ranks = jnp.stack([ranks, move(ranks, CORE_SWAP)])
    ranks = jnp.concatenate([ranks, move(ranks, X_SWAP)])
    segment_rows = ranks[:, expert_count, :tokens].astype(jnp.int32)

    inputs_across = move(inputs, X_SWAP)
    small_in = jnp.stack([attn_gain, query_gain, key_gain, ffn_gain])
    small_in = jnp.concatenate(
        [small_in, router_weight.T, ranks.reshape(REPS * (expert_count + 1), rows_each)], axis=0
    )
    in_pieces = gather_rows(
        thin_columns(in_proj, rep_ref, width), first=(inputs_across, segment_rows)
    )
    small_in = gather_small(small_in, (in_pieces[2][0], in_pieces[1][1], in_pieces[3][1]))
    ranks = small_in[:, 4 + expert_count :, :tokens]
    ranks = jnp.take(ranks, near_shards ^ shard, axis=0)
    ranks = ranks.reshape(SHARDS, REPS, expert_count + 1, tokens)[:, :, :expert_count]
    ranks = ranks.astype(jnp.int32)
    counts = jnp.sum((ranks >= 0).astype(jnp.int32), axis=3)
    before = (near_shards[None, :] < near_shards[:, None])[:, :, None, None]
    bases = jnp.sum(jnp.where(before, counts[None], 0), axis=1)
    slots = bases[..., None] + ranks
    slots = jnp.where((ranks >= 0) & (slots < capacity), slots, -1)
    first_expert = shard * local_experts + c * core_experts
    slots = lax.dynamic_slice_in_dim(slots, first_expert, core_experts, 2)
    slots = slots.transpose(1, 2, 0, 3)
    shard_slots = jnp.take(slots, place_of_shard, axis=2)
    slots = slots.reshape(REPS, core_experts, group_rows)
    shard_slots = shard_slots.reshape(REPS, core_experts, group_rows)
    shifts = jnp.arange(core_experts, dtype=jnp.int32)[:, None] * capacity

    def columns_of(table):
        return jnp.where(table >= 0, table + shifts, -1).transpose(0, 2, 1)

    columns, shard_columns = columns_of(slots[:2]), columns_of(shard_slots[:2])

    in_part = flat(
        [
            (mine, after(beside, slots, shard_slots, columns, shard_columns))
            for mine, beside in in_pieces
        ]
    )

    small_in = jnp.take(small_in[:, : 4 + expert_count], shard_ids ^ shard, axis=0)
    small_in = small_in.transpose(1, 0, 2).reshape(4 + expert_count, width)
    gains = small_in[:4].astype(f32)
    router_rows = small_in[4:]
    part_gains = lax.dynamic_slice(
        gains[1:3].reshape(2, HEADS // 2, 2, HEAD_DIM),
        (0, c * heads, a, 0),
        (2, heads, 1, HEAD_DIM),
    ).reshape(2, part_width)

    hidden = inputs.astype(f32)
    home_rate = lax.rsqrt(jnp.mean(hidden * hidden, axis=-1, keepdims=True) + norm_eps)
    inputs_all = jnp.stack([inputs, inputs_across])
    inputs_all = jnp.stack([inputs_all, move(inputs_all, CORE_SWAP)], axis=1)
    inputs_all = inputs_all.reshape(REPS * tokens, width)
    inputs_all = pick_columns(inputs_all, near_shards, rows_each).astype(f32)
    unit_all = inputs_all * lax.rsqrt(
        jnp.mean(inputs_all * inputs_all, axis=-1, keepdims=True) + norm_eps
    )
    near_gain = jnp.take(gains[0].reshape(SHARDS, rows_each), near_shards, axis=0).reshape(width)
    normed_low = (unit_all * near_gain).astype(bf16)
    cot_across = move(grad_out, X_SWAP)
    normed_low = after(normed_low, cot_across)
    cot_own = after(grad_out, in_part)
    cot_own = lax.all_gather(cot_own, "shard", tiled=True)
    cos_table, sin_table = jax.vmap(rotary_tables)(segment_rows)
    sin_table = jnp.where(jnp.arange(HEAD_DIM) < HEAD_DIM // 2, -sin_table, sin_table)
    cos_table = cos_table.reshape(REPS * tokens, HEAD_DIM)
    sin_table = sin_table.reshape(REPS * tokens, HEAD_DIM)

    out_rows = rows_each // 4
    out_own = lax.dynamic_slice_in_dim(out_proj, rep * out_rows, out_rows, 0)
    out_own = after(out_own, in_pieces[2][0])

    projected = jnp.dot(normed_low, in_part, preferred_element_type=f32)
    squares = jnp.stack(
        [
            jnp.sum(projected[:, k * part_width : (k + 1) * part_width] ** 2, axis=1)
            for k in range(2)
        ],
        axis=1,
    )
    squares = rep_sum(squares.reshape(REPS, tokens, 2)).reshape(REPS * tokens, 2)
    pair_rate = lax.rsqrt(squares / width + norm_eps)
    attention_operands = (
        projected,
        pair_rate,
        part_gains,
        cos_table,
        sin_table,
        segment_rows.reshape(REPS * tokens, 1),
        segment_rows[:, None, :],
    )
    attended = attend(*attention_operands).reshape(2, 2, tokens, part_width)
    out_pieces = gather_rows(out_own, early=projected, late=(attended,))
    out_own = flat(out_pieces).reshape(SHARDS, out_rows, width)
    out_other = move(out_own, CORE_SWAP)
    out_part = jnp.where(
        c == 0,
        jnp.concatenate([out_own, out_other], axis=1),
        jnp.concatenate([out_other, out_own], axis=1),
    ).reshape(SHARDS * 2 * out_rows, width)
    attended = jnp.concatenate([attended[:, 0], move(attended[:, 1], CORE_SWAP)], axis=2)
    attended = attended.reshape(2 * tokens, 2 * part_width)
    head_of_place = ((near_shards // heads) ^ c) * heads + lax.rem(near_shards, heads)
    place_of_head = jnp.sum(
        jnp.where(head_of_place[None, :] == shard_ids[:, None], shard_ids[None, :], 0), axis=1
    )
    attended = pick_columns(attended, head_of_place, HEAD_DIM)
    mixed = jnp.dot(attended, out_part, preferred_element_type=f32).reshape(2, tokens, width)
    residual = hidden + mixed[0] + move(mixed[1].astype(bf16), X_SWAP).astype(f32)

    ffn_rate = lax.rsqrt(jnp.mean(residual * residual, axis=-1, keepdims=True) + norm_eps)
    ffn_unit = residual * ffn_rate
    ffn_low = (ffn_unit * gains[3]).astype(bf16)
    router_probs = softmax_rows(contract_cols(ffn_low, router_rows))

    def cot_part(group, rows, behind=()):
        return cotangent_part(core_ref, shard_slots[group], rows, down_weight, capacity, behind)

    first_ref = jnp.stack([c, first_expert]).astype(jnp.int32)

    def ffn_part(group, rows, slot_cot, behind=(), cost=QUIET):
        return forward_part(
            first_ref,
            slots[group],
            rows,
            router_rows,
            gate_weight,
            up_weight,
            slot_cot,
            behind,
            cost,
        )

    made = {}

    def fill_cot(follow):
        beside = move(cot_own, CORE_SWAP)
        own_part = cot_part(0, cot_own, (follow,))
        made["cot"] = [own_part, cot_part(1, beside, (own_part[1],))]
        return [own_part[1]]

    ffn_pieces = gather_rows(ffn_low, fill=fill_cot)
    near_cot = made["cot"]
    ffn_own = after(flat(ffn_pieces), near_cot[1][1])
    ffn_beside = move(ffn_own, CORE_SWAP)
    ffn_far = [move(jnp.concatenate(pair, axis=0), X_SWAP) for pair in ffn_pieces]
    cot_across = lax.all_gather(after(cot_across, ffn_pieces[2][0]), "shard", tiled=True)

    near = [ffn_part(0, ffn_own, near_cot[0][1])]
    near.append(ffn_part(1, ffn_beside, near_cot[1][1], (near[0][1],)))

    def rows_back(group, behind=()):
        _, _, grad_gate, grad_up, scores = near[group]
        return backward_part(
            core_ref, columns[group], grad_gate, grad_up, scores, gate_weight, up_weight, behind
        ).reshape(SHARDS, tokens, -1)

    grad_other = rows_back(1, (ffn_far[0], ffn_far[1]))
    grad_own = rows_back(0, (grad_other,))
    grad_other = move(grad_other, CORE_SWAP)

    def routed_rows(group, extra, behind):
        return routed_part(
            core_ref, shard_columns[group], near[group][1], down_weight, extra, behind
        )

    def fill_routed_other(follow):
        made["routed_other"] = routed_rows(1, (), follow + (ffn_far[2], cot_across))
        return [made["routed_other"]]

    def fill_far_cot(follow):
        made["far_cot"] = cot_part(2, cot_across, follow)
        return [made["far_cot"][1]]

    def fill_routed_own(follow):
        extra = (move(made["routed_other"], CORE_SWAP),)
        made["routed"] = routed_rows(0, extra, follow)
        return [made["routed"]]

    def fill_other_cot(follow):
        rows = move(after(cot_across, made["routed"]), CORE_SWAP)
        made["other_cot"] = cot_part(3, rows, follow)
        return [made["other_cot"][1]]

    grad_home = scatter_rows(
        [lambda place: grad_own[place], lambda place: grad_other[place]],
        [fill_routed_other, fill_routed_own, fill_far_cot, fill_other_cot, None],
    )
    routed = lax.psum_scatter(
        after(made["routed"], grad_home), "shard", scatter_dimension=0, tiled=True
    )
    ffn_far = jnp.concatenate([after(part, made["other_cot"][1]) for part in ffn_far], axis=0)
    ffn_far = [ffn_far, move(ffn_far, CORE_SWAP)]

    grad_ffn_home = grad_home[:, :width]
    home_score = grad_home[:, width : width + expert_count].astype(f32)
    grad_logits = home_score - router_probs * jnp.sum(home_score, axis=1, keepdims=True)
    grad_logits_low = grad_logits.astype(bf16)

    grad_ffn_in = grad_ffn_home.astype(f32) + jnp.dot(
        grad_logits_low, router_rows, preferred_element_type=f32
    )
    grad_router_local = contract_rows(grad_logits_low, ffn_low)
    grad_ffn_local = jnp.sum(grad_ffn_in * ffn_unit, axis=0)
    scaled = gains[3] * grad_ffn_in
    grad_residual = grad_out.astype(f32) + ffn_rate * (
        scaled - ffn_unit * jnp.mean(scaled * ffn_unit, axis=-1, keepdims=True)
    )
    residual_low = grad_residual.astype(bf16)
    residual_other = move(residual_low, X_SWAP)
    residual_pair = jnp.concatenate([residual_low, residual_other], axis=0)

    grad_attended = contract_cols(residual_pair, out_part).astype(bf16)
    grad_attended = pick_columns(grad_attended, place_of_head, HEAD_DIM)
    grad_attended = grad_attended.reshape(2, tokens, 2 * part_width)
    mine, theirs = grad_attended[:, :, :part_width], grad_attended[:, :, part_width:]
    grad_attended = jnp.stack([mine, move(theirs, CORE_SWAP)], axis=1)
    grad_attended = grad_attended.reshape(REPS * tokens, part_width)
    grad_pair, grad_value, dots, grad_pair_gain = attend_back(*attention_operands, grad_attended)
    grad_pair_gain = jnp.sum(grad_pair_gain, axis=0).reshape(2, heads, HEAD_DIM)
    dots = rep_sum(dots.reshape(REPS, tokens, 2)).reshape(REPS * tokens, 2) / width
    grad_projected = join_grads(projected, pair_rate, grad_pair, grad_value, dots, REPS)

    grad_in_part = contract_rows(normed_low, grad_projected).astype(bf16)
    grad_in_part = grad_in_part.reshape(SHARDS, rows_each, 3 * part_width)
    grad_normed = contract_cols(grad_projected, in_part)
    grad_attn_part = jnp.sum(grad_normed * unit_all, axis=0)

    pair_gains = jnp.zeros((2, HEADS // 2, 2, HEAD_DIM), f32)
    pair_gains = lax.dynamic_update_slice(
        pair_gains, grad_pair_gain[:, :, None], (0, c * heads, a, 0)
    )
    small = jnp.concatenate(
        [grad_ffn_local[None], pair_gains.reshape(2, width), grad_router_local], axis=0
    )
    small = jnp.take(small.reshape(-1, SHARDS, rows_each), near_shards, axis=1)
    small = jnp.concatenate([grad_attn_part.reshape(1, SHARDS, rows_each), small], axis=0)
    small = jnp.pad(small, ((0, HEAD_DIM - small.shape[0]), (0, 0), (0, 0)))
    small = small.astype(bf16).transpose(1, 2, 0)

    grad_out_part = contract_rows(after(attended, grad_projected), residual_pair).astype(bf16)
    out_parts = grad_out_part.reshape(SHARDS, 2, out_rows, width)
    out_own = lax.dynamic_index_in_dim(out_parts, c, 1, keepdims=False)
    out_other = lax.dynamic_index_in_dim(out_parts, 1 - c, 1, keepdims=False)
    out_sum = added(out_own, move(out_other, CORE_SWAP))
    out_sum = jnp.take(out_sum, place_of_shard, axis=0).reshape(SHARDS * out_rows, width)

    far_cot = [made["far_cot"], made["other_cot"]]

    def fill_far(follow):
        made["far"] = ffn_part(2, ffn_far[0], far_cot[0][1], follow, LOUD)
        return [made["far"][3]]

    normed_other = grad_normed.astype(bf16).reshape(2, 2, tokens, width)
    normed_mine = added(normed_other[:, 0], move(normed_other[:, 1], CORE_SWAP))
    normed_across = move(normed_mine[1], X_SWAP)

    def fill_other(follow):
        made["other"] = ffn_part(
            3, ffn_far[1], far_cot[1][1], follow + (made["far"][3], normed_mine, routed), LOUD
        )
        return [made["other"][3]]

    def weight_grad(left, right, follow):
        first, *follow = lax.optimization_barrier((left[0],) + follow)
        left = jnp.concatenate([first] + left[1:], axis=1)
        right = jnp.concatenate(right, axis=1)
        grad = jnp.einsum("ecd,ecf->edf", left, right, preferred_element_type=f32).astype(bf16)
        return grad, follow

    def groups(index):
        return [part[index] for part in (near[0], near[1], made["far"], made["other"])]

    def fill_down(follow):
        cots = [part[0] for part in near_cot + far_cot]
        reduced, low, high, third = follow
        made["down"], (reduced, low, high, _) = weight_grad(
            groups(1), cots, (reduced, low, high, normed_across)
        )
        return after(reduced, made["down"]), low, high, third

    in_sum = scatter_rows(
        [lambda place: jnp.concatenate([grad_in_part[place], small[place]], axis=1)],
        [fill_far, None, None, fill_other, fill_down],
    )
    in_other = move(in_sum, X_SWAP)
    out_sum = lax.psum_scatter(
        after(out_sum, routed), "shard", scatter_dimension=0, tiled=True
    )
    made["gate"], (in_sum, out_sum) = weight_grad(groups(0), groups(2), (in_sum, out_sum))
    out_across = move(out_sum, X_SWAP)
    down_all = widen(
        made["down"],
        move(made["down"], CORE_SWAP),
        core_ref,
        (made["gate"], in_other, out_across),
    )
    in_all = jnp.stack([in_sum, after(in_other, made["gate"])])
    in_beside = move(in_all, CORE_SWAP)
    grad_up, (_, in_beside) = weight_grad(groups(0), groups(3), (down_all, in_beside))
    in_all = jnp.stack([in_all, in_beside], axis=1).reshape((REPS,) + in_sum.shape)
    grad_in = weave_columns(in_all, rep_ref, 3 * part_width, (grad_up,))
    small = jnp.sum(in_all[:, :, 3 * part_width :].astype(f32), axis=0).T
    gate_all = widen(made["gate"], move(made["gate"], CORE_SWAP), core_ref, (grad_up,))
    up_all = widen(grad_up, move(grad_up, CORE_SWAP), core_ref, (gate_all,))

    outputs = (residual + after(routed, in_sum).astype(f32)).astype(bf16)
    grad_normed = added(normed_mine[0], normed_across)
    grad_normed = pick_columns(grad_normed, place_of_shard, rows_each).astype(f32)
    home_unit = hidden * home_rate
    scaled = gains[0] * grad_normed
    grad_inputs = (
        grad_residual
        + home_rate * (scaled - home_unit * jnp.mean(scaled * home_unit, axis=-1, keepdims=True))
    ).astype(bf16)

    out_sum = jnp.stack([out_sum, out_across])
    out_sum = jnp.stack([out_sum, move(out_sum, CORE_SWAP)], axis=1)
    out_sum = out_sum.reshape(REPS, out_rows, width)
    out_sum = jnp.take(out_sum, rep ^ jnp.arange(REPS, dtype=jnp.int32), axis=0)
    grad_out_proj = out_sum.reshape(rows_each, width).astype(f32)
    return (
        outputs,
        grad_inputs,
        small[0],
        grad_in,
        small[2],
        small[3],
        grad_out_proj,
        small[1],
        small[4 : 4 + expert_count].T,
        gate_all,
        up_all,
        down_all,
    )


def solution(mesh):
    fits = dict(mesh.shape) == {"rep": REPS, "shard": SHARDS}
    body = fast_local if fits else local
    in_specs = (
        P(("rep", "shard"), None),
        P("shard"),
        P("shard", None),
        P("shard"),
        P("shard"),
        P("shard", None),
        P("shard"),
        P("shard", None),
        P("shard", None, None),
        P("shard", None, None),
        P("shard", None, None),
        P(("rep", "shard"), None),
        P(("rep", "shard"), None),
        P(("rep", "shard"), None),
        P(("rep", "shard"), None),
    )
    out_specs = (
        P(("rep", "shard"), None),
        P(("rep", "shard"), None),
        P("shard"),
        P("shard", None),
        P("shard"),
        P("shard"),
        P("shard", None),
        P("shard"),
        P("shard", None),
        P("shard", None, None),
        P("shard", None, None),
        P("shard", None, None),
    )
    return jax.shard_map(body, mesh=mesh, in_specs=in_specs, out_specs=out_specs, check_vma=False)
```

```python
import functools

import jax
import jax.numpy as jnp
from jax import lax
from jax.experimental import pallas as pl
from jax.experimental.pallas import tpu as pltpu
from jax.sharding import PartitionSpec as P

HEADS = 16
HEAD_DIM = 128


norm_eps = 1e-05
rope_base = 10000.0
masked_score = -1e30


def rms_scale(values, gains):
    normed = values * lax.rsqrt(jnp.mean(values * values, axis=-1, keepdims=True) + norm_eps)
    return normed * gains


def rotary_tables(segment_row):
    length = segment_row.shape[0]
    places = jnp.arange(length, dtype=jnp.int32)
    starting = jnp.concatenate(
        [jnp.ones((1,), jnp.int32), (segment_row[1:] != segment_row[:-1]).astype(jnp.int32)]
    )
    first_place = lax.cummax(jnp.where(starting > 0, places, 0), axis=0)
    offsets = (places - first_place).astype(jnp.float32)
    halves = HEAD_DIM // 2
    inverse = rope_base ** (-2.0 * jnp.arange(halves, dtype=jnp.float32) / HEAD_DIM)
    angles = offsets[:, None] * inverse[None, :]
    angles = jnp.concatenate([angles, angles], axis=1)
    return (jnp.cos(angles), jnp.sin(angles))


def rotate(values, cos_table, sin_table):
    halves = values.shape[-1] // 2
    turned = jnp.concatenate([-values[..., halves:], values[..., :halves]], axis=-1)
    return values * cos_table[:, None, :] + turned * sin_table[:, None, :]


def query_key(raw_query, raw_key, query_scale, key_scale, cos_table, sin_table):
    row_count = raw_query.shape[0]
    normed_query = rms_scale(raw_query, query_scale).reshape(row_count, HEADS, HEAD_DIM)
    normed_key = rms_scale(raw_key, key_scale).reshape(row_count, HEADS, HEAD_DIM)
    return (rotate(normed_query, cos_table, sin_table), rotate(normed_key, cos_table, sin_table))


def softmax_rows(logits):
    highest = jnp.max(logits, axis=-1, keepdims=True)
    raised = jnp.exp(logits - highest)
    return raised / jnp.sum(raised, axis=-1, keepdims=True)


def swiglu(gate_pre, up_pre):
    return jax.nn.silu(gate_pre) * up_pre


def contract_rows(left_side, right_side):
    return lax.dot_general(
        left_side, right_side, (((0,), (0,)), ((), ())), preferred_element_type=jnp.float32
    )


def contract_cols(left_side, right_side):
    return lax.dot_general(
        left_side, right_side, (((1,), (1,)), ((), ())), preferred_element_type=jnp.float32
    )


def pick_rows(source_rows, row_picks):
    return jax.vmap(lambda expert_rows, picked: expert_rows[picked])(source_rows, row_picks)


def local(
    inputs,
    attn_gain,
    in_proj,
    query_gain,
    key_gain,
    out_proj,
    ffn_gain,
    router_weight,
    gate_weight,
    up_weight,
    down_weight,
    routes,
    priority,
    segments,
    grad_out,
):
    tokens = inputs.shape[0]
    model_width = inputs.shape[1]
    local_experts = gate_weight.shape[0]
    group_count = lax.axis_size("shard")
    my_index = lax.axis_index("shard")
    expert_count = local_experts * group_count
    route_count = routes.shape[1]
    pair_count = tokens * route_count
    capacity = 5 * pair_count * group_count // (4 * expert_count)
    send_most = 2 * pair_count // expert_count
    segment_row = segments[0]
    cos_table, sin_table = rotary_tables(segment_row)
    hidden_in = inputs.astype(jnp.float32)
    unit_rows = hidden_in * lax.rsqrt(
        jnp.mean(hidden_in * hidden_in, axis=-1, keepdims=True) + norm_eps
    )
    weight_piece = lax.all_gather(in_proj, "shard", axis=0, tiled=True)
    attn_piece = lax.all_gather(attn_gain, "shard", axis=0, tiled=True)
    query_piece = lax.all_gather(query_gain, "shard", axis=0, tiled=True)
    key_piece = lax.all_gather(key_gain, "shard", axis=0, tiled=True)
    scaled = (unit_rows * attn_piece.astype(jnp.float32)).astype(jnp.bfloat16)
    result = (
        jnp.dot(scaled, weight_piece, preferred_element_type=jnp.float32),
        attn_piece.astype(jnp.float32),
        query_piece.astype(jnp.float32),
        key_piece.astype(jnp.float32),
    )
    folded_in = result
    projected = folded_in[0]
    normed_attn, attn_norm_back = jax.vjp(rms_scale, hidden_in, folded_in[1])
    normed_low = normed_attn.astype(jnp.bfloat16)
    raw_query = projected[:, :model_width]
    raw_key = projected[:, model_width : 2 * model_width]
    raw_value = projected[:, 2 * model_width :]

    def rotated_pair(query_raw, key_raw, query_scale, key_scale):
        return query_key(query_raw, key_raw, query_scale, key_scale, cos_table, sin_table)

    (turned_query, turned_key), query_key_back = jax.vjp(
        rotated_pair, raw_query, raw_key, folded_in[2], folded_in[3]
    )
    query_low = turned_query.astype(jnp.bfloat16)
    key_low = turned_key.astype(jnp.bfloat16)
    value_low = raw_value.astype(jnp.bfloat16).reshape(tokens, HEADS, HEAD_DIM)
    places = jnp.arange(tokens, dtype=jnp.int32)
    allowed = (segment_row[:, None] == segment_row[None, :]) & (places[None, :] <= places[:, None])
    score_scale = HEAD_DIM ** (-0.5)

    def masked_scores(queries, key_vecs):
        products = jnp.einsum("qhd,khd->hqk", queries, key_vecs, preferred_element_type=jnp.float32)
        return jnp.where(allowed[None], products * score_scale, masked_score)

    scores = masked_scores(query_low, key_low)
    highest = jnp.max(scores, axis=-1, keepdims=True)
    raised = jnp.exp(scores - highest)
    totals = jnp.sum(raised, axis=-1, keepdims=True)
    attn_probs = raised / totals
    log_total = highest + jnp.log(totals)
    mixed = jnp.einsum(
        "hqk,khd->qhd",
        attn_probs.astype(jnp.bfloat16),
        value_low,
        preferred_element_type=jnp.float32,
    )
    attended = mixed.reshape(tokens, model_width).astype(jnp.bfloat16)
    weight_piece = lax.all_gather(out_proj, "shard", axis=0, tiled=True)
    ffn_piece = lax.all_gather(ffn_gain, "shard", axis=0, tiled=True)
    router_piece = lax.all_gather(router_weight, "shard", axis=0, tiled=True)
    result = (
        jnp.dot(attended, weight_piece, preferred_element_type=jnp.float32),
        ffn_piece.astype(jnp.float32),
        router_piece,
    )
    residual = hidden_in + result[0]
    router_full = result[2]
    normed_ffn, ffn_norm_back = jax.vjp(rms_scale, residual, result[1])
    ffn_low = normed_ffn.astype(jnp.bfloat16)
    logits = jnp.dot(ffn_low, router_full, preferred_element_type=jnp.float32)
    router_probs, router_back = jax.vjp(softmax_rows, logits)
    flat_routes = routes.reshape(pair_count)
    order_row = priority[0]
    ranked_expert = flat_routes[order_row]
    labels = jnp.arange(expert_count, dtype=jnp.int32)
    matches = (ranked_expert[:, None] == labels[None, :]).astype(jnp.int32)
    rank_in = (
        jnp.sum(jnp.cumsum(matches, axis=0, dtype=jnp.int32) * matches, axis=1, dtype=jnp.int32) - 1
    )
    counts = jnp.sum(matches, axis=0, dtype=jnp.int32)
    all_counts = lax.all_gather(counts[None, :], "shard", axis=0, tiled=True)
    base_slots = jnp.cumsum(all_counts, axis=0, dtype=jnp.int32) - all_counts
    my_bases = lax.dynamic_index_in_dim(base_slots, my_index, 0, keepdims=False)
    slot_index = jnp.sum(matches * my_bases[None, :], axis=1, dtype=jnp.int32) + rank_in
    cell_index = ranked_expert * send_most + rank_in
    inverse_order = (
        jnp.zeros((pair_count,), jnp.int32)
        .at[order_row]
        .set(jnp.arange(pair_count, dtype=jnp.int32))
    )
    pair_cell = cell_index[inverse_order].reshape(tokens, route_count)
    pair_keep = (
        (slot_index[inverse_order] < capacity).astype(jnp.float32).reshape(tokens, route_count)
    )
    cell_pair = jnp.zeros((expert_count * send_most,), jnp.int32).at[cell_index].set(order_row)
    cell_live = (jnp.arange(send_most, dtype=jnp.int32)[None, :] < counts[:, None]).reshape(
        expert_count * send_most
    )
    cell_token = cell_pair // route_count
    outgoing = jnp.where(cell_live[:, None], ffn_low[cell_token], 0).reshape(
        expert_count, send_most, model_width
    )
    arrived = lax.all_to_all(outgoing, "shard", split_axis=0, concat_axis=1, tiled=True)
    own_counts = lax.dynamic_slice_in_dim(all_counts, my_index * local_experts, local_experts, 1).T
    own_bases = lax.dynamic_slice_in_dim(base_slots, my_index * local_experts, local_experts, 1).T
    slot_ids = jnp.arange(capacity, dtype=jnp.int32)
    slot_ends = own_bases + own_counts
    source_ids = jnp.sum(
        (slot_ends[:, None, :] <= slot_ids[None, :, None]).astype(jnp.int32),
        axis=2,
        dtype=jnp.int32,
    )
    slot_filled = source_ids < group_count
    source_safe = jnp.minimum(source_ids, group_count - 1)
    slot_rows = (
        source_safe * send_most
        + slot_ids[None, :]
        - jnp.take_along_axis(own_bases, source_safe, axis=1)
    )
    slot_rows = jnp.where(slot_filled, slot_rows, 0)
    expert_in = jnp.where(slot_filled[..., None], pick_rows(arrived, slot_rows), 0)
    gate_pre = jnp.einsum(
        "ecd,edf->ecf", expert_in, gate_weight, preferred_element_type=jnp.float32
    )
    up_pre = jnp.einsum("ecd,edf->ecf", expert_in, up_weight, preferred_element_type=jnp.float32)
    activated, swiglu_back = jax.vjp(swiglu, gate_pre, up_pre)
    act_low = activated.astype(jnp.bfloat16)
    expert_out = jnp.einsum(
        "ecf,efd->ecd", act_low, down_weight, preferred_element_type=jnp.float32
    ).astype(jnp.bfloat16)
    cell_positions = jnp.arange(send_most, dtype=jnp.int32)
    cell_slot = own_bases[:, :, None] + cell_positions[None, None, :]
    cell_used = (cell_positions[None, None, :] < own_counts[:, :, None]) & (cell_slot < capacity)
    cell_slot = jnp.where(cell_used, cell_slot, 0).reshape(local_experts, group_count * send_most)
    cell_used = cell_used.reshape(local_experts, group_count * send_most)
    returning = jnp.where(cell_used[..., None], pick_rows(expert_out, cell_slot), 0)
    returned = lax.all_to_all(returning, "shard", split_axis=1, concat_axis=0, tiled=True).reshape(
        expert_count * send_most, model_width
    )
    pair_rows = returned[pair_cell].astype(jnp.float32)
    pair_weight = jnp.take_along_axis(router_probs, routes, axis=1) * pair_keep
    outputs = (residual + jnp.sum(pair_weight[..., None] * pair_rows, axis=1)).astype(jnp.bfloat16)
    cotangent = grad_out.astype(jnp.float32)
    grad_rows = (
        (pair_weight[..., None] * cotangent[:, None, :])
        .astype(jnp.bfloat16)
        .reshape(pair_count, model_width)
    )
    grad_pair_weight = jnp.sum(pair_rows * cotangent[:, None, :], axis=2) * pair_keep
    route_hits = (routes[..., None] == labels[None, None, :]).astype(jnp.float32)
    grad_router_probs = jnp.sum(grad_pair_weight[..., None] * route_hits, axis=1)
    (grad_logits,) = router_back(grad_router_probs)
    grad_logits_low = grad_logits.astype(jnp.bfloat16)
    outgoing_grad = jnp.where(cell_live[:, None], grad_rows[cell_pair], 0).reshape(
        expert_count, send_most, model_width
    )
    arrived_grad = lax.all_to_all(outgoing_grad, "shard", split_axis=0, concat_axis=1, tiled=True)
    grad_expert_out = jnp.where(slot_filled[..., None], pick_rows(arrived_grad, slot_rows), 0)
    grad_act = jnp.einsum(
        "ecd,efd->ecf", grad_expert_out, down_weight, preferred_element_type=jnp.float32
    )
    grad_down = jnp.einsum(
        "ecf,ecd->efd", act_low, grad_expert_out, preferred_element_type=jnp.float32
    )
    grad_gate_pre, grad_up_pre = swiglu_back(grad_act)
    gate_grad_low = grad_gate_pre.astype(jnp.bfloat16)
    up_grad_low = grad_up_pre.astype(jnp.bfloat16)
    grad_gate = jnp.einsum(
        "ecd,ecf->edf", expert_in, gate_grad_low, preferred_element_type=jnp.float32
    )
    grad_up = jnp.einsum("ecd,ecf->edf", expert_in, up_grad_low, preferred_element_type=jnp.float32)
    grad_expert_in = (
        jnp.einsum("ecf,edf->ecd", gate_grad_low, gate_weight, preferred_element_type=jnp.float32)
        + jnp.einsum("ecf,edf->ecd", up_grad_low, up_weight, preferred_element_type=jnp.float32)
    ).astype(jnp.bfloat16)
    returning_grad = jnp.where(cell_used[..., None], pick_rows(grad_expert_in, cell_slot), 0)
    returned_grad = lax.all_to_all(
        returning_grad, "shard", split_axis=1, concat_axis=0, tiled=True
    ).reshape(expert_count * send_most, model_width)
    grad_ffn_in = jnp.sum(returned_grad[pair_cell].astype(jnp.float32), axis=1) + contract_cols(
        grad_logits_low, router_full
    )
    grad_router_local = contract_rows(ffn_low, grad_logits_low)
    grad_residual_norm, grad_ffn_local = ffn_norm_back(grad_ffn_in)
    grad_residual = cotangent + grad_residual_norm
    residual_low = grad_residual.astype(jnp.bfloat16)
    grad_out_local = lax.psum_scatter(
        contract_rows(attended, residual_low).astype(jnp.bfloat16),
        "shard",
        scatter_dimension=0,
        tiled=True,
    )
    grad_attended = contract_cols(
        residual_low, lax.all_gather(out_proj, "shard", axis=0, tiled=True)
    )
    grad_mixed = grad_attended.astype(jnp.bfloat16).reshape(tokens, HEADS, HEAD_DIM)
    scores_again = masked_scores(query_low, key_low)
    probs_again = jnp.exp(scores_again - log_total)
    grad_probs = jnp.einsum(
        "qhd,khd->hqk", grad_mixed, value_low, preferred_element_type=jnp.float32
    )
    spread = jnp.sum(probs_again * grad_probs, axis=-1, keepdims=True)
    grad_scores = (probs_again * (grad_probs - spread)).astype(jnp.bfloat16)
    grad_query = (
        jnp.einsum("hqk,khd->qhd", grad_scores, key_low, preferred_element_type=jnp.float32)
        * score_scale
    )
    grad_key = (
        jnp.einsum("hqk,qhd->khd", grad_scores, query_low, preferred_element_type=jnp.float32)
        * score_scale
    )
    grad_value = jnp.einsum(
        "hqk,qhd->khd",
        probs_again.astype(jnp.bfloat16),
        grad_mixed,
        preferred_element_type=jnp.float32,
    )
    grad_raw_query, grad_raw_key, grad_query_local, grad_key_local = query_key_back(
        (grad_query, grad_key)
    )
    grad_qkv = jnp.concatenate(
        [grad_raw_query, grad_raw_key, grad_value.reshape(tokens, model_width)], axis=1
    ).astype(jnp.bfloat16)
    grad_in_local = lax.psum_scatter(
        contract_rows(normed_low, grad_qkv).astype(jnp.bfloat16),
        "shard",
        scatter_dimension=0,
        tiled=True,
    )
    grad_normed = contract_cols(grad_qkv, lax.all_gather(in_proj, "shard", axis=0, tiled=True))
    grad_hidden_norm, grad_attn_local = attn_norm_back(grad_normed)
    grad_inputs = (grad_residual + grad_hidden_norm).astype(jnp.bfloat16)
    small_parts = (
        lax.psum_scatter(
            grad_attn_local.astype(jnp.bfloat16), "shard", scatter_dimension=0, tiled=True
        ).astype(jnp.float32),
        lax.psum_scatter(
            grad_query_local.astype(jnp.bfloat16), "shard", scatter_dimension=0, tiled=True
        ).astype(jnp.float32),
        lax.psum_scatter(
            grad_key_local.astype(jnp.bfloat16), "shard", scatter_dimension=0, tiled=True
        ).astype(jnp.float32),
        lax.psum_scatter(
            grad_ffn_local.astype(jnp.bfloat16), "shard", scatter_dimension=0, tiled=True
        ).astype(jnp.float32),
        lax.psum_scatter(
            grad_router_local.astype(jnp.bfloat16), "shard", scatter_dimension=0, tiled=True
        ).astype(jnp.float32),
    )
    summed = (
        lax.psum(grad_in_local, "rep").astype(jnp.float32),
        lax.psum(grad_out_local, "rep").astype(jnp.float32),
        lax.psum(small_parts[0].astype(jnp.bfloat16), "rep").astype(jnp.float32),
        lax.psum(small_parts[1].astype(jnp.bfloat16), "rep").astype(jnp.float32),
        lax.psum(small_parts[2].astype(jnp.bfloat16), "rep").astype(jnp.float32),
        lax.psum(small_parts[3].astype(jnp.bfloat16), "rep").astype(jnp.float32),
        lax.psum(small_parts[4].astype(jnp.bfloat16), "rep").astype(jnp.float32),
        lax.psum(grad_gate.astype(jnp.bfloat16), "rep").astype(jnp.float32),
        lax.psum(grad_up.astype(jnp.bfloat16), "rep").astype(jnp.float32),
        lax.psum(grad_down.astype(jnp.bfloat16), "rep").astype(jnp.float32),
    )
    return (
        outputs,
        grad_inputs,
        summed[2],
        summed[0],
        summed[3],
        summed[4],
        summed[1],
        summed[5],
        summed[6],
        summed[7],
        summed[8],
        summed[9],
    )


AXES = ("rep", "shard")
LINE = 4
SHARDS = 8
REPS = 4


def pairs_of(target):
    moves = []
    for rep in range(REPS):
        for shard in range(SHARDS):
            there = target(rep, shard)
            moves.append((rep * SHARDS + shard, there[0] * SHARDS + there[1]))
    return moves


CORE_SWAP = pairs_of(lambda rep, shard: (rep ^ 1, shard))
X_SWAP = pairs_of(lambda rep, shard: (rep ^ 2, shard))
Y_SWAP = pairs_of(lambda rep, shard: (rep, shard ^ 1))
SHARD_SWAP = [
    pairs_of(lambda rep, shard: (rep, shard ^ 1)),
    pairs_of(lambda rep, shard: (rep, shard ^ 2)),
    pairs_of(lambda rep, shard: (rep, shard ^ 4)),
]
Z_FROM = [pairs_of(lambda rep, shard: (rep, (shard - 2 * k) % SHARDS)) for k in range(LINE)]
Z_TO = [pairs_of(lambda rep, shard: (rep, (shard + 2 * k) % SHARDS)) for k in range(LINE)]


def move(values, moves):
    return lax.ppermute(values, AXES, moves)


def after(values, *others):
    return lax.optimization_barrier((values,) + others)[0]


def gather_small(values, hold):
    low = jnp.stack([values, move(values, SHARD_SWAP[1])])
    high = jnp.stack([low, move(low, SHARD_SWAP[2])])
    both = jnp.stack([high, move(after(high, *hold), SHARD_SWAP[0])], axis=2)
    return both.reshape((SHARDS,) + values.shape)


def gather_rows(values, early=(), late=(), fill=None, first=()):
    moved = {k: move(values, Z_FROM[k]) for k in (1, 3)}
    moved[2] = move(after(values, moved[1], *first), Z_FROM[2])
    mine, beside = {0: values}, {0: move(values, Y_SWAP)}
    for k in (1, 3, 2):
        mine[k] = after(moved[k], *early) if early else moved[k]
        if k == 2 and fill is not None:
            mine[k] = after(mine[k], *fill(mine[3]))
        beside[k] = move(mine[k], Y_SWAP)
    if late:
        beside = {k: after(beside[k], *late) for k in beside}
    return [(mine[k], beside[k]) for k in range(LINE)]


def flat(pieces):
    return jnp.concatenate([piece for pair in pieces for piece in pair], axis=0)


def added(first, *others):
    total = first.astype(jnp.float32)
    for other in others:
        total = total + other.astype(jnp.float32)
    return total.astype(first.dtype)


def scatter_rows(parts, fills, hold=False):
    away = {k: added(*[part(2 * k + 1) for part in parts]) for k in (2, 1, 3, 0)}
    moved = {2: move(away[2], Y_SWAP)}
    arrived, reduced = [], away[2]
    for k, fill in zip((2, 1, 3, 0), fills):
        filled = [] if fill is None else fill((reduced,))
        if k == 2:
            for other in (1, 3, 0):
                held = after(away[other], *filled) if hold else away[other]
                moved[other] = move(held, Y_SWAP)
        here = after(moved[k], *filled) if filled else moved[k]
        reduced = added(here, *[part(2 * k) for part in parts])
        if k > 0:
            arrived.append(move(reduced, Z_TO[k]))
    if fills[4] is not None:
        reduced, *arrived = fills[4]((reduced, *arrived))
    return added(reduced, *arrived)


LIMIT = 56 * 2**20
HIDDEN_BLOCK = 256
WIDTH_BLOCK = 512
QUIET = pl.CostEstimate(flops=0, bytes_accessed=0, transcendentals=0)
LOUD = pl.CostEstimate(flops=10**11, bytes_accessed=0, transcendentals=0)


def ordered(kernel, behind):
    def body(scalar_ref, *refs):
        return kernel(scalar_ref, *refs[behind:])

    return body


HELD = pl.BlockSpec(memory_space=pl.ANY)


def copy_block(order_ref, from_ref, into_ref):
    into_ref[...] = from_ref[...]


def pick_columns(values, order, block):
    rows = values.shape[0]
    picks = order.shape[0]
    return pl.pallas_call(
        copy_block,
        grid_spec=pltpu.PrefetchScalarGridSpec(
            num_scalar_prefetch=1,
            grid=(picks,),
            in_specs=[pl.BlockSpec((rows, block), lambda i, order: (0, order[i]))],
            out_specs=pl.BlockSpec((rows, block), lambda i, order: (0, i)),
        ),
        out_shape=jax.ShapeDtypeStruct((rows, picks * block), values.dtype),
        compiler_params=pltpu.CompilerParams(vmem_limit_bytes=32 * 2**20),
    )(order, values)


def thin_kernel(rep_ref, from_ref, into_ref):
    heads = into_ref.shape[1] // HEAD_DIM

    def take(parity):
        for head in range(heads):
            start = (2 * head + parity) * HEAD_DIM
            into_ref[:, head * HEAD_DIM : (head + 1) * HEAD_DIM] = from_ref[
                :, start : start + HEAD_DIM
            ]

    @pl.when(rep_ref[0] < 2)
    def _():
        take(0)

    @pl.when(rep_ref[0] >= 2)
    def _():
        take(1)


def thin_columns(weights, rep, width):
    rows = weights.shape[0]
    return pl.pallas_call(
        thin_kernel,
        grid_spec=pltpu.PrefetchScalarGridSpec(
            num_scalar_prefetch=1,
            grid=(3,),
            in_specs=[
                pl.BlockSpec((rows, width // 2), lambda i, rep: (0, 2 * i + lax.rem(rep[0], 2)))
            ],
            out_specs=pl.BlockSpec((rows, width // 4), lambda i, rep: (0, i)),
        ),
        out_shape=jax.ShapeDtypeStruct((rows, 3 * width // 4), weights.dtype),
        compiler_params=pltpu.CompilerParams(vmem_limit_bytes=32 * 2**20),
    )(rep, weights)


def weave_kernel(rep_ref, even_ref, odd_ref, into_ref):
    for head in range(even_ref.shape[2] // HEAD_DIM):
        part = slice(head * HEAD_DIM, (head + 1) * HEAD_DIM)
        start = 2 * head * HEAD_DIM
        into_ref[:, start : start + HEAD_DIM] = even_ref[0, :, part].astype(jnp.float32)
        into_ref[:, start + HEAD_DIM : start + 2 * HEAD_DIM] = odd_ref[0, :, part].astype(
            jnp.float32
        )


def weave_columns(pieces, rep, columns, behind):
    rows = pieces.shape[1]
    block = columns // 3
    return pl.pallas_call(
        ordered(weave_kernel, len(behind)),
        grid_spec=pltpu.PrefetchScalarGridSpec(
            num_scalar_prefetch=1,
            grid=(3, 2),
            in_specs=[HELD] * len(behind)
            + [
                pl.BlockSpec((1, rows, block), lambda i, j, rep: (j ^ rep[0], 0, i)),
                pl.BlockSpec((1, rows, block), lambda i, j, rep: ((j + 2) ^ rep[0], 0, i)),
            ],
            out_specs=pl.BlockSpec((rows, 2 * block), lambda i, j, rep: (0, 2 * i + j)),
        ),
        out_shape=jax.ShapeDtypeStruct((rows, 4 * columns), jnp.float32),
        compiler_params=pltpu.CompilerParams(vmem_limit_bytes=32 * 2**20),
    )(rep, *behind, pieces, pieces)


def widen_kernel(core_ref, own_ref, other_ref, into_ref):
    mine = pl.program_id(0) == core_ref[0]

    @pl.when(mine)
    def _():
        into_ref[...] = own_ref[...].astype(jnp.float32)

    @pl.when(jnp.logical_not(mine))
    def _():
        into_ref[...] = other_ref[...].astype(jnp.float32)


def widen(own, other, core, behind=()):
    experts, rows, columns = own.shape
    block = rows // 4
    steps = experts * 4

    def place(hold, core, i, j):
        return jnp.where(i == hold, j, jnp.where(hold == 0, steps - 1, 0))

    own_map = lambda i, j, core: (place(core[0], core, i, j), 0)
    other_map = lambda i, j, core: (place(1 - core[0], core, i, j), 0)
    result = pl.pallas_call(
        ordered(widen_kernel, len(behind)),
        grid_spec=pltpu.PrefetchScalarGridSpec(
            num_scalar_prefetch=1,
            grid=(2, steps),
            in_specs=[HELD] * len(behind)
            + [
                pl.BlockSpec((block, columns), own_map),
                pl.BlockSpec((block, columns), other_map),
            ],
            out_specs=pl.BlockSpec((block, columns), lambda i, j, core: (i * steps + j, 0)),
        ),
        out_shape=jax.ShapeDtypeStruct((2 * experts * rows, columns), jnp.float32),
        compiler_params=pltpu.CompilerParams(vmem_limit_bytes=32 * 2**20),
        cost_estimate=QUIET,
    )(
        core,
        *behind,
        own.reshape(experts * rows, columns),
        other.reshape(experts * rows, columns),
    )
    return result.reshape(2 * experts, rows, columns)


def slot_rows(slots, capacity):
    places = lax.broadcasted_iota(jnp.int32, (capacity, slots.shape[1]), 0)
    return jnp.where(places == slots, 1.0, 0.0).astype(jnp.bfloat16)


def slot_columns(slots, columns):
    places = lax.broadcasted_iota(jnp.int32, (slots.shape[0], columns), 1)
    found = places == slots[:, 0:1]
    for expert in range(1, slots.shape[1]):
        found = found | (places == slots[:, expert : expert + 1])
    return jnp.where(found, 1.0, 0.0).astype(jnp.bfloat16)


def dot_wide(left, right):
    return jnp.dot(left, right, preferred_element_type=jnp.float32)


def pick_rows_into(slots_ref, rows_ref, into_ref):
    choice = slot_rows(slots_ref[0], into_ref.shape[1])
    for start in range(0, rows_ref.shape[1], WIDTH_BLOCK):
        part = slice(start, start + WIDTH_BLOCK)
        into_ref[0, :, part] = dot_wide(choice, rows_ref[:, part]).astype(jnp.bfloat16)


def cotangent_kernel(core_ref, slots_ref, rows_ref, down_ref, picked_ref, slot_ref):
    @pl.when(pl.program_id(1) == 0)
    def _():
        pick_rows_into(slots_ref, rows_ref, picked_ref)

    slot_ref[0] = contract_cols(picked_ref[0], down_ref[0])


def cotangent_part(core, slots, rows, down_weight, capacity, behind=()):
    experts, tokens = slots.shape
    width, hidden = rows.shape[1], down_weight.shape[1]
    return pl.pallas_call(
        ordered(cotangent_kernel, len(behind)),
        grid_spec=pltpu.PrefetchScalarGridSpec(
            num_scalar_prefetch=1,
            grid=(experts, hidden // HIDDEN_BLOCK),
            in_specs=[HELD] * len(behind)
            + [
                pl.BlockSpec((1, 1, tokens), lambda e, n, core: (e, 0, 0)),
                pl.BlockSpec((tokens, width), lambda e, n, core: (0, 0)),
                pl.BlockSpec(
                    (1, HIDDEN_BLOCK, width), lambda e, n, core: (core[0] * experts + e, n, 0)
                ),
            ],
            out_specs=[
                pl.BlockSpec((1, capacity, width), lambda e, n, core: (e, 0, 0)),
                pl.BlockSpec((1, capacity, HIDDEN_BLOCK), lambda e, n, core: (e, 0, n)),
            ],
        ),
        out_shape=[
            jax.ShapeDtypeStruct((experts, capacity, width), jnp.bfloat16),
            jax.ShapeDtypeStruct((experts, capacity, hidden), jnp.float32),
        ],
        compiler_params=pltpu.CompilerParams(vmem_limit_bytes=LIMIT),
        cost_estimate=LOUD,
    )(core, *behind, slots[:, None, :], rows, down_weight)


def forward_kernel(
    first_ref,
    slots_ref,
    rows_ref,
    router_ref,
    gate_ref,
    up_ref,
    slot_ref,
    picked_ref,
    act_ref,
    grad_gate_ref,
    grad_up_ref,
    score_ref,
    weight_ref,
    total_ref,
):
    step = pl.program_id(1)
    mine = first_ref[1] + pl.program_id(0)

    @pl.when(step == 0)
    def _():
        pick_rows_into(slots_ref, rows_ref, picked_ref)
        logits = contract_cols(picked_ref[0], router_ref[...])
        raised = jnp.exp(logits - jnp.max(logits, axis=1, keepdims=True))
        label = lax.broadcasted_iota(jnp.int32, raised.shape, 1)
        own = jnp.sum(jnp.where(label == mine, raised, 0.0), axis=1, keepdims=True)
        weight_ref[...] = own / jnp.sum(raised, axis=1, keepdims=True)
        total_ref[...] = jnp.zeros_like(total_ref)

    gate_pre = dot_wide(picked_ref[0], gate_ref[0])
    up_pre = dot_wide(picked_ref[0], up_ref[0])
    sigmoid = 1.0 / (1.0 + jnp.exp(-gate_pre))
    smooth = gate_pre * sigmoid
    grad_act = weight_ref[...] * slot_ref[0]
    act = smooth * up_pre
    act_ref[0] = (weight_ref[...] * act).astype(jnp.bfloat16)
    grad_gate_ref[0] = (grad_act * up_pre * (sigmoid + smooth * (1.0 - sigmoid))).astype(
        jnp.bfloat16
    )
    grad_up_ref[0] = (grad_act * smooth).astype(jnp.bfloat16)
    total_ref[...] += jnp.sum(act * grad_act, axis=1, keepdims=True)

    @pl.when(step == pl.num_programs(1) - 1)
    def _():
        label = lax.broadcasted_iota(jnp.int32, score_ref.shape[1:], 1)
        score_ref[0] = jnp.where(label == mine, total_ref[...], 0.0).astype(jnp.bfloat16)


def forward_part(first, slots, rows, router_rows, gate_weight, up_weight, slot_cot, behind=(), cost=QUIET):
    experts, tokens = slots.shape
    capacity, hidden = slot_cot.shape[1:]
    width = rows.shape[1]
    labels = router_rows.shape[0]
    weight_spec = pl.BlockSpec(
        (1, width, HIDDEN_BLOCK), lambda e, n, first: (first[0] * experts + e, 0, n)
    )
    hidden_spec = pl.BlockSpec((1, capacity, HIDDEN_BLOCK), lambda e, n, first: (e, 0, n))
    hidden_shape = jax.ShapeDtypeStruct((experts, capacity, hidden), jnp.bfloat16)
    return pl.pallas_call(
        ordered(forward_kernel, len(behind)),
        grid_spec=pltpu.PrefetchScalarGridSpec(
            num_scalar_prefetch=1,
            grid=(experts, hidden // HIDDEN_BLOCK),
            in_specs=[HELD] * len(behind)
            + [
                pl.BlockSpec((1, 1, tokens), lambda e, n, first: (e, 0, 0)),
                pl.BlockSpec((tokens, width), lambda e, n, first: (0, 0)),
                pl.BlockSpec((labels, width), lambda e, n, first: (0, 0)),
                weight_spec,
                weight_spec,
                hidden_spec,
            ],
            out_specs=[
                pl.BlockSpec((1, capacity, width), lambda e, n, first: (e, 0, 0)),
                hidden_spec,
                hidden_spec,
                hidden_spec,
                pl.BlockSpec((1, capacity, HEAD_DIM), lambda e, n, first: (e, 0, 0)),
            ],
            scratch_shapes=[
                pltpu.VMEM((capacity, 1), jnp.float32),
                pltpu.VMEM((capacity, 1), jnp.float32),
            ],
        ),
        out_shape=[
            jax.ShapeDtypeStruct((experts, capacity, width), jnp.bfloat16),
            hidden_shape,
            hidden_shape,
            hidden_shape,
            jax.ShapeDtypeStruct((experts, capacity, HEAD_DIM), jnp.bfloat16),
        ],
        compiler_params=pltpu.CompilerParams(vmem_limit_bytes=LIMIT),
        cost_estimate=cost,
    )(first, *behind, slots[:, None, :], rows, router_rows, gate_weight, up_weight, slot_cot)


def backward_kernel(
    core_ref, slots_ref, grad_gate_ref, grad_up_ref, score_ref, *rest
):
    experts, capacity, _ = grad_gate_ref.shape
    gates, ups = rest[:experts], rest[experts : 2 * experts]
    into_ref, spread_ref, slot_ref = rest[2 * experts :]
    step = pl.program_id(0)
    width = pl.num_programs(0) * WIDTH_BLOCK

    @pl.when(step == 0)
    def _():
        spread_ref[...] = slot_columns(slots_ref[...], experts * capacity)
        scores = score_ref[...].reshape(experts * capacity, HEAD_DIM)
        into_ref[:, width:] = dot_wide(spread_ref[...], scores).astype(jnp.bfloat16)

    for expert in range(experts):
        rows = contract_cols(grad_gate_ref[expert], gates[expert][0]) + contract_cols(
            grad_up_ref[expert], ups[expert][0]
        )
        slot_ref[expert * capacity : (expert + 1) * capacity, :] = rows.astype(jnp.bfloat16)
    start = pl.multiple_of(step * WIDTH_BLOCK, WIDTH_BLOCK)
    into_ref[:, pl.ds(start, WIDTH_BLOCK)] = dot_wide(spread_ref[...], slot_ref[...]).astype(
        jnp.bfloat16
    )


def backward_part(core, columns, grad_gate, grad_up, scores, gate_weight, up_weight, behind=()):
    experts, capacity, hidden = grad_gate.shape
    tokens, width = columns.shape[0], gate_weight.shape[1]

    def weight_spec(expert):
        return pl.BlockSpec(
            (1, WIDTH_BLOCK, hidden), lambda n, core: (core[0] * experts + expert, n, 0)
        )

    whole = pl.BlockSpec((experts, capacity, hidden), lambda n, core: (0, 0, 0))
    return pl.pallas_call(
        ordered(backward_kernel, len(behind)),
        grid_spec=pltpu.PrefetchScalarGridSpec(
            num_scalar_prefetch=1,
            grid=(width // WIDTH_BLOCK,),
            in_specs=[HELD] * len(behind)
            + [
                pl.BlockSpec(columns.shape, lambda n, core: (0, 0)),
                whole,
                whole,
                pl.BlockSpec((experts, capacity, HEAD_DIM), lambda n, core: (0, 0, 0)),
            ]
            + [weight_spec(expert) for expert in range(experts)] * 2,
            out_specs=pl.BlockSpec((tokens, width + HEAD_DIM), lambda n, core: (0, 0)),
            scratch_shapes=[
                pltpu.VMEM((tokens, experts * capacity), jnp.bfloat16),
                pltpu.VMEM((experts * capacity, WIDTH_BLOCK), jnp.bfloat16),
            ],
        ),
        out_shape=jax.ShapeDtypeStruct((tokens, width + HEAD_DIM), jnp.bfloat16),
        compiler_params=pltpu.CompilerParams(vmem_limit_bytes=LIMIT),
        cost_estimate=QUIET,
    )(
        core,
        *behind,
        columns,
        grad_gate,
        grad_up,
        scores,
        *[gate_weight] * experts,
        *[up_weight] * experts,
    )


def routed_kernel(more, core_ref, slots_ref, act_ref, *rest):
    experts, capacity, _ = act_ref.shape
    downs = rest[:experts]
    into_ref, spread_ref, slot_ref = rest[experts + more :]

    @pl.when(pl.program_id(0) == 0)
    def _():
        spread_ref[...] = slot_columns(slots_ref[...], experts * capacity)

    for expert in range(experts):
        rows = dot_wide(act_ref[expert], downs[expert][0])
        slot_ref[expert * capacity : (expert + 1) * capacity, :] = rows.astype(jnp.bfloat16)
    total = dot_wide(spread_ref[...], slot_ref[...])
    for extra in rest[experts : experts + more]:
        total += extra[...].astype(jnp.float32)
    into_ref[...] = total.astype(jnp.bfloat16)


def routed_part(core, columns, act, down_weight, extra=(), behind=()):
    experts, capacity, hidden = act.shape
    tokens, width = columns.shape[0], down_weight.shape[2]

    def weight_spec(expert):
        return pl.BlockSpec(
            (1, hidden, WIDTH_BLOCK), lambda n, core: (core[0] * experts + expert, 0, n)
        )

    rows_spec = pl.BlockSpec((tokens, WIDTH_BLOCK), lambda n, core: (0, n))
    return pl.pallas_call(
        ordered(functools.partial(routed_kernel, len(extra)), len(behind)),
        grid_spec=pltpu.PrefetchScalarGridSpec(
            num_scalar_prefetch=1,
            grid=(width // WIDTH_BLOCK,),
            in_specs=[HELD] * len(behind)
            + [
                pl.BlockSpec(columns.shape, lambda n, core: (0, 0)),
                pl.BlockSpec((experts, capacity, hidden), lambda n, core: (0, 0, 0)),
            ]
            + [weight_spec(expert) for expert in range(experts)]
            + [rows_spec] * len(extra),
            out_specs=rows_spec,
            scratch_shapes=[
                pltpu.VMEM((tokens, experts * capacity), jnp.bfloat16),
                pltpu.VMEM((experts * capacity, WIDTH_BLOCK), jnp.bfloat16),
            ],
        ),
        out_shape=jax.ShapeDtypeStruct((tokens, width), jnp.bfloat16),
        compiler_params=pltpu.CompilerParams(vmem_limit_bytes=LIMIT),
        cost_estimate=LOUD,
    )(core, *behind, columns, act, *[down_weight] * experts, *extra)


def roll_half(values):
    return pltpu.roll(values, HEAD_DIM // 2, 1)


def head_parts(raw_ref, rate_ref, gain_ref, cos_ref, sin_ref, head):
    part_width = gain_ref.shape[1]
    units, turned = [], []
    for which in range(2):
        start = which * part_width + head * HEAD_DIM
        unit = raw_ref[:, start : start + HEAD_DIM] * rate_ref[:, which : which + 1]
        gain = gain_ref[which : which + 1, head * HEAD_DIM : (head + 1) * HEAD_DIM]
        scaled = unit * gain
        units.append((unit, gain))
        turned.append(
            (scaled * cos_ref[...] + roll_half(scaled) * sin_ref[...]).astype(jnp.bfloat16)
        )
    start = 2 * part_width + head * HEAD_DIM
    value = raw_ref[:, start : start + HEAD_DIM].astype(jnp.bfloat16)
    return units, turned, value


def head_probs(turned, column_ref, row_ref):
    scores = contract_cols(turned[0], turned[1]) * HEAD_DIM ** (-0.5)
    length = scores.shape[0]
    reader = lax.broadcasted_iota(jnp.int32, (length, length), 0)
    source = lax.broadcasted_iota(jnp.int32, (length, length), 1)
    allowed = (column_ref[...] == row_ref[0]) & (source <= reader)
    scores = jnp.where(allowed, scores, masked_score)
    raised = jnp.exp(scores - jnp.max(scores, axis=1, keepdims=True))
    return raised / jnp.sum(raised, axis=1, keepdims=True)


def attend_kernel(raw_ref, rate_ref, gain_ref, cos_ref, sin_ref, column_ref, row_ref, into_ref):
    for head in range(gain_ref.shape[1] // HEAD_DIM):
        _, turned, value = head_parts(raw_ref, rate_ref, gain_ref, cos_ref, sin_ref, head)
        probs = head_probs(turned, column_ref, row_ref).astype(jnp.bfloat16)
        into_ref[:, head * HEAD_DIM : (head + 1) * HEAD_DIM] = dot_wide(probs, value).astype(
            jnp.bfloat16
        )


def attend_back_kernel(
    raw_ref,
    rate_ref,
    gain_ref,
    cos_ref,
    sin_ref,
    column_ref,
    row_ref,
    grad_ref,
    pair_ref,
    value_ref,
    dots_ref,
    gains_ref,
):
    score_scale = HEAD_DIM ** (-0.5)
    part_width = gain_ref.shape[1]
    dots = [0.0, 0.0]
    for head in range(part_width // HEAD_DIM):
        units, turned, value = head_parts(raw_ref, rate_ref, gain_ref, cos_ref, sin_ref, head)
        probs = head_probs(turned, column_ref, row_ref)
        here = slice(head * HEAD_DIM, (head + 1) * HEAD_DIM)
        grad = grad_ref[:, here]
        grad_probs = contract_cols(grad, value)
        mean_grad = jnp.sum(probs * grad_probs, axis=1, keepdims=True)
        grad_scores = (probs * (grad_probs - mean_grad)).astype(jnp.bfloat16)
        value_ref[:, here] = contract_rows(probs.astype(jnp.bfloat16), grad).astype(jnp.bfloat16)
        grads = (
            dot_wide(grad_scores, turned[1]) * score_scale,
            contract_rows(grad_scores, turned[0]) * score_scale,
        )
        for which in range(2):
            unit, gain = units[which]
            back = grads[which] * cos_ref[...] + roll_half(grads[which] * sin_ref[...])
            gains_ref[0, which : which + 1, here] = jnp.sum(back * unit, axis=0, keepdims=True)
            back = back * gain
            start = which * part_width + head * HEAD_DIM
            pair_ref[:, start : start + HEAD_DIM] = back
            dots[which] += jnp.sum(back * unit, axis=1, keepdims=True)
    dots_ref[:, 0:1] = dots[0]
    dots_ref[:, 1:2] = dots[1]


def join_kernel(raw_ref, rate_ref, pair_ref, value_ref, dots_ref, into_ref):
    part_width = value_ref.shape[1]
    for which in range(2):
        here = slice(which * part_width, (which + 1) * part_width)
        rate = rate_ref[:, which : which + 1]
        shift = dots_ref[:, which : which + 1] * rate
        into_ref[:, here] = (rate * (pair_ref[:, here] - raw_ref[:, here] * shift)).astype(
            jnp.bfloat16
        )
    into_ref[:, 2 * part_width :] = value_ref[...]


def row_blocks(count, *arrays):
    return [pl.BlockSpec((array.shape[0] // count, array.shape[1]), lambda i: (i, 0)) for array in arrays]


def attention_specs(raw, rate, gains, cos_table, sin_table, columns, rows):
    count = rows.shape[0]
    return (
        row_blocks(count, raw, rate)
        + [pl.BlockSpec(gains.shape, lambda i: (0, 0))]
        + row_blocks(count, cos_table, sin_table, columns)
        + [pl.BlockSpec((1, 1, rows.shape[2]), lambda i: (i, 0, 0))]
    )


def attend(raw, rate, gains, cos_table, sin_table, columns, rows):
    count = rows.shape[0]
    operands = (raw, rate, gains, cos_table, sin_table, columns, rows)
    result = jax.ShapeDtypeStruct((raw.shape[0], gains.shape[1]), jnp.bfloat16)
    return pl.pallas_call(
        attend_kernel,
        grid=(count,),
        in_specs=attention_specs(*operands),
        out_specs=row_blocks(count, result)[0],
        out_shape=result,
        compiler_params=pltpu.CompilerParams(vmem_limit_bytes=LIMIT),
        cost_estimate=QUIET,
    )(*operands)


def attend_back(raw, rate, gains, cos_table, sin_table, columns, rows, grads, behind=()):
    count = rows.shape[0]
    operands = (raw, rate, gains, cos_table, sin_table, columns, rows)
    results = [
        jax.ShapeDtypeStruct((raw.shape[0], 2 * gains.shape[1]), jnp.float32),
        jax.ShapeDtypeStruct((raw.shape[0], gains.shape[1]), jnp.bfloat16),
        jax.ShapeDtypeStruct((raw.shape[0], 2), jnp.float32),
    ]
    gain_result = jax.ShapeDtypeStruct((count,) + gains.shape, jnp.float32)
    return pl.pallas_call(
        lambda *refs: attend_back_kernel(*refs[len(behind) :]),
        grid=(count,),
        in_specs=[HELD] * len(behind) + attention_specs(*operands) + row_blocks(count, grads),
        out_specs=row_blocks(count, *results)
        + [pl.BlockSpec((1,) + gains.shape, lambda i: (i, 0, 0))],
        out_shape=results + [gain_result],
        compiler_params=pltpu.CompilerParams(vmem_limit_bytes=LIMIT),
        cost_estimate=QUIET,
    )(*behind, *operands, grads)


def join_grads(raw, rate, pair, value, dots, count):
    operands = (raw, rate, pair, value, dots)
    result = jax.ShapeDtypeStruct(raw.shape, jnp.bfloat16)
    return pl.pallas_call(
        join_kernel,
        grid=(count,),
        in_specs=row_blocks(count, *operands),
        out_specs=row_blocks(count, result)[0],
        out_shape=result,
        compiler_params=pltpu.CompilerParams(vmem_limit_bytes=LIMIT),
        cost_estimate=QUIET,
    )(*operands)


def rep_sum(values):
    values = values + move(values, CORE_SWAP).reshape((2, 2) + values.shape[1:])[:, ::-1].reshape(
        values.shape
    )
    swapped = move(values, X_SWAP)
    return values + jnp.concatenate([swapped[2:], swapped[:2]], axis=0)


def fast_local(
    inputs,
    attn_gain,
    in_proj,
    query_gain,
    key_gain,
    out_proj,
    ffn_gain,
    router_weight,
    gate_weight,
    up_weight,
    down_weight,
    routes,
    priority,
    segments,
    grad_out,
):
    f32, bf16 = jnp.float32, jnp.bfloat16
    tokens, width = inputs.shape
    rows_each = in_proj.shape[0]
    local_experts, _, hidden_units = gate_weight.shape
    expert_count = local_experts * SHARDS
    route_count = routes.shape[1]
    pair_count = tokens * route_count
    capacity = 5 * pair_count * SHARDS // (4 * expert_count)
    core_experts = local_experts // 2
    heads = HEADS // REPS
    part_width = heads * HEAD_DIM
    group_rows = SHARDS * tokens
    rep, shard = lax.axis_index("rep"), lax.axis_index("shard")
    a, c = rep // 2, lax.rem(rep, 2)
    z, y = shard // 2, lax.rem(shard, 2)
    rep_ref = rep.astype(jnp.int32).reshape(1)
    core_ref = c.astype(jnp.int32).reshape(1)
    near_shards = lax.rem(z + jnp.arange(LINE, dtype=jnp.int32), LINE)[:, None] * 2 + (
        y ^ jnp.arange(2, dtype=jnp.int32)[None, :]
    )
    near_shards = near_shards.reshape(SHARDS)
    shard_ids = jnp.arange(SHARDS, dtype=jnp.int32)
    place_of_shard = jnp.sum(
        jnp.where(near_shards[None, :] == shard_ids[:, None], shard_ids[None, :], 0), axis=1
    )

    order_row = priority[0]
    pair_ids = jnp.arange(pair_count, dtype=jnp.int32)
    place_of = jnp.sum(
        jnp.where(order_row[None, :] == pair_ids[:, None], pair_ids[None, :], 0), axis=1
    ).reshape(tokens, route_count)
    labels = jnp.arange(expert_count, dtype=jnp.int32)
    hits = routes.T[None, :, :] == labels[:, None, None]
    place_at = jnp.sum(jnp.where(hits, place_of.T[None], 0), axis=1)
    named = jnp.any(hits, axis=1)
    place_at = jnp.where(named, place_at, pair_count)
    earlier = jnp.sum((place_at[:, None, :] < place_at[:, :, None]).astype(jnp.int32), axis=2)
    ranks = jnp.where(named, earlier, -1).astype(bf16)
    ranks = jnp.concatenate([ranks, segments.astype(bf16)], axis=0)
    ranks = jnp.pad(ranks, ((0, 0), (0, rows_each - tokens)))
    ranks = jnp.stack([ranks, move(ranks, CORE_SWAP)])
    ranks = jnp.concatenate([ranks, move(ranks, X_SWAP)])
    segment_rows = ranks[:, expert_count, :tokens].astype(jnp.int32)

    inputs_across = move(inputs, X_SWAP)
    small_in = jnp.stack([attn_gain, query_gain, key_gain, ffn_gain])
    small_in = jnp.concatenate(
        [small_in, router_weight.T, ranks.reshape(REPS * (expert_count + 1), rows_each)], axis=0
    )
    in_pieces = gather_rows(
        thin_columns(in_proj, rep_ref, width), first=(inputs_across, segment_rows)
    )
    small_in = gather_small(small_in, (in_pieces[2][0], in_pieces[1][1], in_pieces[3][1]))
    ranks = small_in[:, 4 + expert_count :, :tokens]
    ranks = jnp.take(ranks, near_shards ^ shard, axis=0)
    ranks = ranks.reshape(SHARDS, REPS, expert_count + 1, tokens)[:, :, :expert_count]
    in_part = flat(in_pieces)

    small_in = jnp.take(small_in[:, : 4 + expert_count], shard_ids ^ shard, axis=0)
    small_in = small_in.transpose(1, 0, 2).reshape(4 + expert_count, width)
    gains = small_in[:4].astype(f32)
    router_rows = small_in[4:]
    part_gains = lax.dynamic_slice(
        gains[1:3].reshape(2, HEADS // 2, 2, HEAD_DIM),
        (0, c * heads, a, 0),
        (2, heads, 1, HEAD_DIM),
    ).reshape(2, part_width)

    hidden = inputs.astype(f32)
    home_rate = lax.rsqrt(jnp.mean(hidden * hidden, axis=-1, keepdims=True) + norm_eps)
    inputs_all = jnp.stack([inputs, inputs_across])
    inputs_all = jnp.stack([inputs_all, move(inputs_all, CORE_SWAP)], axis=1)
    inputs_all = inputs_all.reshape(REPS * tokens, width)
    inputs_all = pick_columns(inputs_all, near_shards, rows_each).astype(f32)
    unit_all = inputs_all * lax.rsqrt(
        jnp.mean(inputs_all * inputs_all, axis=-1, keepdims=True) + norm_eps
    )
    near_gain = jnp.take(gains[0].reshape(SHARDS, rows_each), near_shards, axis=0).reshape(width)
    normed_low = (unit_all * near_gain).astype(bf16)
    cot_across = move(grad_out, X_SWAP)
    normed_low = after(normed_low, cot_across)
    cot_own = after(grad_out, in_part)
    cot_own = lax.all_gather(cot_own, "shard", tiled=True)
    cos_table, sin_table = jax.vmap(rotary_tables)(segment_rows)
    sin_table = jnp.where(jnp.arange(HEAD_DIM) < HEAD_DIM // 2, -sin_table, sin_table)
    cos_table = cos_table.reshape(REPS * tokens, HEAD_DIM)
    sin_table = sin_table.reshape(REPS * tokens, HEAD_DIM)

    out_rows = rows_each // 4
    out_own = lax.dynamic_slice_in_dim(out_proj, rep * out_rows, out_rows, 0)
    out_own = after(out_own, in_pieces[2][0])

    projected = jnp.dot(normed_low, in_part, preferred_element_type=f32)
    squares = jnp.stack(
        [
            jnp.sum(projected[:, k * part_width : (k + 1) * part_width] ** 2, axis=1)
            for k in range(2)
        ],
        axis=1,
    )
    squares = rep_sum(squares.reshape(REPS, tokens, 2)).reshape(REPS * tokens, 2)
    pair_rate = lax.rsqrt(squares / width + norm_eps)
    attention_operands = (
        projected,
        pair_rate,
        part_gains,
        cos_table,
        sin_table,
        segment_rows.reshape(REPS * tokens, 1),
        segment_rows[:, None, :],
    )
    attended = attend(*attention_operands).reshape(2, 2, tokens, part_width)
    out_pieces = gather_rows(out_own, early=(projected,), late=(attended,))
    out_own = flat(out_pieces).reshape(SHARDS, out_rows, width)
    out_other = move(out_own, CORE_SWAP)
    out_part = jnp.where(
        c == 0,
        jnp.concatenate([out_own, out_other], axis=1),
        jnp.concatenate([out_other, out_own], axis=1),
    ).reshape(SHARDS * 2 * out_rows, width)
    attended = jnp.concatenate([attended[:, 0], move(attended[:, 1], CORE_SWAP)], axis=2)
    attended = attended.reshape(2 * tokens, 2 * part_width)
    head_of_place = ((near_shards // heads) ^ c) * heads + lax.rem(near_shards, heads)
    place_of_head = jnp.sum(
        jnp.where(head_of_place[None, :] == shard_ids[:, None], shard_ids[None, :], 0), axis=1
    )
    attended = pick_columns(attended, head_of_place, HEAD_DIM)
    mixed = jnp.dot(attended, out_part, preferred_element_type=f32).reshape(2, tokens, width)
    mixed_across = move(mixed[1].astype(bf16), X_SWAP)
    residual = hidden + mixed[0] + mixed_across.astype(f32)

    ffn_rate = lax.rsqrt(jnp.mean(residual * residual, axis=-1, keepdims=True) + norm_eps)
    ffn_unit = residual * ffn_rate
    ffn_low = (ffn_unit * gains[3]).astype(bf16)
    router_probs = softmax_rows(contract_cols(ffn_low, router_rows))

    ranks = after(ranks, mixed_across).astype(jnp.int32)
    counts = jnp.sum((ranks >= 0).astype(jnp.int32), axis=3)
    before = (near_shards[None, :] < near_shards[:, None])[:, :, None, None]
    bases = jnp.sum(jnp.where(before, counts[None], 0), axis=1)
    slots = bases[..., None] + ranks
    slots = jnp.where((ranks >= 0) & (slots < capacity), slots, -1)
    first_expert = shard * local_experts + c * core_experts
    slots = lax.dynamic_slice_in_dim(slots, first_expert, core_experts, 2)
    slots = slots.transpose(1, 2, 0, 3)
    shard_slots = jnp.take(slots, place_of_shard, axis=2)
    slots = slots.reshape(REPS, core_experts, group_rows)
    shard_slots = shard_slots.reshape(REPS, core_experts, group_rows)
    shifts = jnp.arange(core_experts, dtype=jnp.int32)[:, None] * capacity

    def columns_of(table):
        return jnp.where(table >= 0, table + shifts, -1).transpose(0, 2, 1)

    columns, shard_columns = columns_of(slots[:2]), columns_of(shard_slots[:2])

    def cot_part(group, rows, behind=()):
        return cotangent_part(core_ref, shard_slots[group], rows, down_weight, capacity, behind)

    first_ref = jnp.stack([c, first_expert]).astype(jnp.int32)

    def ffn_part(group, rows, slot_cot, behind=(), cost=QUIET):
        return forward_part(
            first_ref,
            slots[group],
            rows,
            router_rows,
            gate_weight,
            up_weight,
            slot_cot,
            behind,
            cost,
        )

    made = {}

    def fill_cot(follow):
        beside = move(cot_own, CORE_SWAP)
        own_part = cot_part(0, cot_own, (follow,))
        made["cot"] = [own_part, cot_part(1, beside, (own_part[1],))]
        return [own_part[1]]

    ffn_pieces = gather_rows(
        ffn_low, early=(slots, shard_slots, columns, shard_columns), fill=fill_cot
    )
    near_cot = made["cot"]
    ffn_own = after(flat(ffn_pieces), near_cot[1][1])
    ffn_beside = move(ffn_own, CORE_SWAP)
    ffn_far = [move(jnp.concatenate(pair, axis=0), X_SWAP) for pair in ffn_pieces]
    cot_across = lax.all_gather(after(cot_across, ffn_pieces[2][0]), "shard", tiled=True)

    near = [ffn_part(0, ffn_own, near_cot[0][1])]
    near.append(ffn_part(1, ffn_beside, near_cot[1][1], (near[0][1],)))

    def rows_back(group, behind=()):
        _, _, grad_gate, grad_up, scores = near[group]
        return backward_part(
            core_ref, columns[group], grad_gate, grad_up, scores, gate_weight, up_weight, behind
        ).reshape(SHARDS, tokens, -1)

    grad_other = rows_back(1, (ffn_far[0], ffn_far[1]))
    grad_own = rows_back(0, (grad_other,))
    grad_other = move(grad_other, CORE_SWAP)

    def routed_rows(group, extra, behind):
        return routed_part(
            core_ref, shard_columns[group], near[group][1], down_weight, extra, behind
        )

    def fill_routed_other(follow):
        made["routed_other"] = routed_rows(1, (), follow + (ffn_far[2], cot_across))
        return [made["routed_other"]]

    def fill_far_cot(follow):
        made["far_cot"] = cot_part(2, cot_across, follow)
        return [made["far_cot"][1]]

    def fill_routed_own(follow):
        extra = (move(made["routed_other"], CORE_SWAP),)
        made["routed"] = routed_rows(0, extra, follow)
        return [made["routed"]]

    def fill_other_cot(follow):
        rows = move(after(cot_across, made["routed"]), CORE_SWAP)
        made["other_cot"] = cot_part(3, rows, follow)
        return [made["other_cot"][1]]

    grad_home = scatter_rows(
        [lambda place: grad_own[place], lambda place: grad_other[place]],
        [fill_routed_other, fill_routed_own, fill_far_cot, fill_other_cot, None],
    )
    routed = lax.psum_scatter(
        after(made["routed"], grad_home), "shard", scatter_dimension=0, tiled=True
    )
    ffn_far = jnp.concatenate([after(part, made["other_cot"][1]) for part in ffn_far], axis=0)
    ffn_far = [ffn_far, move(ffn_far, CORE_SWAP)]

    grad_ffn_home = grad_home[:, :width]
    home_score = grad_home[:, width : width + expert_count].astype(f32)
    grad_logits = home_score - router_probs * jnp.sum(home_score, axis=1, keepdims=True)
    grad_logits_low = grad_logits.astype(bf16)

    grad_ffn_in = grad_ffn_home.astype(f32) + jnp.dot(
        grad_logits_low, router_rows, preferred_element_type=f32
    )
    grad_router_local = contract_rows(grad_logits_low, ffn_low)
    grad_ffn_local = jnp.sum(grad_ffn_in * ffn_unit, axis=0)
    scaled = gains[3] * grad_ffn_in
    grad_residual = grad_out.astype(f32) + ffn_rate * (
        scaled - ffn_unit * jnp.mean(scaled * ffn_unit, axis=-1, keepdims=True)
    )
    residual_low = grad_residual.astype(bf16)
    residual_other = move(residual_low, X_SWAP)
    residual_pair = jnp.concatenate([residual_low, residual_other], axis=0)

    grad_attended = contract_cols(residual_pair, out_part).astype(bf16)
    grad_attended = pick_columns(grad_attended, place_of_head, HEAD_DIM)
    grad_attended = grad_attended.reshape(2, tokens, 2 * part_width)
    mine, theirs = grad_attended[:, :, :part_width], grad_attended[:, :, part_width:]
    grad_attended = jnp.stack([mine, move(theirs, CORE_SWAP)], axis=1)
    grad_attended = grad_attended.reshape(REPS * tokens, part_width)
    grad_pair, grad_value, dots, grad_pair_gain = attend_back(*attention_operands, grad_attended)
    grad_pair_gain = jnp.sum(grad_pair_gain, axis=0).reshape(2, heads, HEAD_DIM)
    dots = rep_sum(dots.reshape(REPS, tokens, 2)).reshape(REPS * tokens, 2) / width
    grad_projected = join_grads(projected, pair_rate, grad_pair, grad_value, dots, REPS)

    grad_in_part = contract_rows(normed_low, grad_projected).astype(bf16)
    grad_in_part = grad_in_part.reshape(SHARDS, rows_each, 3 * part_width)
    grad_normed = contract_cols(grad_projected, in_part)
    grad_attn_part = jnp.sum(grad_normed * unit_all, axis=0)

    pair_gains = jnp.zeros((2, HEADS // 2, 2, HEAD_DIM), f32)
    pair_gains = lax.dynamic_update_slice(
        pair_gains, grad_pair_gain[:, :, None], (0, c * heads, a, 0)
    )
    small = jnp.concatenate(
        [grad_ffn_local[None], pair_gains.reshape(2, width), grad_router_local], axis=0
    )
    small = jnp.take(small.reshape(-1, SHARDS, rows_each), near_shards, axis=1)
    small = jnp.concatenate([grad_attn_part.reshape(1, SHARDS, rows_each), small], axis=0)
    small = jnp.pad(small, ((0, HEAD_DIM - small.shape[0]), (0, 0), (0, 0)))
    small = small.astype(bf16).transpose(1, 2, 0)

    grad_out_part = contract_rows(after(attended, grad_projected), residual_pair).astype(bf16)
    out_parts = grad_out_part.reshape(SHARDS, 2, out_rows, width)
    out_own = lax.dynamic_index_in_dim(out_parts, c, 1, keepdims=False)
    out_other = lax.dynamic_index_in_dim(out_parts, 1 - c, 1, keepdims=False)
    out_sum = added(out_own, move(out_other, CORE_SWAP))
    out_sum = jnp.take(out_sum, place_of_shard, axis=0).reshape(SHARDS * out_rows, width)

    far_cot = [made["far_cot"], made["other_cot"]]

    def fill_far(follow):
        made["far"] = ffn_part(
            2, ffn_far[0], far_cot[0][1], follow + (ffn_far[1],), LOUD
        )
        return [made["far"][3]]

    normed_other = grad_normed.astype(bf16).reshape(2, 2, tokens, width)
    normed_mine = added(normed_other[:, 0], move(normed_other[:, 1], CORE_SWAP))
    normed_across = move(normed_mine[1], X_SWAP)

    def fill_other(follow):
        made["other"] = ffn_part(
            3, ffn_far[1], far_cot[1][1], follow + (made["far"][3], normed_mine, routed, out_sum), LOUD
        )
        return [made["other"][3]]

    def weight_grad(left, right, follow):
        first, *follow = lax.optimization_barrier((left[0],) + follow)
        left = jnp.concatenate([first] + left[1:], axis=1)
        right = jnp.concatenate(right, axis=1)
        grad = jnp.einsum("ecd,ecf->edf", left, right, preferred_element_type=f32).astype(bf16)
        return grad, follow

    def groups(index):
        return [part[index] for part in (near[0], near[1], made["far"], made["other"])]

    def fence(follow):
        return [made["other"][3]]

    out_home = lax.psum_scatter(
        after(out_sum, routed), "shard", scatter_dimension=0, tiled=True
    )

    def fill_weights(follow):
        cots = [part[0] for part in near_cot + far_cot]
        reduced, first, second, third = follow
        down, _ = weight_grad(groups(1), cots, ())
        gate, (down, first, reduced, _) = weight_grad(
            groups(0), groups(2), (down, first, reduced, normed_across)
        )
        up, (gate, second, third, home) = weight_grad(
            groups(0), groups(3), (gate, second, third, out_home)
        )
        made["down"], made["gate"], made["up"], made["home"] = down, gate, up, home
        return reduced, first, second, third

    in_sum = scatter_rows(
        [lambda place: jnp.concatenate([grad_in_part[place], small[place]], axis=1)],
        [fill_far, fill_other, fence, fence, fill_weights],
        hold=True,
    )
    in_other = move(in_sum, X_SWAP)
    grad_up, out_home = made["up"], made["home"]
    down_all = widen(
        made["down"], move(made["down"], CORE_SWAP), core_ref, (grad_up,)
    )
    in_all = jnp.stack([in_sum, after(in_other, down_all)])
    in_beside = move(in_all, CORE_SWAP)
    out_across = move(after(out_home, down_all), X_SWAP)
    gate_all = widen(
        made["gate"], move(made["gate"], CORE_SWAP), core_ref, (down_all, out_across)
    )
    in_all = jnp.stack([in_all, in_beside], axis=1).reshape((REPS,) + in_sum.shape)
    grad_in = weave_columns(in_all, rep_ref, 3 * part_width, (gate_all,))
    small = jnp.sum(in_all[:, :, 3 * part_width :].astype(f32), axis=0).T
    up_all = widen(grad_up, move(grad_up, CORE_SWAP), core_ref, (gate_all,))

    outputs = (residual + after(routed, down_all).astype(f32)).astype(bf16)
    grad_normed = after(added(normed_mine[0], normed_across), down_all)
    grad_normed = pick_columns(grad_normed, place_of_shard, rows_each).astype(f32)
    home_unit = hidden * home_rate
    scaled = gains[0] * grad_normed
    grad_inputs = (
        grad_residual
        + home_rate * (scaled - home_unit * jnp.mean(scaled * home_unit, axis=-1, keepdims=True))
    ).astype(bf16)

    out_sum = jnp.stack([out_home, out_across])
    out_sum = jnp.stack([out_sum, move(out_sum, CORE_SWAP)], axis=1)
    out_sum = out_sum.reshape(REPS, out_rows, width)
    out_sum = jnp.take(out_sum, rep ^ jnp.arange(REPS, dtype=jnp.int32), axis=0)
    grad_out_proj = out_sum.reshape(rows_each, width).astype(f32)
    return (
        outputs,
        grad_inputs,
        small[0],
        grad_in,
        small[2],
        small[3],
        grad_out_proj,
        small[1],
        small[4 : 4 + expert_count].T,
        gate_all,
        up_all,
        down_all,
    )


def solution(mesh):
    fits = dict(mesh.shape) == {"rep": REPS, "shard": SHARDS}
    body = fast_local if fits else local
    in_specs = (
        P(("rep", "shard"), None),
        P("shard"),
        P("shard", None),
        P("shard"),
        P("shard"),
        P("shard", None),
        P("shard"),
        P("shard", None),
        P("shard", None, None),
        P("shard", None, None),
        P("shard", None, None),
        P(("rep", "shard"), None),
        P(("rep", "shard"), None),
        P(("rep", "shard"), None),
        P(("rep", "shard"), None),
    )
    out_specs = (
        P(("rep", "shard"), None),
        P(("rep", "shard"), None),
        P("shard"),
        P("shard", None),
        P("shard"),
        P("shard"),
        P("shard", None),
        P("shard"),
        P("shard", None),
        P("shard", None, None),
        P("shard", None, None),
        P("shard", None, None),
    )
    return jax.shard_map(body, mesh=mesh, in_specs=in_specs, out_specs=out_specs, check_vma=False)
```

```python
import functools

import jax
import jax.numpy as jnp
from jax import lax
from jax.experimental import pallas as pl
from jax.experimental.pallas import tpu as pltpu
from jax.sharding import PartitionSpec as P

HEADS = 16
HEAD_DIM = 128


norm_eps = 1e-05
rope_base = 10000.0
masked_score = -1e30


def rms_scale(values, gains):
    normed = values * lax.rsqrt(jnp.mean(values * values, axis=-1, keepdims=True) + norm_eps)
    return normed * gains


def rotary_tables(segment_row):
    length = segment_row.shape[0]
    places = jnp.arange(length, dtype=jnp.int32)
    starting = jnp.concatenate(
        [jnp.ones((1,), jnp.int32), (segment_row[1:] != segment_row[:-1]).astype(jnp.int32)]
    )
    first_place = lax.cummax(jnp.where(starting > 0, places, 0), axis=0)
    offsets = (places - first_place).astype(jnp.float32)
    halves = HEAD_DIM // 2
    inverse = rope_base ** (-2.0 * jnp.arange(halves, dtype=jnp.float32) / HEAD_DIM)
    angles = offsets[:, None] * inverse[None, :]
    angles = jnp.concatenate([angles, angles], axis=1)
    return (jnp.cos(angles), jnp.sin(angles))


def rotate(values, cos_table, sin_table):
    halves = values.shape[-1] // 2
    turned = jnp.concatenate([-values[..., halves:], values[..., :halves]], axis=-1)
    return values * cos_table[:, None, :] + turned * sin_table[:, None, :]


def query_key(raw_query, raw_key, query_scale, key_scale, cos_table, sin_table):
    row_count = raw_query.shape[0]
    normed_query = rms_scale(raw_query, query_scale).reshape(row_count, HEADS, HEAD_DIM)
    normed_key = rms_scale(raw_key, key_scale).reshape(row_count, HEADS, HEAD_DIM)
    return (rotate(normed_query, cos_table, sin_table), rotate(normed_key, cos_table, sin_table))


def softmax_rows(logits):
    highest = jnp.max(logits, axis=-1, keepdims=True)
    raised = jnp.exp(logits - highest)
    return raised / jnp.sum(raised, axis=-1, keepdims=True)


def swiglu(gate_pre, up_pre):
    return jax.nn.silu(gate_pre) * up_pre


def contract_rows(left_side, right_side):
    return lax.dot_general(
        left_side, right_side, (((0,), (0,)), ((), ())), preferred_element_type=jnp.float32
    )


def contract_cols(left_side, right_side):
    return lax.dot_general(
        left_side, right_side, (((1,), (1,)), ((), ())), preferred_element_type=jnp.float32
    )


def pick_rows(source_rows, row_picks):
    return jax.vmap(lambda expert_rows, picked: expert_rows[picked])(source_rows, row_picks)


def local(
    inputs,
    attn_gain,
    in_proj,
    query_gain,
    key_gain,
    out_proj,
    ffn_gain,
    router_weight,
    gate_weight,
    up_weight,
    down_weight,
    routes,
    priority,
    segments,
    grad_out,
):
    tokens = inputs.shape[0]
    model_width = inputs.shape[1]
    local_experts = gate_weight.shape[0]
    group_count = lax.axis_size("shard")
    my_index = lax.axis_index("shard")
    expert_count = local_experts * group_count
    route_count = routes.shape[1]
    pair_count = tokens * route_count
    capacity = 5 * pair_count * group_count // (4 * expert_count)
    send_most = 2 * pair_count // expert_count
    segment_row = segments[0]
    cos_table, sin_table = rotary_tables(segment_row)
    hidden_in = inputs.astype(jnp.float32)
    unit_rows = hidden_in * lax.rsqrt(
        jnp.mean(hidden_in * hidden_in, axis=-1, keepdims=True) + norm_eps
    )
    weight_piece = lax.all_gather(in_proj, "shard", axis=0, tiled=True)
    attn_piece = lax.all_gather(attn_gain, "shard", axis=0, tiled=True)
    query_piece = lax.all_gather(query_gain, "shard", axis=0, tiled=True)
    key_piece = lax.all_gather(key_gain, "shard", axis=0, tiled=True)
    scaled = (unit_rows * attn_piece.astype(jnp.float32)).astype(jnp.bfloat16)
    result = (
        jnp.dot(scaled, weight_piece, preferred_element_type=jnp.float32),
        attn_piece.astype(jnp.float32),
        query_piece.astype(jnp.float32),
        key_piece.astype(jnp.float32),
    )
    folded_in = result
    projected = folded_in[0]
    normed_attn, attn_norm_back = jax.vjp(rms_scale, hidden_in, folded_in[1])
    normed_low = normed_attn.astype(jnp.bfloat16)
    raw_query = projected[:, :model_width]
    raw_key = projected[:, model_width : 2 * model_width]
    raw_value = projected[:, 2 * model_width :]

    def rotated_pair(query_raw, key_raw, query_scale, key_scale):
        return query_key(query_raw, key_raw, query_scale, key_scale, cos_table, sin_table)

    (turned_query, turned_key), query_key_back = jax.vjp(
        rotated_pair, raw_query, raw_key, folded_in[2], folded_in[3]
    )
    query_low = turned_query.astype(jnp.bfloat16)
    key_low = turned_key.astype(jnp.bfloat16)
    value_low = raw_value.astype(jnp.bfloat16).reshape(tokens, HEADS, HEAD_DIM)
    places = jnp.arange(tokens, dtype=jnp.int32)
    allowed = (segment_row[:, None] == segment_row[None, :]) & (places[None, :] <= places[:, None])
    score_scale = HEAD_DIM ** (-0.5)

    def masked_scores(queries, key_vecs):
        products = jnp.einsum("qhd,khd->hqk", queries, key_vecs, preferred_element_type=jnp.float32)
        return jnp.where(allowed[None], products * score_scale, masked_score)

    scores = masked_scores(query_low, key_low)
    highest = jnp.max(scores, axis=-1, keepdims=True)
    raised = jnp.exp(scores - highest)
    totals = jnp.sum(raised, axis=-1, keepdims=True)
    attn_probs = raised / totals
    log_total = highest + jnp.log(totals)
    mixed = jnp.einsum(
        "hqk,khd->qhd",
        attn_probs.astype(jnp.bfloat16),
        value_low,
        preferred_element_type=jnp.float32,
    )
    attended = mixed.reshape(tokens, model_width).astype(jnp.bfloat16)
    weight_piece = lax.all_gather(out_proj, "shard", axis=0, tiled=True)
    ffn_piece = lax.all_gather(ffn_gain, "shard", axis=0, tiled=True)
    router_piece = lax.all_gather(router_weight, "shard", axis=0, tiled=True)
    result = (
        jnp.dot(attended, weight_piece, preferred_element_type=jnp.float32),
        ffn_piece.astype(jnp.float32),
        router_piece,
    )
    residual = hidden_in + result[0]
    router_full = result[2]
    normed_ffn, ffn_norm_back = jax.vjp(rms_scale, residual, result[1])
    ffn_low = normed_ffn.astype(jnp.bfloat16)
    logits = jnp.dot(ffn_low, router_full, preferred_element_type=jnp.float32)
    router_probs, router_back = jax.vjp(softmax_rows, logits)
    flat_routes = routes.reshape(pair_count)
    order_row = priority[0]
    ranked_expert = flat_routes[order_row]
    labels = jnp.arange(expert_count, dtype=jnp.int32)
    matches = (ranked_expert[:, None] == labels[None, :]).astype(jnp.int32)
    rank_in = (
        jnp.sum(jnp.cumsum(matches, axis=0, dtype=jnp.int32) * matches, axis=1, dtype=jnp.int32) - 1
    )
    counts = jnp.sum(matches, axis=0, dtype=jnp.int32)
    all_counts = lax.all_gather(counts[None, :], "shard", axis=0, tiled=True)
    base_slots = jnp.cumsum(all_counts, axis=0, dtype=jnp.int32) - all_counts
    my_bases = lax.dynamic_index_in_dim(base_slots, my_index, 0, keepdims=False)
    slot_index = jnp.sum(matches * my_bases[None, :], axis=1, dtype=jnp.int32) + rank_in
    cell_index = ranked_expert * send_most + rank_in
    inverse_order = (
        jnp.zeros((pair_count,), jnp.int32)
        .at[order_row]
        .set(jnp.arange(pair_count, dtype=jnp.int32))
    )
    pair_cell = cell_index[inverse_order].reshape(tokens, route_count)
    pair_keep = (
        (slot_index[inverse_order] < capacity).astype(jnp.float32).reshape(tokens, route_count)
    )
    cell_pair = jnp.zeros((expert_count * send_most,), jnp.int32).at[cell_index].set(order_row)
    cell_live = (jnp.arange(send_most, dtype=jnp.int32)[None, :] < counts[:, None]).reshape(
        expert_count * send_most
    )
    cell_token = cell_pair // route_count
    outgoing = jnp.where(cell_live[:, None], ffn_low[cell_token], 0).reshape(
        expert_count, send_most, model_width
    )
    arrived = lax.all_to_all(outgoing, "shard", split_axis=0, concat_axis=1, tiled=True)
    own_counts = lax.dynamic_slice_in_dim(all_counts, my_index * local_experts, local_experts, 1).T
    own_bases = lax.dynamic_slice_in_dim(base_slots, my_index * local_experts, local_experts, 1).T
    slot_ids = jnp.arange(capacity, dtype=jnp.int32)
    slot_ends = own_bases + own_counts
    source_ids = jnp.sum(
        (slot_ends[:, None, :] <= slot_ids[None, :, None]).astype(jnp.int32),
        axis=2,
        dtype=jnp.int32,
    )
    slot_filled = source_ids < group_count
    source_safe = jnp.minimum(source_ids, group_count - 1)
    slot_rows = (
        source_safe * send_most
        + slot_ids[None, :]
        - jnp.take_along_axis(own_bases, source_safe, axis=1)
    )
    slot_rows = jnp.where(slot_filled, slot_rows, 0)
    expert_in = jnp.where(slot_filled[..., None], pick_rows(arrived, slot_rows), 0)
    gate_pre = jnp.einsum(
        "ecd,edf->ecf", expert_in, gate_weight, preferred_element_type=jnp.float32
    )
    up_pre = jnp.einsum("ecd,edf->ecf", expert_in, up_weight, preferred_element_type=jnp.float32)
    activated, swiglu_back = jax.vjp(swiglu, gate_pre, up_pre)
    act_low = activated.astype(jnp.bfloat16)
    expert_out = jnp.einsum(
        "ecf,efd->ecd", act_low, down_weight, preferred_element_type=jnp.float32
    ).astype(jnp.bfloat16)
    cell_positions = jnp.arange(send_most, dtype=jnp.int32)
    cell_slot = own_bases[:, :, None] + cell_positions[None, None, :]
    cell_used = (cell_positions[None, None, :] < own_counts[:, :, None]) & (cell_slot < capacity)
    cell_slot = jnp.where(cell_used, cell_slot, 0).reshape(local_experts, group_count * send_most)
    cell_used = cell_used.reshape(local_experts, group_count * send_most)
    returning = jnp.where(cell_used[..., None], pick_rows(expert_out, cell_slot), 0)
    returned = lax.all_to_all(returning, "shard", split_axis=1, concat_axis=0, tiled=True).reshape(
        expert_count * send_most, model_width
    )
    pair_rows = returned[pair_cell].astype(jnp.float32)
    pair_weight = jnp.take_along_axis(router_probs, routes, axis=1) * pair_keep
    outputs = (residual + jnp.sum(pair_weight[..., None] * pair_rows, axis=1)).astype(jnp.bfloat16)
    cotangent = grad_out.astype(jnp.float32)
    grad_rows = (
        (pair_weight[..., None] * cotangent[:, None, :])
        .astype(jnp.bfloat16)
        .reshape(pair_count, model_width)
    )
    grad_pair_weight = jnp.sum(pair_rows * cotangent[:, None, :], axis=2) * pair_keep
    route_hits = (routes[..., None] == labels[None, None, :]).astype(jnp.float32)
    grad_router_probs = jnp.sum(grad_pair_weight[..., None] * route_hits, axis=1)
    (grad_logits,) = router_back(grad_router_probs)
    grad_logits_low = grad_logits.astype(jnp.bfloat16)
    outgoing_grad = jnp.where(cell_live[:, None], grad_rows[cell_pair], 0).reshape(
        expert_count, send_most, model_width
    )
    arrived_grad = lax.all_to_all(outgoing_grad, "shard", split_axis=0, concat_axis=1, tiled=True)
    grad_expert_out = jnp.where(slot_filled[..., None], pick_rows(arrived_grad, slot_rows), 0)
    grad_act = jnp.einsum(
        "ecd,efd->ecf", grad_expert_out, down_weight, preferred_element_type=jnp.float32
    )
    grad_down = jnp.einsum(
        "ecf,ecd->efd", act_low, grad_expert_out, preferred_element_type=jnp.float32
    )
    grad_gate_pre, grad_up_pre = swiglu_back(grad_act)
    gate_grad_low = grad_gate_pre.astype(jnp.bfloat16)
    up_grad_low = grad_up_pre.astype(jnp.bfloat16)
    grad_gate = jnp.einsum(
        "ecd,ecf->edf", expert_in, gate_grad_low, preferred_element_type=jnp.float32
    )
    grad_up = jnp.einsum("ecd,ecf->edf", expert_in, up_grad_low, preferred_element_type=jnp.float32)
    grad_expert_in = (
        jnp.einsum("ecf,edf->ecd", gate_grad_low, gate_weight, preferred_element_type=jnp.float32)
        + jnp.einsum("ecf,edf->ecd", up_grad_low, up_weight, preferred_element_type=jnp.float32)
    ).astype(jnp.bfloat16)
    returning_grad = jnp.where(cell_used[..., None], pick_rows(grad_expert_in, cell_slot), 0)
    returned_grad = lax.all_to_all(
        returning_grad, "shard", split_axis=1, concat_axis=0, tiled=True
    ).reshape(expert_count * send_most, model_width)
    grad_ffn_in = jnp.sum(returned_grad[pair_cell].astype(jnp.float32), axis=1) + contract_cols(
        grad_logits_low, router_full
    )
    grad_router_local = contract_rows(ffn_low, grad_logits_low)
    grad_residual_norm, grad_ffn_local = ffn_norm_back(grad_ffn_in)
    grad_residual = cotangent + grad_residual_norm
    residual_low = grad_residual.astype(jnp.bfloat16)
    grad_out_local = lax.psum_scatter(
        contract_rows(attended, residual_low).astype(jnp.bfloat16),
        "shard",
        scatter_dimension=0,
        tiled=True,
    )
    grad_attended = contract_cols(
        residual_low, lax.all_gather(out_proj, "shard", axis=0, tiled=True)
    )
    grad_mixed = grad_attended.astype(jnp.bfloat16).reshape(tokens, HEADS, HEAD_DIM)
    scores_again = masked_scores(query_low, key_low)
    probs_again = jnp.exp(scores_again - log_total)
    grad_probs = jnp.einsum(
        "qhd,khd->hqk", grad_mixed, value_low, preferred_element_type=jnp.float32
    )
    spread = jnp.sum(probs_again * grad_probs, axis=-1, keepdims=True)
    grad_scores = (probs_again * (grad_probs - spread)).astype(jnp.bfloat16)
    grad_query = (
        jnp.einsum("hqk,khd->qhd", grad_scores, key_low, preferred_element_type=jnp.float32)
        * score_scale
    )
    grad_key = (
        jnp.einsum("hqk,qhd->khd", grad_scores, query_low, preferred_element_type=jnp.float32)
        * score_scale
    )
    grad_value = jnp.einsum(
        "hqk,qhd->khd",
        probs_again.astype(jnp.bfloat16),
        grad_mixed,
        preferred_element_type=jnp.float32,
    )
    grad_raw_query, grad_raw_key, grad_query_local, grad_key_local = query_key_back(
        (grad_query, grad_key)
    )
    grad_qkv = jnp.concatenate(
        [grad_raw_query, grad_raw_key, grad_value.reshape(tokens, model_width)], axis=1
    ).astype(jnp.bfloat16)
    grad_in_local = lax.psum_scatter(
        contract_rows(normed_low, grad_qkv).astype(jnp.bfloat16),
        "shard",
        scatter_dimension=0,
        tiled=True,
    )
    grad_normed = contract_cols(grad_qkv, lax.all_gather(in_proj, "shard", axis=0, tiled=True))
    grad_hidden_norm, grad_attn_local = attn_norm_back(grad_normed)
    grad_inputs = (grad_residual + grad_hidden_norm).astype(jnp.bfloat16)
    small_parts = (
        lax.psum_scatter(
            grad_attn_local.astype(jnp.bfloat16), "shard", scatter_dimension=0, tiled=True
        ).astype(jnp.float32),
        lax.psum_scatter(
            grad_query_local.astype(jnp.bfloat16), "shard", scatter_dimension=0, tiled=True
        ).astype(jnp.float32),
        lax.psum_scatter(
            grad_key_local.astype(jnp.bfloat16), "shard", scatter_dimension=0, tiled=True
        ).astype(jnp.float32),
        lax.psum_scatter(
            grad_ffn_local.astype(jnp.bfloat16), "shard", scatter_dimension=0, tiled=True
        ).astype(jnp.float32),
        lax.psum_scatter(
            grad_router_local.astype(jnp.bfloat16), "shard", scatter_dimension=0, tiled=True
        ).astype(jnp.float32),
    )
    summed = (
        lax.psum(grad_in_local, "rep").astype(jnp.float32),
        lax.psum(grad_out_local, "rep").astype(jnp.float32),
        lax.psum(small_parts[0].astype(jnp.bfloat16), "rep").astype(jnp.float32),
        lax.psum(small_parts[1].astype(jnp.bfloat16), "rep").astype(jnp.float32),
        lax.psum(small_parts[2].astype(jnp.bfloat16), "rep").astype(jnp.float32),
        lax.psum(small_parts[3].astype(jnp.bfloat16), "rep").astype(jnp.float32),
        lax.psum(small_parts[4].astype(jnp.bfloat16), "rep").astype(jnp.float32),
        lax.psum(grad_gate.astype(jnp.bfloat16), "rep").astype(jnp.float32),
        lax.psum(grad_up.astype(jnp.bfloat16), "rep").astype(jnp.float32),
        lax.psum(grad_down.astype(jnp.bfloat16), "rep").astype(jnp.float32),
    )
    return (
        outputs,
        grad_inputs,
        summed[2],
        summed[0],
        summed[3],
        summed[4],
        summed[1],
        summed[5],
        summed[6],
        summed[7],
        summed[8],
        summed[9],
    )


AXES = ("rep", "shard")
LINE = 4
SHARDS = 8
REPS = 4


def pairs_of(target):
    moves = []
    for rep in range(REPS):
        for shard in range(SHARDS):
            there = target(rep, shard)
            moves.append((rep * SHARDS + shard, there[0] * SHARDS + there[1]))
    return moves


CORE_SWAP = pairs_of(lambda rep, shard: (rep ^ 1, shard))
X_SWAP = pairs_of(lambda rep, shard: (rep ^ 2, shard))
Y_SWAP = pairs_of(lambda rep, shard: (rep, shard ^ 1))
SHARD_SWAP = [
    pairs_of(lambda rep, shard: (rep, shard ^ 1)),
    pairs_of(lambda rep, shard: (rep, shard ^ 2)),
    pairs_of(lambda rep, shard: (rep, shard ^ 4)),
]
Z_FROM = [pairs_of(lambda rep, shard: (rep, (shard - 2 * k) % SHARDS)) for k in range(LINE)]
Z_TO = [pairs_of(lambda rep, shard: (rep, (shard + 2 * k) % SHARDS)) for k in range(LINE)]


def move(values, moves):
    return lax.ppermute(values, AXES, moves)


def after(values, *others):
    return lax.optimization_barrier((values,) + others)[0]


def gather_small(values, hold):
    low = jnp.stack([values, move(values, SHARD_SWAP[1])])
    high = jnp.stack([low, move(after(low, *hold), SHARD_SWAP[2])])
    both = jnp.stack([high, move(high, SHARD_SWAP[0])], axis=2)
    return both.reshape((SHARDS,) + values.shape)


def gather_rows(values, early=(), late=(), fill=None, first=()):
    moved = {k: move(values, Z_FROM[k]) for k in (1, 3)}
    moved[2] = move(after(values, moved[1], *first), Z_FROM[2])
    mine, beside = {0: values}, {0: move(values, Y_SWAP)}
    for k in (1, 3, 2):
        mine[k] = after(moved[k], *early) if early else moved[k]
        if k == 2 and fill is not None:
            mine[k] = after(mine[k], *fill(mine[3]))
        beside[k] = move(mine[k], Y_SWAP)
    if late:
        beside = {k: after(beside[k], *late) for k in beside}
    return [(mine[k], beside[k]) for k in range(LINE)]


def flat(pieces):
    return jnp.concatenate([piece for pair in pieces for piece in pair], axis=0)


def added(first, *others):
    total = first.astype(jnp.float32)
    for other in others:
        total = total + other.astype(jnp.float32)
    return total.astype(first.dtype)


def scatter_rows(parts, fills, hold=False):
    away = {k: added(*[part(2 * k + 1) for part in parts]) for k in (2, 1, 3, 0)}
    moved = {2: move(away[2], Y_SWAP)}
    arrived, reduced = [], away[2]
    for k, fill in zip((2, 1, 3, 0), fills):
        filled = [] if fill is None else fill((reduced,))
        if k == 2:
            for other in (1, 3, 0):
                held = after(away[other], *filled) if hold else away[other]
                moved[other] = move(held, Y_SWAP)
        here = after(moved[k], *filled) if filled else moved[k]
        reduced = added(here, *[part(2 * k) for part in parts])
        if k > 0:
            arrived.append(move(reduced, Z_TO[k]))
    if fills[4] is not None:
        reduced, *arrived = fills[4]((reduced, *arrived))
    return added(reduced, *arrived)


LIMIT = 56 * 2**20
HIDDEN_BLOCK = 256
WIDTH_BLOCK = 512
QUIET = pl.CostEstimate(flops=0, bytes_accessed=0, transcendentals=0)
LOUD = pl.CostEstimate(flops=10**11, bytes_accessed=0, transcendentals=0)


def ordered(kernel, behind):
    def body(scalar_ref, *refs):
        return kernel(scalar_ref, *refs[behind:])

    return body


HELD = pl.BlockSpec(memory_space=pl.ANY)


def copy_block(order_ref, from_ref, into_ref):
    into_ref[...] = from_ref[...]


def pick_columns(values, order, block):
    rows = values.shape[0]
    picks = order.shape[0]
    return pl.pallas_call(
        copy_block,
        grid_spec=pltpu.PrefetchScalarGridSpec(
            num_scalar_prefetch=1,
            grid=(picks,),
            in_specs=[pl.BlockSpec((rows, block), lambda i, order: (0, order[i]))],
            out_specs=pl.BlockSpec((rows, block), lambda i, order: (0, i)),
        ),
        out_shape=jax.ShapeDtypeStruct((rows, picks * block), values.dtype),
        compiler_params=pltpu.CompilerParams(vmem_limit_bytes=32 * 2**20),
    )(order, values)


def thin_kernel(rep_ref, from_ref, into_ref):
    heads = into_ref.shape[1] // HEAD_DIM

    def take(parity):
        for head in range(heads):
            start = (2 * head + parity) * HEAD_DIM
            into_ref[:, head * HEAD_DIM : (head + 1) * HEAD_DIM] = from_ref[
                :, start : start + HEAD_DIM
            ]

    @pl.when(rep_ref[0] < 2)
    def _():
        take(0)

    @pl.when(rep_ref[0] >= 2)
    def _():
        take(1)


def thin_columns(weights, rep, width):
    rows = weights.shape[0]
    return pl.pallas_call(
        thin_kernel,
        grid_spec=pltpu.PrefetchScalarGridSpec(
            num_scalar_prefetch=1,
            grid=(3,),
            in_specs=[
                pl.BlockSpec((rows, width // 2), lambda i, rep: (0, 2 * i + lax.rem(rep[0], 2)))
            ],
            out_specs=pl.BlockSpec((rows, width // 4), lambda i, rep: (0, i)),
        ),
        out_shape=jax.ShapeDtypeStruct((rows, 3 * width // 4), weights.dtype),
        compiler_params=pltpu.CompilerParams(vmem_limit_bytes=32 * 2**20),
    )(rep, weights)


def weave_kernel(rep_ref, even_ref, odd_ref, into_ref):
    for head in range(even_ref.shape[2] // HEAD_DIM):
        part = slice(head * HEAD_DIM, (head + 1) * HEAD_DIM)
        start = 2 * head * HEAD_DIM
        into_ref[:, start : start + HEAD_DIM] = even_ref[0, :, part].astype(jnp.float32)
        into_ref[:, start + HEAD_DIM : start + 2 * HEAD_DIM] = odd_ref[0, :, part].astype(
            jnp.float32
        )


def weave_columns(pieces, rep, columns, behind):
    rows = pieces.shape[1]
    block = columns // 3
    return pl.pallas_call(
        ordered(weave_kernel, len(behind)),
        grid_spec=pltpu.PrefetchScalarGridSpec(
            num_scalar_prefetch=1,
            grid=(3, 2),
            in_specs=[HELD] * len(behind)
            + [
                pl.BlockSpec((1, rows, block), lambda i, j, rep: (j ^ rep[0], 0, i)),
                pl.BlockSpec((1, rows, block), lambda i, j, rep: ((j + 2) ^ rep[0], 0, i)),
            ],
            out_specs=pl.BlockSpec((rows, 2 * block), lambda i, j, rep: (0, 2 * i + j)),
        ),
        out_shape=jax.ShapeDtypeStruct((rows, 4 * columns), jnp.float32),
        compiler_params=pltpu.CompilerParams(vmem_limit_bytes=32 * 2**20),
    )(rep, *behind, pieces, pieces)


def widen_kernel(core_ref, own_ref, other_ref, into_ref):
    mine = pl.program_id(0) == core_ref[0]

    @pl.when(mine)
    def _():
        into_ref[...] = own_ref[...].astype(jnp.float32)

    @pl.when(jnp.logical_not(mine))
    def _():
        into_ref[...] = other_ref[...].astype(jnp.float32)


def widen(own, other, core, behind=()):
    experts, rows, columns = own.shape
    block = rows // 4
    steps = experts * 4

    def place(hold, core, i, j):
        return jnp.where(i == hold, j, jnp.where(hold == 0, steps - 1, 0))

    own_map = lambda i, j, core: (place(core[0], core, i, j), 0)
    other_map = lambda i, j, core: (place(1 - core[0], core, i, j), 0)
    result = pl.pallas_call(
        ordered(widen_kernel, len(behind)),
        grid_spec=pltpu.PrefetchScalarGridSpec(
            num_scalar_prefetch=1,
            grid=(2, steps),
            in_specs=[HELD] * len(behind)
            + [
                pl.BlockSpec((block, columns), own_map),
                pl.BlockSpec((block, columns), other_map),
            ],
            out_specs=pl.BlockSpec((block, columns), lambda i, j, core: (i * steps + j, 0)),
        ),
        out_shape=jax.ShapeDtypeStruct((2 * experts * rows, columns), jnp.float32),
        compiler_params=pltpu.CompilerParams(vmem_limit_bytes=32 * 2**20),
        cost_estimate=QUIET,
    )(
        core,
        *behind,
        own.reshape(experts * rows, columns),
        other.reshape(experts * rows, columns),
    )
    return result.reshape(2 * experts, rows, columns)


def slot_rows(slots, capacity):
    places = lax.broadcasted_iota(jnp.int32, (capacity, slots.shape[1]), 0)
    return jnp.where(places == slots, 1.0, 0.0).astype(jnp.bfloat16)


def slot_columns(slots, columns):
    places = lax.broadcasted_iota(jnp.int32, (slots.shape[0], columns), 1)
    found = places == slots[:, 0:1]
    for expert in range(1, slots.shape[1]):
        found = found | (places == slots[:, expert : expert + 1])
    return jnp.where(found, 1.0, 0.0).astype(jnp.bfloat16)


def dot_wide(left, right):
    return jnp.dot(left, right, preferred_element_type=jnp.float32)


def pick_rows_into(slots_ref, rows_ref, into_ref):
    choice = slot_rows(slots_ref[0], into_ref.shape[1])
    for start in range(0, rows_ref.shape[1], WIDTH_BLOCK):
        part = slice(start, start + WIDTH_BLOCK)
        into_ref[0, :, part] = dot_wide(choice, rows_ref[:, part]).astype(jnp.bfloat16)


def cotangent_kernel(core_ref, slots_ref, rows_ref, down_ref, picked_ref, slot_ref):
    @pl.when(pl.program_id(1) == 0)
    def _():
        pick_rows_into(slots_ref, rows_ref, picked_ref)

    slot_ref[0] = contract_cols(picked_ref[0], down_ref[0])


def cotangent_part(core, slots, rows, down_weight, capacity, behind=()):
    experts, tokens = slots.shape
    width, hidden = rows.shape[1], down_weight.shape[1]
    return pl.pallas_call(
        ordered(cotangent_kernel, len(behind)),
        grid_spec=pltpu.PrefetchScalarGridSpec(
            num_scalar_prefetch=1,
            grid=(experts, hidden // HIDDEN_BLOCK),
            in_specs=[HELD] * len(behind)
            + [
                pl.BlockSpec((1, 1, tokens), lambda e, n, core: (e, 0, 0)),
                pl.BlockSpec((tokens, width), lambda e, n, core: (0, 0)),
                pl.BlockSpec(
                    (1, HIDDEN_BLOCK, width), lambda e, n, core: (core[0] * experts + e, n, 0)
                ),
            ],
            out_specs=[
                pl.BlockSpec((1, capacity, width), lambda e, n, core: (e, 0, 0)),
                pl.BlockSpec((1, capacity, HIDDEN_BLOCK), lambda e, n, core: (e, 0, n)),
            ],
        ),
        out_shape=[
            jax.ShapeDtypeStruct((experts, capacity, width), jnp.bfloat16),
            jax.ShapeDtypeStruct((experts, capacity, hidden), jnp.float32),
        ],
        compiler_params=pltpu.CompilerParams(vmem_limit_bytes=LIMIT),
        cost_estimate=LOUD,
    )(core, *behind, slots[:, None, :], rows, down_weight)


def forward_kernel(
    first_ref,
    slots_ref,
    rows_ref,
    router_ref,
    gate_ref,
    up_ref,
    slot_ref,
    picked_ref,
    act_ref,
    grad_gate_ref,
    grad_up_ref,
    score_ref,
    weight_ref,
    total_ref,
):
    step = pl.program_id(1)
    mine = first_ref[1] + pl.program_id(0)

    @pl.when(step == 0)
    def _():
        pick_rows_into(slots_ref, rows_ref, picked_ref)
        logits = contract_cols(picked_ref[0], router_ref[...])
        raised = jnp.exp(logits - jnp.max(logits, axis=1, keepdims=True))
        label = lax.broadcasted_iota(jnp.int32, raised.shape, 1)
        own = jnp.sum(jnp.where(label == mine, raised, 0.0), axis=1, keepdims=True)
        weight_ref[...] = own / jnp.sum(raised, axis=1, keepdims=True)
        total_ref[...] = jnp.zeros_like(total_ref)

    gate_pre = dot_wide(picked_ref[0], gate_ref[0])
    up_pre = dot_wide(picked_ref[0], up_ref[0])
    sigmoid = 1.0 / (1.0 + jnp.exp(-gate_pre))
    smooth = gate_pre * sigmoid
    grad_act = weight_ref[...] * slot_ref[0]
    act = smooth * up_pre
    act_ref[0] = (weight_ref[...] * act).astype(jnp.bfloat16)
    grad_gate_ref[0] = (grad_act * up_pre * (sigmoid + smooth * (1.0 - sigmoid))).astype(
        jnp.bfloat16
    )
    grad_up_ref[0] = (grad_act * smooth).astype(jnp.bfloat16)
    total_ref[...] += jnp.sum(act * grad_act, axis=1, keepdims=True)

    @pl.when(step == pl.num_programs(1) - 1)
    def _():
        label = lax.broadcasted_iota(jnp.int32, score_ref.shape[1:], 1)
        score_ref[0] = jnp.where(label == mine, total_ref[...], 0.0).astype(jnp.bfloat16)


def forward_part(first, slots, rows, router_rows, gate_weight, up_weight, slot_cot, behind=(), cost=QUIET):
    experts, tokens = slots.shape
    capacity, hidden = slot_cot.shape[1:]
    width = rows.shape[1]
    labels = router_rows.shape[0]
    weight_spec = pl.BlockSpec(
        (1, width, HIDDEN_BLOCK), lambda e, n, first: (first[0] * experts + e, 0, n)
    )
    hidden_spec = pl.BlockSpec((1, capacity, HIDDEN_BLOCK), lambda e, n, first: (e, 0, n))
    hidden_shape = jax.ShapeDtypeStruct((experts, capacity, hidden), jnp.bfloat16)
    return pl.pallas_call(
        ordered(forward_kernel, len(behind)),
        grid_spec=pltpu.PrefetchScalarGridSpec(
            num_scalar_prefetch=1,
            grid=(experts, hidden // HIDDEN_BLOCK),
            in_specs=[HELD] * len(behind)
            + [
                pl.BlockSpec((1, 1, tokens), lambda e, n, first: (e, 0, 0)),
                pl.BlockSpec((tokens, width), lambda e, n, first: (0, 0)),
                pl.BlockSpec((labels, width), lambda e, n, first: (0, 0)),
                weight_spec,
                weight_spec,
                hidden_spec,
            ],
            out_specs=[
                pl.BlockSpec((1, capacity, width), lambda e, n, first: (e, 0, 0)),
                hidden_spec,
                hidden_spec,
                hidden_spec,
                pl.BlockSpec((1, capacity, HEAD_DIM), lambda e, n, first: (e, 0, 0)),
            ],
            scratch_shapes=[
                pltpu.VMEM((capacity, 1), jnp.float32),
                pltpu.VMEM((capacity, 1), jnp.float32),
            ],
        ),
        out_shape=[
            jax.ShapeDtypeStruct((experts, capacity, width), jnp.bfloat16),
            hidden_shape,
            hidden_shape,
            hidden_shape,
            jax.ShapeDtypeStruct((experts, capacity, HEAD_DIM), jnp.bfloat16),
        ],
        compiler_params=pltpu.CompilerParams(vmem_limit_bytes=LIMIT),
        cost_estimate=cost,
    )(first, *behind, slots[:, None, :], rows, router_rows, gate_weight, up_weight, slot_cot)


def backward_kernel(
    core_ref, slots_ref, grad_gate_ref, grad_up_ref, score_ref, *rest
):
    experts, capacity, _ = grad_gate_ref.shape
    gates, ups = rest[:experts], rest[experts : 2 * experts]
    into_ref, spread_ref, slot_ref = rest[2 * experts :]
    step = pl.program_id(0)
    width = pl.num_programs(0) * WIDTH_BLOCK

    @pl.when(step == 0)
    def _():
        spread_ref[...] = slot_columns(slots_ref[...], experts * capacity)
        scores = score_ref[...].reshape(experts * capacity, HEAD_DIM)
        into_ref[:, width:] = dot_wide(spread_ref[...], scores).astype(jnp.bfloat16)

    for expert in range(experts):
        rows = contract_cols(grad_gate_ref[expert], gates[expert][0]) + contract_cols(
            grad_up_ref[expert], ups[expert][0]
        )
        slot_ref[expert * capacity : (expert + 1) * capacity, :] = rows.astype(jnp.bfloat16)
    start = pl.multiple_of(step * WIDTH_BLOCK, WIDTH_BLOCK)
    into_ref[:, pl.ds(start, WIDTH_BLOCK)] = dot_wide(spread_ref[...], slot_ref[...]).astype(
        jnp.bfloat16
    )


def backward_part(core, columns, grad_gate, grad_up, scores, gate_weight, up_weight, behind=()):
    experts, capacity, hidden = grad_gate.shape
    tokens, width = columns.shape[0], gate_weight.shape[1]

    def weight_spec(expert):
        return pl.BlockSpec(
            (1, WIDTH_BLOCK, hidden), lambda n, core: (core[0] * experts + expert, n, 0)
        )

    whole = pl.BlockSpec((experts, capacity, hidden), lambda n, core: (0, 0, 0))
    return pl.pallas_call(
        ordered(backward_kernel, len(behind)),
        grid_spec=pltpu.PrefetchScalarGridSpec(
            num_scalar_prefetch=1,
            grid=(width // WIDTH_BLOCK,),
            in_specs=[HELD] * len(behind)
            + [
                pl.BlockSpec(columns.shape, lambda n, core: (0, 0)),
                whole,
                whole,
                pl.BlockSpec((experts, capacity, HEAD_DIM), lambda n, core: (0, 0, 0)),
            ]
            + [weight_spec(expert) for expert in range(experts)] * 2,
            out_specs=pl.BlockSpec((tokens, width + HEAD_DIM), lambda n, core: (0, 0)),
            scratch_shapes=[
                pltpu.VMEM((tokens, experts * capacity), jnp.bfloat16),
                pltpu.VMEM((experts * capacity, WIDTH_BLOCK), jnp.bfloat16),
            ],
        ),
        out_shape=jax.ShapeDtypeStruct((tokens, width + HEAD_DIM), jnp.bfloat16),
        compiler_params=pltpu.CompilerParams(vmem_limit_bytes=LIMIT),
        cost_estimate=QUIET,
    )(
        core,
        *behind,
        columns,
        grad_gate,
        grad_up,
        scores,
        *[gate_weight] * experts,
        *[up_weight] * experts,
    )


def routed_kernel(more, core_ref, slots_ref, act_ref, *rest):
    experts, capacity, _ = act_ref.shape
    downs = rest[:experts]
    into_ref, spread_ref, slot_ref = rest[experts + more :]

    @pl.when(pl.program_id(0) == 0)
    def _():
        spread_ref[...] = slot_columns(slots_ref[...], experts * capacity)

    for expert in range(experts):
        rows = dot_wide(act_ref[expert], downs[expert][0])
        slot_ref[expert * capacity : (expert + 1) * capacity, :] = rows.astype(jnp.bfloat16)
    total = dot_wide(spread_ref[...], slot_ref[...])
    for extra in rest[experts : experts + more]:
        total += extra[...].astype(jnp.float32)
    into_ref[...] = total.astype(jnp.bfloat16)


def routed_part(core, columns, act, down_weight, extra=(), behind=()):
    experts, capacity, hidden = act.shape
    tokens, width = columns.shape[0], down_weight.shape[2]

    def weight_spec(expert):
        return pl.BlockSpec(
            (1, hidden, WIDTH_BLOCK), lambda n, core: (core[0] * experts + expert, 0, n)
        )

    rows_spec = pl.BlockSpec((tokens, WIDTH_BLOCK), lambda n, core: (0, n))
    return pl.pallas_call(
        ordered(functools.partial(routed_kernel, len(extra)), len(behind)),
        grid_spec=pltpu.PrefetchScalarGridSpec(
            num_scalar_prefetch=1,
            grid=(width // WIDTH_BLOCK,),
            in_specs=[HELD] * len(behind)
            + [
                pl.BlockSpec(columns.shape, lambda n, core: (0, 0)),
                pl.BlockSpec((experts, capacity, hidden), lambda n, core: (0, 0, 0)),
            ]
            + [weight_spec(expert) for expert in range(experts)]
            + [rows_spec] * len(extra),
            out_specs=rows_spec,
            scratch_shapes=[
                pltpu.VMEM((tokens, experts * capacity), jnp.bfloat16),
                pltpu.VMEM((experts * capacity, WIDTH_BLOCK), jnp.bfloat16),
            ],
        ),
        out_shape=jax.ShapeDtypeStruct((tokens, width), jnp.bfloat16),
        compiler_params=pltpu.CompilerParams(vmem_limit_bytes=LIMIT),
        cost_estimate=LOUD,
    )(core, *behind, columns, act, *[down_weight] * experts, *extra)


def roll_half(values):
    return pltpu.roll(values, HEAD_DIM // 2, 1)


def head_parts(raw_ref, rate_ref, gain_ref, cos_ref, sin_ref, head):
    part_width = gain_ref.shape[1]
    units, turned = [], []
    for which in range(2):
        start = which * part_width + head * HEAD_DIM
        unit = raw_ref[:, start : start + HEAD_DIM] * rate_ref[:, which : which + 1]
        gain = gain_ref[which : which + 1, head * HEAD_DIM : (head + 1) * HEAD_DIM]
        scaled = unit * gain
        units.append((unit, gain))
        turned.append(
            (scaled * cos_ref[...] + roll_half(scaled) * sin_ref[...]).astype(jnp.bfloat16)
        )
    start = 2 * part_width + head * HEAD_DIM
    value = raw_ref[:, start : start + HEAD_DIM].astype(jnp.bfloat16)
    return units, turned, value


def head_probs(turned, column_ref, row_ref):
    scores = contract_cols(turned[0], turned[1]) * HEAD_DIM ** (-0.5)
    length = scores.shape[0]
    reader = lax.broadcasted_iota(jnp.int32, (length, length), 0)
    source = lax.broadcasted_iota(jnp.int32, (length, length), 1)
    allowed = (column_ref[...] == row_ref[0]) & (source <= reader)
    scores = jnp.where(allowed, scores, masked_score)
    raised = jnp.exp(scores - jnp.max(scores, axis=1, keepdims=True))
    return raised / jnp.sum(raised, axis=1, keepdims=True)


def attend_kernel(raw_ref, rate_ref, gain_ref, cos_ref, sin_ref, column_ref, row_ref, into_ref):
    for head in range(gain_ref.shape[1] // HEAD_DIM):
        _, turned, value = head_parts(raw_ref, rate_ref, gain_ref, cos_ref, sin_ref, head)
        probs = head_probs(turned, column_ref, row_ref).astype(jnp.bfloat16)
        into_ref[:, head * HEAD_DIM : (head + 1) * HEAD_DIM] = dot_wide(probs, value).astype(
            jnp.bfloat16
        )


def attend_back_kernel(
    raw_ref,
    rate_ref,
    gain_ref,
    cos_ref,
    sin_ref,
    column_ref,
    row_ref,
    grad_ref,
    pair_ref,
    value_ref,
    dots_ref,
    gains_ref,
):
    score_scale = HEAD_DIM ** (-0.5)
    part_width = gain_ref.shape[1]
    dots = [0.0, 0.0]
    for head in range(part_width // HEAD_DIM):
        units, turned, value = head_parts(raw_ref, rate_ref, gain_ref, cos_ref, sin_ref, head)
        probs = head_probs(turned, column_ref, row_ref)
        here = slice(head * HEAD_DIM, (head + 1) * HEAD_DIM)
        grad = grad_ref[:, here]
        grad_probs = contract_cols(grad, value)
        mean_grad = jnp.sum(probs * grad_probs, axis=1, keepdims=True)
        grad_scores = (probs * (grad_probs - mean_grad)).astype(jnp.bfloat16)
        value_ref[:, here] = contract_rows(probs.astype(jnp.bfloat16), grad).astype(jnp.bfloat16)
        grads = (
            dot_wide(grad_scores, turned[1]) * score_scale,
            contract_rows(grad_scores, turned[0]) * score_scale,
        )
        for which in range(2):
            unit, gain = units[which]
            back = grads[which] * cos_ref[...] + roll_half(grads[which] * sin_ref[...])
            gains_ref[0, which : which + 1, here] = jnp.sum(back * unit, axis=0, keepdims=True)
            back = back * gain
            start = which * part_width + head * HEAD_DIM
            pair_ref[:, start : start + HEAD_DIM] = back
            dots[which] += jnp.sum(back * unit, axis=1, keepdims=True)
    dots_ref[:, 0:1] = dots[0]
    dots_ref[:, 1:2] = dots[1]


def join_kernel(raw_ref, rate_ref, pair_ref, value_ref, dots_ref, into_ref):
    part_width = value_ref.shape[1]
    for which in range(2):
        here = slice(which * part_width, (which + 1) * part_width)
        rate = rate_ref[:, which : which + 1]
        shift = dots_ref[:, which : which + 1] * rate
        into_ref[:, here] = (rate * (pair_ref[:, here] - raw_ref[:, here] * shift)).astype(
            jnp.bfloat16
        )
    into_ref[:, 2 * part_width :] = value_ref[...]


def row_blocks(count, *arrays):
    return [pl.BlockSpec((array.shape[0] // count, array.shape[1]), lambda i: (i, 0)) for array in arrays]


def attention_specs(raw, rate, gains, cos_table, sin_table, columns, rows):
    count = rows.shape[0]
    return (
        row_blocks(count, raw, rate)
        + [pl.BlockSpec(gains.shape, lambda i: (0, 0))]
        + row_blocks(count, cos_table, sin_table, columns)
        + [pl.BlockSpec((1, 1, rows.shape[2]), lambda i: (i, 0, 0))]
    )


def attend(raw, rate, gains, cos_table, sin_table, columns, rows):
    count = rows.shape[0]
    operands = (raw, rate, gains, cos_table, sin_table, columns, rows)
    result = jax.ShapeDtypeStruct((raw.shape[0], gains.shape[1]), jnp.bfloat16)
    return pl.pallas_call(
        attend_kernel,
        grid=(count,),
        in_specs=attention_specs(*operands),
        out_specs=row_blocks(count, result)[0],
        out_shape=result,
        compiler_params=pltpu.CompilerParams(vmem_limit_bytes=LIMIT),
        cost_estimate=QUIET,
    )(*operands)


def attend_back(raw, rate, gains, cos_table, sin_table, columns, rows, grads, behind=()):
    count = rows.shape[0]
    operands = (raw, rate, gains, cos_table, sin_table, columns, rows)
    results = [
        jax.ShapeDtypeStruct((raw.shape[0], 2 * gains.shape[1]), jnp.float32),
        jax.ShapeDtypeStruct((raw.shape[0], gains.shape[1]), jnp.bfloat16),
        jax.ShapeDtypeStruct((raw.shape[0], 2), jnp.float32),
    ]
    gain_result = jax.ShapeDtypeStruct((count,) + gains.shape, jnp.float32)
    return pl.pallas_call(
        lambda *refs: attend_back_kernel(*refs[len(behind) :]),
        grid=(count,),
        in_specs=[HELD] * len(behind) + attention_specs(*operands) + row_blocks(count, grads),
        out_specs=row_blocks(count, *results)
        + [pl.BlockSpec((1,) + gains.shape, lambda i: (i, 0, 0))],
        out_shape=results + [gain_result],
        compiler_params=pltpu.CompilerParams(vmem_limit_bytes=LIMIT),
        cost_estimate=QUIET,
    )(*behind, *operands, grads)


def join_grads(raw, rate, pair, value, dots, count):
    operands = (raw, rate, pair, value, dots)
    result = jax.ShapeDtypeStruct(raw.shape, jnp.bfloat16)
    return pl.pallas_call(
        join_kernel,
        grid=(count,),
        in_specs=row_blocks(count, *operands),
        out_specs=row_blocks(count, result)[0],
        out_shape=result,
        compiler_params=pltpu.CompilerParams(vmem_limit_bytes=LIMIT),
        cost_estimate=QUIET,
    )(*operands)


def rep_sum(values):
    values = values + move(values, CORE_SWAP).reshape((2, 2) + values.shape[1:])[:, ::-1].reshape(
        values.shape
    )
    swapped = move(values, X_SWAP)
    return values + jnp.concatenate([swapped[2:], swapped[:2]], axis=0)


def fast_local(
    inputs,
    attn_gain,
    in_proj,
    query_gain,
    key_gain,
    out_proj,
    ffn_gain,
    router_weight,
    gate_weight,
    up_weight,
    down_weight,
    routes,
    priority,
    segments,
    grad_out,
):
    f32, bf16 = jnp.float32, jnp.bfloat16
    tokens, width = inputs.shape
    rows_each = in_proj.shape[0]
    local_experts, _, hidden_units = gate_weight.shape
    expert_count = local_experts * SHARDS
    route_count = routes.shape[1]
    pair_count = tokens * route_count
    capacity = 5 * pair_count * SHARDS // (4 * expert_count)
    core_experts = local_experts // 2
    heads = HEADS // REPS
    part_width = heads * HEAD_DIM
    group_rows = SHARDS * tokens
    rep, shard = lax.axis_index("rep"), lax.axis_index("shard")
    a, c = rep // 2, lax.rem(rep, 2)
    z, y = shard // 2, lax.rem(shard, 2)
    rep_ref = rep.astype(jnp.int32).reshape(1)
    core_ref = c.astype(jnp.int32).reshape(1)
    near_shards = lax.rem(z + jnp.arange(LINE, dtype=jnp.int32), LINE)[:, None] * 2 + (
        y ^ jnp.arange(2, dtype=jnp.int32)[None, :]
    )
    near_shards = near_shards.reshape(SHARDS)
    shard_ids = jnp.arange(SHARDS, dtype=jnp.int32)
    place_of_shard = jnp.sum(
        jnp.where(near_shards[None, :] == shard_ids[:, None], shard_ids[None, :], 0), axis=1
    )

    order_row = priority[0]
    pair_ids = jnp.arange(pair_count, dtype=jnp.int32)
    place_of = jnp.sum(
        jnp.where(order_row[None, :] == pair_ids[:, None], pair_ids[None, :], 0), axis=1
    ).reshape(tokens, route_count)
    labels = jnp.arange(expert_count, dtype=jnp.int32)
    hits = routes.T[None, :, :] == labels[:, None, None]
    place_at = jnp.sum(jnp.where(hits, place_of.T[None], 0), axis=1)
    named = jnp.any(hits, axis=1)
    place_at = jnp.where(named, place_at, pair_count)
    earlier = jnp.sum((place_at[:, None, :] < place_at[:, :, None]).astype(jnp.int32), axis=2)
    ranks = jnp.where(named, earlier, -1).astype(bf16)
    ranks = jnp.concatenate([ranks, segments.astype(bf16)], axis=0)
    ranks = jnp.pad(ranks, ((0, 0), (0, rows_each - tokens)))
    ranks = jnp.stack([ranks, move(ranks, CORE_SWAP)])
    ranks = jnp.concatenate([ranks, move(ranks, X_SWAP)])
    segment_rows = ranks[:, expert_count, :tokens].astype(jnp.int32)

    inputs_across = move(inputs, X_SWAP)
    small_in = jnp.stack([attn_gain, query_gain, key_gain, ffn_gain])
    small_in = jnp.concatenate(
        [small_in, router_weight.T, ranks.reshape(REPS * (expert_count + 1), rows_each)], axis=0
    )
    in_pieces = gather_rows(
        thin_columns(in_proj, rep_ref, width), first=(inputs_across, segment_rows)
    )
    small_in = gather_small(small_in, (in_pieces[2][0], in_pieces[1][1], in_pieces[3][1]))
    ranks = small_in[:, 4 + expert_count :, :tokens]
    ranks = jnp.take(ranks, near_shards ^ shard, axis=0)
    ranks = ranks.reshape(SHARDS, REPS, expert_count + 1, tokens)[:, :, :expert_count]
    in_part = flat(in_pieces)

    small_in = jnp.take(small_in[:, : 4 + expert_count], shard_ids ^ shard, axis=0)
    small_in = small_in.transpose(1, 0, 2).reshape(4 + expert_count, width)
    gains = small_in[:4].astype(f32)
    router_rows = small_in[4:]
    part_gains = lax.dynamic_slice(
        gains[1:3].reshape(2, HEADS // 2, 2, HEAD_DIM),
        (0, c * heads, a, 0),
        (2, heads, 1, HEAD_DIM),
    ).reshape(2, part_width)

    hidden = inputs.astype(f32)
    home_rate = lax.rsqrt(jnp.mean(hidden * hidden, axis=-1, keepdims=True) + norm_eps)
    inputs_all = jnp.stack([inputs, inputs_across])
    inputs_all = jnp.stack([inputs_all, move(inputs_all, CORE_SWAP)], axis=1)
    inputs_all = inputs_all.reshape(REPS * tokens, width)
    inputs_all = pick_columns(inputs_all, near_shards, rows_each).astype(f32)
    unit_all = inputs_all * lax.rsqrt(
        jnp.mean(inputs_all * inputs_all, axis=-1, keepdims=True) + norm_eps
    )
    near_gain = jnp.take(gains[0].reshape(SHARDS, rows_each), near_shards, axis=0).reshape(width)
    normed_low = (unit_all * near_gain).astype(bf16)
    cot_across = move(grad_out, X_SWAP)
    normed_low = after(normed_low, cot_across)
    cot_own = after(grad_out, in_part)
    cot_own = lax.all_gather(cot_own, "shard", tiled=True)
    cos_table, sin_table = jax.vmap(rotary_tables)(segment_rows)
    sin_table = jnp.where(jnp.arange(HEAD_DIM) < HEAD_DIM // 2, -sin_table, sin_table)
    cos_table = cos_table.reshape(REPS * tokens, HEAD_DIM)
    sin_table = sin_table.reshape(REPS * tokens, HEAD_DIM)

    out_rows = rows_each // 4
    out_own = lax.dynamic_slice_in_dim(out_proj, rep * out_rows, out_rows, 0)
    out_own = after(out_own, in_pieces[2][0])

    projected = jnp.dot(normed_low, in_part, preferred_element_type=f32)
    squares = jnp.stack(
        [
            jnp.sum(projected[:, k * part_width : (k + 1) * part_width] ** 2, axis=1)
            for k in range(2)
        ],
        axis=1,
    )
    squares = rep_sum(squares.reshape(REPS, tokens, 2)).reshape(REPS * tokens, 2)
    pair_rate = lax.rsqrt(squares / width + norm_eps)
    attention_operands = (
        projected,
        pair_rate,
        part_gains,
        cos_table,
        sin_table,
        segment_rows.reshape(REPS * tokens, 1),
        segment_rows[:, None, :],
    )
    attended = attend(*attention_operands).reshape(2, 2, tokens, part_width)
    out_pieces = gather_rows(out_own, early=(projected,), late=(attended,))
    out_own = flat(out_pieces).reshape(SHARDS, out_rows, width)
    out_other = move(out_own, CORE_SWAP)
    out_part = jnp.where(
        c == 0,
        jnp.concatenate([out_own, out_other], axis=1),
        jnp.concatenate([out_other, out_own], axis=1),
    ).reshape(SHARDS * 2 * out_rows, width)
    attended = jnp.concatenate([attended[:, 0], move(attended[:, 1], CORE_SWAP)], axis=2)
    attended = attended.reshape(2 * tokens, 2 * part_width)
    head_of_place = ((near_shards // heads) ^ c) * heads + lax.rem(near_shards, heads)
    place_of_head = jnp.sum(
        jnp.where(head_of_place[None, :] == shard_ids[:, None], shard_ids[None, :], 0), axis=1
    )
    attended = pick_columns(attended, head_of_place, HEAD_DIM)
    mixed = jnp.dot(attended, out_part, preferred_element_type=f32).reshape(2, tokens, width)
    mixed_across = move(mixed[1].astype(bf16), X_SWAP)
    residual = hidden + mixed[0] + mixed_across.astype(f32)

    ffn_rate = lax.rsqrt(jnp.mean(residual * residual, axis=-1, keepdims=True) + norm_eps)
    ffn_unit = residual * ffn_rate
    ffn_low = (ffn_unit * gains[3]).astype(bf16)
    router_probs = softmax_rows(contract_cols(ffn_low, router_rows))

    ranks = after(ranks, mixed_across).astype(jnp.int32)
    counts = jnp.sum((ranks >= 0).astype(jnp.int32), axis=3)
    before = (near_shards[None, :] < near_shards[:, None])[:, :, None, None]
    bases = jnp.sum(jnp.where(before, counts[None], 0), axis=1)
    slots = bases[..., None] + ranks
    slots = jnp.where((ranks >= 0) & (slots < capacity), slots, -1)
    first_expert = shard * local_experts + c * core_experts
    slots = lax.dynamic_slice_in_dim(slots, first_expert, core_experts, 2)
    slots = slots.transpose(1, 2, 0, 3)
    shard_slots = jnp.take(slots, place_of_shard, axis=2)
    slots = slots.reshape(REPS, core_experts, group_rows)
    shard_slots = shard_slots.reshape(REPS, core_experts, group_rows)
    shifts = jnp.arange(core_experts, dtype=jnp.int32)[:, None] * capacity

    def columns_of(table):
        return jnp.where(table >= 0, table + shifts, -1).transpose(0, 2, 1)

    columns, shard_columns = columns_of(slots[:2]), columns_of(shard_slots[:2])

    def cot_part(group, rows, behind=()):
        return cotangent_part(core_ref, shard_slots[group], rows, down_weight, capacity, behind)

    first_ref = jnp.stack([c, first_expert]).astype(jnp.int32)

    def ffn_part(group, rows, slot_cot, behind=(), cost=QUIET):
        return forward_part(
            first_ref,
            slots[group],
            rows,
            router_rows,
            gate_weight,
            up_weight,
            slot_cot,
            behind,
            cost,
        )

    made = {}

    def fill_cot(follow):
        beside = move(cot_own, CORE_SWAP)
        own_part = cot_part(0, cot_own, (follow,))
        made["cot"] = [own_part, cot_part(1, beside, (own_part[1],))]
        return [own_part[1]]

    ffn_pieces = gather_rows(
        ffn_low, fill=fill_cot
    )
    near_cot = made["cot"]
    ffn_own = after(flat(ffn_pieces), near_cot[1][1])
    ffn_beside = move(ffn_own, CORE_SWAP)
    ffn_far = [move(jnp.concatenate(pair, axis=0), X_SWAP) for pair in ffn_pieces]
    cot_across = lax.all_gather(after(cot_across, ffn_pieces[2][0]), "shard", tiled=True)

    near = [ffn_part(0, ffn_own, near_cot[0][1])]
    near.append(ffn_part(1, ffn_beside, near_cot[1][1], (near[0][1],)))

    def rows_back(group, behind=()):
        _, _, grad_gate, grad_up, scores = near[group]
        return backward_part(
            core_ref, columns[group], grad_gate, grad_up, scores, gate_weight, up_weight, behind
        ).reshape(SHARDS, tokens, -1)

    grad_other = rows_back(1, (ffn_far[0], ffn_far[1]))
    grad_own = rows_back(0, (grad_other,))
    grad_other = move(grad_other, CORE_SWAP)

    def routed_rows(group, extra, behind):
        return routed_part(
            core_ref, shard_columns[group], near[group][1], down_weight, extra, behind
        )

    def fill_routed_other(follow):
        made["routed_other"] = routed_rows(1, (), follow + (ffn_far[2], cot_across))
        return [made["routed_other"]]

    def fill_far_cot(follow):
        made["far_cot"] = cot_part(2, cot_across, follow)
        return [made["far_cot"][1]]

    def fill_routed_own(follow):
        extra = (move(made["routed_other"], CORE_SWAP),)
        made["routed"] = routed_rows(0, extra, follow)
        return [made["routed"]]

    def fill_other_cot(follow):
        rows = move(after(cot_across, made["routed"]), CORE_SWAP)
        made["other_cot"] = cot_part(3, rows, follow)
        return [made["other_cot"][1]]

    grad_home = scatter_rows(
        [lambda place: grad_own[place], lambda place: grad_other[place]],
        [fill_routed_other, fill_routed_own, fill_far_cot, fill_other_cot, None],
    )
    routed = lax.psum_scatter(
        after(made["routed"], grad_home), "shard", scatter_dimension=0, tiled=True
    )
    ffn_far = jnp.concatenate([after(part, made["other_cot"][1]) for part in ffn_far], axis=0)
    ffn_far = [ffn_far, move(ffn_far, CORE_SWAP)]

    grad_ffn_home = grad_home[:, :width]
    home_score = grad_home[:, width : width + expert_count].astype(f32)
    grad_logits = home_score - router_probs * jnp.sum(home_score, axis=1, keepdims=True)
    grad_logits_low = grad_logits.astype(bf16)

    grad_ffn_in = grad_ffn_home.astype(f32) + jnp.dot(
        grad_logits_low, router_rows, preferred_element_type=f32
    )
    grad_router_local = contract_rows(grad_logits_low, ffn_low)
    grad_ffn_local = jnp.sum(grad_ffn_in * ffn_unit, axis=0)
    scaled = gains[3] * grad_ffn_in
    grad_residual = grad_out.astype(f32) + ffn_rate * (
        scaled - ffn_unit * jnp.mean(scaled * ffn_unit, axis=-1, keepdims=True)
    )
    residual_low = grad_residual.astype(bf16)
    residual_other = move(residual_low, X_SWAP)
    residual_pair = jnp.concatenate([residual_low, residual_other], axis=0)

    grad_attended = contract_cols(residual_pair, out_part).astype(bf16)
    grad_attended = pick_columns(grad_attended, place_of_head, HEAD_DIM)
    grad_attended = grad_attended.reshape(2, tokens, 2 * part_width)
    mine, theirs = grad_attended[:, :, :part_width], grad_attended[:, :, part_width:]
    grad_attended = jnp.stack([mine, move(theirs, CORE_SWAP)], axis=1)
    grad_attended = grad_attended.reshape(REPS * tokens, part_width)
    grad_pair, grad_value, dots, grad_pair_gain = attend_back(*attention_operands, grad_attended)
    grad_pair_gain = jnp.sum(grad_pair_gain, axis=0).reshape(2, heads, HEAD_DIM)
    dots = rep_sum(dots.reshape(REPS, tokens, 2)).reshape(REPS * tokens, 2) / width
    grad_projected = join_grads(projected, pair_rate, grad_pair, grad_value, dots, REPS)

    grad_in_part = contract_rows(normed_low, grad_projected).astype(bf16)
    grad_in_part = grad_in_part.reshape(SHARDS, rows_each, 3 * part_width)
    grad_normed = contract_cols(grad_projected, in_part)
    grad_attn_part = jnp.sum(grad_normed * unit_all, axis=0)

    pair_gains = jnp.zeros((2, HEADS // 2, 2, HEAD_DIM), f32)
    pair_gains = lax.dynamic_update_slice(
        pair_gains, grad_pair_gain[:, :, None], (0, c * heads, a, 0)
    )
    small = jnp.concatenate(
        [grad_ffn_local[None], pair_gains.reshape(2, width), grad_router_local], axis=0
    )
    small = jnp.take(small.reshape(-1, SHARDS, rows_each), near_shards, axis=1)
    small = jnp.concatenate([grad_attn_part.reshape(1, SHARDS, rows_each), small], axis=0)
    small = jnp.pad(small, ((0, HEAD_DIM - small.shape[0]), (0, 0), (0, 0)))
    small = small.astype(bf16).transpose(1, 2, 0)

    grad_out_part = contract_rows(after(attended, grad_projected), residual_pair).astype(bf16)
    out_parts = grad_out_part.reshape(SHARDS, 2, out_rows, width)
    out_own = lax.dynamic_index_in_dim(out_parts, c, 1, keepdims=False)
    out_other = lax.dynamic_index_in_dim(out_parts, 1 - c, 1, keepdims=False)
    out_sum = added(out_own, move(out_other, CORE_SWAP))
    out_sum = jnp.take(out_sum, place_of_shard, axis=0).reshape(SHARDS * out_rows, width)

    far_cot = [made["far_cot"], made["other_cot"]]

    def fill_far(follow):
        made["far"] = ffn_part(
            2, ffn_far[0], far_cot[0][1], follow + (ffn_far[1],), LOUD
        )
        return [made["far"][3]]

    normed_other = grad_normed.astype(bf16).reshape(2, 2, tokens, width)
    normed_mine = added(normed_other[:, 0], move(normed_other[:, 1], CORE_SWAP))
    normed_across = move(normed_mine[1], X_SWAP)

    def fill_other(follow):
        made["other"] = ffn_part(
            3, ffn_far[1], far_cot[1][1], follow + (made["far"][3], normed_mine, routed, out_sum), LOUD
        )
        return [made["other"][3]]

    def weight_grad(left, right, follow):
        first, *follow = lax.optimization_barrier((left[0],) + follow)
        left = jnp.concatenate([first] + left[1:], axis=1)
        right = jnp.concatenate(right, axis=1)
        grad = jnp.einsum("ecd,ecf->edf", left, right, preferred_element_type=f32).astype(bf16)
        return grad, follow

    def groups(index):
        return [part[index] for part in (near[0], near[1], made["far"], made["other"])]

    def fence(follow):
        return [made["other"][3]]

    out_home = lax.psum_scatter(
        after(out_sum, routed), "shard", scatter_dimension=0, tiled=True
    )

    def fill_weights(follow):
        cots = [part[0] for part in near_cot + far_cot]
        reduced, first, second, third = follow
        down, _ = weight_grad(groups(1), cots, ())
        gate, (down, first, reduced, _) = weight_grad(
            groups(0), groups(2), (down, first, reduced, normed_across)
        )
        up, (gate, second, third, home) = weight_grad(
            groups(0), groups(3), (gate, second, third, out_home)
        )
        made["down"], made["gate"], made["up"], made["home"] = down, gate, up, home
        return reduced, first, second, third

    in_sum = scatter_rows(
        [lambda place: jnp.concatenate([grad_in_part[place], small[place]], axis=1)],
        [fill_far, fill_other, fence, fence, fill_weights],
        hold=True,
    )
    in_other = move(in_sum, X_SWAP)
    grad_up, out_home = made["up"], made["home"]
    down_all = widen(
        made["down"], move(made["down"], CORE_SWAP), core_ref, (grad_up,)
    )
    in_all = jnp.stack([in_sum, after(in_other, down_all)])
    in_beside = move(in_all, CORE_SWAP)
    out_across = move(after(out_home, down_all), X_SWAP)
    gate_all = widen(
        made["gate"], move(made["gate"], CORE_SWAP), core_ref, (down_all, out_across)
    )
    in_all = jnp.stack([in_all, in_beside], axis=1).reshape((REPS,) + in_sum.shape)
    grad_in = weave_columns(in_all, rep_ref, 3 * part_width, (gate_all,))
    small = jnp.sum(in_all[:, :, 3 * part_width :].astype(f32), axis=0).T
    up_all = widen(grad_up, move(grad_up, CORE_SWAP), core_ref, (gate_all,))

    outputs = (residual + after(routed, down_all).astype(f32)).astype(bf16)
    grad_normed = after(added(normed_mine[0], normed_across), down_all)
    grad_normed = pick_columns(grad_normed, place_of_shard, rows_each).astype(f32)
    home_unit = hidden * home_rate
    scaled = gains[0] * grad_normed
    grad_inputs = (
        grad_residual
        + home_rate * (scaled - home_unit * jnp.mean(scaled * home_unit, axis=-1, keepdims=True))
    ).astype(bf16)

    out_sum = jnp.stack([out_home, out_across])
    out_sum = jnp.stack([out_sum, move(out_sum, CORE_SWAP)], axis=1)
    out_sum = out_sum.reshape(REPS, out_rows, width)
    out_sum = jnp.take(out_sum, rep ^ jnp.arange(REPS, dtype=jnp.int32), axis=0)
    grad_out_proj = out_sum.reshape(rows_each, width).astype(f32)
    return (
        outputs,
        grad_inputs,
        small[0],
        grad_in,
        small[2],
        small[3],
        grad_out_proj,
        small[1],
        small[4 : 4 + expert_count].T,
        gate_all,
        up_all,
        down_all,
    )


def solution(mesh):
    fits = dict(mesh.shape) == {"rep": REPS, "shard": SHARDS}
    body = fast_local if fits else local
    in_specs = (
        P(("rep", "shard"), None),
        P("shard"),
        P("shard", None),
        P("shard"),
        P("shard"),
        P("shard", None),
        P("shard"),
        P("shard", None),
        P("shard", None, None),
        P("shard", None, None),
        P("shard", None, None),
        P(("rep", "shard"), None),
        P(("rep", "shard"), None),
        P(("rep", "shard"), None),
        P(("rep", "shard"), None),
    )
    out_specs = (
        P(("rep", "shard"), None),
        P(("rep", "shard"), None),
        P("shard"),
        P("shard", None),
        P("shard"),
        P("shard"),
        P("shard", None),
        P("shard"),
        P("shard", None),
        P("shard", None, None),
        P("shard", None, None),
        P("shard", None, None),
    )
    return jax.shard_map(body, mesh=mesh, in_specs=in_specs, out_specs=out_specs, check_vma=False)
```

```python
import functools

import jax
import jax.numpy as jnp
from jax import lax
from jax.experimental import pallas as pl
from jax.experimental.pallas import tpu as pltpu
from jax.sharding import PartitionSpec as P

HEADS = 16
HEAD_DIM = 128


norm_eps = 1e-05
rope_base = 10000.0
masked_score = -1e30


def rms_scale(values, gains):
    normed = values * lax.rsqrt(jnp.mean(values * values, axis=-1, keepdims=True) + norm_eps)
    return normed * gains


def rotary_tables(segment_row):
    length = segment_row.shape[0]
    places = jnp.arange(length, dtype=jnp.int32)
    starting = jnp.concatenate(
        [jnp.ones((1,), jnp.int32), (segment_row[1:] != segment_row[:-1]).astype(jnp.int32)]
    )
    first_place = lax.cummax(jnp.where(starting > 0, places, 0), axis=0)
    offsets = (places - first_place).astype(jnp.float32)
    halves = HEAD_DIM // 2
    inverse = rope_base ** (-2.0 * jnp.arange(halves, dtype=jnp.float32) / HEAD_DIM)
    angles = offsets[:, None] * inverse[None, :]
    angles = jnp.concatenate([angles, angles], axis=1)
    return (jnp.cos(angles), jnp.sin(angles))


def rotate(values, cos_table, sin_table):
    halves = values.shape[-1] // 2
    turned = jnp.concatenate([-values[..., halves:], values[..., :halves]], axis=-1)
    return values * cos_table[:, None, :] + turned * sin_table[:, None, :]


def query_key(raw_query, raw_key, query_scale, key_scale, cos_table, sin_table):
    row_count = raw_query.shape[0]
    normed_query = rms_scale(raw_query, query_scale).reshape(row_count, HEADS, HEAD_DIM)
    normed_key = rms_scale(raw_key, key_scale).reshape(row_count, HEADS, HEAD_DIM)
    return (rotate(normed_query, cos_table, sin_table), rotate(normed_key, cos_table, sin_table))


def softmax_rows(logits):
    highest = jnp.max(logits, axis=-1, keepdims=True)
    raised = jnp.exp(logits - highest)
    return raised / jnp.sum(raised, axis=-1, keepdims=True)


def swiglu(gate_pre, up_pre):
    return jax.nn.silu(gate_pre) * up_pre


def contract_rows(left_side, right_side):
    return lax.dot_general(
        left_side, right_side, (((0,), (0,)), ((), ())), preferred_element_type=jnp.float32
    )


def contract_cols(left_side, right_side):
    return lax.dot_general(
        left_side, right_side, (((1,), (1,)), ((), ())), preferred_element_type=jnp.float32
    )


def pick_rows(source_rows, row_picks):
    return jax.vmap(lambda expert_rows, picked: expert_rows[picked])(source_rows, row_picks)


def local(
    inputs,
    attn_gain,
    in_proj,
    query_gain,
    key_gain,
    out_proj,
    ffn_gain,
    router_weight,
    gate_weight,
    up_weight,
    down_weight,
    routes,
    priority,
    segments,
    grad_out,
):
    tokens = inputs.shape[0]
    model_width = inputs.shape[1]
    local_experts = gate_weight.shape[0]
    group_count = lax.axis_size("shard")
    my_index = lax.axis_index("shard")
    expert_count = local_experts * group_count
    route_count = routes.shape[1]
    pair_count = tokens * route_count
    capacity = 5 * pair_count * group_count // (4 * expert_count)
    send_most = 2 * pair_count // expert_count
    segment_row = segments[0]
    cos_table, sin_table = rotary_tables(segment_row)
    hidden_in = inputs.astype(jnp.float32)
    unit_rows = hidden_in * lax.rsqrt(
        jnp.mean(hidden_in * hidden_in, axis=-1, keepdims=True) + norm_eps
    )
    weight_piece = lax.all_gather(in_proj, "shard", axis=0, tiled=True)
    attn_piece = lax.all_gather(attn_gain, "shard", axis=0, tiled=True)
    query_piece = lax.all_gather(query_gain, "shard", axis=0, tiled=True)
    key_piece = lax.all_gather(key_gain, "shard", axis=0, tiled=True)
    scaled = (unit_rows * attn_piece.astype(jnp.float32)).astype(jnp.bfloat16)
    result = (
        jnp.dot(scaled, weight_piece, preferred_element_type=jnp.float32),
        attn_piece.astype(jnp.float32),
        query_piece.astype(jnp.float32),
        key_piece.astype(jnp.float32),
    )
    folded_in = result
    projected = folded_in[0]
    normed_attn, attn_norm_back = jax.vjp(rms_scale, hidden_in, folded_in[1])
    normed_low = normed_attn.astype(jnp.bfloat16)
    raw_query = projected[:, :model_width]
    raw_key = projected[:, model_width : 2 * model_width]
    raw_value = projected[:, 2 * model_width :]

    def rotated_pair(query_raw, key_raw, query_scale, key_scale):
        return query_key(query_raw, key_raw, query_scale, key_scale, cos_table, sin_table)

    (turned_query, turned_key), query_key_back = jax.vjp(
        rotated_pair, raw_query, raw_key, folded_in[2], folded_in[3]
    )
    query_low = turned_query.astype(jnp.bfloat16)
    key_low = turned_key.astype(jnp.bfloat16)
    value_low = raw_value.astype(jnp.bfloat16).reshape(tokens, HEADS, HEAD_DIM)
    places = jnp.arange(tokens, dtype=jnp.int32)
    allowed = (segment_row[:, None] == segment_row[None, :]) & (places[None, :] <= places[:, None])
    score_scale = HEAD_DIM ** (-0.5)

    def masked_scores(queries, key_vecs):
        products = jnp.einsum("qhd,khd->hqk", queries, key_vecs, preferred_element_type=jnp.float32)
        return jnp.where(allowed[None], products * score_scale, masked_score)

    scores = masked_scores(query_low, key_low)
    highest = jnp.max(scores, axis=-1, keepdims=True)
    raised = jnp.exp(scores - highest)
    totals = jnp.sum(raised, axis=-1, keepdims=True)
    attn_probs = raised / totals
    log_total = highest + jnp.log(totals)
    mixed = jnp.einsum(
        "hqk,khd->qhd",
        attn_probs.astype(jnp.bfloat16),
        value_low,
        preferred_element_type=jnp.float32,
    )
    attended = mixed.reshape(tokens, model_width).astype(jnp.bfloat16)
    weight_piece = lax.all_gather(out_proj, "shard", axis=0, tiled=True)
    ffn_piece = lax.all_gather(ffn_gain, "shard", axis=0, tiled=True)
    router_piece = lax.all_gather(router_weight, "shard", axis=0, tiled=True)
    result = (
        jnp.dot(attended, weight_piece, preferred_element_type=jnp.float32),
        ffn_piece.astype(jnp.float32),
        router_piece,
    )
    residual = hidden_in + result[0]
    router_full = result[2]
    normed_ffn, ffn_norm_back = jax.vjp(rms_scale, residual, result[1])
    ffn_low = normed_ffn.astype(jnp.bfloat16)
    logits = jnp.dot(ffn_low, router_full, preferred_element_type=jnp.float32)
    router_probs, router_back = jax.vjp(softmax_rows, logits)
    flat_routes = routes.reshape(pair_count)
    order_row = priority[0]
    ranked_expert = flat_routes[order_row]
    labels = jnp.arange(expert_count, dtype=jnp.int32)
    matches = (ranked_expert[:, None] == labels[None, :]).astype(jnp.int32)
    rank_in = (
        jnp.sum(jnp.cumsum(matches, axis=0, dtype=jnp.int32) * matches, axis=1, dtype=jnp.int32) - 1
    )
    counts = jnp.sum(matches, axis=0, dtype=jnp.int32)
    all_counts = lax.all_gather(counts[None, :], "shard", axis=0, tiled=True)
    base_slots = jnp.cumsum(all_counts, axis=0, dtype=jnp.int32) - all_counts
    my_bases = lax.dynamic_index_in_dim(base_slots, my_index, 0, keepdims=False)
    slot_index = jnp.sum(matches * my_bases[None, :], axis=1, dtype=jnp.int32) + rank_in
    cell_index = ranked_expert * send_most + rank_in
    inverse_order = (
        jnp.zeros((pair_count,), jnp.int32)
        .at[order_row]
        .set(jnp.arange(pair_count, dtype=jnp.int32))
    )
    pair_cell = cell_index[inverse_order].reshape(tokens, route_count)
    pair_keep = (
        (slot_index[inverse_order] < capacity).astype(jnp.float32).reshape(tokens, route_count)
    )
    cell_pair = jnp.zeros((expert_count * send_most,), jnp.int32).at[cell_index].set(order_row)
    cell_live = (jnp.arange(send_most, dtype=jnp.int32)[None, :] < counts[:, None]).reshape(
        expert_count * send_most
    )
    cell_token = cell_pair // route_count
    outgoing = jnp.where(cell_live[:, None], ffn_low[cell_token], 0).reshape(
        expert_count, send_most, model_width
    )
    arrived = lax.all_to_all(outgoing, "shard", split_axis=0, concat_axis=1, tiled=True)
    own_counts = lax.dynamic_slice_in_dim(all_counts, my_index * local_experts, local_experts, 1).T
    own_bases = lax.dynamic_slice_in_dim(base_slots, my_index * local_experts, local_experts, 1).T
    slot_ids = jnp.arange(capacity, dtype=jnp.int32)
    slot_ends = own_bases + own_counts
    source_ids = jnp.sum(
        (slot_ends[:, None, :] <= slot_ids[None, :, None]).astype(jnp.int32),
        axis=2,
        dtype=jnp.int32,
    )
    slot_filled = source_ids < group_count
    source_safe = jnp.minimum(source_ids, group_count - 1)
    slot_rows = (
        source_safe * send_most
        + slot_ids[None, :]
        - jnp.take_along_axis(own_bases, source_safe, axis=1)
    )
    slot_rows = jnp.where(slot_filled, slot_rows, 0)
    expert_in = jnp.where(slot_filled[..., None], pick_rows(arrived, slot_rows), 0)
    gate_pre = jnp.einsum(
        "ecd,edf->ecf", expert_in, gate_weight, preferred_element_type=jnp.float32
    )
    up_pre = jnp.einsum("ecd,edf->ecf", expert_in, up_weight, preferred_element_type=jnp.float32)
    activated, swiglu_back = jax.vjp(swiglu, gate_pre, up_pre)
    act_low = activated.astype(jnp.bfloat16)
    expert_out = jnp.einsum(
        "ecf,efd->ecd", act_low, down_weight, preferred_element_type=jnp.float32
    ).astype(jnp.bfloat16)
    cell_positions = jnp.arange(send_most, dtype=jnp.int32)
    cell_slot = own_bases[:, :, None] + cell_positions[None, None, :]
    cell_used = (cell_positions[None, None, :] < own_counts[:, :, None]) & (cell_slot < capacity)
    cell_slot = jnp.where(cell_used, cell_slot, 0).reshape(local_experts, group_count * send_most)
    cell_used = cell_used.reshape(local_experts, group_count * send_most)
    returning = jnp.where(cell_used[..., None], pick_rows(expert_out, cell_slot), 0)
    returned = lax.all_to_all(returning, "shard", split_axis=1, concat_axis=0, tiled=True).reshape(
        expert_count * send_most, model_width
    )
    pair_rows = returned[pair_cell].astype(jnp.float32)
    pair_weight = jnp.take_along_axis(router_probs, routes, axis=1) * pair_keep
    outputs = (residual + jnp.sum(pair_weight[..., None] * pair_rows, axis=1)).astype(jnp.bfloat16)
    cotangent = grad_out.astype(jnp.float32)
    grad_rows = (
        (pair_weight[..., None] * cotangent[:, None, :])
        .astype(jnp.bfloat16)
        .reshape(pair_count, model_width)
    )
    grad_pair_weight = jnp.sum(pair_rows * cotangent[:, None, :], axis=2) * pair_keep
    route_hits = (routes[..., None] == labels[None, None, :]).astype(jnp.float32)
    grad_router_probs = jnp.sum(grad_pair_weight[..., None] * route_hits, axis=1)
    (grad_logits,) = router_back(grad_router_probs)
    grad_logits_low = grad_logits.astype(jnp.bfloat16)
    outgoing_grad = jnp.where(cell_live[:, None], grad_rows[cell_pair], 0).reshape(
        expert_count, send_most, model_width
    )
    arrived_grad = lax.all_to_all(outgoing_grad, "shard", split_axis=0, concat_axis=1, tiled=True)
    grad_expert_out = jnp.where(slot_filled[..., None], pick_rows(arrived_grad, slot_rows), 0)
    grad_act = jnp.einsum(
        "ecd,efd->ecf", grad_expert_out, down_weight, preferred_element_type=jnp.float32
    )
    grad_down = jnp.einsum(
        "ecf,ecd->efd", act_low, grad_expert_out, preferred_element_type=jnp.float32
    )
    grad_gate_pre, grad_up_pre = swiglu_back(grad_act)
    gate_grad_low = grad_gate_pre.astype(jnp.bfloat16)
    up_grad_low = grad_up_pre.astype(jnp.bfloat16)
    grad_gate = jnp.einsum(
        "ecd,ecf->edf", expert_in, gate_grad_low, preferred_element_type=jnp.float32
    )
    grad_up = jnp.einsum("ecd,ecf->edf", expert_in, up_grad_low, preferred_element_type=jnp.float32)
    grad_expert_in = (
        jnp.einsum("ecf,edf->ecd", gate_grad_low, gate_weight, preferred_element_type=jnp.float32)
        + jnp.einsum("ecf,edf->ecd", up_grad_low, up_weight, preferred_element_type=jnp.float32)
    ).astype(jnp.bfloat16)
    returning_grad = jnp.where(cell_used[..., None], pick_rows(grad_expert_in, cell_slot), 0)
    returned_grad = lax.all_to_all(
        returning_grad, "shard", split_axis=1, concat_axis=0, tiled=True
    ).reshape(expert_count * send_most, model_width)
    grad_ffn_in = jnp.sum(returned_grad[pair_cell].astype(jnp.float32), axis=1) + contract_cols(
        grad_logits_low, router_full
    )
    grad_router_local = contract_rows(ffn_low, grad_logits_low)
    grad_residual_norm, grad_ffn_local = ffn_norm_back(grad_ffn_in)
    grad_residual = cotangent + grad_residual_norm
    residual_low = grad_residual.astype(jnp.bfloat16)
    grad_out_local = lax.psum_scatter(
        contract_rows(attended, residual_low).astype(jnp.bfloat16),
        "shard",
        scatter_dimension=0,
        tiled=True,
    )
    grad_attended = contract_cols(
        residual_low, lax.all_gather(out_proj, "shard", axis=0, tiled=True)
    )
    grad_mixed = grad_attended.astype(jnp.bfloat16).reshape(tokens, HEADS, HEAD_DIM)
    scores_again = masked_scores(query_low, key_low)
    probs_again = jnp.exp(scores_again - log_total)
    grad_probs = jnp.einsum(
        "qhd,khd->hqk", grad_mixed, value_low, preferred_element_type=jnp.float32
    )
    spread = jnp.sum(probs_again * grad_probs, axis=-1, keepdims=True)
    grad_scores = (probs_again * (grad_probs - spread)).astype(jnp.bfloat16)
    grad_query = (
        jnp.einsum("hqk,khd->qhd", grad_scores, key_low, preferred_element_type=jnp.float32)
        * score_scale
    )
    grad_key = (
        jnp.einsum("hqk,qhd->khd", grad_scores, query_low, preferred_element_type=jnp.float32)
        * score_scale
    )
    grad_value = jnp.einsum(
        "hqk,qhd->khd",
        probs_again.astype(jnp.bfloat16),
        grad_mixed,
        preferred_element_type=jnp.float32,
    )
    grad_raw_query, grad_raw_key, grad_query_local, grad_key_local = query_key_back(
        (grad_query, grad_key)
    )
    grad_qkv = jnp.concatenate(
        [grad_raw_query, grad_raw_key, grad_value.reshape(tokens, model_width)], axis=1
    ).astype(jnp.bfloat16)
    grad_in_local = lax.psum_scatter(
        contract_rows(normed_low, grad_qkv).astype(jnp.bfloat16),
        "shard",
        scatter_dimension=0,
        tiled=True,
    )
    grad_normed = contract_cols(grad_qkv, lax.all_gather(in_proj, "shard", axis=0, tiled=True))
    grad_hidden_norm, grad_attn_local = attn_norm_back(grad_normed)
    grad_inputs = (grad_residual + grad_hidden_norm).astype(jnp.bfloat16)
    small_parts = (
        lax.psum_scatter(
            grad_attn_local.astype(jnp.bfloat16), "shard", scatter_dimension=0, tiled=True
        ).astype(jnp.float32),
        lax.psum_scatter(
            grad_query_local.astype(jnp.bfloat16), "shard", scatter_dimension=0, tiled=True
        ).astype(jnp.float32),
        lax.psum_scatter(
            grad_key_local.astype(jnp.bfloat16), "shard", scatter_dimension=0, tiled=True
        ).astype(jnp.float32),
        lax.psum_scatter(
            grad_ffn_local.astype(jnp.bfloat16), "shard", scatter_dimension=0, tiled=True
        ).astype(jnp.float32),
        lax.psum_scatter(
            grad_router_local.astype(jnp.bfloat16), "shard", scatter_dimension=0, tiled=True
        ).astype(jnp.float32),
    )
    summed = (
        lax.psum(grad_in_local, "rep").astype(jnp.float32),
        lax.psum(grad_out_local, "rep").astype(jnp.float32),
        lax.psum(small_parts[0].astype(jnp.bfloat16), "rep").astype(jnp.float32),
        lax.psum(small_parts[1].astype(jnp.bfloat16), "rep").astype(jnp.float32),
        lax.psum(small_parts[2].astype(jnp.bfloat16), "rep").astype(jnp.float32),
        lax.psum(small_parts[3].astype(jnp.bfloat16), "rep").astype(jnp.float32),
        lax.psum(small_parts[4].astype(jnp.bfloat16), "rep").astype(jnp.float32),
        lax.psum(grad_gate.astype(jnp.bfloat16), "rep").astype(jnp.float32),
        lax.psum(grad_up.astype(jnp.bfloat16), "rep").astype(jnp.float32),
        lax.psum(grad_down.astype(jnp.bfloat16), "rep").astype(jnp.float32),
    )
    return (
        outputs,
        grad_inputs,
        summed[2],
        summed[0],
        summed[3],
        summed[4],
        summed[1],
        summed[5],
        summed[6],
        summed[7],
        summed[8],
        summed[9],
    )


AXES = ("rep", "shard")
LINE = 4
SHARDS = 8
REPS = 4


def pairs_of(target):
    moves = []
    for rep in range(REPS):
        for shard in range(SHARDS):
            there = target(rep, shard)
            moves.append((rep * SHARDS + shard, there[0] * SHARDS + there[1]))
    return moves


CORE_SWAP = pairs_of(lambda rep, shard: (rep ^ 1, shard))
X_SWAP = pairs_of(lambda rep, shard: (rep ^ 2, shard))
Y_SWAP = pairs_of(lambda rep, shard: (rep, shard ^ 1))
SHARD_SWAP = [
    pairs_of(lambda rep, shard: (rep, shard ^ 1)),
    pairs_of(lambda rep, shard: (rep, shard ^ 2)),
    pairs_of(lambda rep, shard: (rep, shard ^ 4)),
]
Z_FROM = [pairs_of(lambda rep, shard: (rep, (shard - 2 * k) % SHARDS)) for k in range(LINE)]
Z_TO = [pairs_of(lambda rep, shard: (rep, (shard + 2 * k) % SHARDS)) for k in range(LINE)]


def move(values, moves):
    return lax.ppermute(values, AXES, moves)


def after(values, *others):
    return lax.optimization_barrier((values,) + others)[0]


def gather_small(values, hold):
    low = jnp.stack([values, move(values, SHARD_SWAP[1])])
    high = jnp.stack([low, move(after(low, *hold), SHARD_SWAP[2])])
    last = move(high, SHARD_SWAP[0])
    both = jnp.stack([high, last], axis=2)
    return both.reshape((SHARDS,) + values.shape), last


def gather_rows(values, early=(), late=None, fill=None, first=()):
    moved = {k: move(values, Z_FROM[k]) for k in (1, 3)}
    moved[2] = move(after(values, moved[1], *first), Z_FROM[2])
    mine, beside = {0: values}, {0: move(values, Y_SWAP)}
    for k in (1, 3, 2):
        mine[k] = after(moved[k], *early) if early else moved[k]
        if k == 2 and fill is not None:
            mine[k] = after(mine[k], *fill(mine[3]))
        beside[k] = move(mine[k], Y_SWAP)
    if late is not None:
        beside = {k: after(beside[k], *late()) for k in beside}
    return [(mine[k], beside[k]) for k in range(LINE)]


def flat(pieces):
    return jnp.concatenate([piece for pair in pieces for piece in pair], axis=0)


def added(first, *others):
    total = first.astype(jnp.float32)
    for other in others:
        total = total + other.astype(jnp.float32)
    return total.astype(first.dtype)


def scatter_rows(parts, fills, hold=False):
    away = {k: added(*[part(2 * k + 1) for part in parts]) for k in (2, 1, 3, 0)}
    moved = {2: move(away[2], Y_SWAP)}
    arrived, reduced = [], away[2]
    for k, fill in zip((2, 1, 3, 0), fills):
        filled = [] if fill is None else fill((reduced,))
        if k == 2:
            for other in (1, 3, 0):
                held = after(away[other], *filled) if hold else away[other]
                moved[other] = move(held, Y_SWAP)
        here = after(moved[k], *filled) if filled else moved[k]
        reduced = added(here, *[part(2 * k) for part in parts])
        if k > 0:
            arrived.append(move(reduced, Z_TO[k]))
    if fills[4] is not None:
        reduced, *arrived = fills[4]((reduced, *arrived))
    return added(reduced, *arrived)


LIMIT = 56 * 2**20
HIDDEN_BLOCK = 256
WIDTH_BLOCK = 512
QUIET = pl.CostEstimate(flops=0, bytes_accessed=0, transcendentals=0)
LOUD = pl.CostEstimate(flops=10**11, bytes_accessed=0, transcendentals=0)


def ordered(kernel, behind):
    def body(scalar_ref, *refs):
        return kernel(scalar_ref, *refs[behind:])

    return body


HELD = pl.BlockSpec(memory_space=pl.ANY)


def copy_block(order_ref, from_ref, into_ref):
    into_ref[...] = from_ref[...]


def pick_columns(values, order, block):
    rows = values.shape[0]
    picks = order.shape[0]
    return pl.pallas_call(
        copy_block,
        grid_spec=pltpu.PrefetchScalarGridSpec(
            num_scalar_prefetch=1,
            grid=(picks,),
            in_specs=[pl.BlockSpec((rows, block), lambda i, order: (0, order[i]))],
            out_specs=pl.BlockSpec((rows, block), lambda i, order: (0, i)),
        ),
        out_shape=jax.ShapeDtypeStruct((rows, picks * block), values.dtype),
        compiler_params=pltpu.CompilerParams(vmem_limit_bytes=32 * 2**20),
    )(order, values)


def thin_kernel(rep_ref, from_ref, into_ref):
    heads = into_ref.shape[1] // HEAD_DIM

    def take(parity):
        for head in range(heads):
            start = (2 * head + parity) * HEAD_DIM
            into_ref[:, head * HEAD_DIM : (head + 1) * HEAD_DIM] = from_ref[
                :, start : start + HEAD_DIM
            ]

    @pl.when(rep_ref[0] < 2)
    def _():
        take(0)

    @pl.when(rep_ref[0] >= 2)
    def _():
        take(1)


def thin_columns(weights, rep, width):
    rows = weights.shape[0]
    return pl.pallas_call(
        thin_kernel,
        grid_spec=pltpu.PrefetchScalarGridSpec(
            num_scalar_prefetch=1,
            grid=(3,),
            in_specs=[
                pl.BlockSpec((rows, width // 2), lambda i, rep: (0, 2 * i + lax.rem(rep[0], 2)))
            ],
            out_specs=pl.BlockSpec((rows, width // 4), lambda i, rep: (0, i)),
        ),
        out_shape=jax.ShapeDtypeStruct((rows, 3 * width // 4), weights.dtype),
        compiler_params=pltpu.CompilerParams(vmem_limit_bytes=32 * 2**20),
    )(rep, weights)


def weave_kernel(rep_ref, even_ref, odd_ref, into_ref):
    for head in range(even_ref.shape[2] // HEAD_DIM):
        part = slice(head * HEAD_DIM, (head + 1) * HEAD_DIM)
        start = 2 * head * HEAD_DIM
        into_ref[:, start : start + HEAD_DIM] = even_ref[0, :, part].astype(jnp.float32)
        into_ref[:, start + HEAD_DIM : start + 2 * HEAD_DIM] = odd_ref[0, :, part].astype(
            jnp.float32
        )


def weave_columns(pieces, rep, columns, behind):
    rows = pieces.shape[1]
    block = columns // 3
    return pl.pallas_call(
        ordered(weave_kernel, len(behind)),
        grid_spec=pltpu.PrefetchScalarGridSpec(
            num_scalar_prefetch=1,
            grid=(3, 2),
            in_specs=[HELD] * len(behind)
            + [
                pl.BlockSpec((1, rows, block), lambda i, j, rep: (j ^ rep[0], 0, i)),
                pl.BlockSpec((1, rows, block), lambda i, j, rep: ((j + 2) ^ rep[0], 0, i)),
            ],
            out_specs=pl.BlockSpec((rows, 2 * block), lambda i, j, rep: (0, 2 * i + j)),
        ),
        out_shape=jax.ShapeDtypeStruct((rows, 4 * columns), jnp.float32),
        compiler_params=pltpu.CompilerParams(vmem_limit_bytes=32 * 2**20),
    )(rep, *behind, pieces, pieces)


def widen_kernel(core_ref, own_ref, other_ref, into_ref):
    mine = pl.program_id(0) == core_ref[0]

    @pl.when(mine)
    def _():
        into_ref[...] = own_ref[...].astype(jnp.float32)

    @pl.when(jnp.logical_not(mine))
    def _():
        into_ref[...] = other_ref[...].astype(jnp.float32)


def widen(own, other, core, behind=()):
    experts, rows, columns = own.shape
    block = rows // 4
    steps = experts * 4

    def place(hold, core, i, j):
        return jnp.where(i == hold, j, jnp.where(hold == 0, steps - 1, 0))

    own_map = lambda i, j, core: (place(core[0], core, i, j), 0)
    other_map = lambda i, j, core: (place(1 - core[0], core, i, j), 0)
    result = pl.pallas_call(
        ordered(widen_kernel, len(behind)),
        grid_spec=pltpu.PrefetchScalarGridSpec(
            num_scalar_prefetch=1,
            grid=(2, steps),
            in_specs=[HELD] * len(behind)
            + [
                pl.BlockSpec((block, columns), own_map),
                pl.BlockSpec((block, columns), other_map),
            ],
            out_specs=pl.BlockSpec((block, columns), lambda i, j, core: (i * steps + j, 0)),
        ),
        out_shape=jax.ShapeDtypeStruct((2 * experts * rows, columns), jnp.float32),
        compiler_params=pltpu.CompilerParams(vmem_limit_bytes=32 * 2**20),
        cost_estimate=QUIET,
    )(
        core,
        *behind,
        own.reshape(experts * rows, columns),
        other.reshape(experts * rows, columns),
    )
    return result.reshape(2 * experts, rows, columns)


def slot_rows(slots, capacity):
    places = lax.broadcasted_iota(jnp.int32, (capacity, slots.shape[1]), 0)
    return jnp.where(places == slots, 1.0, 0.0).astype(jnp.bfloat16)


def slot_columns(slots, columns):
    places = lax.broadcasted_iota(jnp.int32, (slots.shape[0], columns), 1)
    found = places == slots[:, 0:1]
    for expert in range(1, slots.shape[1]):
        found = found | (places == slots[:, expert : expert + 1])
    return jnp.where(found, 1.0, 0.0).astype(jnp.bfloat16)


def dot_wide(left, right):
    return jnp.dot(left, right, preferred_element_type=jnp.float32)


def pick_rows_into(slots_ref, rows_ref, into_ref):
    choice = slot_rows(slots_ref[0], into_ref.shape[1])
    for start in range(0, rows_ref.shape[1], WIDTH_BLOCK):
        part = slice(start, start + WIDTH_BLOCK)
        into_ref[0, :, part] = dot_wide(choice, rows_ref[:, part]).astype(jnp.bfloat16)


def cotangent_kernel(core_ref, slots_ref, rows_ref, down_ref, picked_ref, slot_ref):
    @pl.when(pl.program_id(1) == 0)
    def _():
        pick_rows_into(slots_ref, rows_ref, picked_ref)

    slot_ref[0] = contract_cols(picked_ref[0], down_ref[0])


def cotangent_part(core, slots, rows, down_weight, capacity, behind=()):
    experts, tokens = slots.shape
    width, hidden = rows.shape[1], down_weight.shape[1]
    return pl.pallas_call(
        ordered(cotangent_kernel, len(behind)),
        grid_spec=pltpu.PrefetchScalarGridSpec(
            num_scalar_prefetch=1,
            grid=(experts, hidden // HIDDEN_BLOCK),
            in_specs=[HELD] * len(behind)
            + [
                pl.BlockSpec((1, 1, tokens), lambda e, n, core: (e, 0, 0)),
                pl.BlockSpec((tokens, width), lambda e, n, core: (0, 0)),
                pl.BlockSpec(
                    (1, HIDDEN_BLOCK, width), lambda e, n, core: (core[0] * experts + e, n, 0)
                ),
            ],
            out_specs=[
                pl.BlockSpec((1, capacity, width), lambda e, n, core: (e, 0, 0)),
                pl.BlockSpec((1, capacity, HIDDEN_BLOCK), lambda e, n, core: (e, 0, n)),
            ],
        ),
        out_shape=[
            jax.ShapeDtypeStruct((experts, capacity, width), jnp.bfloat16),
            jax.ShapeDtypeStruct((experts, capacity, hidden), jnp.float32),
        ],
        compiler_params=pltpu.CompilerParams(vmem_limit_bytes=LIMIT),
        cost_estimate=LOUD,
    )(core, *behind, slots[:, None, :], rows, down_weight)


def forward_kernel(
    first_ref,
    slots_ref,
    rows_ref,
    router_ref,
    gate_ref,
    up_ref,
    slot_ref,
    picked_ref,
    act_ref,
    grad_gate_ref,
    grad_up_ref,
    score_ref,
    weight_ref,
    total_ref,
):
    step = pl.program_id(1)
    mine = first_ref[1] + pl.program_id(0)

    @pl.when(step == 0)
    def _():
        pick_rows_into(slots_ref, rows_ref, picked_ref)
        logits = contract_cols(picked_ref[0], router_ref[...])
        raised = jnp.exp(logits - jnp.max(logits, axis=1, keepdims=True))
        label = lax.broadcasted_iota(jnp.int32, raised.shape, 1)
        own = jnp.sum(jnp.where(label == mine, raised, 0.0), axis=1, keepdims=True)
        weight_ref[...] = own / jnp.sum(raised, axis=1, keepdims=True)
        total_ref[...] = jnp.zeros_like(total_ref)

    gate_pre = dot_wide(picked_ref[0], gate_ref[0])
    up_pre = dot_wide(picked_ref[0], up_ref[0])
    sigmoid = 1.0 / (1.0 + jnp.exp(-gate_pre))
    smooth = gate_pre * sigmoid
    grad_act = weight_ref[...] * slot_ref[0]
    act = smooth * up_pre
    act_ref[0] = (weight_ref[...] * act).astype(jnp.bfloat16)
    grad_gate_ref[0] = (grad_act * up_pre * (sigmoid + smooth * (1.0 - sigmoid))).astype(
        jnp.bfloat16
    )
    grad_up_ref[0] = (grad_act * smooth).astype(jnp.bfloat16)
    total_ref[...] += jnp.sum(act * grad_act, axis=1, keepdims=True)

    @pl.when(step == pl.num_programs(1) - 1)
    def _():
        label = lax.broadcasted_iota(jnp.int32, score_ref.shape[1:], 1)
        score_ref[0] = jnp.where(label == mine, total_ref[...], 0.0).astype(jnp.bfloat16)


def forward_part(first, slots, rows, router_rows, gate_weight, up_weight, slot_cot, behind=(), cost=QUIET):
    experts, tokens = slots.shape
    capacity, hidden = slot_cot.shape[1:]
    width = rows.shape[1]
    labels = router_rows.shape[0]
    weight_spec = pl.BlockSpec(
        (1, width, HIDDEN_BLOCK), lambda e, n, first: (first[0] * experts + e, 0, n)
    )
    hidden_spec = pl.BlockSpec((1, capacity, HIDDEN_BLOCK), lambda e, n, first: (e, 0, n))
    hidden_shape = jax.ShapeDtypeStruct((experts, capacity, hidden), jnp.bfloat16)
    return pl.pallas_call(
        ordered(forward_kernel, len(behind)),
        grid_spec=pltpu.PrefetchScalarGridSpec(
            num_scalar_prefetch=1,
            grid=(experts, hidden // HIDDEN_BLOCK),
            in_specs=[HELD] * len(behind)
            + [
                pl.BlockSpec((1, 1, tokens), lambda e, n, first: (e, 0, 0)),
                pl.BlockSpec((tokens, width), lambda e, n, first: (0, 0)),
                pl.BlockSpec((labels, width), lambda e, n, first: (0, 0)),
                weight_spec,
                weight_spec,
                hidden_spec,
            ],
            out_specs=[
                pl.BlockSpec((1, capacity, width), lambda e, n, first: (e, 0, 0)),
                hidden_spec,
                hidden_spec,
                hidden_spec,
                pl.BlockSpec((1, capacity, HEAD_DIM), lambda e, n, first: (e, 0, 0)),
            ],
            scratch_shapes=[
                pltpu.VMEM((capacity, 1), jnp.float32),
                pltpu.VMEM((capacity, 1), jnp.float32),
            ],
        ),
        out_shape=[
            jax.ShapeDtypeStruct((experts, capacity, width), jnp.bfloat16),
            hidden_shape,
            hidden_shape,
            hidden_shape,
            jax.ShapeDtypeStruct((experts, capacity, HEAD_DIM), jnp.bfloat16),
        ],
        compiler_params=pltpu.CompilerParams(vmem_limit_bytes=LIMIT),
        cost_estimate=cost,
    )(first, *behind, slots[:, None, :], rows, router_rows, gate_weight, up_weight, slot_cot)


def backward_kernel(
    core_ref, slots_ref, grad_gate_ref, grad_up_ref, score_ref, *rest
):
    experts, capacity, _ = grad_gate_ref.shape
    gates, ups = rest[:experts], rest[experts : 2 * experts]
    into_ref, spread_ref, slot_ref = rest[2 * experts :]
    step = pl.program_id(0)
    width = pl.num_programs(0) * WIDTH_BLOCK

    @pl.when(step == 0)
    def _():
        spread_ref[...] = slot_columns(slots_ref[...], experts * capacity)
        scores = score_ref[...].reshape(experts * capacity, HEAD_DIM)
        into_ref[:, width:] = dot_wide(spread_ref[...], scores).astype(jnp.bfloat16)

    for expert in range(experts):
        rows = contract_cols(grad_gate_ref[expert], gates[expert][0]) + contract_cols(
            grad_up_ref[expert], ups[expert][0]
        )
        slot_ref[expert * capacity : (expert + 1) * capacity, :] = rows.astype(jnp.bfloat16)
    start = pl.multiple_of(step * WIDTH_BLOCK, WIDTH_BLOCK)
    into_ref[:, pl.ds(start, WIDTH_BLOCK)] = dot_wide(spread_ref[...], slot_ref[...]).astype(
        jnp.bfloat16
    )


def backward_part(core, columns, grad_gate, grad_up, scores, gate_weight, up_weight, behind=()):
    experts, capacity, hidden = grad_gate.shape
    tokens, width = columns.shape[0], gate_weight.shape[1]

    def weight_spec(expert):
        return pl.BlockSpec(
            (1, WIDTH_BLOCK, hidden), lambda n, core: (core[0] * experts + expert, n, 0)
        )

    whole = pl.BlockSpec((experts, capacity, hidden), lambda n, core: (0, 0, 0))
    return pl.pallas_call(
        ordered(backward_kernel, len(behind)),
        grid_spec=pltpu.PrefetchScalarGridSpec(
            num_scalar_prefetch=1,
            grid=(width // WIDTH_BLOCK,),
            in_specs=[HELD] * len(behind)
            + [
                pl.BlockSpec(columns.shape, lambda n, core: (0, 0)),
                whole,
                whole,
                pl.BlockSpec((experts, capacity, HEAD_DIM), lambda n, core: (0, 0, 0)),
            ]
            + [weight_spec(expert) for expert in range(experts)] * 2,
            out_specs=pl.BlockSpec((tokens, width + HEAD_DIM), lambda n, core: (0, 0)),
            scratch_shapes=[
                pltpu.VMEM((tokens, experts * capacity), jnp.bfloat16),
                pltpu.VMEM((experts * capacity, WIDTH_BLOCK), jnp.bfloat16),
            ],
        ),
        out_shape=jax.ShapeDtypeStruct((tokens, width + HEAD_DIM), jnp.bfloat16),
        compiler_params=pltpu.CompilerParams(vmem_limit_bytes=LIMIT),
        cost_estimate=QUIET,
    )(
        core,
        *behind,
        columns,
        grad_gate,
        grad_up,
        scores,
        *[gate_weight] * experts,
        *[up_weight] * experts,
    )


def routed_kernel(more, core_ref, slots_ref, act_ref, *rest):
    experts, capacity, _ = act_ref.shape
    downs = rest[:experts]
    into_ref, spread_ref, slot_ref = rest[experts + more :]

    @pl.when(pl.program_id(0) == 0)
    def _():
        spread_ref[...] = slot_columns(slots_ref[...], experts * capacity)

    for expert in range(experts):
        rows = dot_wide(act_ref[expert], downs[expert][0])
        slot_ref[expert * capacity : (expert + 1) * capacity, :] = rows.astype(jnp.bfloat16)
    total = dot_wide(spread_ref[...], slot_ref[...])
    for extra in rest[experts : experts + more]:
        total += extra[...].astype(jnp.float32)
    into_ref[...] = total.astype(jnp.bfloat16)


def routed_part(core, columns, act, down_weight, extra=(), behind=()):
    experts, capacity, hidden = act.shape
    tokens, width = columns.shape[0], down_weight.shape[2]

    def weight_spec(expert):
        return pl.BlockSpec(
            (1, hidden, WIDTH_BLOCK), lambda n, core: (core[0] * experts + expert, 0, n)
        )

    rows_spec = pl.BlockSpec((tokens, WIDTH_BLOCK), lambda n, core: (0, n))
    return pl.pallas_call(
        ordered(functools.partial(routed_kernel, len(extra)), len(behind)),
        grid_spec=pltpu.PrefetchScalarGridSpec(
            num_scalar_prefetch=1,
            grid=(width // WIDTH_BLOCK,),
            in_specs=[HELD] * len(behind)
            + [
                pl.BlockSpec(columns.shape, lambda n, core: (0, 0)),
                pl.BlockSpec((experts, capacity, hidden), lambda n, core: (0, 0, 0)),
            ]
            + [weight_spec(expert) for expert in range(experts)]
            + [rows_spec] * len(extra),
            out_specs=rows_spec,
            scratch_shapes=[
                pltpu.VMEM((tokens, experts * capacity), jnp.bfloat16),
                pltpu.VMEM((experts * capacity, WIDTH_BLOCK), jnp.bfloat16),
            ],
        ),
        out_shape=jax.ShapeDtypeStruct((tokens, width), jnp.bfloat16),
        compiler_params=pltpu.CompilerParams(vmem_limit_bytes=LIMIT),
        cost_estimate=LOUD,
    )(core, *behind, columns, act, *[down_weight] * experts, *extra)


def roll_half(values):
    return pltpu.roll(values, HEAD_DIM // 2, 1)


def head_parts(raw_ref, rate_ref, gain_ref, cos_ref, sin_ref, head):
    part_width = gain_ref.shape[1]
    units, turned = [], []
    for which in range(2):
        start = which * part_width + head * HEAD_DIM
        unit = raw_ref[:, start : start + HEAD_DIM] * rate_ref[:, which : which + 1]
        gain = gain_ref[which : which + 1, head * HEAD_DIM : (head + 1) * HEAD_DIM]
        scaled = unit * gain
        units.append((unit, gain))
        turned.append(
            (scaled * cos_ref[...] + roll_half(scaled) * sin_ref[...]).astype(jnp.bfloat16)
        )
    start = 2 * part_width + head * HEAD_DIM
    value = raw_ref[:, start : start + HEAD_DIM].astype(jnp.bfloat16)
    return units, turned, value


def head_probs(turned, column_ref, row_ref):
    scores = contract_cols(turned[0], turned[1]) * HEAD_DIM ** (-0.5)
    length = scores.shape[0]
    reader = lax.broadcasted_iota(jnp.int32, (length, length), 0)
    source = lax.broadcasted_iota(jnp.int32, (length, length), 1)
    allowed = (column_ref[...] == row_ref[0]) & (source <= reader)
    scores = jnp.where(allowed, scores, masked_score)
    raised = jnp.exp(scores - jnp.max(scores, axis=1, keepdims=True))
    return raised / jnp.sum(raised, axis=1, keepdims=True)


def attend_kernel(raw_ref, rate_ref, gain_ref, cos_ref, sin_ref, column_ref, row_ref, into_ref):
    for head in range(gain_ref.shape[1] // HEAD_DIM):
        _, turned, value = head_parts(raw_ref, rate_ref, gain_ref, cos_ref, sin_ref, head)
        probs = head_probs(turned, column_ref, row_ref).astype(jnp.bfloat16)
        into_ref[:, head * HEAD_DIM : (head + 1) * HEAD_DIM] = dot_wide(probs, value).astype(
            jnp.bfloat16
        )


def attend_back_kernel(
    raw_ref,
    rate_ref,
    gain_ref,
    cos_ref,
    sin_ref,
    column_ref,
    row_ref,
    grad_ref,
    pair_ref,
    value_ref,
    dots_ref,
    gains_ref,
):
    score_scale = HEAD_DIM ** (-0.5)
    part_width = gain_ref.shape[1]
    dots = [0.0, 0.0]
    for head in range(part_width // HEAD_DIM):
        units, turned, value = head_parts(raw_ref, rate_ref, gain_ref, cos_ref, sin_ref, head)
        probs = head_probs(turned, column_ref, row_ref)
        here = slice(head * HEAD_DIM, (head + 1) * HEAD_DIM)
        grad = grad_ref[:, here]
        grad_probs = contract_cols(grad, value)
        mean_grad = jnp.sum(probs * grad_probs, axis=1, keepdims=True)
        grad_scores = (probs * (grad_probs - mean_grad)).astype(jnp.bfloat16)
        value_ref[:, here] = contract_rows(probs.astype(jnp.bfloat16), grad).astype(jnp.bfloat16)
        grads = (
            dot_wide(grad_scores, turned[1]) * score_scale,
            contract_rows(grad_scores, turned[0]) * score_scale,
        )
        for which in range(2):
            unit, gain = units[which]
            back = grads[which] * cos_ref[...] + roll_half(grads[which] * sin_ref[...])
            gains_ref[0, which : which + 1, here] = jnp.sum(back * unit, axis=0, keepdims=True)
            back = back * gain
            start = which * part_width + head * HEAD_DIM
            pair_ref[:, start : start + HEAD_DIM] = back
            dots[which] += jnp.sum(back * unit, axis=1, keepdims=True)
    dots_ref[:, 0:1] = dots[0]
    dots_ref[:, 1:2] = dots[1]


def join_kernel(raw_ref, rate_ref, pair_ref, value_ref, dots_ref, into_ref):
    part_width = value_ref.shape[1]
    for which in range(2):
        here = slice(which * part_width, (which + 1) * part_width)
        rate = rate_ref[:, which : which + 1]
        shift = dots_ref[:, which : which + 1] * rate
        into_ref[:, here] = (rate * (pair_ref[:, here] - raw_ref[:, here] * shift)).astype(
            jnp.bfloat16
        )
    into_ref[:, 2 * part_width :] = value_ref[...]


def row_blocks(count, *arrays):
    return [pl.BlockSpec((array.shape[0] // count, array.shape[1]), lambda i: (i, 0)) for array in arrays]


def attention_specs(raw, rate, gains, cos_table, sin_table, columns, rows):
    count = rows.shape[0]
    return (
        row_blocks(count, raw, rate)
        + [pl.BlockSpec(gains.shape, lambda i: (0, 0))]
        + row_blocks(count, cos_table, sin_table, columns)
        + [pl.BlockSpec((1, 1, rows.shape[2]), lambda i: (i, 0, 0))]
    )


def attend(raw, rate, gains, cos_table, sin_table, columns, rows):
    count = rows.shape[0]
    operands = (raw, rate, gains, cos_table, sin_table, columns, rows)
    result = jax.ShapeDtypeStruct((raw.shape[0], gains.shape[1]), jnp.bfloat16)
    return pl.pallas_call(
        attend_kernel,
        grid=(count,),
        in_specs=attention_specs(*operands),
        out_specs=row_blocks(count, result)[0],
        out_shape=result,
        compiler_params=pltpu.CompilerParams(vmem_limit_bytes=LIMIT),
        cost_estimate=QUIET,
    )(*operands)


def attend_back(raw, rate, gains, cos_table, sin_table, columns, rows, grads, behind=()):
    count = rows.shape[0]
    operands = (raw, rate, gains, cos_table, sin_table, columns, rows)
    results = [
        jax.ShapeDtypeStruct((raw.shape[0], 2 * gains.shape[1]), jnp.float32),
        jax.ShapeDtypeStruct((raw.shape[0], gains.shape[1]), jnp.bfloat16),
        jax.ShapeDtypeStruct((raw.shape[0], 2), jnp.float32),
    ]
    gain_result = jax.ShapeDtypeStruct((count,) + gains.shape, jnp.float32)
    return pl.pallas_call(
        lambda *refs: attend_back_kernel(*refs[len(behind) :]),
        grid=(count,),
        in_specs=[HELD] * len(behind) + attention_specs(*operands) + row_blocks(count, grads),
        out_specs=row_blocks(count, *results)
        + [pl.BlockSpec((1,) + gains.shape, lambda i: (i, 0, 0))],
        out_shape=results + [gain_result],
        compiler_params=pltpu.CompilerParams(vmem_limit_bytes=LIMIT),
        cost_estimate=QUIET,
    )(*behind, *operands, grads)


def join_grads(raw, rate, pair, value, dots, count):
    operands = (raw, rate, pair, value, dots)
    result = jax.ShapeDtypeStruct(raw.shape, jnp.bfloat16)
    return pl.pallas_call(
        join_kernel,
        grid=(count,),
        in_specs=row_blocks(count, *operands),
        out_specs=row_blocks(count, result)[0],
        out_shape=result,
        compiler_params=pltpu.CompilerParams(vmem_limit_bytes=LIMIT),
        cost_estimate=QUIET,
    )(*operands)


def rep_sum(values):
    values = values + move(values, CORE_SWAP).reshape((2, 2) + values.shape[1:])[:, ::-1].reshape(
        values.shape
    )
    swapped = move(values, X_SWAP)
    return values + jnp.concatenate([swapped[2:], swapped[:2]], axis=0)


def fast_local(
    inputs,
    attn_gain,
    in_proj,
    query_gain,
    key_gain,
    out_proj,
    ffn_gain,
    router_weight,
    gate_weight,
    up_weight,
    down_weight,
    routes,
    priority,
    segments,
    grad_out,
):
    f32, bf16 = jnp.float32, jnp.bfloat16
    tokens, width = inputs.shape
    rows_each = in_proj.shape[0]
    local_experts, _, hidden_units = gate_weight.shape
    expert_count = local_experts * SHARDS
    route_count = routes.shape[1]
    pair_count = tokens * route_count
    capacity = 5 * pair_count * SHARDS // (4 * expert_count)
    core_experts = local_experts // 2
    heads = HEADS // REPS
    part_width = heads * HEAD_DIM
    group_rows = SHARDS * tokens
    rep, shard = lax.axis_index("rep"), lax.axis_index("shard")
    a, c = rep // 2, lax.rem(rep, 2)
    z, y = shard // 2, lax.rem(shard, 2)
    rep_ref = rep.astype(jnp.int32).reshape(1)
    core_ref = c.astype(jnp.int32).reshape(1)
    near_shards = lax.rem(z + jnp.arange(LINE, dtype=jnp.int32), LINE)[:, None] * 2 + (
        y ^ jnp.arange(2, dtype=jnp.int32)[None, :]
    )
    near_shards = near_shards.reshape(SHARDS)
    shard_ids = jnp.arange(SHARDS, dtype=jnp.int32)
    place_of_shard = jnp.sum(
        jnp.where(near_shards[None, :] == shard_ids[:, None], shard_ids[None, :], 0), axis=1
    )

    order_row = priority[0]
    pair_ids = jnp.arange(pair_count, dtype=jnp.int32)
    place_of = jnp.sum(
        jnp.where(order_row[None, :] == pair_ids[:, None], pair_ids[None, :], 0), axis=1
    ).reshape(tokens, route_count)
    labels = jnp.arange(expert_count, dtype=jnp.int32)
    hits = routes.T[None, :, :] == labels[:, None, None]
    place_at = jnp.sum(jnp.where(hits, place_of.T[None], 0), axis=1)
    named = jnp.any(hits, axis=1)
    place_at = jnp.where(named, place_at, pair_count)
    earlier = jnp.sum((place_at[:, None, :] < place_at[:, :, None]).astype(jnp.int32), axis=2)
    ranks = jnp.where(named, earlier, -1).astype(bf16)
    ranks = jnp.concatenate([ranks, segments.astype(bf16)], axis=0)
    ranks = jnp.pad(ranks, ((0, 0), (0, rows_each - tokens)))
    ranks = jnp.stack([ranks, move(ranks, CORE_SWAP)])
    ranks = jnp.concatenate([ranks, move(ranks, X_SWAP)])
    segment_rows = ranks[:, expert_count, :tokens].astype(jnp.int32)

    inputs_across = move(inputs, X_SWAP)
    small_in = jnp.stack([attn_gain, query_gain, key_gain, ffn_gain])
    small_in = jnp.concatenate(
        [small_in, router_weight.T, ranks.reshape(REPS * (expert_count + 1), rows_each)], axis=0
    )
    in_pieces = gather_rows(
        thin_columns(in_proj, rep_ref, width), first=(inputs_across, segment_rows)
    )
    small_in, small_last = gather_small(small_in, (in_pieces[2][0], in_pieces[1][1], in_pieces[3][1]))
    ranks = small_in[:, 4 + expert_count :, :tokens]
    ranks = jnp.take(ranks, near_shards ^ shard, axis=0)
    ranks = ranks.reshape(SHARDS, REPS, expert_count + 1, tokens)[:, :, :expert_count]
    in_part = flat(in_pieces)

    small_in = jnp.take(small_in[:, : 4 + expert_count], shard_ids ^ shard, axis=0)
    small_in = small_in.transpose(1, 0, 2).reshape(4 + expert_count, width)
    gains = small_in[:4].astype(f32)
    router_rows = small_in[4:]
    part_gains = lax.dynamic_slice(
        gains[1:3].reshape(2, HEADS // 2, 2, HEAD_DIM),
        (0, c * heads, a, 0),
        (2, heads, 1, HEAD_DIM),
    ).reshape(2, part_width)

    hidden = inputs.astype(f32)
    home_rate = lax.rsqrt(jnp.mean(hidden * hidden, axis=-1, keepdims=True) + norm_eps)
    inputs_all = jnp.stack([inputs, inputs_across])
    inputs_all = jnp.stack([inputs_all, move(inputs_all, CORE_SWAP)], axis=1)
    inputs_all = inputs_all.reshape(REPS * tokens, width)
    inputs_all = pick_columns(inputs_all, near_shards, rows_each).astype(f32)
    unit_all = inputs_all * lax.rsqrt(
        jnp.mean(inputs_all * inputs_all, axis=-1, keepdims=True) + norm_eps
    )
    near_gain = jnp.take(gains[0].reshape(SHARDS, rows_each), near_shards, axis=0).reshape(width)
    normed_low = (unit_all * near_gain).astype(bf16)
    cot_across = move(grad_out, X_SWAP)
    normed_low = after(normed_low, cot_across)
    cot_own = after(grad_out, in_part)
    cot_own = lax.all_gather(cot_own, "shard", tiled=True)
    cos_table, sin_table = jax.vmap(rotary_tables)(segment_rows)
    sin_table = jnp.where(jnp.arange(HEAD_DIM) < HEAD_DIM // 2, -sin_table, sin_table)
    cos_table = cos_table.reshape(REPS * tokens, HEAD_DIM)
    sin_table = sin_table.reshape(REPS * tokens, HEAD_DIM)

    out_rows = rows_each // 4
    out_own = lax.dynamic_slice_in_dim(out_proj, rep * out_rows, out_rows, 0)
    out_own = after(out_own, small_last)

    projected = jnp.dot(normed_low, in_part, preferred_element_type=f32)
    squares = jnp.stack(
        [
            jnp.sum(projected[:, k * part_width : (k + 1) * part_width] ** 2, axis=1)
            for k in range(2)
        ],
        axis=1,
    )
    squares = rep_sum(squares.reshape(REPS, tokens, 2)).reshape(REPS * tokens, 2)
    pair_rate = lax.rsqrt(squares / width + norm_eps)
    attention_operands = (
        projected,
        pair_rate,
        part_gains,
        cos_table,
        sin_table,
        segment_rows.reshape(REPS * tokens, 1),
        segment_rows[:, None, :],
    )
    attended = attend(*attention_operands).reshape(2, 2, tokens, part_width)
    out_pieces = gather_rows(out_own, early=(projected,), late=lambda: (attended,))
    out_own = flat(out_pieces).reshape(SHARDS, out_rows, width)
    out_other = move(out_own, CORE_SWAP)
    out_part = jnp.where(
        c == 0,
        jnp.concatenate([out_own, out_other], axis=1),
        jnp.concatenate([out_other, out_own], axis=1),
    ).reshape(SHARDS * 2 * out_rows, width)
    attended = jnp.concatenate([attended[:, 0], move(attended[:, 1], CORE_SWAP)], axis=2)
    attended = attended.reshape(2 * tokens, 2 * part_width)
    head_of_place = ((near_shards // heads) ^ c) * heads + lax.rem(near_shards, heads)
    place_of_head = jnp.sum(
        jnp.where(head_of_place[None, :] == shard_ids[:, None], shard_ids[None, :], 0), axis=1
    )
    attended = pick_columns(attended, head_of_place, HEAD_DIM)
    mixed = jnp.dot(attended, out_part, preferred_element_type=f32).reshape(2, tokens, width)
    mixed_across = move(mixed[1].astype(bf16), X_SWAP)
    residual = hidden + mixed[0] + mixed_across.astype(f32)

    ffn_rate = lax.rsqrt(jnp.mean(residual * residual, axis=-1, keepdims=True) + norm_eps)
    ffn_unit = residual * ffn_rate
    ffn_low = (ffn_unit * gains[3]).astype(bf16)
    router_probs = softmax_rows(contract_cols(ffn_low, router_rows))

    ranks = after(ranks, mixed_across).astype(jnp.int32)
    counts = jnp.sum((ranks >= 0).astype(jnp.int32), axis=3)
    before = (near_shards[None, :] < near_shards[:, None])[:, :, None, None]
    bases = jnp.sum(jnp.where(before, counts[None], 0), axis=1)
    slots = bases[..., None] + ranks
    slots = jnp.where((ranks >= 0) & (slots < capacity), slots, -1)
    first_expert = shard * local_experts + c * core_experts
    slots = lax.dynamic_slice_in_dim(slots, first_expert, core_experts, 2)
    slots = slots.transpose(1, 2, 0, 3)
    shard_slots = jnp.take(slots, place_of_shard, axis=2)
    slots = slots.reshape(REPS, core_experts, group_rows)
    shard_slots = shard_slots.reshape(REPS, core_experts, group_rows)
    shifts = jnp.arange(core_experts, dtype=jnp.int32)[:, None] * capacity

    def columns_of(table):
        return jnp.where(table >= 0, table + shifts, -1).transpose(0, 2, 1)

    columns, shard_columns = columns_of(slots[:2]), columns_of(shard_slots[:2])

    def cot_part(group, rows, behind=()):
        return cotangent_part(core_ref, shard_slots[group], rows, down_weight, capacity, behind)

    first_ref = jnp.stack([c, first_expert]).astype(jnp.int32)

    def ffn_part(group, rows, slot_cot, behind=(), cost=QUIET):
        return forward_part(
            first_ref,
            slots[group],
            rows,
            router_rows,
            gate_weight,
            up_weight,
            slot_cot,
            behind,
            cost,
        )

    made = {}

    def fill_cot(follow):
        beside = move(cot_own, CORE_SWAP)
        own_part = cot_part(0, cot_own, (follow,))
        made["cot"] = [own_part, cot_part(1, beside, (own_part[1],))]
        return [own_part[1]]

    ffn_pieces = gather_rows(
        ffn_low, fill=fill_cot, late=lambda: (made["cot"][1][1],)
    )
    near_cot = made["cot"]
    ffn_own = flat(ffn_pieces)
    ffn_beside = move(ffn_own, CORE_SWAP)
    ffn_far = [move(jnp.concatenate(pair, axis=0), X_SWAP) for pair in ffn_pieces]
    cot_across = lax.all_gather(after(cot_across, ffn_pieces[2][0]), "shard", tiled=True)

    near = [ffn_part(0, ffn_own, near_cot[0][1])]
    near.append(ffn_part(1, ffn_beside, near_cot[1][1], (near[0][1],)))

    def rows_back(group, behind=()):
        _, _, grad_gate, grad_up, scores = near[group]
        return backward_part(
            core_ref, columns[group], grad_gate, grad_up, scores, gate_weight, up_weight, behind
        ).reshape(SHARDS, tokens, -1)

    grad_other = rows_back(1, (ffn_far[0], ffn_far[1]))
    grad_own = rows_back(0, (grad_other,))
    grad_other = move(grad_other, CORE_SWAP)

    def routed_rows(group, extra, behind):
        return routed_part(
            core_ref, shard_columns[group], near[group][1], down_weight, extra, behind
        )

    def fill_routed_other(follow):
        made["routed_other"] = routed_rows(1, (), follow + (ffn_far[2], cot_across))
        return [made["routed_other"]]

    def fill_far_cot(follow):
        made["far_cot"] = cot_part(2, cot_across, follow)
        return [made["far_cot"][1]]

    def fill_routed_own(follow):
        extra = (move(made["routed_other"], CORE_SWAP),)
        made["routed"] = routed_rows(0, extra, follow)
        return [made["routed"]]

    def fill_other_cot(follow):
        rows = move(after(cot_across, made["routed"]), CORE_SWAP)
        made["other_cot"] = cot_part(3, rows, follow)
        return [made["other_cot"][1]]

    grad_home = scatter_rows(
        [lambda place: grad_own[place], lambda place: grad_other[place]],
        [fill_routed_other, fill_routed_own, fill_far_cot, fill_other_cot, None],
    )
    routed = lax.psum_scatter(
        after(made["routed"], grad_home), "shard", scatter_dimension=0, tiled=True
    )
    ffn_far = jnp.concatenate([after(part, made["other_cot"][1]) for part in ffn_far], axis=0)
    ffn_far = [ffn_far, move(ffn_far, CORE_SWAP)]

    grad_ffn_home = grad_home[:, :width]
    home_score = grad_home[:, width : width + expert_count].astype(f32)
    grad_logits = home_score - router_probs * jnp.sum(home_score, axis=1, keepdims=True)
    grad_logits_low = grad_logits.astype(bf16)

    grad_ffn_in = grad_ffn_home.astype(f32) + jnp.dot(
        grad_logits_low, router_rows, preferred_element_type=f32
    )
    grad_router_local = contract_rows(grad_logits_low, ffn_low)
    grad_ffn_local = jnp.sum(grad_ffn_in * ffn_unit, axis=0)
    scaled = gains[3] * grad_ffn_in
    grad_residual = grad_out.astype(f32) + ffn_rate * (
        scaled - ffn_unit * jnp.mean(scaled * ffn_unit, axis=-1, keepdims=True)
    )
    residual_low = grad_residual.astype(bf16)
    residual_other = move(residual_low, X_SWAP)
    residual_pair = jnp.concatenate([residual_low, residual_other], axis=0)

    grad_attended = contract_cols(residual_pair, out_part).astype(bf16)
    grad_attended = pick_columns(grad_attended, place_of_head, HEAD_DIM)
    grad_attended = grad_attended.reshape(2, tokens, 2 * part_width)
    mine, theirs = grad_attended[:, :, :part_width], grad_attended[:, :, part_width:]
    grad_attended = jnp.stack([mine, move(theirs, CORE_SWAP)], axis=1)
    grad_attended = grad_attended.reshape(REPS * tokens, part_width)
    grad_pair, grad_value, dots, grad_pair_gain = attend_back(*attention_operands, grad_attended)
    grad_pair_gain = jnp.sum(grad_pair_gain, axis=0).reshape(2, heads, HEAD_DIM)
    dots = rep_sum(dots.reshape(REPS, tokens, 2)).reshape(REPS * tokens, 2) / width
    grad_projected = join_grads(projected, pair_rate, grad_pair, grad_value, dots, REPS)

    grad_in_part = contract_rows(normed_low, grad_projected).astype(bf16)
    grad_in_part = grad_in_part.reshape(SHARDS, rows_each, 3 * part_width)
    grad_normed = contract_cols(grad_projected, in_part)
    grad_attn_part = jnp.sum(grad_normed * unit_all, axis=0)

    pair_gains = jnp.zeros((2, HEADS // 2, 2, HEAD_DIM), f32)
    pair_gains = lax.dynamic_update_slice(
        pair_gains, grad_pair_gain[:, :, None], (0, c * heads, a, 0)
    )
    small = jnp.concatenate(
        [grad_ffn_local[None], pair_gains.reshape(2, width), grad_router_local], axis=0
    )
    small = jnp.take(small.reshape(-1, SHARDS, rows_each), near_shards, axis=1)
    small = jnp.concatenate([grad_attn_part.reshape(1, SHARDS, rows_each), small], axis=0)
    small = jnp.pad(small, ((0, HEAD_DIM - small.shape[0]), (0, 0), (0, 0)))
    small = small.astype(bf16).transpose(1, 2, 0)

    grad_out_part = contract_rows(after(attended, grad_projected), residual_pair).astype(bf16)
    out_parts = grad_out_part.reshape(SHARDS, 2, out_rows, width)
    out_own = lax.dynamic_index_in_dim(out_parts, c, 1, keepdims=False)
    out_other = lax.dynamic_index_in_dim(out_parts, 1 - c, 1, keepdims=False)
    out_sum = added(out_own, move(out_other, CORE_SWAP))
    out_sum = jnp.take(out_sum, place_of_shard, axis=0).reshape(SHARDS * out_rows, width)

    far_cot = [made["far_cot"], made["other_cot"]]

    def fill_far(follow):
        made["far"] = ffn_part(
            2, ffn_far[0], far_cot[0][1], follow + (ffn_far[1],), LOUD
        )
        return [made["far"][3]]

    normed_other = grad_normed.astype(bf16).reshape(2, 2, tokens, width)
    normed_mine = added(normed_other[:, 0], move(normed_other[:, 1], CORE_SWAP))
    normed_across = move(normed_mine[1], X_SWAP)

    def fill_other(follow):
        made["other"] = ffn_part(
            3, ffn_far[1], far_cot[1][1], follow + (made["far"][3], normed_mine, routed, out_sum), LOUD
        )
        return [made["other"][3]]

    def weight_grad(left, right, follow):
        first, *follow = lax.optimization_barrier((left[0],) + follow)
        left = jnp.concatenate([first] + left[1:], axis=1)
        right = jnp.concatenate(right, axis=1)
        grad = jnp.einsum("ecd,ecf->edf", left, right, preferred_element_type=f32).astype(bf16)
        return grad, follow

    def groups(index):
        return [part[index] for part in (near[0], near[1], made["far"], made["other"])]

    def fence(follow):
        return [made["other"][3]]

    out_home = lax.psum_scatter(
        after(out_sum, routed), "shard", scatter_dimension=0, tiled=True
    )

    def fill_weights(follow):
        cots = [part[0] for part in near_cot + far_cot]
        reduced, first, second, third = follow
        down, _ = weight_grad(groups(1), cots, ())
        gate, (down, first, reduced, _) = weight_grad(
            groups(0), groups(2), (down, first, reduced, normed_across)
        )
        up, (gate, second, third, home) = weight_grad(
            groups(0), groups(3), (gate, second, third, out_home)
        )
        made["down"], made["gate"], made["up"], made["home"] = down, gate, up, home
        return reduced, first, second, third

    in_sum = scatter_rows(
        [lambda place: jnp.concatenate([grad_in_part[place], small[place]], axis=1)],
        [fill_far, fill_other, fence, fence, fill_weights],
        hold=True,
    )
    in_other = move(in_sum, X_SWAP)
    grad_up, out_home = made["up"], made["home"]
    down_all = widen(
        made["down"], move(made["down"], CORE_SWAP), core_ref, (grad_up,)
    )
    in_all = jnp.stack([in_sum, after(in_other, down_all)])
    in_beside = move(in_all, CORE_SWAP)
    out_across = move(after(out_home, down_all), X_SWAP)
    gate_all = widen(
        made["gate"], move(made["gate"], CORE_SWAP), core_ref, (down_all, out_across)
    )
    in_all = jnp.stack([in_all, in_beside], axis=1).reshape((REPS,) + in_sum.shape)
    grad_in = weave_columns(in_all, rep_ref, 3 * part_width, (gate_all,))
    small = jnp.sum(in_all[:, :, 3 * part_width :].astype(f32), axis=0).T
    up_all = widen(grad_up, move(grad_up, CORE_SWAP), core_ref, (gate_all,))

    outputs = (residual + after(routed, down_all).astype(f32)).astype(bf16)
    grad_normed = after(added(normed_mine[0], normed_across), down_all)
    grad_normed = pick_columns(grad_normed, place_of_shard, rows_each).astype(f32)
    home_unit = hidden * home_rate
    scaled = gains[0] * grad_normed
    grad_inputs = (
        grad_residual
        + home_rate * (scaled - home_unit * jnp.mean(scaled * home_unit, axis=-1, keepdims=True))
    ).astype(bf16)

    out_sum = jnp.stack([out_home, out_across])
    out_sum = jnp.stack([out_sum, move(out_sum, CORE_SWAP)], axis=1)
    out_sum = out_sum.reshape(REPS, out_rows, width)
    out_sum = jnp.take(out_sum, rep ^ jnp.arange(REPS, dtype=jnp.int32), axis=0)
    grad_out_proj = out_sum.reshape(rows_each, width).astype(f32)
    return (
        outputs,
        grad_inputs,
        small[0],
        grad_in,
        small[2],
        small[3],
        grad_out_proj,
        small[1],
        small[4 : 4 + expert_count].T,
        gate_all,
        up_all,
        down_all,
    )


def solution(mesh):
    fits = dict(mesh.shape) == {"rep": REPS, "shard": SHARDS}
    body = fast_local if fits else local
    in_specs = (
        P(("rep", "shard"), None),
        P("shard"),
        P("shard", None),
        P("shard"),
        P("shard"),
        P("shard", None),
        P("shard"),
        P("shard", None),
        P("shard", None, None),
        P("shard", None, None),
        P("shard", None, None),
        P(("rep", "shard"), None),
        P(("rep", "shard"), None),
        P(("rep", "shard"), None),
        P(("rep", "shard"), None),
    )
    out_specs = (
        P(("rep", "shard"), None),
        P(("rep", "shard"), None),
        P("shard"),
        P("shard", None),
        P("shard"),
        P("shard"),
        P("shard", None),
        P("shard"),
        P("shard", None),
        P("shard", None, None),
        P("shard", None, None),
        P("shard", None, None),
    )
    return jax.shard_map(body, mesh=mesh, in_specs=in_specs, out_specs=out_specs, check_vma=False)
```

```python
import functools

import jax
import jax.numpy as jnp
from jax import lax
from jax.experimental import pallas as pl
from jax.experimental.pallas import tpu as pltpu
from jax.sharding import PartitionSpec as P

HEADS = 16
HEAD_DIM = 128


norm_eps = 1e-05
rope_base = 10000.0
masked_score = -1e30


def rms_scale(values, gains):
    normed = values * lax.rsqrt(jnp.mean(values * values, axis=-1, keepdims=True) + norm_eps)
    return normed * gains


def rotary_tables(segment_row):
    length = segment_row.shape[0]
    places = jnp.arange(length, dtype=jnp.int32)
    starting = jnp.concatenate(
        [jnp.ones((1,), jnp.int32), (segment_row[1:] != segment_row[:-1]).astype(jnp.int32)]
    )
    first_place = lax.cummax(jnp.where(starting > 0, places, 0), axis=0)
    offsets = (places - first_place).astype(jnp.float32)
    halves = HEAD_DIM // 2
    inverse = rope_base ** (-2.0 * jnp.arange(halves, dtype=jnp.float32) / HEAD_DIM)
    angles = offsets[:, None] * inverse[None, :]
    angles = jnp.concatenate([angles, angles], axis=1)
    return (jnp.cos(angles), jnp.sin(angles))


def rotate(values, cos_table, sin_table):
    halves = values.shape[-1] // 2
    turned = jnp.concatenate([-values[..., halves:], values[..., :halves]], axis=-1)
    return values * cos_table[:, None, :] + turned * sin_table[:, None, :]


def query_key(raw_query, raw_key, query_scale, key_scale, cos_table, sin_table):
    row_count = raw_query.shape[0]
    normed_query = rms_scale(raw_query, query_scale).reshape(row_count, HEADS, HEAD_DIM)
    normed_key = rms_scale(raw_key, key_scale).reshape(row_count, HEADS, HEAD_DIM)
    return (rotate(normed_query, cos_table, sin_table), rotate(normed_key, cos_table, sin_table))


def softmax_rows(logits):
    highest = jnp.max(logits, axis=-1, keepdims=True)
    raised = jnp.exp(logits - highest)
    return raised / jnp.sum(raised, axis=-1, keepdims=True)


def swiglu(gate_pre, up_pre):
    return jax.nn.silu(gate_pre) * up_pre


def contract_rows(left_side, right_side):
    return lax.dot_general(
        left_side, right_side, (((0,), (0,)), ((), ())), preferred_element_type=jnp.float32
    )


def contract_cols(left_side, right_side):
    return lax.dot_general(
        left_side, right_side, (((1,), (1,)), ((), ())), preferred_element_type=jnp.float32
    )


def pick_rows(source_rows, row_picks):
    return jax.vmap(lambda expert_rows, picked: expert_rows[picked])(source_rows, row_picks)


def local(
    inputs,
    attn_gain,
    in_proj,
    query_gain,
    key_gain,
    out_proj,
    ffn_gain,
    router_weight,
    gate_weight,
    up_weight,
    down_weight,
    routes,
    priority,
    segments,
    grad_out,
):
    tokens = inputs.shape[0]
    model_width = inputs.shape[1]
    local_experts = gate_weight.shape[0]
    group_count = lax.axis_size("shard")
    my_index = lax.axis_index("shard")
    expert_count = local_experts * group_count
    route_count = routes.shape[1]
    pair_count = tokens * route_count
    capacity = 5 * pair_count * group_count // (4 * expert_count)
    send_most = 2 * pair_count // expert_count
    segment_row = segments[0]
    cos_table, sin_table = rotary_tables(segment_row)
    hidden_in = inputs.astype(jnp.float32)
    unit_rows = hidden_in * lax.rsqrt(
        jnp.mean(hidden_in * hidden_in, axis=-1, keepdims=True) + norm_eps
    )
    weight_piece = lax.all_gather(in_proj, "shard", axis=0, tiled=True)
    attn_piece = lax.all_gather(attn_gain, "shard", axis=0, tiled=True)
    query_piece = lax.all_gather(query_gain, "shard", axis=0, tiled=True)
    key_piece = lax.all_gather(key_gain, "shard", axis=0, tiled=True)
    scaled = (unit_rows * attn_piece.astype(jnp.float32)).astype(jnp.bfloat16)
    result = (
        jnp.dot(scaled, weight_piece, preferred_element_type=jnp.float32),
        attn_piece.astype(jnp.float32),
        query_piece.astype(jnp.float32),
        key_piece.astype(jnp.float32),
    )
    folded_in = result
    projected = folded_in[0]
    normed_attn, attn_norm_back = jax.vjp(rms_scale, hidden_in, folded_in[1])
    normed_low = normed_attn.astype(jnp.bfloat16)
    raw_query = projected[:, :model_width]
    raw_key = projected[:, model_width : 2 * model_width]
    raw_value = projected[:, 2 * model_width :]

    def rotated_pair(query_raw, key_raw, query_scale, key_scale):
        return query_key(query_raw, key_raw, query_scale, key_scale, cos_table, sin_table)

    (turned_query, turned_key), query_key_back = jax.vjp(
        rotated_pair, raw_query, raw_key, folded_in[2], folded_in[3]
    )
    query_low = turned_query.astype(jnp.bfloat16)
    key_low = turned_key.astype(jnp.bfloat16)
    value_low = raw_value.astype(jnp.bfloat16).reshape(tokens, HEADS, HEAD_DIM)
    places = jnp.arange(tokens, dtype=jnp.int32)
    allowed = (segment_row[:, None] == segment_row[None, :]) & (places[None, :] <= places[:, None])
    score_scale = HEAD_DIM ** (-0.5)

    def masked_scores(queries, key_vecs):
        products = jnp.einsum("qhd,khd->hqk", queries, key_vecs, preferred_element_type=jnp.float32)
        return jnp.where(allowed[None], products * score_scale, masked_score)

    scores = masked_scores(query_low, key_low)
    highest = jnp.max(scores, axis=-1, keepdims=True)
    raised = jnp.exp(scores - highest)
    totals = jnp.sum(raised, axis=-1, keepdims=True)
    attn_probs = raised / totals
    log_total = highest + jnp.log(totals)
    mixed = jnp.einsum(
        "hqk,khd->qhd",
        attn_probs.astype(jnp.bfloat16),
        value_low,
        preferred_element_type=jnp.float32,
    )
    attended = mixed.reshape(tokens, model_width).astype(jnp.bfloat16)
    weight_piece = lax.all_gather(out_proj, "shard", axis=0, tiled=True)
    ffn_piece = lax.all_gather(ffn_gain, "shard", axis=0, tiled=True)
    router_piece = lax.all_gather(router_weight, "shard", axis=0, tiled=True)
    result = (
        jnp.dot(attended, weight_piece, preferred_element_type=jnp.float32),
        ffn_piece.astype(jnp.float32),
        router_piece,
    )
    residual = hidden_in + result[0]
    router_full = result[2]
    normed_ffn, ffn_norm_back = jax.vjp(rms_scale, residual, result[1])
    ffn_low = normed_ffn.astype(jnp.bfloat16)
    logits = jnp.dot(ffn_low, router_full, preferred_element_type=jnp.float32)
    router_probs, router_back = jax.vjp(softmax_rows, logits)
    flat_routes = routes.reshape(pair_count)
    order_row = priority[0]
    ranked_expert = flat_routes[order_row]
    labels = jnp.arange(expert_count, dtype=jnp.int32)
    matches = (ranked_expert[:, None] == labels[None, :]).astype(jnp.int32)
    rank_in = (
        jnp.sum(jnp.cumsum(matches, axis=0, dtype=jnp.int32) * matches, axis=1, dtype=jnp.int32) - 1
    )
    counts = jnp.sum(matches, axis=0, dtype=jnp.int32)
    all_counts = lax.all_gather(counts[None, :], "shard", axis=0, tiled=True)
    base_slots = jnp.cumsum(all_counts, axis=0, dtype=jnp.int32) - all_counts
    my_bases = lax.dynamic_index_in_dim(base_slots, my_index, 0, keepdims=False)
    slot_index = jnp.sum(matches * my_bases[None, :], axis=1, dtype=jnp.int32) + rank_in
    cell_index = ranked_expert * send_most + rank_in
    inverse_order = (
        jnp.zeros((pair_count,), jnp.int32)
        .at[order_row]
        .set(jnp.arange(pair_count, dtype=jnp.int32))
    )
    pair_cell = cell_index[inverse_order].reshape(tokens, route_count)
    pair_keep = (
        (slot_index[inverse_order] < capacity).astype(jnp.float32).reshape(tokens, route_count)
    )
    cell_pair = jnp.zeros((expert_count * send_most,), jnp.int32).at[cell_index].set(order_row)
    cell_live = (jnp.arange(send_most, dtype=jnp.int32)[None, :] < counts[:, None]).reshape(
        expert_count * send_most
    )
    cell_token = cell_pair // route_count
    outgoing = jnp.where(cell_live[:, None], ffn_low[cell_token], 0).reshape(
        expert_count, send_most, model_width
    )
    arrived = lax.all_to_all(outgoing, "shard", split_axis=0, concat_axis=1, tiled=True)
    own_counts = lax.dynamic_slice_in_dim(all_counts, my_index * local_experts, local_experts, 1).T
    own_bases = lax.dynamic_slice_in_dim(base_slots, my_index * local_experts, local_experts, 1).T
    slot_ids = jnp.arange(capacity, dtype=jnp.int32)
    slot_ends = own_bases + own_counts
    source_ids = jnp.sum(
        (slot_ends[:, None, :] <= slot_ids[None, :, None]).astype(jnp.int32),
        axis=2,
        dtype=jnp.int32,
    )
    slot_filled = source_ids < group_count
    source_safe = jnp.minimum(source_ids, group_count - 1)
    slot_rows = (
        source_safe * send_most
        + slot_ids[None, :]
        - jnp.take_along_axis(own_bases, source_safe, axis=1)
    )
    slot_rows = jnp.where(slot_filled, slot_rows, 0)
    expert_in = jnp.where(slot_filled[..., None], pick_rows(arrived, slot_rows), 0)
    gate_pre = jnp.einsum(
        "ecd,edf->ecf", expert_in, gate_weight, preferred_element_type=jnp.float32
    )
    up_pre = jnp.einsum("ecd,edf->ecf", expert_in, up_weight, preferred_element_type=jnp.float32)
    activated, swiglu_back = jax.vjp(swiglu, gate_pre, up_pre)
    act_low = activated.astype(jnp.bfloat16)
    expert_out = jnp.einsum(
        "ecf,efd->ecd", act_low, down_weight, preferred_element_type=jnp.float32
    ).astype(jnp.bfloat16)
    cell_positions = jnp.arange(send_most, dtype=jnp.int32)
    cell_slot = own_bases[:, :, None] + cell_positions[None, None, :]
    cell_used = (cell_positions[None, None, :] < own_counts[:, :, None]) & (cell_slot < capacity)
    cell_slot = jnp.where(cell_used, cell_slot, 0).reshape(local_experts, group_count * send_most)
    cell_used = cell_used.reshape(local_experts, group_count * send_most)
    returning = jnp.where(cell_used[..., None], pick_rows(expert_out, cell_slot), 0)
    returned = lax.all_to_all(returning, "shard", split_axis=1, concat_axis=0, tiled=True).reshape(
        expert_count * send_most, model_width
    )
    pair_rows = returned[pair_cell].astype(jnp.float32)
    pair_weight = jnp.take_along_axis(router_probs, routes, axis=1) * pair_keep
    outputs = (residual + jnp.sum(pair_weight[..., None] * pair_rows, axis=1)).astype(jnp.bfloat16)
    cotangent = grad_out.astype(jnp.float32)
    grad_rows = (
        (pair_weight[..., None] * cotangent[:, None, :])
        .astype(jnp.bfloat16)
        .reshape(pair_count, model_width)
    )
    grad_pair_weight = jnp.sum(pair_rows * cotangent[:, None, :], axis=2) * pair_keep
    route_hits = (routes[..., None] == labels[None, None, :]).astype(jnp.float32)
    grad_router_probs = jnp.sum(grad_pair_weight[..., None] * route_hits, axis=1)
    (grad_logits,) = router_back(grad_router_probs)
    grad_logits_low = grad_logits.astype(jnp.bfloat16)
    outgoing_grad = jnp.where(cell_live[:, None], grad_rows[cell_pair], 0).reshape(
        expert_count, send_most, model_width
    )
    arrived_grad = lax.all_to_all(outgoing_grad, "shard", split_axis=0, concat_axis=1, tiled=True)
    grad_expert_out = jnp.where(slot_filled[..., None], pick_rows(arrived_grad, slot_rows), 0)
    grad_act = jnp.einsum(
        "ecd,efd->ecf", grad_expert_out, down_weight, preferred_element_type=jnp.float32
    )
    grad_down = jnp.einsum(
        "ecf,ecd->efd", act_low, grad_expert_out, preferred_element_type=jnp.float32
    )
    grad_gate_pre, grad_up_pre = swiglu_back(grad_act)
    gate_grad_low = grad_gate_pre.astype(jnp.bfloat16)
    up_grad_low = grad_up_pre.astype(jnp.bfloat16)
    grad_gate = jnp.einsum(
        "ecd,ecf->edf", expert_in, gate_grad_low, preferred_element_type=jnp.float32
    )
    grad_up = jnp.einsum("ecd,ecf->edf", expert_in, up_grad_low, preferred_element_type=jnp.float32)
    grad_expert_in = (
        jnp.einsum("ecf,edf->ecd", gate_grad_low, gate_weight, preferred_element_type=jnp.float32)
        + jnp.einsum("ecf,edf->ecd", up_grad_low, up_weight, preferred_element_type=jnp.float32)
    ).astype(jnp.bfloat16)
    returning_grad = jnp.where(cell_used[..., None], pick_rows(grad_expert_in, cell_slot), 0)
    returned_grad = lax.all_to_all(
        returning_grad, "shard", split_axis=1, concat_axis=0, tiled=True
    ).reshape(expert_count * send_most, model_width)
    grad_ffn_in = jnp.sum(returned_grad[pair_cell].astype(jnp.float32), axis=1) + contract_cols(
        grad_logits_low, router_full
    )
    grad_router_local = contract_rows(ffn_low, grad_logits_low)
    grad_residual_norm, grad_ffn_local = ffn_norm_back(grad_ffn_in)
    grad_residual = cotangent + grad_residual_norm
    residual_low = grad_residual.astype(jnp.bfloat16)
    grad_out_local = lax.psum_scatter(
        contract_rows(attended, residual_low).astype(jnp.bfloat16),
        "shard",
        scatter_dimension=0,
        tiled=True,
    )
    grad_attended = contract_cols(
        residual_low, lax.all_gather(out_proj, "shard", axis=0, tiled=True)
    )
    grad_mixed = grad_attended.astype(jnp.bfloat16).reshape(tokens, HEADS, HEAD_DIM)
    scores_again = masked_scores(query_low, key_low)
    probs_again = jnp.exp(scores_again - log_total)
    grad_probs = jnp.einsum(
        "qhd,khd->hqk", grad_mixed, value_low, preferred_element_type=jnp.float32
    )
    spread = jnp.sum(probs_again * grad_probs, axis=-1, keepdims=True)
    grad_scores = (probs_again * (grad_probs - spread)).astype(jnp.bfloat16)
    grad_query = (
        jnp.einsum("hqk,khd->qhd", grad_scores, key_low, preferred_element_type=jnp.float32)
        * score_scale
    )
    grad_key = (
        jnp.einsum("hqk,qhd->khd", grad_scores, query_low, preferred_element_type=jnp.float32)
        * score_scale
    )
    grad_value = jnp.einsum(
        "hqk,qhd->khd",
        probs_again.astype(jnp.bfloat16),
        grad_mixed,
        preferred_element_type=jnp.float32,
    )
    grad_raw_query, grad_raw_key, grad_query_local, grad_key_local = query_key_back(
        (grad_query, grad_key)
    )
    grad_qkv = jnp.concatenate(
        [grad_raw_query, grad_raw_key, grad_value.reshape(tokens, model_width)], axis=1
    ).astype(jnp.bfloat16)
    grad_in_local = lax.psum_scatter(
        contract_rows(normed_low, grad_qkv).astype(jnp.bfloat16),
        "shard",
        scatter_dimension=0,
        tiled=True,
    )
    grad_normed = contract_cols(grad_qkv, lax.all_gather(in_proj, "shard", axis=0, tiled=True))
    grad_hidden_norm, grad_attn_local = attn_norm_back(grad_normed)
    grad_inputs = (grad_residual + grad_hidden_norm).astype(jnp.bfloat16)
    small_parts = (
        lax.psum_scatter(
            grad_attn_local.astype(jnp.bfloat16), "shard", scatter_dimension=0, tiled=True
        ).astype(jnp.float32),
        lax.psum_scatter(
            grad_query_local.astype(jnp.bfloat16), "shard", scatter_dimension=0, tiled=True
        ).astype(jnp.float32),
        lax.psum_scatter(
            grad_key_local.astype(jnp.bfloat16), "shard", scatter_dimension=0, tiled=True
        ).astype(jnp.float32),
        lax.psum_scatter(
            grad_ffn_local.astype(jnp.bfloat16), "shard", scatter_dimension=0, tiled=True
        ).astype(jnp.float32),
        lax.psum_scatter(
            grad_router_local.astype(jnp.bfloat16), "shard", scatter_dimension=0, tiled=True
        ).astype(jnp.float32),
    )
    summed = (
        lax.psum(grad_in_local, "rep").astype(jnp.float32),
        lax.psum(grad_out_local, "rep").astype(jnp.float32),
        lax.psum(small_parts[0].astype(jnp.bfloat16), "rep").astype(jnp.float32),
        lax.psum(small_parts[1].astype(jnp.bfloat16), "rep").astype(jnp.float32),
        lax.psum(small_parts[2].astype(jnp.bfloat16), "rep").astype(jnp.float32),
        lax.psum(small_parts[3].astype(jnp.bfloat16), "rep").astype(jnp.float32),
        lax.psum(small_parts[4].astype(jnp.bfloat16), "rep").astype(jnp.float32),
        lax.psum(grad_gate.astype(jnp.bfloat16), "rep").astype(jnp.float32),
        lax.psum(grad_up.astype(jnp.bfloat16), "rep").astype(jnp.float32),
        lax.psum(grad_down.astype(jnp.bfloat16), "rep").astype(jnp.float32),
    )
    return (
        outputs,
        grad_inputs,
        summed[2],
        summed[0],
        summed[3],
        summed[4],
        summed[1],
        summed[5],
        summed[6],
        summed[7],
        summed[8],
        summed[9],
    )


AXES = ("rep", "shard")
LINE = 4
SHARDS = 8
REPS = 4


def pairs_of(target):
    moves = []
    for rep in range(REPS):
        for shard in range(SHARDS):
            there = target(rep, shard)
            moves.append((rep * SHARDS + shard, there[0] * SHARDS + there[1]))
    return moves


CORE_SWAP = pairs_of(lambda rep, shard: (rep ^ 1, shard))
X_SWAP = pairs_of(lambda rep, shard: (rep ^ 2, shard))
Y_SWAP = pairs_of(lambda rep, shard: (rep, shard ^ 1))
SHARD_SWAP = [
    pairs_of(lambda rep, shard: (rep, shard ^ 1)),
    pairs_of(lambda rep, shard: (rep, shard ^ 2)),
    pairs_of(lambda rep, shard: (rep, shard ^ 4)),
]
Z_FROM = [pairs_of(lambda rep, shard: (rep, (shard - 2 * k) % SHARDS)) for k in range(LINE)]
Z_TO = [pairs_of(lambda rep, shard: (rep, (shard + 2 * k) % SHARDS)) for k in range(LINE)]


def move(values, moves):
    return lax.ppermute(values, AXES, moves)


def after(values, *others):
    return lax.optimization_barrier((values,) + others)[0]


def gather_small(values, hold):
    low = jnp.stack([values, move(values, SHARD_SWAP[1])])
    high = jnp.stack([low, move(after(low, *hold), SHARD_SWAP[2])])
    last = move(high, SHARD_SWAP[0])
    both = jnp.stack([high, last], axis=2)
    return both.reshape((SHARDS,) + values.shape), last


def gather_rows(values, early=(), late=None, fill=None, first=()):
    moved = {k: move(values, Z_FROM[k]) for k in (1, 3)}
    moved[2] = move(after(values, moved[1], *first), Z_FROM[2])
    mine, beside = {0: values}, {0: move(values, Y_SWAP)}
    for k in (1, 3, 2):
        mine[k] = after(moved[k], *early) if early else moved[k]
        if k == 2 and fill is not None:
            mine[k] = after(mine[k], *fill(mine[3]))
        beside[k] = move(mine[k], Y_SWAP)
    if late is not None:
        beside = {k: after(beside[k], *late()) for k in beside}
    return [(mine[k], beside[k]) for k in range(LINE)]


def flat(pieces):
    return jnp.concatenate([piece for pair in pieces for piece in pair], axis=0)


def added(first, *others):
    total = first.astype(jnp.float32)
    for other in others:
        total = total + other.astype(jnp.float32)
    return total.astype(first.dtype)


def scatter_rows(parts, fills, hold=False):
    away = {k: added(*[part(2 * k + 1) for part in parts]) for k in (2, 1, 3, 0)}
    moved = {2: move(away[2], Y_SWAP)}
    arrived, reduced = [], away[2]
    for k, fill in zip((2, 1, 3, 0), fills):
        filled = [] if fill is None else fill((reduced,))
        if k == 2:
            for other in (1, 3, 0):
                held = after(away[other], *filled) if hold else away[other]
                moved[other] = move(held, Y_SWAP)
        here = after(moved[k], *filled) if filled else moved[k]
        reduced = added(here, *[part(2 * k) for part in parts])
        if k > 0:
            arrived.append(move(reduced, Z_TO[k]))
    if fills[4] is not None:
        reduced, *arrived = fills[4]((reduced, *arrived))
    return added(reduced, *arrived)


LIMIT = 56 * 2**20
HIDDEN_BLOCK = 1024
WIDTH_BLOCK = 512
QUIET = pl.CostEstimate(flops=0, bytes_accessed=0, transcendentals=0)
LOUD = pl.CostEstimate(flops=10**11, bytes_accessed=0, transcendentals=0)


def ordered(kernel, behind):
    def body(scalar_ref, *refs):
        return kernel(scalar_ref, *refs[behind:])

    return body


HELD = pl.BlockSpec(memory_space=pl.ANY)


def copy_block(order_ref, from_ref, into_ref):
    into_ref[...] = from_ref[...]


def pick_columns(values, order, block):
    rows = values.shape[0]
    picks = order.shape[0]
    return pl.pallas_call(
        copy_block,
        grid_spec=pltpu.PrefetchScalarGridSpec(
            num_scalar_prefetch=1,
            grid=(picks,),
            in_specs=[pl.BlockSpec((rows, block), lambda i, order: (0, order[i]))],
            out_specs=pl.BlockSpec((rows, block), lambda i, order: (0, i)),
        ),
        out_shape=jax.ShapeDtypeStruct((rows, picks * block), values.dtype),
        compiler_params=pltpu.CompilerParams(vmem_limit_bytes=32 * 2**20),
    )(order, values)


def thin_kernel(rep_ref, from_ref, into_ref):
    heads = into_ref.shape[1] // HEAD_DIM

    def take(parity):
        for head in range(heads):
            start = (2 * head + parity) * HEAD_DIM
            into_ref[:, head * HEAD_DIM : (head + 1) * HEAD_DIM] = from_ref[
                :, start : start + HEAD_DIM
            ]

    @pl.when(rep_ref[0] < 2)
    def _():
        take(0)

    @pl.when(rep_ref[0] >= 2)
    def _():
        take(1)


def thin_columns(weights, rep, width):
    rows = weights.shape[0]
    return pl.pallas_call(
        thin_kernel,
        grid_spec=pltpu.PrefetchScalarGridSpec(
            num_scalar_prefetch=1,
            grid=(3,),
            in_specs=[
                pl.BlockSpec((rows, width // 2), lambda i, rep: (0, 2 * i + lax.rem(rep[0], 2)))
            ],
            out_specs=pl.BlockSpec((rows, width // 4), lambda i, rep: (0, i)),
        ),
        out_shape=jax.ShapeDtypeStruct((rows, 3 * width // 4), weights.dtype),
        compiler_params=pltpu.CompilerParams(vmem_limit_bytes=32 * 2**20),
    )(rep, weights)


def weave_kernel(rep_ref, even_ref, odd_ref, into_ref):
    for head in range(even_ref.shape[2] // HEAD_DIM):
        part = slice(head * HEAD_DIM, (head + 1) * HEAD_DIM)
        start = 2 * head * HEAD_DIM
        into_ref[:, start : start + HEAD_DIM] = even_ref[0, :, part].astype(jnp.float32)
        into_ref[:, start + HEAD_DIM : start + 2 * HEAD_DIM] = odd_ref[0, :, part].astype(
            jnp.float32
        )


def weave_columns(pieces, rep, columns, behind):
    rows = pieces.shape[1]
    block = columns // 3
    return pl.pallas_call(
        ordered(weave_kernel, len(behind)),
        grid_spec=pltpu.PrefetchScalarGridSpec(
            num_scalar_prefetch=1,
            grid=(3, 2),
            in_specs=[HELD] * len(behind)
            + [
                pl.BlockSpec((1, rows, block), lambda i, j, rep: (j ^ rep[0], 0, i)),
                pl.BlockSpec((1, rows, block), lambda i, j, rep: ((j + 2) ^ rep[0], 0, i)),
            ],
            out_specs=pl.BlockSpec((rows, 2 * block), lambda i, j, rep: (0, 2 * i + j)),
        ),
        out_shape=jax.ShapeDtypeStruct((rows, 4 * columns), jnp.float32),
        compiler_params=pltpu.CompilerParams(vmem_limit_bytes=32 * 2**20),
    )(rep, *behind, pieces, pieces)


def widen_kernel(core_ref, own_ref, other_ref, into_ref):
    mine = pl.program_id(0) == core_ref[0]

    @pl.when(mine)
    def _():
        into_ref[...] = own_ref[...].astype(jnp.float32)

    @pl.when(jnp.logical_not(mine))
    def _():
        into_ref[...] = other_ref[...].astype(jnp.float32)


def widen(own, other, core, behind=()):
    experts, rows, columns = own.shape
    block = rows // 4
    steps = experts * 4

    def place(hold, core, i, j):
        return jnp.where(i == hold, j, jnp.where(hold == 0, steps - 1, 0))

    own_map = lambda i, j, core: (place(core[0], core, i, j), 0)
    other_map = lambda i, j, core: (place(1 - core[0], core, i, j), 0)
    result = pl.pallas_call(
        ordered(widen_kernel, len(behind)),
        grid_spec=pltpu.PrefetchScalarGridSpec(
            num_scalar_prefetch=1,
            grid=(2, steps),
            in_specs=[HELD] * len(behind)
            + [
                pl.BlockSpec((block, columns), own_map),
                pl.BlockSpec((block, columns), other_map),
            ],
            out_specs=pl.BlockSpec((block, columns), lambda i, j, core: (i * steps + j, 0)),
        ),
        out_shape=jax.ShapeDtypeStruct((2 * experts * rows, columns), jnp.float32),
        compiler_params=pltpu.CompilerParams(vmem_limit_bytes=32 * 2**20),
        cost_estimate=QUIET,
    )(
        core,
        *behind,
        own.reshape(experts * rows, columns),
        other.reshape(experts * rows, columns),
    )
    return result.reshape(2 * experts, rows, columns)


def slot_rows(slots, capacity):
    places = lax.broadcasted_iota(jnp.int32, (capacity, slots.shape[1]), 0)
    return jnp.where(places == slots, 1.0, 0.0).astype(jnp.bfloat16)


def slot_columns(slots, columns):
    places = lax.broadcasted_iota(jnp.int32, (slots.shape[0], columns), 1)
    found = places == slots[:, 0:1]
    for expert in range(1, slots.shape[1]):
        found = found | (places == slots[:, expert : expert + 1])
    return jnp.where(found, 1.0, 0.0).astype(jnp.bfloat16)


def dot_wide(left, right):
    return jnp.dot(left, right, preferred_element_type=jnp.float32)


def pick_rows_into(slots_ref, rows_ref, into_ref):
    choice = slot_rows(slots_ref[0], into_ref.shape[1])
    for start in range(0, rows_ref.shape[1], WIDTH_BLOCK):
        part = slice(start, start + WIDTH_BLOCK)
        into_ref[0, :, part] = dot_wide(choice, rows_ref[:, part]).astype(jnp.bfloat16)


def cotangent_kernel(core_ref, slots_ref, rows_ref, down_ref, picked_ref, slot_ref):
    @pl.when(pl.program_id(1) == 0)
    def _():
        pick_rows_into(slots_ref, rows_ref, picked_ref)

    slot_ref[0] = contract_cols(picked_ref[0], down_ref[0])


def cotangent_part(core, slots, rows, down_weight, capacity, behind=()):
    experts, tokens = slots.shape
    width, hidden = rows.shape[1], down_weight.shape[1]
    return pl.pallas_call(
        ordered(cotangent_kernel, len(behind)),
        grid_spec=pltpu.PrefetchScalarGridSpec(
            num_scalar_prefetch=1,
            grid=(experts, hidden // HIDDEN_BLOCK),
            in_specs=[HELD] * len(behind)
            + [
                pl.BlockSpec((1, 1, tokens), lambda e, n, core: (e, 0, 0)),
                pl.BlockSpec((tokens, width), lambda e, n, core: (0, 0)),
                pl.BlockSpec(
                    (1, HIDDEN_BLOCK, width), lambda e, n, core: (core[0] * experts + e, n, 0)
                ),
            ],
            out_specs=[
                pl.BlockSpec((1, capacity, width), lambda e, n, core: (e, 0, 0)),
                pl.BlockSpec((1, capacity, HIDDEN_BLOCK), lambda e, n, core: (e, 0, n)),
            ],
        ),
        out_shape=[
            jax.ShapeDtypeStruct((experts, capacity, width), jnp.bfloat16),
            jax.ShapeDtypeStruct((experts, capacity, hidden), jnp.float32),
        ],
        compiler_params=pltpu.CompilerParams(vmem_limit_bytes=LIMIT),
        cost_estimate=LOUD,
    )(core, *behind, slots[:, None, :], rows, down_weight)


def forward_kernel(
    first_ref,
    slots_ref,
    rows_ref,
    router_ref,
    gate_ref,
    up_ref,
    slot_ref,
    picked_ref,
    act_ref,
    grad_gate_ref,
    grad_up_ref,
    score_ref,
    weight_ref,
    total_ref,
):
    step = pl.program_id(1)
    mine = first_ref[1] + pl.program_id(0)

    @pl.when(step == 0)
    def _():
        pick_rows_into(slots_ref, rows_ref, picked_ref)
        logits = contract_cols(picked_ref[0], router_ref[...])
        raised = jnp.exp(logits - jnp.max(logits, axis=1, keepdims=True))
        label = lax.broadcasted_iota(jnp.int32, raised.shape, 1)
        own = jnp.sum(jnp.where(label == mine, raised, 0.0), axis=1, keepdims=True)
        weight_ref[...] = own / jnp.sum(raised, axis=1, keepdims=True)
        total_ref[...] = jnp.zeros_like(total_ref)

    gate_pre = dot_wide(picked_ref[0], gate_ref[0])
    up_pre = dot_wide(picked_ref[0], up_ref[0])
    sigmoid = 1.0 / (1.0 + jnp.exp(-gate_pre))
    smooth = gate_pre * sigmoid
    grad_act = weight_ref[...] * slot_ref[0]
    act = smooth * up_pre
    act_ref[0] = (weight_ref[...] * act).astype(jnp.bfloat16)
    grad_gate_ref[0] = (grad_act * up_pre * (sigmoid + smooth * (1.0 - sigmoid))).astype(
        jnp.bfloat16
    )
    grad_up_ref[0] = (grad_act * smooth).astype(jnp.bfloat16)
    total_ref[...] += jnp.sum(act * grad_act, axis=1, keepdims=True)

    @pl.when(step == pl.num_programs(1) - 1)
    def _():
        label = lax.broadcasted_iota(jnp.int32, score_ref.shape[1:], 1)
        score_ref[0] = jnp.where(label == mine, total_ref[...], 0.0).astype(jnp.bfloat16)


def forward_part(first, slots, rows, router_rows, gate_weight, up_weight, slot_cot, behind=(), cost=QUIET):
    experts, tokens = slots.shape
    capacity, hidden = slot_cot.shape[1:]
    width = rows.shape[1]
    labels = router_rows.shape[0]
    weight_spec = pl.BlockSpec(
        (1, width, HIDDEN_BLOCK), lambda e, n, first: (first[0] * experts + e, 0, n)
    )
    hidden_spec = pl.BlockSpec((1, capacity, HIDDEN_BLOCK), lambda e, n, first: (e, 0, n))
    hidden_shape = jax.ShapeDtypeStruct((experts, capacity, hidden), jnp.bfloat16)
    return pl.pallas_call(
        ordered(forward_kernel, len(behind)),
        grid_spec=pltpu.PrefetchScalarGridSpec(
            num_scalar_prefetch=1,
            grid=(experts, hidden // HIDDEN_BLOCK),
            in_specs=[HELD] * len(behind)
            + [
                pl.BlockSpec((1, 1, tokens), lambda e, n, first: (e, 0, 0)),
                pl.BlockSpec((tokens, width), lambda e, n, first: (0, 0)),
                pl.BlockSpec((labels, width), lambda e, n, first: (0, 0)),
                weight_spec,
                weight_spec,
                hidden_spec,
            ],
            out_specs=[
                pl.BlockSpec((1, capacity, width), lambda e, n, first: (e, 0, 0)),
                hidden_spec,
                hidden_spec,
                hidden_spec,
                pl.BlockSpec((1, capacity, HEAD_DIM), lambda e, n, first: (e, 0, 0)),
            ],
            scratch_shapes=[
                pltpu.VMEM((capacity, 1), jnp.float32),
                pltpu.VMEM((capacity, 1), jnp.float32),
            ],
        ),
        out_shape=[
            jax.ShapeDtypeStruct((experts, capacity, width), jnp.bfloat16),
            hidden_shape,
            hidden_shape,
            hidden_shape,
            jax.ShapeDtypeStruct((experts, capacity, HEAD_DIM), jnp.bfloat16),
        ],
        compiler_params=pltpu.CompilerParams(vmem_limit_bytes=LIMIT),
        cost_estimate=cost,
    )(first, *behind, slots[:, None, :], rows, router_rows, gate_weight, up_weight, slot_cot)


def backward_kernel(
    core_ref, slots_ref, grad_gate_ref, grad_up_ref, score_ref, *rest
):
    experts, capacity, _ = grad_gate_ref.shape
    gates, ups = rest[:experts], rest[experts : 2 * experts]
    into_ref, spread_ref, slot_ref = rest[2 * experts :]
    step = pl.program_id(0)
    width = pl.num_programs(0) * WIDTH_BLOCK

    @pl.when(step == 0)
    def _():
        spread_ref[...] = slot_columns(slots_ref[...], experts * capacity)
        scores = score_ref[...].reshape(experts * capacity, HEAD_DIM)
        into_ref[:, width:] = dot_wide(spread_ref[...], scores).astype(jnp.bfloat16)

    for expert in range(experts):
        rows = contract_cols(grad_gate_ref[expert], gates[expert][0]) + contract_cols(
            grad_up_ref[expert], ups[expert][0]
        )
        slot_ref[expert * capacity : (expert + 1) * capacity, :] = rows.astype(jnp.bfloat16)
    start = pl.multiple_of(step * WIDTH_BLOCK, WIDTH_BLOCK)
    into_ref[:, pl.ds(start, WIDTH_BLOCK)] = dot_wide(spread_ref[...], slot_ref[...]).astype(
        jnp.bfloat16
    )


def backward_part(core, columns, grad_gate, grad_up, scores, gate_weight, up_weight, behind=()):
    experts, capacity, hidden = grad_gate.shape
    tokens, width = columns.shape[0], gate_weight.shape[1]

    def weight_spec(expert):
        return pl.BlockSpec(
            (1, WIDTH_BLOCK, hidden), lambda n, core: (core[0] * experts + expert, n, 0)
        )

    whole = pl.BlockSpec((experts, capacity, hidden), lambda n, core: (0, 0, 0))
    return pl.pallas_call(
        ordered(backward_kernel, len(behind)),
        grid_spec=pltpu.PrefetchScalarGridSpec(
            num_scalar_prefetch=1,
            grid=(width // WIDTH_BLOCK,),
            in_specs=[HELD] * len(behind)
            + [
                pl.BlockSpec(columns.shape, lambda n, core: (0, 0)),
                whole,
                whole,
                pl.BlockSpec((experts, capacity, HEAD_DIM), lambda n, core: (0, 0, 0)),
            ]
            + [weight_spec(expert) for expert in range(experts)] * 2,
            out_specs=pl.BlockSpec((tokens, width + HEAD_DIM), lambda n, core: (0, 0)),
            scratch_shapes=[
                pltpu.VMEM((tokens, experts * capacity), jnp.bfloat16),
                pltpu.VMEM((experts * capacity, WIDTH_BLOCK), jnp.bfloat16),
            ],
        ),
        out_shape=jax.ShapeDtypeStruct((tokens, width + HEAD_DIM), jnp.bfloat16),
        compiler_params=pltpu.CompilerParams(vmem_limit_bytes=LIMIT),
        cost_estimate=QUIET,
    )(
        core,
        *behind,
        columns,
        grad_gate,
        grad_up,
        scores,
        *[gate_weight] * experts,
        *[up_weight] * experts,
    )


def routed_kernel(more, core_ref, slots_ref, act_ref, *rest):
    experts, capacity, _ = act_ref.shape
    downs = rest[:experts]
    into_ref, spread_ref, slot_ref = rest[experts + more :]

    @pl.when(pl.program_id(0) == 0)
    def _():
        spread_ref[...] = slot_columns(slots_ref[...], experts * capacity)

    for expert in range(experts):
        rows = dot_wide(act_ref[expert], downs[expert][0])
        slot_ref[expert * capacity : (expert + 1) * capacity, :] = rows.astype(jnp.bfloat16)
    total = dot_wide(spread_ref[...], slot_ref[...])
    for extra in rest[experts : experts + more]:
        total += extra[...].astype(jnp.float32)
    into_ref[...] = total.astype(jnp.bfloat16)


def routed_part(core, columns, act, down_weight, extra=(), behind=()):
    experts, capacity, hidden = act.shape
    tokens, width = columns.shape[0], down_weight.shape[2]

    def weight_spec(expert):
        return pl.BlockSpec(
            (1, hidden, WIDTH_BLOCK), lambda n, core: (core[0] * experts + expert, 0, n)
        )

    rows_spec = pl.BlockSpec((tokens, WIDTH_BLOCK), lambda n, core: (0, n))
    return pl.pallas_call(
        ordered(functools.partial(routed_kernel, len(extra)), len(behind)),
        grid_spec=pltpu.PrefetchScalarGridSpec(
            num_scalar_prefetch=1,
            grid=(width // WIDTH_BLOCK,),
            in_specs=[HELD] * len(behind)
            + [
                pl.BlockSpec(columns.shape, lambda n, core: (0, 0)),
                pl.BlockSpec((experts, capacity, hidden), lambda n, core: (0, 0, 0)),
            ]
            + [weight_spec(expert) for expert in range(experts)]
            + [rows_spec] * len(extra),
            out_specs=rows_spec,
            scratch_shapes=[
                pltpu.VMEM((tokens, experts * capacity), jnp.bfloat16),
                pltpu.VMEM((experts * capacity, WIDTH_BLOCK), jnp.bfloat16),
            ],
        ),
        out_shape=jax.ShapeDtypeStruct((tokens, width), jnp.bfloat16),
        compiler_params=pltpu.CompilerParams(vmem_limit_bytes=LIMIT),
        cost_estimate=LOUD,
    )(core, *behind, columns, act, *[down_weight] * experts, *extra)


def roll_half(values):
    return pltpu.roll(values, HEAD_DIM // 2, 1)


def head_parts(raw_ref, rate_ref, gain_ref, cos_ref, sin_ref, head):
    part_width = gain_ref.shape[1]
    units, turned = [], []
    for which in range(2):
        start = which * part_width + head * HEAD_DIM
        unit = raw_ref[:, start : start + HEAD_DIM] * rate_ref[:, which : which + 1]
        gain = gain_ref[which : which + 1, head * HEAD_DIM : (head + 1) * HEAD_DIM]
        scaled = unit * gain
        units.append((unit, gain))
        turned.append(
            (scaled * cos_ref[...] + roll_half(scaled) * sin_ref[...]).astype(jnp.bfloat16)
        )
    start = 2 * part_width + head * HEAD_DIM
    value = raw_ref[:, start : start + HEAD_DIM].astype(jnp.bfloat16)
    return units, turned, value


def head_probs(turned, column_ref, row_ref):
    scores = contract_cols(turned[0], turned[1]) * HEAD_DIM ** (-0.5)
    length = scores.shape[0]
    reader = lax.broadcasted_iota(jnp.int32, (length, length), 0)
    source = lax.broadcasted_iota(jnp.int32, (length, length), 1)
    allowed = (column_ref[...] == row_ref[0]) & (source <= reader)
    scores = jnp.where(allowed, scores, masked_score)
    raised = jnp.exp(scores - jnp.max(scores, axis=1, keepdims=True))
    return raised / jnp.sum(raised, axis=1, keepdims=True)


def attend_kernel(raw_ref, rate_ref, gain_ref, cos_ref, sin_ref, column_ref, row_ref, into_ref):
    for head in range(gain_ref.shape[1] // HEAD_DIM):
        _, turned, value = head_parts(raw_ref, rate_ref, gain_ref, cos_ref, sin_ref, head)
        probs = head_probs(turned, column_ref, row_ref).astype(jnp.bfloat16)
        into_ref[:, head * HEAD_DIM : (head + 1) * HEAD_DIM] = dot_wide(probs, value).astype(
            jnp.bfloat16
        )


def attend_back_kernel(
    raw_ref,
    rate_ref,
    gain_ref,
    cos_ref,
    sin_ref,
    column_ref,
    row_ref,
    grad_ref,
    pair_ref,
    value_ref,
    dots_ref,
    gains_ref,
):
    score_scale = HEAD_DIM ** (-0.5)
    part_width = gain_ref.shape[1]
    dots = [0.0, 0.0]
    for head in range(part_width // HEAD_DIM):
        units, turned, value = head_parts(raw_ref, rate_ref, gain_ref, cos_ref, sin_ref, head)
        probs = head_probs(turned, column_ref, row_ref)
        here = slice(head * HEAD_DIM, (head + 1) * HEAD_DIM)
        grad = grad_ref[:, here]
        grad_probs = contract_cols(grad, value)
        mean_grad = jnp.sum(probs * grad_probs, axis=1, keepdims=True)
        grad_scores = (probs * (grad_probs - mean_grad)).astype(jnp.bfloat16)
        value_ref[:, here] = contract_rows(probs.astype(jnp.bfloat16), grad).astype(jnp.bfloat16)
        grads = (
            dot_wide(grad_scores, turned[1]) * score_scale,
            contract_rows(grad_scores, turned[0]) * score_scale,
        )
        for which in range(2):
            unit, gain = units[which]
            back = grads[which] * cos_ref[...] + roll_half(grads[which] * sin_ref[...])
            gains_ref[0, which : which + 1, here] = jnp.sum(back * unit, axis=0, keepdims=True)
            back = back * gain
            start = which * part_width + head * HEAD_DIM
            pair_ref[:, start : start + HEAD_DIM] = back
            dots[which] += jnp.sum(back * unit, axis=1, keepdims=True)
    dots_ref[:, 0:1] = dots[0]
    dots_ref[:, 1:2] = dots[1]


def join_kernel(raw_ref, rate_ref, pair_ref, value_ref, dots_ref, into_ref):
    part_width = value_ref.shape[1]
    for which in range(2):
        here = slice(which * part_width, (which + 1) * part_width)
        rate = rate_ref[:, which : which + 1]
        shift = dots_ref[:, which : which + 1] * rate
        into_ref[:, here] = (rate * (pair_ref[:, here] - raw_ref[:, here] * shift)).astype(
            jnp.bfloat16
        )
    into_ref[:, 2 * part_width :] = value_ref[...]


def row_blocks(count, *arrays):
    return [pl.BlockSpec((array.shape[0] // count, array.shape[1]), lambda i: (i, 0)) for array in arrays]


def attention_specs(raw, rate, gains, cos_table, sin_table, columns, rows):
    count = rows.shape[0]
    return (
        row_blocks(count, raw, rate)
        + [pl.BlockSpec(gains.shape, lambda i: (0, 0))]
        + row_blocks(count, cos_table, sin_table, columns)
        + [pl.BlockSpec((1, 1, rows.shape[2]), lambda i: (i, 0, 0))]
    )


def attend(raw, rate, gains, cos_table, sin_table, columns, rows):
    count = rows.shape[0]
    operands = (raw, rate, gains, cos_table, sin_table, columns, rows)
    result = jax.ShapeDtypeStruct((raw.shape[0], gains.shape[1]), jnp.bfloat16)
    return pl.pallas_call(
        attend_kernel,
        grid=(count,),
        in_specs=attention_specs(*operands),
        out_specs=row_blocks(count, result)[0],
        out_shape=result,
        compiler_params=pltpu.CompilerParams(vmem_limit_bytes=LIMIT),
        cost_estimate=QUIET,
    )(*operands)


def attend_back(raw, rate, gains, cos_table, sin_table, columns, rows, grads, behind=()):
    count = rows.shape[0]
    operands = (raw, rate, gains, cos_table, sin_table, columns, rows)
    results = [
        jax.ShapeDtypeStruct((raw.shape[0], 2 * gains.shape[1]), jnp.float32),
        jax.ShapeDtypeStruct((raw.shape[0], gains.shape[1]), jnp.bfloat16),
        jax.ShapeDtypeStruct((raw.shape[0], 2), jnp.float32),
    ]
    gain_result = jax.ShapeDtypeStruct((count,) + gains.shape, jnp.float32)
    return pl.pallas_call(
        lambda *refs: attend_back_kernel(*refs[len(behind) :]),
        grid=(count,),
        in_specs=[HELD] * len(behind) + attention_specs(*operands) + row_blocks(count, grads),
        out_specs=row_blocks(count, *results)
        + [pl.BlockSpec((1,) + gains.shape, lambda i: (i, 0, 0))],
        out_shape=results + [gain_result],
        compiler_params=pltpu.CompilerParams(vmem_limit_bytes=LIMIT),
        cost_estimate=QUIET,
    )(*behind, *operands, grads)


def join_grads(raw, rate, pair, value, dots, count):
    operands = (raw, rate, pair, value, dots)
    result = jax.ShapeDtypeStruct(raw.shape, jnp.bfloat16)
    return pl.pallas_call(
        join_kernel,
        grid=(count,),
        in_specs=row_blocks(count, *operands),
        out_specs=row_blocks(count, result)[0],
        out_shape=result,
        compiler_params=pltpu.CompilerParams(vmem_limit_bytes=LIMIT),
        cost_estimate=QUIET,
    )(*operands)


def rep_sum(values):
    values = values + move(values, CORE_SWAP).reshape((2, 2) + values.shape[1:])[:, ::-1].reshape(
        values.shape
    )
    swapped = move(values, X_SWAP)
    return values + jnp.concatenate([swapped[2:], swapped[:2]], axis=0)


def fast_local(
    inputs,
    attn_gain,
    in_proj,
    query_gain,
    key_gain,
    out_proj,
    ffn_gain,
    router_weight,
    gate_weight,
    up_weight,
    down_weight,
    routes,
    priority,
    segments,
    grad_out,
):
    f32, bf16 = jnp.float32, jnp.bfloat16
    tokens, width = inputs.shape
    rows_each = in_proj.shape[0]
    local_experts, _, hidden_units = gate_weight.shape
    expert_count = local_experts * SHARDS
    route_count = routes.shape[1]
    pair_count = tokens * route_count
    capacity = 5 * pair_count * SHARDS // (4 * expert_count)
    core_experts = local_experts // 2
    heads = HEADS // REPS
    part_width = heads * HEAD_DIM
    group_rows = SHARDS * tokens
    rep, shard = lax.axis_index("rep"), lax.axis_index("shard")
    a, c = rep // 2, lax.rem(rep, 2)
    z, y = shard // 2, lax.rem(shard, 2)
    rep_ref = rep.astype(jnp.int32).reshape(1)
    core_ref = c.astype(jnp.int32).reshape(1)
    near_shards = lax.rem(z + jnp.arange(LINE, dtype=jnp.int32), LINE)[:, None] * 2 + (
        y ^ jnp.arange(2, dtype=jnp.int32)[None, :]
    )
    near_shards = near_shards.reshape(SHARDS)
    shard_ids = jnp.arange(SHARDS, dtype=jnp.int32)
    place_of_shard = jnp.sum(
        jnp.where(near_shards[None, :] == shard_ids[:, None], shard_ids[None, :], 0), axis=1
    )

    order_row = priority[0]
    pair_ids = jnp.arange(pair_count, dtype=jnp.int32)
    place_of = jnp.sum(
        jnp.where(order_row[None, :] == pair_ids[:, None], pair_ids[None, :], 0), axis=1
    ).reshape(tokens, route_count)
    labels = jnp.arange(expert_count, dtype=jnp.int32)
    hits = routes.T[None, :, :] == labels[:, None, None]
    place_at = jnp.sum(jnp.where(hits, place_of.T[None], 0), axis=1)
    named = jnp.any(hits, axis=1)
    place_at = jnp.where(named, place_at, pair_count)
    earlier = jnp.sum((place_at[:, None, :] < place_at[:, :, None]).astype(jnp.int32), axis=2)
    ranks = jnp.where(named, earlier, -1).astype(bf16)
    ranks = jnp.concatenate([ranks, segments.astype(bf16)], axis=0)
    ranks = jnp.pad(ranks, ((0, 0), (0, rows_each - tokens)))
    ranks = jnp.stack([ranks, move(ranks, CORE_SWAP)])
    ranks = jnp.concatenate([ranks, move(ranks, X_SWAP)])
    segment_rows = ranks[:, expert_count, :tokens].astype(jnp.int32)

    inputs_across = move(inputs, X_SWAP)
    small_in = jnp.stack([attn_gain, query_gain, key_gain, ffn_gain])
    small_in = jnp.concatenate(
        [small_in, router_weight.T, ranks.reshape(REPS * (expert_count + 1), rows_each)], axis=0
    )
    in_pieces = gather_rows(
        thin_columns(in_proj, rep_ref, width), first=(inputs_across, segment_rows)
    )
    small_in, small_last = gather_small(small_in, (in_pieces[2][0], in_pieces[1][1], in_pieces[3][1]))
    ranks = small_in[:, 4 + expert_count :, :tokens]
    ranks = jnp.take(ranks, near_shards ^ shard, axis=0)
    ranks = ranks.reshape(SHARDS, REPS, expert_count + 1, tokens)[:, :, :expert_count]
    in_part = flat(in_pieces)

    small_in = jnp.take(small_in[:, : 4 + expert_count], shard_ids ^ shard, axis=0)
    small_in = small_in.transpose(1, 0, 2).reshape(4 + expert_count, width)
    gains = small_in[:4].astype(f32)
    router_rows = small_in[4:]
    part_gains = lax.dynamic_slice(
        gains[1:3].reshape(2, HEADS // 2, 2, HEAD_DIM),
        (0, c * heads, a, 0),
        (2, heads, 1, HEAD_DIM),
    ).reshape(2, part_width)

    hidden = inputs.astype(f32)
    home_rate = lax.rsqrt(jnp.mean(hidden * hidden, axis=-1, keepdims=True) + norm_eps)
    inputs_all = jnp.stack([inputs, inputs_across])
    inputs_all = jnp.stack([inputs_all, move(inputs_all, CORE_SWAP)], axis=1)
    inputs_all = inputs_all.reshape(REPS * tokens, width)
    inputs_all = pick_columns(inputs_all, near_shards, rows_each).astype(f32)
    unit_all = inputs_all * lax.rsqrt(
        jnp.mean(inputs_all * inputs_all, axis=-1, keepdims=True) + norm_eps
    )
    near_gain = jnp.take(gains[0].reshape(SHARDS, rows_each), near_shards, axis=0).reshape(width)
    normed_low = (unit_all * near_gain).astype(bf16)
    cot_across = move(grad_out, X_SWAP)
    normed_low = after(normed_low, cot_across)
    cot_own = after(grad_out, in_part)
    cot_own = lax.all_gather(cot_own, "shard", tiled=True)
    cos_table, sin_table = jax.vmap(rotary_tables)(segment_rows)
    sin_table = jnp.where(jnp.arange(HEAD_DIM) < HEAD_DIM // 2, -sin_table, sin_table)
    cos_table = cos_table.reshape(REPS * tokens, HEAD_DIM)
    sin_table = sin_table.reshape(REPS * tokens, HEAD_DIM)

    out_rows = rows_each // 4
    out_own = lax.dynamic_slice_in_dim(out_proj, rep * out_rows, out_rows, 0)
    out_own = after(out_own, small_last)

    projected = jnp.dot(normed_low, in_part, preferred_element_type=f32)
    squares = jnp.stack(
        [
            jnp.sum(projected[:, k * part_width : (k + 1) * part_width] ** 2, axis=1)
            for k in range(2)
        ],
        axis=1,
    )
    squares = rep_sum(squares.reshape(REPS, tokens, 2)).reshape(REPS * tokens, 2)
    pair_rate = lax.rsqrt(squares / width + norm_eps)
    attention_operands = (
        projected,
        pair_rate,
        part_gains,
        cos_table,
        sin_table,
        segment_rows.reshape(REPS * tokens, 1),
        segment_rows[:, None, :],
    )
    attended = attend(*attention_operands).reshape(2, 2, tokens, part_width)
    out_pieces = gather_rows(out_own, early=(projected,), late=lambda: (attended,))
    out_own = flat(out_pieces).reshape(SHARDS, out_rows, width)
    out_other = move(out_own, CORE_SWAP)
    out_part = jnp.where(
        c == 0,
        jnp.concatenate([out_own, out_other], axis=1),
        jnp.concatenate([out_other, out_own], axis=1),
    ).reshape(SHARDS * 2 * out_rows, width)
    attended = jnp.concatenate([attended[:, 0], move(attended[:, 1], CORE_SWAP)], axis=2)
    attended = attended.reshape(2 * tokens, 2 * part_width)
    head_of_place = ((near_shards // heads) ^ c) * heads + lax.rem(near_shards, heads)
    place_of_head = jnp.sum(
        jnp.where(head_of_place[None, :] == shard_ids[:, None], shard_ids[None, :], 0), axis=1
    )
    attended = pick_columns(attended, head_of_place, HEAD_DIM)
    mixed = jnp.dot(attended, out_part, preferred_element_type=f32).reshape(2, tokens, width)
    mixed_across = move(mixed[1].astype(bf16), X_SWAP)
    residual = hidden + mixed[0] + mixed_across.astype(f32)

    ffn_rate = lax.rsqrt(jnp.mean(residual * residual, axis=-1, keepdims=True) + norm_eps)
    ffn_unit = residual * ffn_rate
    ffn_low = (ffn_unit * gains[3]).astype(bf16)
    router_probs = softmax_rows(contract_cols(ffn_low, router_rows))

    ranks = after(ranks, mixed_across).astype(jnp.int32)
    counts = jnp.sum((ranks >= 0).astype(jnp.int32), axis=3)
    before = (near_shards[None, :] < near_shards[:, None])[:, :, None, None]
    bases = jnp.sum(jnp.where(before, counts[None], 0), axis=1)
    slots = bases[..., None] + ranks
    slots = jnp.where((ranks >= 0) & (slots < capacity), slots, -1)
    first_expert = shard * local_experts + c * core_experts
    slots = lax.dynamic_slice_in_dim(slots, first_expert, core_experts, 2)
    slots = slots.transpose(1, 2, 0, 3)
    shard_slots = jnp.take(slots, place_of_shard, axis=2)
    slots = slots.reshape(REPS, core_experts, group_rows)
    shard_slots = shard_slots.reshape(REPS, core_experts, group_rows)
    shifts = jnp.arange(core_experts, dtype=jnp.int32)[:, None] * capacity

    def columns_of(table):
        return jnp.where(table >= 0, table + shifts, -1).transpose(0, 2, 1)

    columns, shard_columns = columns_of(slots[:2]), columns_of(shard_slots[:2])

    def cot_part(group, rows, behind=()):
        return cotangent_part(core_ref, shard_slots[group], rows, down_weight, capacity, behind)

    first_ref = jnp.stack([c, first_expert]).astype(jnp.int32)

    def ffn_part(group, rows, slot_cot, behind=(), cost=QUIET):
        return forward_part(
            first_ref,
            slots[group],
            rows,
            router_rows,
            gate_weight,
            up_weight,
            slot_cot,
            behind,
            cost,
        )

    made = {}

    def fill_cot(follow):
        beside = move(cot_own, CORE_SWAP)
        own_part = cot_part(0, cot_own, (follow,))
        made["cot"] = [own_part, cot_part(1, beside, (own_part[1],))]
        return [own_part[1]]

    ffn_pieces = gather_rows(
        ffn_low, fill=fill_cot, late=lambda: (made["cot"][1][1],)
    )
    near_cot = made["cot"]
    ffn_own = flat(ffn_pieces)
    ffn_beside = move(ffn_own, CORE_SWAP)
    ffn_far = [move(jnp.concatenate(pair, axis=0), X_SWAP) for pair in ffn_pieces]
    cot_across = lax.all_gather(after(cot_across, ffn_pieces[2][0]), "shard", tiled=True)

    near = [ffn_part(0, ffn_own, near_cot[0][1])]
    near.append(ffn_part(1, ffn_beside, near_cot[1][1], (near[0][1],)))

    def rows_back(group, behind=()):
        _, _, grad_gate, grad_up, scores = near[group]
        return backward_part(
            core_ref, columns[group], grad_gate, grad_up, scores, gate_weight, up_weight, behind
        ).reshape(SHARDS, tokens, -1)

    grad_other = rows_back(1, (ffn_far[0], ffn_far[1]))
    grad_own = rows_back(0, (grad_other,))
    grad_other = move(grad_other, CORE_SWAP)

    def routed_rows(group, extra, behind):
        return routed_part(
            core_ref, shard_columns[group], near[group][1], down_weight, extra, behind
        )

    def fill_routed_other(follow):
        made["routed_other"] = routed_rows(1, (), follow + (ffn_far[2], cot_across))
        return [made["routed_other"]]

    def fill_far_cot(follow):
        made["far_cot"] = cot_part(2, cot_across, follow)
        return [made["far_cot"][1]]

    def fill_routed_own(follow):
        extra = (move(made["routed_other"], CORE_SWAP),)
        made["routed"] = routed_rows(0, extra, follow)
        return [made["routed"]]

    def fill_other_cot(follow):
        rows = move(after(cot_across, made["routed"]), CORE_SWAP)
        made["other_cot"] = cot_part(3, rows, follow)
        return [made["other_cot"][1]]

    grad_home = scatter_rows(
        [lambda place: grad_own[place], lambda place: grad_other[place]],
        [fill_routed_other, fill_routed_own, fill_far_cot, fill_other_cot, None],
    )
    routed = lax.psum_scatter(
        after(made["routed"], grad_home), "shard", scatter_dimension=0, tiled=True
    )
    ffn_far = jnp.concatenate([after(part, made["other_cot"][1]) for part in ffn_far], axis=0)
    ffn_far = [ffn_far, move(ffn_far, CORE_SWAP)]

    grad_ffn_home = grad_home[:, :width]
    home_score = grad_home[:, width : width + expert_count].astype(f32)
    grad_logits = home_score - router_probs * jnp.sum(home_score, axis=1, keepdims=True)
    grad_logits_low = grad_logits.astype(bf16)

    grad_ffn_in = grad_ffn_home.astype(f32) + jnp.dot(
        grad_logits_low, router_rows, preferred_element_type=f32
    )
    grad_router_local = contract_rows(grad_logits_low, ffn_low)
    grad_ffn_local = jnp.sum(grad_ffn_in * ffn_unit, axis=0)
    scaled = gains[3] * grad_ffn_in
    grad_residual = grad_out.astype(f32) + ffn_rate * (
        scaled - ffn_unit * jnp.mean(scaled * ffn_unit, axis=-1, keepdims=True)
    )
    residual_low = grad_residual.astype(bf16)
    residual_other = move(residual_low, X_SWAP)
    residual_pair = jnp.concatenate([residual_low, residual_other], axis=0)

    grad_attended = contract_cols(residual_pair, out_part).astype(bf16)
    grad_attended = pick_columns(grad_attended, place_of_head, HEAD_DIM)
    grad_attended = grad_attended.reshape(2, tokens, 2 * part_width)
    mine, theirs = grad_attended[:, :, :part_width], grad_attended[:, :, part_width:]
    grad_attended = jnp.stack([mine, move(theirs, CORE_SWAP)], axis=1)
    grad_attended = grad_attended.reshape(REPS * tokens, part_width)
    grad_pair, grad_value, dots, grad_pair_gain = attend_back(*attention_operands, grad_attended)
    grad_pair_gain = jnp.sum(grad_pair_gain, axis=0).reshape(2, heads, HEAD_DIM)
    dots = rep_sum(dots.reshape(REPS, tokens, 2)).reshape(REPS * tokens, 2) / width
    grad_projected = join_grads(projected, pair_rate, grad_pair, grad_value, dots, REPS)

    grad_in_part = contract_rows(normed_low, grad_projected).astype(bf16)
    grad_in_part = grad_in_part.reshape(SHARDS, rows_each, 3 * part_width)
    grad_normed = contract_cols(grad_projected, in_part)
    grad_attn_part = jnp.sum(grad_normed * unit_all, axis=0)

    pair_gains = jnp.zeros((2, HEADS // 2, 2, HEAD_DIM), f32)
    pair_gains = lax.dynamic_update_slice(
        pair_gains, grad_pair_gain[:, :, None], (0, c * heads, a, 0)
    )
    small = jnp.concatenate(
        [grad_ffn_local[None], pair_gains.reshape(2, width), grad_router_local], axis=0
    )
    small = jnp.take(small.reshape(-1, SHARDS, rows_each), near_shards, axis=1)
    small = jnp.concatenate([grad_attn_part.reshape(1, SHARDS, rows_each), small], axis=0)
    small = jnp.pad(small, ((0, HEAD_DIM - small.shape[0]), (0, 0), (0, 0)))
    small = small.astype(bf16).transpose(1, 2, 0)

    grad_out_part = contract_rows(after(attended, grad_projected), residual_pair).astype(bf16)
    out_parts = grad_out_part.reshape(SHARDS, 2, out_rows, width)
    out_own = lax.dynamic_index_in_dim(out_parts, c, 1, keepdims=False)
    out_other = lax.dynamic_index_in_dim(out_parts, 1 - c, 1, keepdims=False)
    out_sum = added(out_own, move(out_other, CORE_SWAP))
    out_sum = jnp.take(out_sum, place_of_shard, axis=0).reshape(SHARDS * out_rows, width)

    far_cot = [made["far_cot"], made["other_cot"]]

    def fill_far(follow):
        made["far"] = ffn_part(
            2, ffn_far[0], far_cot[0][1], follow + (ffn_far[1],), LOUD
        )
        return [made["far"][3]]

    normed_other = grad_normed.astype(bf16).reshape(2, 2, tokens, width)
    normed_mine = added(normed_other[:, 0], move(normed_other[:, 1], CORE_SWAP))
    normed_across = move(normed_mine[1], X_SWAP)

    def fill_other(follow):
        made["other"] = ffn_part(
            3, ffn_far[1], far_cot[1][1], follow + (made["far"][3], normed_mine, routed, out_sum), LOUD
        )
        return [made["other"][3]]

    def weight_grad(left, right, follow):
        first, *follow = lax.optimization_barrier((left[0],) + follow)
        left = jnp.concatenate([first] + left[1:], axis=1)
        right = jnp.concatenate(right, axis=1)
        grad = jnp.einsum("ecd,ecf->edf", left, right, preferred_element_type=f32).astype(bf16)
        return grad, follow

    def groups(index):
        return [part[index] for part in (near[0], near[1], made["far"], made["other"])]

    def fence(follow):
        return [made["other"][3]]

    out_home = lax.psum_scatter(
        after(out_sum, routed), "shard", scatter_dimension=0, tiled=True
    )

    def fill_weights(follow):
        cots = [part[0] for part in near_cot + far_cot]
        reduced, first, second, third = follow
        down, _ = weight_grad(groups(1), cots, ())
        gate, (down, first, reduced, _) = weight_grad(
            groups(0), groups(2), (down, first, reduced, normed_across)
        )
        up, (gate, second, third, home) = weight_grad(
            groups(0), groups(3), (gate, second, third, out_home)
        )
        made["down"], made["gate"], made["up"], made["home"] = down, gate, up, home
        return reduced, first, second, third

    in_sum = scatter_rows(
        [lambda place: jnp.concatenate([grad_in_part[place], small[place]], axis=1)],
        [fill_far, fill_other, fence, fence, fill_weights],
        hold=True,
    )
    in_other = move(in_sum, X_SWAP)
    grad_up, out_home = made["up"], made["home"]
    down_all = widen(
        made["down"], move(made["down"], CORE_SWAP), core_ref, (grad_up,)
    )
    in_all = jnp.stack([in_sum, after(in_other, down_all)])
    in_beside = move(in_all, CORE_SWAP)
    out_across = move(after(out_home, down_all), X_SWAP)
    gate_all = widen(
        made["gate"], move(made["gate"], CORE_SWAP), core_ref, (down_all, out_across)
    )
    in_all = jnp.stack([in_all, in_beside], axis=1).reshape((REPS,) + in_sum.shape)
    grad_in = weave_columns(in_all, rep_ref, 3 * part_width, (gate_all,))
    small = jnp.sum(in_all[:, :, 3 * part_width :].astype(f32), axis=0).T
    up_all = widen(grad_up, move(grad_up, CORE_SWAP), core_ref, (gate_all,))

    outputs = (residual + after(routed, down_all).astype(f32)).astype(bf16)
    grad_normed = after(added(normed_mine[0], normed_across), down_all)
    grad_normed = pick_columns(grad_normed, place_of_shard, rows_each).astype(f32)
    home_unit = hidden * home_rate
    scaled = gains[0] * grad_normed
    grad_inputs = (
        grad_residual
        + home_rate * (scaled - home_unit * jnp.mean(scaled * home_unit, axis=-1, keepdims=True))
    ).astype(bf16)

    out_sum = jnp.stack([out_home, out_across])
    out_sum = jnp.stack([out_sum, move(out_sum, CORE_SWAP)], axis=1)
    out_sum = out_sum.reshape(REPS, out_rows, width)
    out_sum = jnp.take(out_sum, rep ^ jnp.arange(REPS, dtype=jnp.int32), axis=0)
    grad_out_proj = out_sum.reshape(rows_each, width).astype(f32)
    return (
        outputs,
        grad_inputs,
        small[0],
        grad_in,
        small[2],
        small[3],
        grad_out_proj,
        small[1],
        small[4 : 4 + expert_count].T,
        gate_all,
        up_all,
        down_all,
    )


def solution(mesh):
    fits = dict(mesh.shape) == {"rep": REPS, "shard": SHARDS}
    body = fast_local if fits else local
    in_specs = (
        P(("rep", "shard"), None),
        P("shard"),
        P("shard", None),
        P("shard"),
        P("shard"),
        P("shard", None),
        P("shard"),
        P("shard", None),
        P("shard", None, None),
        P("shard", None, None),
        P("shard", None, None),
        P(("rep", "shard"), None),
        P(("rep", "shard"), None),
        P(("rep", "shard"), None),
        P(("rep", "shard"), None),
    )
    out_specs = (
        P(("rep", "shard"), None),
        P(("rep", "shard"), None),
        P("shard"),
        P("shard", None),
        P("shard"),
        P("shard"),
        P("shard", None),
        P("shard"),
        P("shard", None),
        P("shard", None, None),
        P("shard", None, None),
        P("shard", None, None),
    )
    return jax.shard_map(body, mesh=mesh, in_specs=in_specs, out_specs=out_specs, check_vma=False)
```
